32 devices in a mesh: proto: 8 (over y, x, core), batch: 4 (over z).
Axes of the slice: x: 2, y: 2, z: 4, core: 2. Of those that a mesh axis runs over, the one named last changes fastest.
Arguments:
- teacher_feats: bfloat16 [1024, 512], P('batch'), may hold values from -200 to 200
- student_feats: bfloat16 [1024, 512], P('batch'), may hold values from -200 to 200
- proto_weight: bfloat16 [512, 65536], P(None, 'proto'), may hold values from -40 to 40
Outputs:
- grad_weight: bfloat16 [512, 65536], P('batch', 'proto')
- grad_student: float32 [1024, 512], P('batch')
- loss: float32 [], replicated
The draws below stay inside these ranges and needn't reach their ends.
All inputs are finite; a program needn't handle non-finite values.
Results may differ from the reference program's by a relative error of at most 0.012.
Values may be sent and summed in bfloat16 or wider, within the bound.
No kernel may reach another device: no remote copies, remote signals or barrier semaphores. Data moves between devices by JAX's collectives and lax.ppermute only.
A program may use at most 128 MiB of HBM per device.

```python
import math
import jax
import jax.numpy as jnp
from jax import lax

BOT = 512
ROW_DEV = 256
SWEEPS = 3
ROWS = 1024
PROTOS = 65536
N_BATCH = 4


def draw_proto_weight(key, part):
    key = jax.random.fold_in(key, 11)
    first, second = jax.random.split(key)
    ramp = 0.6 + 1.2 * jnp.arange(PROTOS, dtype=jnp.float32) / PROTOS
    spread = jnp.exp(jax.random.uniform(second, (PROTOS,), jnp.float32, -0.6, 0.6))
    values = jax.random.normal(first, (BOT, PROTOS), jnp.float32) / math.sqrt(BOT) * (ramp * spread)[None, :]
    return values.astype(jnp.bfloat16)


def feature_rows(key):
    values = jax.random.normal(key, (ROWS, BOT), jnp.float32)
    return values.astype(jnp.bfloat16)


def draw_teacher_feats(key, part):
    key = jax.random.fold_in(key, 21)
    return feature_rows(key)


def draw_student_feats(key, part):
    key = jax.random.fold_in(key, 31)
    return feature_rows(key)


def setup_inputs(seed: int = 0) -> dict:
    streams_of = jax.random.split(jax.random.key(seed), 4)
    return {
        "teacher_feats": draw_teacher_feats(jax.random.fold_in(streams_of[3], 71), 0),
        "student_feats": draw_student_feats(jax.random.fold_in(streams_of[3], 71), 0),
        "proto_weight": draw_proto_weight(jax.random.fold_in(streams_of[3], 71), 0),
    }


TEMP_TEACHER = 0.04
TEMP_STUDENT = 0.1

def unit_rows(values):
    wide = values.astype(jnp.float32)
    length = jnp.sqrt(lax.optimization_barrier(jnp.sum(wide * wide, axis=-1, keepdims=True)) + 1e-06)
    return (wide / length, length)

def reference(teacher_feats, student_feats, proto_weight):
    teacher_unit, _ = unit_rows(teacher_feats)
    teacher_half = teacher_unit.astype(jnp.bfloat16).reshape(N_BATCH, ROW_DEV, BOT)

    def teacher_block(block):
        logits = jnp.dot(block, proto_weight, preferred_element_type=jnp.float32) / TEMP_TEACHER
        top = lax.optimization_barrier(jnp.max(logits, axis=1, keepdims=True))
        raised = jnp.exp(logits - top)
        return raised / lax.optimization_barrier(jnp.sum(raised, axis=1, keepdims=True))
    prob = lax.map(teacher_block, teacher_half).reshape(ROWS, PROTOS)
    row_scale = jnp.ones((ROWS,), jnp.float32)
    col_scale = jnp.ones((PROTOS,), jnp.float32)
    for sweep in range(SWEEPS):
        col_scale = 1.0 / jnp.dot(row_scale, prob, precision=lax.Precision.HIGHEST)
        row_scale = 1.0 / jnp.dot(prob, col_scale, precision=lax.Precision.HIGHEST)

    def block_step(carry, start):
        grad_sum, loss_sum = carry
        inputs = lax.dynamic_slice(student_feats, (start, jnp.int32(0)), (ROW_DEV, BOT))
        student_unit, student_len = unit_rows(inputs)
        student_half = student_unit.astype(jnp.bfloat16)
        partner = ((start + ROWS // 2) % ROWS).astype(jnp.int32)
        prob_rows = lax.dynamic_slice(prob, (partner, jnp.int32(0)), (ROW_DEV, PROTOS))
        scale_rows = lax.dynamic_slice(row_scale, (partner,), (ROW_DEV,))
        paired = prob_rows * scale_rows[:, None] * col_scale[None, :]
        student_logits = jnp.dot(student_half, proto_weight, preferred_element_type=jnp.float32) / TEMP_STUDENT
        smax = lax.optimization_barrier(jnp.max(student_logits, axis=1, keepdims=True))
        log_total = smax + jnp.log(lax.optimization_barrier(jnp.sum(jnp.exp(student_logits - smax), axis=1, keepdims=True)))
        student_prob = jnp.exp(student_logits - log_total)
        loss_sum = loss_sum + jnp.sum(paired * (log_total - student_logits))
        dlogits = (PROTOS * (student_prob - paired)).astype(jnp.bfloat16)
        grad_sum = grad_sum + jnp.dot(student_half.T, dlogits, preferred_element_type=jnp.float32)
        back_sum = jnp.dot(dlogits, proto_weight.T, preferred_element_type=jnp.float32)
        grad_rows = (back_sum - student_unit * lax.optimization_barrier(jnp.sum(student_unit * back_sum, axis=-1, keepdims=True))) / student_len
        return ((grad_sum, loss_sum), grad_rows)
    starts = jnp.arange(N_BATCH, dtype=jnp.int32) * ROW_DEV
    init = (jnp.zeros((BOT, PROTOS), jnp.float32), jnp.zeros((), jnp.float32))
    (grad_sum, loss_sum), grad_blocks = lax.scan(block_step, init, starts)
    grad_student = grad_blocks.reshape(ROWS, BOT)
    return (grad_sum.astype(jnp.bfloat16), grad_student, loss_sum / ROWS)
```

```python
import functools
import math

import jax
import jax.numpy as jnp
from jax import lax
from jax.experimental import pallas as pl
from jax.experimental.pallas import tpu as pltpu
from jax.sharding import PartitionSpec as P

SWEEPS = 3
TEMP_TEACHER = 0.04
TEMP_STUDENT = 0.1
LOG2E = math.log2(math.e)
SCALE_TEACHER = LOG2E / TEMP_TEACHER
SCALE_STUDENT = LOG2E / TEMP_STUDENT
LANES = 128
GROUP = 128
TILE = 256
F32 = jnp.float32
BF16 = jnp.bfloat16


def unit_rows(values):
    wide = values.astype(F32)
    length = jnp.sqrt(jnp.sum(wide * wide, axis=-1, keepdims=True) + 1e-06)
    return wide / length, length


def diagonal():
    shape = (LANES, LANES)
    return lax.broadcasted_iota(jnp.int32, shape, 0) == lax.broadcasted_iota(jnp.int32, shape, 1)


def to_column(row):
    spread = jnp.where(diagonal(), jnp.broadcast_to(row, (LANES, LANES)), 0.0)
    return jnp.sum(spread, axis=1, keepdims=True)


def to_row(column):
    spread = jnp.where(diagonal(), jnp.broadcast_to(column, (LANES, LANES)), 0.0)
    return jnp.sum(spread, axis=0, keepdims=True)


def spread_rows(ref, rows):
    for a in range(rows.shape[0]):
        ref[a * LANES : (a + 1) * LANES, :] = jnp.broadcast_to(
            to_column(rows[a : a + 1, :]), (LANES, LANES)
        )


def pack_rows(ref, columns):
    for a in range(columns.shape[0] // LANES):
        ref[a : a + 1, :] = to_row(columns[a * LANES : (a + 1) * LANES, :])


def lane_tiles(values):
    return [values[:, t * LANES : (t + 1) * LANES] for t in range(values.shape[1] // LANES)]


def fold(values):
    return functools.reduce(jnp.add, lane_tiles(values))


def column_sums(values):
    rows, cols = values.shape
    return jnp.sum(values.reshape(rows // 8, 8, cols), axis=0)


def tree(values):
    while len(values) > 1:
        values = [a + b for a, b in zip(values[::2], values[1::2])]
    return values[0]


def nt_dot(a, b):
    return lax.dot_general(a, b, (((1,), (1,)), ((), ())), preferred_element_type=F32)


def groups_of(total):
    return [slice(g * GROUP, (g + 1) * GROUP) for g in range(total // GROUP)]


def unit_kernel(place_ref, t_ref, s_ref, t_unit, s_unit, t_half, s_half):
    half = t_half.shape[0]
    mine = pl.ds(pl.multiple_of(place_ref[2] * half, half), half)
    for raw, unit, part in ((t_ref, t_unit, t_half), (s_ref, s_unit, s_half)):
        unit[...] = unit_rows(raw[...])[0].astype(BF16)
        part[...] = unit[mine, :]


def stats_kernel(t_ref, s_ref, w_ref, out_ref, top, total):
    step = pl.program_id(0)

    @pl.when(step == 0)
    def _():
        top[...] = jnp.full(top.shape, -1e30, F32)
        total[...] = jnp.zeros(total.shape, F32)

    for which, (unit, scale) in enumerate(((t_ref, SCALE_TEACHER), (s_ref, SCALE_STUDENT))):
        logits = jnp.dot(unit[...], w_ref[...], preferred_element_type=F32) * scale
        tiles = lane_tiles(logits)
        old = top[which]
        new = functools.reduce(jnp.maximum, tiles, old)
        sums = total[which] * jnp.exp2(old - new)
        for tile in tiles:
            sums = sums + jnp.exp2(tile - new)
        top[which] = new
        total[which] = sums

    @pl.when(step == pl.num_programs(0) - 1)
    def _():
        quarter = out_ref.shape[0] // 4
        for which in range(2):
            lanes = top[which]
            peak = jnp.max(lanes, axis=1, keepdims=True)
            sums = jnp.sum(total[which] * jnp.exp2(lanes - peak), axis=1, keepdims=True)
            for k, column in enumerate((peak, sums)):
                first = (2 * which + k) * quarter
                pack_rows(out_ref.at[first : first + quarter], column)


def merge_kernel(*refs):
    *stats, out_ref = refs
    out_ref[...] = jnp.zeros(out_ref.shape, F32)
    quarter = stats[0].shape[0] // 4
    for which in range(2):
        first = 2 * which * quarter
        tops = [ref[first : first + quarter, :] for ref in stats]
        top = functools.reduce(jnp.maximum, tops)
        total = tree(
            [
                ref[first + quarter : first + 2 * quarter, :] * jnp.exp2(peak - top)
                for ref, peak in zip(stats, tops)
            ]
        )
        out_ref[which * quarter : (which + 1) * quarter, :] = top + jnp.log2(total)


def gather_units(place_ref, unit, own_ref, mine, other):
    own = own_ref.shape[0]
    half = own // 2
    unit[:own, :] = own_ref[...]
    core = place_ref[2]
    for g, (a, b) in enumerate(zip(mine, other)):
        start = (g + 1) * own
        unit[pl.ds(pl.multiple_of(start + core * half, half), half), :] = a[...]
        unit[pl.ds(pl.multiple_of(start + (1 - core) * half, half), half), :] = b[...]


def spread_logs(lse, logs, which, shift=0.0):
    quarter = lse.shape[0] // (len(logs) * LANES)
    own = quarter * LANES
    for g, ref in enumerate(logs):
        rows = ref[which * quarter : (which + 1) * quarter, :] - shift
        spread_rows(lse.at[g * own : (g + 1) * own], rows)


def probabilities(unit, w_ref, lse, logits, scale, prob_ref, after):
    rows = unit.shape[0]
    count = w_ref.shape[1] // TILE

    def product(n):
        logits[n % 2] = jnp.dot(
            unit[...], w_ref[:, n * TILE : (n + 1) * TILE], preferred_element_type=F32
        )

    product(0)
    for n in range(count):
        if n + 1 < count:
            product(n + 1)
        here = slice(n * TILE, (n + 1) * TILE)
        sums = jnp.zeros((8, TILE), F32)
        for g in groups_of(rows):
            shift = lse[g, :]
            prob = jnp.concatenate(
                [jnp.exp2(tile * scale - shift) for tile in lane_tiles(logits[n % 2, g, :])], axis=1
            )
            if after is not None:
                sums = sums + column_sums(prob)
            prob_ref[g, here] = prob.astype(BF16)
        if after is not None:
            after(here, 1.0 / jnp.sum(sums, axis=0, keepdims=True))


def add_row_sums(rows, prob_ref, here, scale):
    for g in groups_of(rows.shape[0]):
        rows[g, :] += fold(prob_ref[g, here].astype(F32) * scale)


def teacher_kernel(groups, place_ref, own_ref, *refs):
    mine, refs = refs[: groups - 1], refs[groups - 1 :]
    other, refs = refs[: groups - 1], refs[groups - 1 :]
    logs, refs = refs[:groups], refs[groups:]
    w_ref, prob_ref, sums_ref, unit, lse, rows, logits = refs
    step = pl.program_id(0)

    @pl.when(step == 0)
    def _():
        gather_units(place_ref, unit, own_ref, mine, other)
        spread_logs(lse, logs, 0)
        rows[...] = jnp.zeros(rows.shape, F32)

    probabilities(
        unit, w_ref, lse, logits, SCALE_TEACHER, prob_ref,
        lambda here, scale: add_row_sums(rows, prob_ref, here, scale),
    )

    @pl.when(step == pl.num_programs(0) - 1)
    def _():
        pack_rows(sums_ref, jnp.sum(rows[...], axis=1, keepdims=True))


def row_scales(sums, tiles):
    return 1.0 / tree([ref[:tiles, :] for ref in sums])


def sweep(prob_ref, weight, rows, use):
    for n in range(prob_ref.shape[1] // TILE):
        here = slice(n * TILE, (n + 1) * TILE)
        sums = jnp.zeros((8, TILE), F32)
        for g in groups_of(prob_ref.shape[0]):
            shift = weight[g, :]
            tiles = lane_tiles(prob_ref[g, here].astype(F32))
            sums = sums + column_sums(jnp.concatenate([tile * shift for tile in tiles], axis=1))
        scale = 1.0 / jnp.sum(sums, axis=0, keepdims=True)
        add_row_sums(rows, prob_ref, here, scale)
        if use is not None:
            use(here, scale)


def sweep_kernel(parts, prob_ref, *refs):
    sums, (sums_ref, weight, rows) = refs[:parts], refs[parts:]
    step = pl.program_id(0)

    @pl.when(step == 0)
    def _():
        spread_rows(weight, row_scales(sums, sums_ref.shape[0]))
        rows[...] = jnp.zeros(rows.shape, F32)

    sweep(prob_ref, weight, rows, None)

    @pl.when(step == pl.num_programs(0) - 1)
    def _():
        pack_rows(sums_ref, jnp.sum(rows[...], axis=1, keepdims=True))


def split_rows(place_ref, back, outs):
    for s, out in enumerate(outs):
        share = out.shape[0]
        start = jnp.bitwise_xor(place_ref[1], s) * share
        out[...] = back[pl.ds(pl.multiple_of(start, share), share), :].astype(BF16)


def last_sweep_kernel(parts, place_ref, prob_ref, w_ref, s_ref, *refs):
    sums, refs = refs[:parts], refs[parts:]
    sums_ref, scale_ref, *outs = refs[: 2 + parts]
    weight, rows, back, scaled = refs[2 + parts :]
    step = pl.program_id(0)
    total_rows, own = prob_ref.shape[0], back.shape[0]
    tiles = total_rows // LANES

    @pl.when(step == 0)
    def _():
        spread_rows(weight, row_scales(sums, tiles))
        rows[...] = jnp.zeros(rows.shape, F32)
        back[...] = jnp.zeros(back.shape, F32)

    partner = slice(total_rows // 2, total_rows // 2 + own)

    def use(here, scale):
        scale_ref[:, here] = scale
        scaled[:, here] = (prob_ref[partner, here].astype(F32) * scale).astype(BF16)

    sweep(prob_ref, weight, rows, use)
    back[...] += nt_dot(scaled[...], w_ref[...])

    @pl.when(step == pl.num_programs(0) - 1)
    def _():
        sums_ref[...] = jnp.zeros(sums_ref.shape, F32)
        pack_rows(sums_ref.at[:tiles], jnp.sum(rows[...], axis=1, keepdims=True))
        split_rows(place_ref, back, outs)
        inner = jnp.sum(s_ref[...].astype(F32) * back[...], axis=1, keepdims=True)
        pack_rows(sums_ref.at[tiles : tiles + own // LANES], inner)


def student_kernel(parts, groups, log_protos, place_ref, own_ref, *refs):
    mine, refs = refs[: groups - 1], refs[groups - 1 :]
    other, refs = refs[: groups - 1], refs[groups - 1 :]
    logs, refs = refs[:groups], refs[groups:]
    w_ref, grad_ref, feat_ref, *refs = refs
    outs, refs = refs[:parts], refs[parts:]
    unit, turned, lse, prob, back, logits = refs
    step = pl.program_id(0)
    feats, own = feat_ref.shape[0], back.shape[0]

    @pl.when(step == 0)
    def _():
        gather_units(place_ref, unit, own_ref, mine, other)
        for g in groups_of(unit.shape[0]):
            turned[:, g] = jnp.transpose(unit[g, :].astype(F32)).astype(BF16)
        feat_ref[...] = turned[pl.ds(pl.multiple_of(place_ref[0] * feats, feats), feats), :]
        spread_logs(lse, logs, 1, log_protos)
        back[...] = jnp.zeros(back.shape, F32)

    probabilities(unit, w_ref, lse, logits, SCALE_STUDENT, prob, None)
    grad_ref[...] = jnp.dot(feat_ref[...], prob[...], preferred_element_type=F32)
    back[...] += nt_dot(prob[:own, :], w_ref[...])

    @pl.when(step == pl.num_programs(0) - 1)
    def _():
        split_rows(place_ref, back, outs)


def grad_kernel(parts, protos, prob_ref, feat_ref, part_ref, scale_ref, *refs):
    sums, (out_ref, scaled) = refs[:parts], refs[parts:]

    @pl.when(pl.program_id(0) == 0)
    def _():
        tiles = prob_ref.shape[0] // LANES
        rows = row_scales(sums, tiles) * protos
        for a in range(tiles):
            other = (a + tiles // 2) % tiles
            feat = feat_ref[:, other * LANES : (other + 1) * LANES].astype(F32)
            scaled[:, a * LANES : (a + 1) * LANES] = (feat * rows[a : a + 1, :]).astype(BF16)

    paired = jnp.dot(scaled[...], prob_ref[...], preferred_element_type=F32)
    out_ref[...] = (part_ref[...] - paired * scale_ref[...]).astype(BF16)


def loss_part_kernel(parts, tiles, *refs):
    sums, (logs_ref, out_ref) = refs[:parts], refs[parts:]
    quarter = logs_ref.shape[0] // 4
    total = tree([ref[...] for ref in sums])
    first = tiles // 2
    scale = 1.0 / total[first : first + quarter, :]
    inner = total[tiles : tiles + quarter, :]
    log_total = logs_ref[quarter : 2 * quarter, :] / LOG2E
    terms = log_total - scale * inner / TEMP_STUDENT
    out_ref[...] = jnp.broadcast_to(jnp.sum(terms), out_ref.shape)


def rows_kernel(parts, protos, place_ref, s_ref, *refs):
    student, paired, sums = refs[:parts], refs[parts : 2 * parts], refs[2 * parts : 3 * parts]
    out_ref, weight = refs[3 * parts :]
    share, quarter = out_ref.shape[0], weight.shape[0] // LANES
    tiles = sums[0].shape[0] - 8
    scale = 1.0 / tree([ref[tiles // 2 : tiles // 2 + quarter, :] for ref in sums])
    spread_rows(weight, scale)
    mine = pl.ds(pl.multiple_of(place_ref[1] * share, share), share)
    factor = weight[mine, :1] * protos
    total = tree([ref[...].astype(F32) for ref in student])
    total = total - tree([ref[...].astype(F32) for ref in paired]) * factor
    unit, length = unit_rows(s_ref[mine, :])
    out_ref[...] = (total - unit * jnp.sum(unit * total, axis=-1, keepdims=True)) / length


def join_kernel(place_ref, *refs):
    *blocks, out_ref = refs
    for s, ref in enumerate(blocks):
        share = ref.shape[0]
        start = jnp.bitwise_xor(place_ref[1], s) * share
        out_ref[pl.ds(pl.multiple_of(start, share), share), :] = ref[...]


def whole(array):
    rank = len(array.shape)
    return pl.BlockSpec(array.shape, lambda i: (0,) * rank)


def fixed(*shape):
    return pl.BlockSpec(shape, lambda i: (0,) * len(shape))


def columns(rows, cols):
    return pl.BlockSpec((rows, cols), lambda i: (0, i))


SMEM = pl.BlockSpec(memory_space=pltpu.SMEM)
VMEM = pl.BlockSpec(memory_space=pltpu.VMEM)


def params(mib=None):
    if mib is None:
        return pltpu.CompilerParams()
    return pltpu.CompilerParams(
        dimension_semantics=("arbitrary",), vmem_limit_bytes=mib * 2**20
    )


def cost(flops, nbytes, exps=0):
    return pl.CostEstimate(flops=int(flops), bytes_accessed=int(nbytes), transcendentals=int(exps))


def swapped(values, axis):
    n = lax.axis_size(axis)
    return [values[0]] + [
        lax.ppermute(values[s], axis, [(i, i ^ s) for i in range(n)]) for s in range(1, n)
    ]


def following(value, axis):
    n = lax.axis_size(axis)
    return [lax.ppermute(value, axis, [(i, (i - s) % n) for i in range(n)]) for s in range(1, n)]


def gathered(half):
    mine = following(half, "batch")
    pairs = [(i, i ^ 1) for i in range(lax.axis_size("proto"))]
    return mine + [lax.ppermute(part, "proto", pairs) for part in mine]


def local(teacher_feats, student_feats, proto_weight):
    parts, groups = lax.axis_size("proto"), lax.axis_size("batch")
    own, width = teacher_feats.shape
    local_protos = proto_weight.shape[1]
    rows = own * groups
    protos = local_protos * parts
    feats = width // groups
    share = own // parts
    tiles = rows // LANES
    place = jnp.stack(
        [lax.axis_index("batch"), lax.axis_index("proto"), lax.axis_index("proto") % 2]
    ).astype(jnp.int32)
    struct = jax.ShapeDtypeStruct
    spread = pltpu.VMEM((rows, LANES), F32)
    weight_bytes = 2 * width * local_protos
    prob_bytes = 2 * rows * local_protos

    unit = struct((own, width), BF16)
    half = struct((own // 2, width), BF16)
    teacher, student, teacher_half, student_half = pl.pallas_call(
        unit_kernel,
        in_specs=[SMEM, VMEM, VMEM],
        out_shape=[unit, unit, half, half],
        cost_estimate=cost(8 * own * width, 6 * own * width),
        name="unit_rows",
    )(place, teacher_feats, student_feats)
    teacher_all = gathered(teacher_half)
    student_all = gathered(student_half)

    chunk = 1024
    grid = (local_protos // chunk,)
    stats = pl.pallas_call(
        stats_kernel,
        grid=grid,
        in_specs=[whole(teacher), whole(student), columns(width, chunk)],
        out_specs=fixed(4 * own // LANES, LANES),
        out_shape=struct((4 * own // LANES, LANES), F32),
        scratch_shapes=[pltpu.VMEM((2, own, LANES), F32), pltpu.VMEM((2, own, LANES), F32)],
        compiler_params=params(56),
        cost_estimate=cost(4 * own * width * local_protos, weight_bytes),
        name="row_stats",
    )(teacher, student, proto_weight)
    logs = pl.pallas_call(
        merge_kernel, out_shape=struct(stats.shape, F32), name="merge_stats"
    )(*swapped([stats] * parts, "proto"))
    logs_all = [logs] + following(logs, "batch")

    sums_struct = struct((tiles, LANES), F32)
    prob, sums = pl.pallas_call(
        functools.partial(teacher_kernel, groups),
        grid=grid,
        in_specs=[SMEM, whole(teacher)]
        + [whole(x) for x in teacher_all]
        + [whole(x) for x in logs_all]
        + [columns(width, chunk)],
        out_specs=[columns(rows, chunk), fixed(tiles, LANES)],
        out_shape=[struct((rows, local_protos), BF16), sums_struct],
        scratch_shapes=[
            pltpu.VMEM((rows, width), BF16), spread, spread, pltpu.VMEM((2, rows, TILE), F32),
        ],
        compiler_params=params(56),
        cost_estimate=cost(2 * rows * width * local_protos, prob_bytes),
        name="teacher_prob",
    )(place, teacher, *teacher_all, *logs_all, proto_weight)

    block = struct((share, width), BF16)
    grad_part, feat, *back_student = pl.pallas_call(
        functools.partial(student_kernel, parts, groups, math.log2(protos)),
        grid=grid,
        in_specs=[SMEM, whole(student)]
        + [whole(x) for x in student_all]
        + [whole(x) for x in logs_all]
        + [columns(width, chunk)],
        out_specs=[columns(feats, chunk), fixed(feats, rows)] + [fixed(share, width)] * parts,
        out_shape=[struct((feats, local_protos), F32), struct((feats, rows), BF16)]
        + [block] * parts,
        scratch_shapes=[
            pltpu.VMEM((rows, width), BF16),
            pltpu.VMEM((width, rows), BF16),
            spread,
            pltpu.VMEM((rows, chunk), BF16),
            pltpu.VMEM((own, width), F32),
            pltpu.VMEM((2, rows, TILE), F32),
        ],
        compiler_params=params(56),
        cost_estimate=cost(3 * rows * width * local_protos, weight_bytes),
        name="student_side",
    )(place, student, *student_all, *logs_all, proto_weight)
    back_student = swapped(back_student, "proto")

    for _ in range(SWEEPS - 2):
        sums_all = swapped([sums] * parts, "proto")
        sums = pl.pallas_call(
            functools.partial(sweep_kernel, parts),
            grid=grid,
            in_specs=[columns(rows, chunk)] + [whole(x) for x in sums_all],
            out_specs=fixed(tiles, LANES),
            out_shape=sums_struct,
            scratch_shapes=[spread, spread],
            compiler_params=params(56),
            cost_estimate=cost(4 * rows * local_protos, prob_bytes),
            name="sweep",
        )(prob, *sums_all)
    sums_all = swapped([sums] * parts, "proto")
    sums, col_scale, *back_paired = pl.pallas_call(
        functools.partial(last_sweep_kernel, parts),
        grid=grid,
        in_specs=[SMEM, columns(rows, chunk), columns(width, chunk), whole(student)]
        + [whole(x) for x in sums_all],
        out_specs=[fixed(tiles + 8, LANES), columns(1, chunk)] + [fixed(share, width)] * parts,
        out_shape=[struct((tiles + 8, LANES), F32), struct((1, local_protos), F32)]
        + [block] * parts,
        scratch_shapes=[
            spread, spread, pltpu.VMEM((own, width), F32), pltpu.VMEM((own, chunk), BF16),
        ],
        compiler_params=params(56),
        cost_estimate=cost(2 * own * width * local_protos, prob_bytes),
        name="last_sweep",
    )(place, prob, proto_weight, student, *sums_all)
    sums_all = swapped([sums] * parts, "proto")
    back_paired = swapped(back_paired, "proto")

    loss_part = pl.pallas_call(
        functools.partial(loss_part_kernel, parts, tiles),
        out_shape=struct((8, LANES), F32),
        name="loss_part",
    )(*sums_all, logs)
    loss = tree([x[0, 0] for x in swapped([loss_part] * groups, "batch")]) / rows

    grad_rows = pl.pallas_call(
        functools.partial(rows_kernel, parts, float(protos)),
        in_specs=[SMEM] + [VMEM] * (1 + 3 * parts),
        out_shape=struct((share, width), F32),
        scratch_shapes=[pltpu.VMEM((own, LANES), F32)],
        name="row_grads",
    )(place, student_feats, *back_student, *back_paired, *sums_all)
    grad_rows = pl.pallas_call(
        join_kernel,
        in_specs=[SMEM] + [VMEM] * parts,
        out_shape=struct((own, width), F32),
        name="join_rows",
    )(place, *swapped([grad_rows] * parts, "proto"))

    grad_weight = pl.pallas_call(
        functools.partial(grad_kernel, parts, float(protos)),
        grid=grid,
        in_specs=[
            columns(rows, chunk), whole(feat), columns(feats, chunk), columns(1, chunk),
        ]
        + [whole(x) for x in sums_all],
        out_specs=columns(feats, chunk),
        out_shape=struct((feats, local_protos), BF16),
        scratch_shapes=[pltpu.VMEM((feats, rows), BF16)],
        compiler_params=params(56),
        cost_estimate=cost(2 * feats * rows * local_protos, prob_bytes),
        name="weight_grads",
    )(prob, feat, grad_part, col_scale, *sums_all)
    return grad_weight, grad_rows, loss


def solution(mesh):
    return jax.shard_map(
        local,
        mesh=mesh,
        in_specs=(P("batch", None), P("batch", None), P(None, "proto")),
        out_specs=(P("batch", "proto"), P("batch", None), P()),
        check_vma=False,
    )
```

```python
import functools
import math

import jax
import jax.numpy as jnp
from jax import lax
from jax.experimental import pallas as pl
from jax.experimental.pallas import tpu as pltpu
from jax.sharding import PartitionSpec as P

SWEEPS = 3
TEMP_TEACHER = 0.04
TEMP_STUDENT = 0.1
LOG2E = math.log2(math.e)
SCALE_TEACHER = LOG2E / TEMP_TEACHER
SCALE_STUDENT = LOG2E / TEMP_STUDENT
LANES = 128
WIDE = 1024
F32 = jnp.float32
BF16 = jnp.bfloat16


def unit_rows(values):
    wide = values.astype(F32)
    length = jnp.sqrt(jnp.sum(wide * wide, axis=-1, keepdims=True) + 1e-06)
    return wide / length, length


def diagonal():
    shape = (LANES, LANES)
    return lax.broadcasted_iota(jnp.int32, shape, 0) == lax.broadcasted_iota(jnp.int32, shape, 1)


def to_column(row):
    spread = jnp.where(diagonal(), jnp.broadcast_to(row, (LANES, LANES)), 0.0)
    return jnp.sum(spread, axis=1, keepdims=True)


def to_row(column):
    spread = jnp.where(diagonal(), jnp.broadcast_to(column, (LANES, LANES)), 0.0)
    return jnp.sum(spread, axis=0, keepdims=True)


def spread_rows(ref, rows):
    for a in range(rows.shape[0]):
        ref[a * LANES : (a + 1) * LANES, :] = jnp.broadcast_to(
            to_column(rows[a : a + 1, :]), (LANES, LANES)
        )


def pack_rows(ref, columns):
    for a in range(columns.shape[0] // LANES):
        ref[a : a + 1, :] = to_row(columns[a * LANES : (a + 1) * LANES, :])


def lane_tiles(values):
    return [values[:, t * LANES : (t + 1) * LANES] for t in range(values.shape[1] // LANES)]


def fold(values):
    return functools.reduce(jnp.add, lane_tiles(values))


def column_sums(values):
    rows, cols = values.shape
    return jnp.sum(values.reshape(rows // 8, 8, cols), axis=0)


def nt_dot(a, b):
    return lax.dot_general(a, b, (((1,), (1,)), ((), ())), preferred_element_type=F32)


def add_up(values):
    return functools.reduce(jnp.add, values)


def stats_kernel(t_ref, s_ref, w_ref, t_exp, s_exp, out_ref, unit, logits, top, total):
    chunk = 512
    cols = w_ref.shape[1]
    pieces = [slice(c, c + chunk) for c in range(0, cols, chunk)]
    quarter = out_ref.shape[1] // 4
    outs = (t_exp, s_exp)
    scales = (SCALE_TEACHER, SCALE_STUDENT)
    for which, ref in enumerate((t_ref, s_ref)):
        unit[which] = unit_rows(ref[...])[0].astype(BF16)
    top[...] = jnp.full(top.shape, -1e30, F32)
    total[...] = jnp.zeros(total.shape, F32)

    def product(which, here):
        values = jnp.dot(unit[which], w_ref[:, here], preferred_element_type=F32) * scales[which]
        logits[which, :, here] = values
        top[which] = functools.reduce(jnp.maximum, lane_tiles(values), top[which])

    def peak(which):
        return jnp.max(top[which], axis=1, keepdims=True)

    def raised(which, here, shift):
        values = jnp.exp2(logits[which, :, here] - shift)
        outs[which][:, here] = values.astype(BF16)
        total[which] += fold(values)

    for here in pieces:
        product(0, here)
    peaks = [peak(0)]
    shift = jnp.broadcast_to(peaks[0], (peaks[0].shape[0], chunk))
    for here in pieces:
        product(1, here)
        raised(0, here, shift)
    peaks.append(peak(1))
    shift = jnp.broadcast_to(peaks[1], (peaks[1].shape[0], chunk))
    for here in pieces:
        raised(1, here, shift)
    for which in range(2):
        sums = jnp.sum(total[which], axis=1, keepdims=True)
        for k, column in enumerate((peaks[which], sums)):
            first = (2 * which + k) * quarter
            pack_rows(out_ref.at[0, first : first + quarter], column)
    for p in range(1, out_ref.shape[0]):
        out_ref[p] = out_ref[0]


def merged(stats_ref, which):
    parts, height, _ = stats_ref.shape
    quarter = height // 4
    first = 2 * which * quarter
    tops = [stats_ref[p, first : first + quarter, :] for p in range(parts)]
    top = functools.reduce(jnp.maximum, tops)
    sums = [
        stats_ref[p, first + quarter : first + 2 * quarter, :] * jnp.exp2(tops[p] - top)
        for p in range(parts)
    ]
    return top + jnp.log2(add_up(sums))


def column_pass(exp_ref, weight, out_ref):
    rows, cols = exp_ref.shape
    for a in range(cols // WIDE):
        sums = jnp.zeros((8, WIDE), F32)
        for g in range(0, rows, 16):
            shift = weight[g : g + 16, :]
            tiles = lane_tiles(exp_ref[g : g + 16, a * WIDE : (a + 1) * WIDE].astype(F32))
            sums = sums + column_sums(jnp.concatenate([tile * shift for tile in tiles], axis=1))
        out_ref[0, a : a + 1, :] = jnp.sum(sums, axis=0, keepdims=True)


def repeat(out_ref):
    for p in range(1, out_ref.shape[0]):
        out_ref[p] = out_ref[0]


def first_column_kernel(place_ref, stats_ref, exp_ref, factor_ref, out_ref, weight):
    height = stats_ref.shape[1]
    quarter = height // 4
    parts_rows = exp_ref.shape[1] // WIDE
    own = stats_ref[pl.ds(place_ref[1], 1)][0]
    factor_ref[...] = jnp.zeros(factor_ref.shape, F32)
    out_ref[0, parts_rows:, :] = jnp.zeros((out_ref.shape[1] - parts_rows, WIDE), F32)
    for which in range(2):
        log_sum = merged(stats_ref, which)
        factor_ref[which * quarter : (which + 1) * quarter, :] = jnp.exp2(
            own[2 * which * quarter : (2 * which + 1) * quarter, :] - log_sum
        )
        for a in range(quarter):
            lanes = slice((which * quarter + a) * LANES, (which * quarter + a + 1) * LANES)
            out_ref[0, parts_rows : parts_rows + 1, lanes] = log_sum[a : a + 1, :]
    spread_rows(weight, factor_ref[:quarter, :])
    column_pass(exp_ref, weight, out_ref)
    repeat(out_ref)


def column_kernel(sums_ref, factor_ref, exp_ref, out_ref, weight):
    parts = sums_ref.shape[0]
    quarter = exp_ref.shape[0] // LANES
    scale = 1.0 / add_up([sums_ref[p, :quarter, :] for p in range(parts)])
    spread_rows(weight, scale * factor_ref[:quarter, :])
    column_pass(exp_ref, weight, out_ref)
    repeat(out_ref)


def column_scales(cols_ref, height):
    return 1.0 / add_up([cols_ref[g, :height, :] for g in range(cols_ref.shape[0])])


def row_kernel(cols_ref, factor_ref, exp_ref, out_ref, scales):
    rows, cols = exp_ref.shape
    quarter = rows // LANES
    scales[...] = column_scales(cols_ref, cols // WIDE)
    out_ref[0] = jnp.zeros(out_ref.shape[1:], F32)
    for q in range(quarter):
        sums = []
        for g in range(q * LANES, (q + 1) * LANES, 32):
            total = jnp.zeros((32, LANES), F32)
            for a in range(cols // WIDE):
                tiles = lane_tiles(exp_ref[g : g + 32, a * WIDE : (a + 1) * WIDE].astype(F32))
                for t, tile in enumerate(tiles):
                    total = total + tile * scales[a : a + 1, t * LANES : (t + 1) * LANES]
            sums.append(jnp.sum(total, axis=1, keepdims=True))
        row = to_row(jnp.concatenate(sums, axis=0))
        out_ref[0, q : q + 1, :] = row * factor_ref[q : q + 1, :]
    repeat(out_ref)


def relative_units(place_ref, all_ref, unit, groups, first):
    own = all_ref.shape[0] // groups
    for g in range(first, groups):
        start = lax.rem(place_ref[0] + g, groups) * own
        raw = all_ref[pl.ds(pl.multiple_of(start, own), own), :]
        unit[(g - first) * own : (g - first + 1) * own, :] = unit_rows(raw)[0].astype(BF16)


def relative_logs(place_ref, cols_ref, lse, which, height, shift=0.0):
    groups = cols_ref.shape[0]
    own = lse.shape[0] // (groups - 1)
    quarter = own // LANES
    for g in range(1, groups):
        there = cols_ref[pl.ds(lax.rem(place_ref[0] + g, groups), 1)][0]
        for a in range(quarter):
            first = (which * quarter + a) * LANES
            row = there[height : height + 1, first : first + LANES] - shift
            start = ((g - 1) * quarter + a) * LANES
            lse[start : start + LANES, :] = jnp.broadcast_to(to_column(row), (LANES, LANES))


def probabilities(unit, w_ref, lse, scale, prob_ref):
    for n in range(0, w_ref.shape[1], 256):
        logits = jnp.dot(unit[...], w_ref[:, n : n + 256], preferred_element_type=F32)
        for k, tile in enumerate(lane_tiles(logits)):
            lanes = slice(n + k * LANES, n + (k + 1) * LANES)
            prob_ref[:, lanes] = jnp.exp2(tile * scale - lse[...]).astype(BF16)


def others_kernel(groups, height, place_ref, all_ref, cols_ref, w_ref, prob_ref, unit, lse):
    @pl.when(pl.program_id(0) == 0)
    def _():
        relative_units(place_ref, all_ref, unit, groups, 1)
        relative_logs(place_ref, cols_ref, lse, 0, height)

    probabilities(unit, w_ref, lse, SCALE_TEACHER, prob_ref)


def student_kernel(
    groups, height, log_protos, place_ref, all_ref, cols_ref, factor_ref, w_ref, exp_ref,
    grad_ref, feat_ref, back_ref, unit, turned, scaled, lse, prob, back,
):
    step = pl.program_id(0)
    feats, own = feat_ref.shape[0], back.shape[0]
    quarter = own // LANES
    protos = 2.0**log_protos

    @pl.when(step == 0)
    def _():
        relative_units(place_ref, all_ref, unit, groups, 0)
        for g in range(0, unit.shape[0], LANES):
            half = unit[g : g + LANES, :].astype(F32)
            turned[:, g : g + LANES] = jnp.transpose(half).astype(BF16)
        feat_ref[...] = turned[pl.ds(pl.multiple_of(place_ref[0] * feats, feats), feats), :]
        relative_logs(place_ref, cols_ref, lse, 1, height, log_protos)
        back[...] = jnp.zeros(back.shape, F32)
        for a in range(quarter):
            lanes = slice(a * LANES, (a + 1) * LANES)
            factor = factor_ref[quarter + a : quarter + a + 1, :] * protos
            scaled[:, lanes] = (feat_ref[:, lanes].astype(F32) * factor).astype(BF16)

    probabilities(unit.at[own:], w_ref, lse, SCALE_STUDENT, prob)
    grad_ref[...] = jnp.dot(scaled[...], exp_ref[...], preferred_element_type=F32) + jnp.dot(
        feat_ref[:, own:], prob[...], preferred_element_type=F32
    )
    back[...] += nt_dot(exp_ref[...], w_ref[...])

    @pl.when(step == pl.num_programs(0) - 1)
    def _():
        for a in range(quarter):
            here = slice(a * LANES, (a + 1) * LANES)
            factor = to_column(factor_ref[quarter + a : quarter + a + 1, :] * protos)
            back_ref[here, :] = (back[here, :] * factor).astype(BF16)


def last_kernel(
    cols_ref, factor_ref, s_ref, student_ref, exp_ref, prob_ref, w_ref,
    sums_ref, scale_ref, back_ref, scales, rows, back, scaled,
):
    step = pl.program_id(0)
    own, others = exp_ref.shape[0], prob_ref.shape[0]
    tiles = (own + others) // LANES
    quarter = own // LANES

    @pl.when(step == 0)
    def _():
        scales[...] = column_scales(cols_ref, scales.shape[0])
        scale_ref[...] = scales[...]
        rows[...] = jnp.zeros(rows.shape, F32)
        back[...] = jnp.zeros(back.shape, F32)

    scale = scales[pl.ds(step, 1), :]
    for ref, first in ((exp_ref, 0), (prob_ref, own)):
        for g in range(0, ref.shape[0], 64):
            here = slice(first + g, first + g + 64)
            rows[here, :] += fold(ref[g : g + 64, :].astype(F32) * scale)
    partner = (own + others) // 2 - own
    for g in range(0, own, 64):
        values = prob_ref[partner + g : partner + g + 64, :].astype(F32) * scale
        scaled[g : g + 64, :] = values.astype(BF16)
    back[...] += nt_dot(scaled[...], w_ref[...])

    @pl.when(step == pl.num_programs(0) - 1)
    def _():
        sums_ref[...] = jnp.zeros(sums_ref.shape, F32)
        pack_rows(sums_ref.at[0, :tiles], jnp.sum(rows[...], axis=1, keepdims=True))
        sums_ref[0, :quarter, :] = sums_ref[0, :quarter, :] * factor_ref[:quarter, :]
        half = unit_rows(s_ref[...])[0].astype(BF16).astype(F32)
        inner = jnp.sum(half * back[...], axis=1, keepdims=True)
        pack_rows(sums_ref.at[0, tiles : tiles + quarter], inner)
        repeat(sums_ref)
        share = back_ref.shape[1] // 2
        for p in range(back_ref.shape[0]):
            here = slice(p * share, (p + 1) * share)
            back_ref[p, :share, :] = student_ref[here, :]
            back_ref[p, share:, :] = back[here, :].astype(BF16)


def all_row_scales(sums_ref, tiles):
    return 1.0 / add_up([sums_ref[p, :tiles, :] for p in range(sums_ref.shape[0])])


def rows_kernel(tiles, protos, height, place_ref, s_ref, back_ref, sums_ref, cols_ref, out_ref, loss_ref, weight):
    parts, double, _ = back_ref.shape
    share = double // 2
    quarter = weight.shape[0] // LANES
    first = tiles // 2
    totals = add_up([sums_ref[p] for p in range(parts)])
    scale = 1.0 / totals[first : first + quarter, :]
    spread_rows(weight, scale)
    mine = pl.ds(pl.multiple_of(place_ref[1] * share, share), share)
    total = add_up([back_ref[p, :share, :].astype(F32) for p in range(parts)])
    paired = add_up([back_ref[p, share:, :].astype(F32) for p in range(parts)])
    total = total - paired * (weight[mine, :1] * protos)
    unit, length = unit_rows(s_ref[mine, :])
    out_ref[0] = (total - unit * jnp.sum(unit * total, axis=-1, keepdims=True)) / length
    repeat(out_ref)
    logs = cols_ref[pl.ds(place_ref[0], 1)][0]
    terms = jnp.zeros((1, LANES), F32)
    for a in range(quarter):
        lanes = slice((quarter + a) * LANES, (quarter + a + 1) * LANES)
        inner = totals[tiles + a : tiles + a + 1, :] * scale[a : a + 1, :]
        terms = terms + logs[height : height + 1, lanes] / LOG2E - inner / TEMP_STUDENT
    loss_ref[...] = jnp.broadcast_to(jnp.sum(terms), loss_ref.shape)


def grad_kernel(protos, exp_ref, prob_ref, feat_ref, part_ref, scale_ref, sums_ref, factor_ref, out_ref, scaled):
    own = exp_ref.shape[0]

    @pl.when(pl.program_id(0) == 0)
    def _():
        tiles = (own + prob_ref.shape[0]) // LANES
        rows = all_row_scales(sums_ref, tiles) * protos
        for a in range(tiles):
            other = (a + tiles // 2) % tiles
            feat = feat_ref[:, other * LANES : (other + 1) * LANES].astype(F32)
            row = rows[a : a + 1, :]
            if a < own // LANES:
                row = row * factor_ref[a : a + 1, :]
            scaled[:, a * LANES : (a + 1) * LANES] = (feat * row).astype(BF16)

    paired = jnp.dot(scaled[:, :own], exp_ref[...], preferred_element_type=F32)
    paired = paired + jnp.dot(scaled[:, own:], prob_ref[...], preferred_element_type=F32)
    scale = scale_ref[pl.ds(pl.program_id(0), 1), :]
    out_ref[...] = (part_ref[...] - paired * scale).astype(BF16)


def whole(array):
    rank = len(array.shape)
    return pl.BlockSpec(array.shape, lambda i: (0,) * rank)


def fixed(*shape):
    return pl.BlockSpec(shape, lambda i: (0,) * len(shape))


def columns(rows, cols):
    return pl.BlockSpec((rows, cols), lambda i: (0, i))


SMEM = pl.BlockSpec(memory_space=pltpu.SMEM)
VMEM = pl.BlockSpec(memory_space=pltpu.VMEM)


def params(mib):
    return pltpu.CompilerParams(vmem_limit_bytes=mib * 2**20)


def cost(flops, nbytes, exps=0):
    return pl.CostEstimate(flops=int(flops), bytes_accessed=int(nbytes), transcendentals=int(exps))


def exchange(value, axis):
    return lax.all_to_all(value, axis, 0, 0)


def local(teacher_feats, student_feats, proto_weight):
    parts, groups = lax.axis_size("proto"), lax.axis_size("batch")
    own, width = teacher_feats.shape
    local_protos = proto_weight.shape[1]
    rows = own * groups
    protos = local_protos * parts
    feats = width // groups
    share = own // parts
    tiles = rows // LANES
    height = local_protos // WIDE
    place = jnp.stack([lax.axis_index("batch"), lax.axis_index("proto")]).astype(jnp.int32)
    struct = jax.ShapeDtypeStruct
    weight_bytes = 2 * width * local_protos
    exp_bytes = 2 * own * local_protos
    others_bytes = 2 * (rows - own) * local_protos
    spread = pltpu.VMEM((own, LANES), F32)

    teacher_all = lax.all_gather(teacher_feats, "batch", tiled=True)
    student_all = lax.all_gather(student_feats, "batch", tiled=True)

    exp_struct = struct((own, local_protos), BF16)
    teacher_exp, student_exp, stats = pl.pallas_call(
        stats_kernel,
        in_specs=[VMEM] * 3,
        out_specs=[VMEM] * 3,
        out_shape=[exp_struct, exp_struct, struct((parts, 4 * own // LANES, LANES), F32)],
        scratch_shapes=[
            pltpu.VMEM((2, own, width), BF16),
            pltpu.VMEM((2, own, local_protos), F32),
            pltpu.VMEM((2, own, LANES), F32),
            pltpu.VMEM((2, own, LANES), F32),
        ],
        compiler_params=params(48),
        cost_estimate=cost(4 * own * width * local_protos, weight_bytes),
        name="own_rows",
    )(teacher_feats, student_feats, proto_weight)
    stats = exchange(stats, "proto")

    message = struct((groups, height + 8, WIDE), F32)
    factor, cols = pl.pallas_call(
        first_column_kernel,
        in_specs=[SMEM, VMEM, VMEM],
        out_specs=[VMEM] * 2,
        out_shape=[struct((8, LANES), F32), message],
        scratch_shapes=[spread],
        compiler_params=params(16),
        cost_estimate=cost(2 * own * local_protos, exp_bytes),
        name="first_columns",
    )(place, stats, teacher_exp)
    cols = exchange(cols, "batch")
    logs = cols

    for _ in range(SWEEPS - 1):
        sums = pl.pallas_call(
            row_kernel,
            in_specs=[VMEM] * 3,
            out_specs=VMEM,
            out_shape=struct((parts, 8, LANES), F32),
            scratch_shapes=[pltpu.VMEM((height, WIDE), F32)],
            compiler_params=params(16),
            cost_estimate=cost(2 * own * local_protos, exp_bytes),
            name="rows",
        )(cols, factor, teacher_exp)
        sums = exchange(sums, "proto")
        cols = pl.pallas_call(
            column_kernel,
            in_specs=[VMEM] * 3,
            out_specs=VMEM,
            out_shape=struct((groups, height, WIDE), F32),
            scratch_shapes=[spread],
            compiler_params=params(16),
            cost_estimate=cost(2 * own * local_protos, exp_bytes),
            name="columns",
        )(sums, factor, teacher_exp)
        cols = exchange(cols, "batch")

    grid = (height,)
    prob = pl.pallas_call(
        functools.partial(others_kernel, groups, height),
        grid=grid,
        in_specs=[SMEM, whole(teacher_all), whole(logs), columns(width, WIDE)],
        out_specs=columns(rows - own, WIDE),
        out_shape=struct((rows - own, local_protos), BF16),
        scratch_shapes=[pltpu.VMEM((rows - own, width), BF16), pltpu.VMEM((rows - own, LANES), F32)],
        compiler_params=params(40),
        cost_estimate=cost(2 * (rows - own) * width * local_protos, others_bytes),
        name="other_teachers",
    )(place, teacher_all, logs, proto_weight)

    grad_part, feat, back_student = pl.pallas_call(
        functools.partial(student_kernel, groups, height, math.log2(protos)),
        grid=grid,
        in_specs=[
            SMEM, whole(student_all), whole(logs), whole(factor), columns(width, WIDE),
            columns(own, WIDE),
        ],
        out_specs=[columns(feats, WIDE), fixed(feats, rows), fixed(own, width)],
        out_shape=[
            struct((feats, local_protos), F32), struct((feats, rows), BF16), struct((own, width), BF16),
        ],
        scratch_shapes=[
            pltpu.VMEM((rows, width), BF16),
            pltpu.VMEM((width, rows), BF16),
            pltpu.VMEM((feats, own), BF16),
            pltpu.VMEM((rows - own, LANES), F32),
            pltpu.VMEM((rows - own, WIDE), BF16),
            pltpu.VMEM((own, width), F32),
        ],
        compiler_params=params(40),
        cost_estimate=cost(3 * rows * width * local_protos, weight_bytes),
        name="student_side",
    )(place, student_all, logs, factor, proto_weight, student_exp)

    sums_shape = (parts, tiles + 8, LANES)
    back_shape = (parts, 2 * share, width)
    sums, col_scale, back = pl.pallas_call(
        last_kernel,
        grid=grid,
        in_specs=[
            whole(cols), whole(factor), whole(student_feats), whole(back_student),
            columns(own, WIDE), columns(rows - own, WIDE), columns(width, WIDE),
        ],
        out_specs=[fixed(*sums_shape), fixed(height, WIDE), fixed(*back_shape)],
        out_shape=[struct(sums_shape, F32), struct((height, WIDE), F32), struct(back_shape, BF16)],
        scratch_shapes=[
            pltpu.VMEM((height, WIDE), F32),
            pltpu.VMEM((rows, LANES), F32),
            pltpu.VMEM((own, width), F32),
            pltpu.VMEM((own, WIDE), BF16),
        ],
        compiler_params=params(40),
        cost_estimate=cost(2 * own * width * local_protos, others_bytes),
        name="last_rows",
    )(cols, factor, student_feats, back_student, teacher_exp, prob, proto_weight)
    sums = exchange(sums, "proto")
    back = exchange(back, "proto")

    grad_rows, loss_part = pl.pallas_call(
        functools.partial(rows_kernel, tiles, float(protos), height),
        in_specs=[SMEM] + [VMEM] * 4,
        out_specs=[VMEM] * 2,
        out_shape=[struct((parts, share, width), F32), struct((groups, 8, LANES), F32)],
        scratch_shapes=[spread],
        name="row_grads",
    )(place, student_feats, back, sums, logs)
    grad_rows = exchange(grad_rows, "proto").reshape(own, width)
    loss = jnp.sum(exchange(loss_part, "batch")[:, 0, 0]) / rows

    grad_weight = pl.pallas_call(
        functools.partial(grad_kernel, float(protos)),
        grid=grid,
        in_specs=[
            columns(own, WIDE), columns(rows - own, WIDE), whole(feat), columns(feats, WIDE),
            whole(col_scale), whole(sums), whole(factor),
        ],
        out_specs=columns(feats, WIDE),
        out_shape=struct((feats, local_protos), BF16),
        scratch_shapes=[pltpu.VMEM((feats, rows), BF16)],
        compiler_params=params(40),
        cost_estimate=cost(2 * feats * rows * local_protos, others_bytes),
        name="weight_grads",
    )(teacher_exp, prob, feat, grad_part, col_scale, sums, factor)
    return grad_weight, grad_rows, loss


def solution(mesh):
    return jax.shard_map(
        local,
        mesh=mesh,
        in_specs=(P("batch", None), P("batch", None), P(None, "proto")),
        out_specs=(P("batch", "proto"), P("batch", None), P()),
        check_vma=False,
    )
```

```python
import functools
import math

import jax
import jax.numpy as jnp
from jax import lax
from jax.experimental import pallas as pl
from jax.experimental.pallas import tpu as pltpu
from jax.sharding import PartitionSpec as P

SWEEPS = 3
TEMP_TEACHER = 0.04
TEMP_STUDENT = 0.1
LOG2E = math.log2(math.e)
SCALE_TEACHER = LOG2E / TEMP_TEACHER
SCALE_STUDENT = LOG2E / TEMP_STUDENT
LANES = 128
WIDE = 1024
VMEM_MIB = 60
F32 = jnp.float32
BF16 = jnp.bfloat16


def unit_rows(values):
    wide = values.astype(F32)
    length = jnp.sqrt(jnp.sum(wide * wide, axis=-1, keepdims=True) + 1e-06)
    return wide / length, length


def diagonal():
    shape = (LANES, LANES)
    return lax.broadcasted_iota(jnp.int32, shape, 0) == lax.broadcasted_iota(jnp.int32, shape, 1)


def to_column(row):
    spread = jnp.where(diagonal(), jnp.broadcast_to(row, (LANES, LANES)), 0.0)
    return jnp.sum(spread, axis=1, keepdims=True)


def to_row(column):
    spread = jnp.where(diagonal(), jnp.broadcast_to(column, (LANES, LANES)), 0.0)
    return jnp.sum(spread, axis=0, keepdims=True)


def spread_rows(ref, rows):
    for a in range(rows.shape[0]):
        ref[a * LANES : (a + 1) * LANES, :] = jnp.broadcast_to(
            to_column(rows[a : a + 1, :]), (LANES, LANES)
        )


def pack_rows(ref, columns):
    for a in range(columns.shape[0] // LANES):
        ref[a : a + 1, :] = to_row(columns[a * LANES : (a + 1) * LANES, :])


def lane_tiles(values):
    return [values[:, t * LANES : (t + 1) * LANES] for t in range(values.shape[1] // LANES)]


def fold(values):
    return functools.reduce(jnp.add, lane_tiles(values))


def column_sums(values):
    rows, cols = values.shape
    return jnp.sum(values.reshape(rows // 8, 8, cols), axis=0)


def nt_dot(a, b):
    return lax.dot_general(a, b, (((1,), (1,)), ((), ())), preferred_element_type=F32)


def add_up(values):
    return functools.reduce(jnp.add, values)


def repeat(out_ref):
    for p in range(1, out_ref.shape[0]):
        out_ref[p] = out_ref[0]


def unit_kernel(t_ref, s_ref, t_unit, s_unit, s_out):
    t_unit[...] = unit_rows(t_ref[...])[0].astype(BF16)
    half = unit_rows(s_ref[...])[0].astype(BF16)
    s_unit[...] = half
    for g in range(s_out.shape[0]):
        s_out[g] = half


def stats_kernel(
    t_ref, s_ref, w_hbm, t_out, s_out, out_ref, w_ref, exps, logits, top, total, w_sem, out_sem
):
    chunk = 512
    cols = w_ref.shape[1]
    pieces = [slice(c, c + chunk) for c in range(0, cols, chunk)]
    quarter = out_ref.shape[1] // 4
    units = (t_ref, s_ref)
    outs = (t_out, s_out)
    scales = (SCALE_TEACHER, SCALE_STUDENT)
    loads = [
        pltpu.make_async_copy(
            w_hbm.at[:, c : c + WIDE], w_ref.at[:, c : c + WIDE], w_sem.at[c // WIDE]
        )
        for c in range(0, cols, WIDE)
    ]
    stores = [
        pltpu.make_async_copy(exps.at[which], outs[which], out_sem.at[which]) for which in range(2)
    ]
    for load in loads:
        load.start()
    top[...] = jnp.full(top.shape, -1e30, F32)
    total[...] = jnp.zeros(total.shape, F32)

    def product(which, here):
        values = jnp.dot(units[which][...], w_ref[:, here], preferred_element_type=F32) * scales[which]
        logits[which, :, here] = values
        top[which] = functools.reduce(jnp.maximum, lane_tiles(values), top[which])

    def peak(which):
        return jnp.max(top[which], axis=1, keepdims=True)

    def raised(which, here, shift):
        values = jnp.exp2(logits[which, :, here] - shift)
        exps[which, :, here] = values.astype(BF16)
        total[which] += fold(values)

    for k, here in enumerate(pieces):
        if here.start % WIDE == 0:
            loads[here.start // WIDE].wait()
        product(0, here)
    peaks = [peak(0)]
    shift = jnp.broadcast_to(peaks[0], (peaks[0].shape[0], chunk))
    for here in pieces:
        product(1, here)
        raised(0, here, shift)
    stores[0].start()
    peaks.append(peak(1))
    shift = jnp.broadcast_to(peaks[1], (peaks[1].shape[0], chunk))
    for here in pieces:
        raised(1, here, shift)
    stores[1].start()
    for which in range(2):
        sums = jnp.sum(total[which], axis=1, keepdims=True)
        for k, column in enumerate((peaks[which], sums)):
            first = (2 * which + k) * quarter
            pack_rows(out_ref.at[0, first : first + quarter], column)
    repeat(out_ref)
    for store in stores:
        store.wait()


def merged(stats_ref, which):
    parts, height, _ = stats_ref.shape
    quarter = height // 4
    first = 2 * which * quarter
    tops = [stats_ref[p, first : first + quarter, :] for p in range(parts)]
    top = functools.reduce(jnp.maximum, tops)
    sums = [
        stats_ref[p, first + quarter : first + 2 * quarter, :] * jnp.exp2(tops[p] - top)
        for p in range(parts)
    ]
    return top + jnp.log2(add_up(sums))


def column_pass(exp_ref, weight, out_ref):
    rows, cols = exp_ref.shape
    first = pl.program_id(0) * (cols // LANES)
    for a in range(0, cols, WIDE):
        sums = jnp.zeros((8, WIDE), F32)
        for g in range(0, rows, 16):
            shift = weight[g : g + 16, :]
            tiles = lane_tiles(exp_ref[g : g + 16, a : a + WIDE].astype(F32))
            sums = sums + column_sums(jnp.concatenate([tile * shift for tile in tiles], axis=1))
        sums = jnp.sum(sums, axis=0, keepdims=True)
        block = jnp.concatenate(lane_tiles(sums), axis=0)
        start = pl.multiple_of(first + a // LANES, 8)
        for g in range(out_ref.shape[0]):
            out_ref[g, pl.ds(start, WIDE // LANES), :] = block


def first_column_kernel(place_ref, stats_ref, exp_ref, factor_ref, out_ref, weight):
    @pl.when(pl.program_id(0) == 0)
    def _():
        quarter = stats_ref.shape[1] // 4
        height = out_ref.shape[1] - 8
        own = stats_ref[pl.ds(place_ref[1], 1)][0]
        factor_ref[...] = jnp.zeros(factor_ref.shape, F32)
        out_ref[0, height:, :] = jnp.zeros((8, LANES), F32)
        for which in range(2):
            log_sum = merged(stats_ref, which)
            here = slice(which * quarter, (which + 1) * quarter)
            factor_ref[here, :] = jnp.exp2(
                own[2 * which * quarter : (2 * which + 1) * quarter, :] - log_sum
            )
            out_ref[0, height + here.start : height + here.stop, :] = log_sum
        for g in range(1, out_ref.shape[0]):
            out_ref[g, height:, :] = out_ref[0, height:, :]
        spread_rows(weight, factor_ref[:quarter, :])

    column_pass(exp_ref, weight, out_ref)


def column_kernel(sums_ref, factor_ref, token_ref, exp_ref, out_ref, weight):
    @pl.when(pl.program_id(0) == 0)
    def _():
        quarter = weight.shape[0] // LANES
        scale = 1.0 / add_up([sums_ref[p, :quarter, :] for p in range(sums_ref.shape[0])])
        spread_rows(weight, scale * factor_ref[:quarter, :])

    column_pass(exp_ref, weight, out_ref)


def column_scales(cols_ref, height):
    return 1.0 / add_up([cols_ref[g, :height, :] for g in range(cols_ref.shape[0])])


def add_row_sums(rows, ref, first, scales, start, step):
    for g in range(0, ref.shape[0], step):
        total = rows[first + g : first + g + step, :]
        for t, tile in enumerate(lane_tiles(ref[g : g + step, :].astype(F32))):
            total = total + tile * scales[pl.ds(start + t, 1), :]
        rows[first + g : first + g + step, :] = total


def row_kernel(cols_ref, factor_ref, token_ref, exp_ref, out_ref, scales, rows):
    step = pl.program_id(0)

    @pl.when(step == 0)
    def _():
        scales[...] = column_scales(cols_ref, scales.shape[0])
        rows[...] = jnp.zeros(rows.shape, F32)

    add_row_sums(rows, exp_ref, 0, scales, step * (exp_ref.shape[1] // LANES), 32)

    @pl.when(step == pl.num_programs(0) - 1)
    def _():
        quarter = rows.shape[0] // LANES
        out_ref[0] = jnp.zeros(out_ref.shape[1:], F32)
        pack_rows(out_ref.at[0, :quarter], jnp.sum(rows[...], axis=1, keepdims=True))
        out_ref[0, :quarter, :] = out_ref[0, :quarter, :] * factor_ref[:quarter, :]
        repeat(out_ref)


def relative(place_ref, g, groups):
    return pl.ds(lax.rem(place_ref[0] + g, groups), 1)


def relative_logs(place_ref, logs_ref, lse, which, shift=0.0):
    groups = logs_ref.shape[0]
    own = lse.shape[0] // (groups - 1)
    quarter = own // LANES
    height = logs_ref.shape[1] - 8
    for g in range(1, groups):
        there = logs_ref[relative(place_ref, g, groups)][0]
        first = height + which * quarter
        spread_rows(lse.at[(g - 1) * own : g * own], there[first : first + quarter, :] - shift)


def probabilities(place_ref, all_ref, w_ref, lse, scale, prob_ref, use):
    groups, own, _ = all_ref.shape
    for g in range(1, groups):
        unit = all_ref[relative(place_ref, g, groups)][0]
        here = slice((g - 1) * own, g * own)
        for n in range(0, w_ref.shape[1], 512):
            logits = jnp.dot(unit, w_ref[:, n : n + 512], preferred_element_type=F32)
            shift = lse[here, :]
            tiles = [jnp.exp2(tile * scale - shift) for tile in lane_tiles(logits)]
            for k, tile in enumerate(tiles):
                prob_ref[here, n + k * LANES : n + (k + 1) * LANES] = tile.astype(BF16)
            if use is not None:
                use(g, n, tiles)


def own_back_kernel(protos, factor_ref, t_unit, w_ref, exp_ref, back_ref, t_out, back):
    step = pl.program_id(0)

    @pl.when(step == 0)
    def _():
        back[...] = jnp.zeros(back.shape, F32)
        for g in range(t_out.shape[0]):
            t_out[g] = t_unit[...]

    back[...] += nt_dot(exp_ref[...], w_ref[...])

    @pl.when(step == pl.num_programs(0) - 1)
    def _():
        quarter = back.shape[0] // LANES
        for a in range(quarter):
            here = slice(a * LANES, (a + 1) * LANES)
            factor = to_column(factor_ref[quarter + a : quarter + a + 1, :] * protos)
            back_ref[here, :] = (back[here, :] * factor).astype(BF16)


def feature_kernel(place_ref, all_ref, feat_ref, turned):
    groups, own, _ = all_ref.shape
    feats = feat_ref.shape[0]
    for g in range(groups):
        half = all_ref[relative(place_ref, g, groups)][0].astype(F32)
        for a in range(0, own, LANES):
            first = g * own + a
            turned[:, first : first + LANES] = jnp.transpose(half[a : a + LANES, :]).astype(BF16)
    feat_ref[...] = turned[pl.ds(pl.multiple_of(place_ref[0] * feats, feats), feats), :]


def student_kernel(
    log_protos, place_ref, all_ref, logs_ref, factor_ref, feat_ref, w_ref, exp_ref, *refs
):
    grad_ref, token_ref, scaled, lse, prob = refs[-5:]

    @pl.when(pl.program_id(0) == 0)
    def _():
        own = exp_ref.shape[0]
        quarter = own // LANES
        relative_logs(place_ref, logs_ref, lse, 1, log_protos)
        for a in range(quarter):
            lanes = slice(a * LANES, (a + 1) * LANES)
            factor = factor_ref[quarter + a : quarter + a + 1, :] * 2.0**log_protos
            scaled[:, lanes] = (feat_ref[:, lanes].astype(F32) * factor).astype(BF16)
        token_ref[...] = jnp.zeros(token_ref.shape, F32)

    probabilities(place_ref, all_ref, w_ref, lse, SCALE_STUDENT, prob, None)
    own = exp_ref.shape[0]
    grad_ref[...] = jnp.dot(scaled[...], exp_ref[...], preferred_element_type=F32) + jnp.dot(
        feat_ref[:, own:], prob[...], preferred_element_type=F32
    )


def as_three(value):
    high = value.astype(BF16)
    rest = value - high.astype(F32)
    middle = rest.astype(BF16)
    return high, middle, (rest - middle.astype(F32)).astype(BF16)


def last_kernel(
    place_ref, all_ref, logs_ref, cols_ref, factor_ref, token_ref, s_unit, student_ref, exp_ref, w_ref,
    prob_ref, scale_ref, out_ref, scales, rows, back, scaled, lse, sums,
):
    step = pl.program_id(0)
    own, others = exp_ref.shape[0], prob_ref.shape[0]
    groups = all_ref.shape[0]
    tiles = (own + others) // LANES
    quarter = own // LANES

    @pl.when(step == 0)
    def _():
        scales[...] = column_scales(cols_ref, scales.shape[0])
        scale_ref[...] = scales[...]
        rows[...] = jnp.zeros(rows.shape, F32)
        back[...] = jnp.zeros(back.shape, F32)
        relative_logs(place_ref, logs_ref, lse, 0)

    first = step * (w_ref.shape[1] // LANES)
    add_row_sums(rows, exp_ref, 0, scales, first, 32)

    def use(g, n, values):
        here = slice(g * own, (g + 1) * own)
        values = [
            tile * scales[pl.ds(first + n // LANES + k, 1), :] for k, tile in enumerate(values)
        ]
        rows[here, :] += add_up(values)
        if g == groups // 2:
            for k, tile in enumerate(values):
                scaled[:, n + k * LANES : n + (k + 1) * LANES] = tile.astype(BF16)

    probabilities(place_ref, all_ref, w_ref, lse, SCALE_TEACHER, prob_ref, use)
    back[...] += nt_dot(scaled[...], w_ref[...])

    @pl.when(step == pl.num_programs(0) - 1)
    def _():
        sums[...] = jnp.zeros(sums.shape, F32)
        pack_rows(sums.at[:tiles], jnp.sum(rows[...], axis=1, keepdims=True))
        sums[:quarter, :] = sums[:quarter, :] * factor_ref[:quarter, :]
        inner = jnp.sum(s_unit[...].astype(F32) * back[...], axis=1, keepdims=True)
        pack_rows(sums.at[tiles : tiles + quarter], inner)
        parts = out_ref.shape[0]
        share = own // parts
        for k, term in enumerate(as_three(sums[...])):
            for p in range(parts):
                out_ref[p, 2 * share :, k * LANES : (k + 1) * LANES] = term
        for p in range(parts):
            here = slice(p * share, (p + 1) * share)
            out_ref[p, : 2 * share, :] = jnp.concatenate(
                [student_ref[here, :], back[here, :].astype(BF16)], axis=0
            )
            out_ref[p, 2 * share :, 3 * LANES :] = jnp.zeros(
                (sums.shape[0], out_ref.shape[2] - 3 * LANES), BF16
            )


def total_sums(message_ref, first):
    parts = message_ref.shape[0]
    each = [
        add_up([t.astype(F32) for t in lane_tiles(message_ref[p, first:, : 3 * LANES])[::-1]])
        for p in range(parts)
    ]
    return add_up(each)


def rows_kernel(tiles, protos, place_ref, s_ref, message_ref, logs_ref, out_ref, loss_ref, sums_ref, weight):
    parts = message_ref.shape[0]
    share, own = out_ref.shape[1], weight.shape[0]
    quarter = own // LANES
    first = tiles // 2
    totals = total_sums(message_ref, 2 * share)
    sums_ref[...] = totals
    scale = 1.0 / totals[first : first + quarter, :]
    spread_rows(weight, scale)
    mine = pl.ds(pl.multiple_of(place_ref[1] * share, share), share)
    total = add_up([message_ref[p, :share, :].astype(F32) for p in range(parts)])
    paired = add_up([message_ref[p, share : 2 * share, :].astype(F32) for p in range(parts)])
    total = total - paired * (weight[mine, :1] * protos)
    unit, length = unit_rows(s_ref[mine, :])
    out_ref[0] = (total - unit * jnp.sum(unit * total, axis=-1, keepdims=True)) / length
    repeat(out_ref)
    height = logs_ref.shape[1] - 8
    logs = logs_ref[pl.ds(place_ref[0], 1)][0][height + quarter : height + 2 * quarter, :]
    terms = logs / LOG2E - totals[tiles : tiles + quarter, :] * scale / TEMP_STUDENT
    loss_ref[...] = jnp.broadcast_to(jnp.sum(terms), loss_ref.shape)


def grad_kernel(protos, exp_ref, prob_ref, feat_ref, part_ref, scale_ref, sums_ref, factor_ref, out_ref, scaled):
    own = exp_ref.shape[0]

    @pl.when(pl.program_id(0) == 0)
    def _():
        tiles = (own + prob_ref.shape[0]) // LANES
        rows = protos / sums_ref[:tiles, :]
        for a in range(tiles):
            other = (a + tiles // 2) % tiles
            feat = feat_ref[:, other * LANES : (other + 1) * LANES].astype(F32)
            row = rows[a : a + 1, :]
            if a < own // LANES:
                row = row * factor_ref[a : a + 1, :]
            scaled[:, a * LANES : (a + 1) * LANES] = (feat * row).astype(BF16)

    paired = jnp.dot(scaled[:, :own], exp_ref[...], preferred_element_type=F32)
    paired = paired + jnp.dot(scaled[:, own:], prob_ref[...], preferred_element_type=F32)
    first = pl.program_id(0) * (out_ref.shape[1] // LANES)
    for t, tile in enumerate(lane_tiles(paired)):
        lanes = slice(t * LANES, (t + 1) * LANES)
        scale = scale_ref[pl.ds(first + t, 1), :]
        out_ref[:, lanes] = (part_ref[:, lanes] - tile * scale).astype(BF16)


def whole(array):
    rank = len(array.shape)
    return pl.BlockSpec(array.shape, lambda i: (0,) * rank)


def fixed(*shape):
    return pl.BlockSpec(shape, lambda i: (0,) * len(shape))


def columns(rows, cols, first=0):
    return pl.BlockSpec((rows, cols), lambda i: (0, first + i))


SMEM = pl.BlockSpec(memory_space=pltpu.SMEM)
VMEM = pl.BlockSpec(memory_space=pltpu.VMEM)
ANY = pl.BlockSpec(memory_space=pl.ANY)


def params():
    return pltpu.CompilerParams(vmem_limit_bytes=VMEM_MIB * 2**20)


def cost(flops, nbytes, exps=0):
    return pl.CostEstimate(flops=int(flops), bytes_accessed=int(nbytes), transcendentals=int(exps))


def exchange(value, axis):
    return lax.all_to_all(value, axis, 0, 0)


def local(teacher_feats, student_feats, proto_weight):
    parts, groups = lax.axis_size("proto"), lax.axis_size("batch")
    own, width = teacher_feats.shape
    local_protos = proto_weight.shape[1]
    rows = own * groups
    others = rows - own
    protos = local_protos * parts
    feats = width // groups
    share = own // parts
    tiles = rows // LANES
    height = local_protos // LANES
    place = jnp.stack([lax.axis_index("batch"), lax.axis_index("proto")]).astype(jnp.int32)
    struct = jax.ShapeDtypeStruct
    weight_bytes = 2 * width * local_protos
    exp_bytes = 2 * own * local_protos
    others_bytes = 2 * others * local_protos
    spread = pltpu.VMEM((own, LANES), F32)
    unit = struct((own, width), BF16)
    all_units = struct((groups, own, width), BF16)
    token = struct((8, LANES), F32)

    t_unit, s_unit, s_all = pl.pallas_call(
        unit_kernel,
        out_shape=[unit, unit, all_units],
        compiler_params=params(),
        cost_estimate=cost(8 * own * width, 12 * own * width),
        name="unit_rows",
    )(teacher_feats, student_feats)
    s_all = exchange(s_all, "batch")

    exps = struct((own, local_protos), BF16)
    t_exp, s_exp, stats = pl.pallas_call(
        stats_kernel,
        in_specs=[VMEM, VMEM, ANY],
        out_specs=[ANY, ANY, VMEM],
        out_shape=[exps, exps, struct((parts, 4 * own // LANES, LANES), F32)],
        scratch_shapes=[
            pltpu.VMEM((width, local_protos), BF16),
            pltpu.VMEM((2, own, local_protos), BF16),
            pltpu.VMEM((2, own, local_protos), F32),
            pltpu.VMEM((2, own, LANES), F32),
            pltpu.VMEM((2, own, LANES), F32),
            pltpu.SemaphoreType.DMA((local_protos // WIDE,)),
            pltpu.SemaphoreType.DMA((2,)),
        ],
        compiler_params=params(),
        cost_estimate=cost(4 * own * width * local_protos, weight_bytes),
        name="own_rows",
    )(t_unit, s_unit, proto_weight)
    stats = exchange(stats, "proto")

    half_sweep = 2048
    sweep_grid = (local_protos // half_sweep,)
    first_shape = (groups, height + 8, LANES)
    factor, cols = pl.pallas_call(
        first_column_kernel,
        grid=sweep_grid,
        in_specs=[SMEM, whole(stats), columns(own, half_sweep)],
        out_specs=[fixed(8, LANES), fixed(*first_shape)],
        out_shape=[token, struct(first_shape, F32)],
        scratch_shapes=[spread],
        compiler_params=params(),
        cost_estimate=cost(2 * own * local_protos, exp_bytes),
        name="first_columns",
    )(place, stats, t_exp)

    back_student, t_all = pl.pallas_call(
        functools.partial(own_back_kernel, float(protos)),
        grid=sweep_grid,
        in_specs=[
            fixed(8, LANES), whole(t_unit), columns(width, half_sweep), columns(own, half_sweep),
        ],
        out_specs=[fixed(own, width), fixed(groups, own, width)],
        out_shape=[unit, all_units],
        scratch_shapes=[pltpu.VMEM((own, width), F32)],
        compiler_params=params(),
        cost_estimate=cost(2 * own * width * local_protos, weight_bytes),
        name="own_back",
    )(factor, t_unit, proto_weight, s_exp)
    t_all = exchange(t_all, "batch")
    cols = exchange(cols, "batch")
    logs = cols

    feat = pl.pallas_call(
        feature_kernel,
        in_specs=[SMEM, VMEM],
        out_specs=VMEM,
        out_shape=struct((feats, rows), BF16),
        scratch_shapes=[pltpu.VMEM((width, rows), BF16)],
        compiler_params=params(),
        cost_estimate=cost(8 * rows * width, 2 * rows * width),
        name="features",
    )(place, s_all)

    def student_piece(first, count, grad, before):
        out_struct = struct((feats, local_protos), F32)
        prior = [] if grad is None else [grad]
        return pl.pallas_call(
            functools.partial(student_kernel, math.log2(protos)),
            grid=(count,),
            in_specs=[
                SMEM, whole(s_all), whole(logs), whole(factor), whole(feat),
                columns(width, WIDE, first), columns(own, WIDE, first), ANY,
            ]
            + [ANY] * len(prior),
            out_specs=[columns(feats, WIDE, first), fixed(8, LANES)],
            out_shape=[out_struct, token],
            scratch_shapes=[
                pltpu.VMEM((feats, own), BF16),
                pltpu.VMEM((others, LANES), F32),
                pltpu.VMEM((others, WIDE), BF16),
            ],
            input_output_aliases={8: 0} if prior else {},
            compiler_params=params(),
            cost_estimate=cost(
                2.5 * rows * width * WIDE * count, 2 * width * WIDE * count
            ),
            name="student_side",
        )(place, s_all, logs, factor, feat, proto_weight, s_exp, before, *prior)

    grad_part, first, done = None, 0, None
    counts = [1, 2, 1, 2, 2]
    chunks = local_protos // WIDE
    for turn in range(SWEEPS - 1):
        sums = pl.pallas_call(
            row_kernel,
            grid=sweep_grid,
            in_specs=[whole(cols), fixed(8, LANES), ANY, columns(own, half_sweep)],
            out_specs=fixed(parts, 8, LANES),
            out_shape=struct((parts, 8, LANES), F32),
            scratch_shapes=[pltpu.VMEM((height, LANES), F32), spread],
            compiler_params=params(),
            cost_estimate=cost(2 * own * local_protos, exp_bytes),
            name="rows",
        )(cols, factor, back_student if done is None else done, t_exp)
        count = counts[2 * turn] * chunks // 8
        grad_part, done = student_piece(first, count, grad_part, sums)
        first += count
        sums = exchange(sums, "proto")
        cols = pl.pallas_call(
            column_kernel,
            grid=sweep_grid,
            in_specs=[whole(sums), fixed(8, LANES), ANY, columns(own, half_sweep)],
            out_specs=fixed(groups, height, LANES),
            out_shape=struct((groups, height, LANES), F32),
            scratch_shapes=[spread],
            compiler_params=params(),
            cost_estimate=cost(2 * own * local_protos, exp_bytes),
            name="columns",
        )(sums, factor, done, t_exp)
        count = counts[2 * turn + 1] * chunks // 8
        grad_part, done = student_piece(first, count, grad_part, cols)
        first += count
        cols = exchange(cols, "batch")

    grid = (chunks,)
    sum_rows = -(-(tiles + own // LANES) // 16) * 16
    message_shape = (parts, 2 * share + sum_rows, width)
    prob, col_scale, message = pl.pallas_call(
        last_kernel,
        grid=grid,
        in_specs=[
            SMEM, whole(t_all), whole(logs), whole(cols), whole(factor), ANY, whole(s_unit),
            whole(back_student), columns(own, WIDE), columns(width, WIDE),
        ],
        out_specs=[columns(others, WIDE), fixed(height, LANES), fixed(*message_shape)],
        out_shape=[
            struct((others, local_protos), BF16),
            struct((height, LANES), F32),
            struct(message_shape, BF16),
        ],
        scratch_shapes=[
            pltpu.VMEM((height, LANES), F32),
            pltpu.VMEM((rows, LANES), F32),
            pltpu.VMEM((own, width), F32),
            pltpu.VMEM((own, WIDE), BF16),
            pltpu.VMEM((others, LANES), F32),
            pltpu.VMEM((sum_rows, LANES), F32),
        ],
        compiler_params=params(),
        cost_estimate=cost(2 * rows * width * local_protos, others_bytes),
        name="last_rows",
    )(place, t_all, logs, cols, factor, done, s_unit, back_student, t_exp, proto_weight)
    grad_part, done = student_piece(first, chunks - first, grad_part, message)
    message = exchange(message, "proto")

    grad_rows, loss_part, sums = pl.pallas_call(
        functools.partial(rows_kernel, tiles, float(protos)),
        in_specs=[SMEM] + [VMEM] * 3,
        out_specs=[VMEM] * 3,
        out_shape=[
            struct((parts, share, width), F32),
            struct((groups, 8, LANES), F32),
            struct((sum_rows, LANES), F32),
        ],
        scratch_shapes=[spread],
        compiler_params=params(),
        name="row_grads",
    )(place, student_feats, message, logs)
    grad_rows = exchange(grad_rows, "proto").reshape(own, width)
    loss = jnp.sum(exchange(loss_part, "batch")[:, 0, 0]) / rows

    grad_weight = pl.pallas_call(
        functools.partial(grad_kernel, float(protos)),
        grid=grid,
        in_specs=[
            columns(own, WIDE), columns(others, WIDE), whole(feat), columns(feats, WIDE),
            whole(col_scale), whole(sums), fixed(8, LANES),
        ],
        out_specs=columns(feats, WIDE),
        out_shape=struct((feats, local_protos), BF16),
        scratch_shapes=[pltpu.VMEM((feats, rows), BF16)],
        compiler_params=params(),
        cost_estimate=cost(2 * feats * rows * local_protos, others_bytes),
        name="weight_grads",
    )(t_exp, prob, feat, grad_part, col_scale, sums, factor)
    return grad_weight, grad_rows, loss


def solution(mesh):
    return jax.shard_map(
        local,
        mesh=mesh,
        in_specs=(P("batch", None), P("batch", None), P(None, "proto")),
        out_specs=(P("batch", "proto"), P("batch", None), P()),
        check_vma=False,
    )
```

```python
import functools
import math

import jax
import jax.numpy as jnp
from jax import lax
from jax.experimental import pallas as pl
from jax.experimental.pallas import tpu as pltpu
from jax.sharding import PartitionSpec as P

SWEEPS = 3
TEMP_TEACHER = 0.04
TEMP_STUDENT = 0.1
LOG2E = math.log2(math.e)
SCALE_TEACHER = LOG2E / TEMP_TEACHER
SCALE_STUDENT = LOG2E / TEMP_STUDENT
LANES = 128
WIDE = 1024
F32 = jnp.float32
BF16 = jnp.bfloat16


def unit_rows(values):
    wide = values.astype(F32)
    length = jnp.sqrt(jnp.sum(wide * wide, axis=-1, keepdims=True) + 1e-06)
    return wide / length, length


def diagonal():
    shape = (LANES, LANES)
    return lax.broadcasted_iota(jnp.int32, shape, 0) == lax.broadcasted_iota(jnp.int32, shape, 1)


def to_column(row):
    spread = jnp.where(diagonal(), jnp.broadcast_to(row, (LANES, LANES)), 0.0)
    return jnp.sum(spread, axis=1, keepdims=True)


def to_row(column):
    spread = jnp.where(diagonal(), jnp.broadcast_to(column, (LANES, LANES)), 0.0)
    return jnp.sum(spread, axis=0, keepdims=True)


def spread_rows(ref, rows):
    for a in range(rows.shape[0]):
        ref[a * LANES : (a + 1) * LANES, :] = jnp.broadcast_to(
            to_column(rows[a : a + 1, :]), (LANES, LANES)
        )


def pack_rows(ref, columns):
    for a in range(columns.shape[0] // LANES):
        ref[a : a + 1, :] = to_row(columns[a * LANES : (a + 1) * LANES, :])


def lane_tiles(values):
    return [values[:, t * LANES : (t + 1) * LANES] for t in range(values.shape[1] // LANES)]


def fold(values):
    return functools.reduce(jnp.add, lane_tiles(values))


def column_sums(values):
    rows, cols = values.shape
    return jnp.sum(values.reshape(rows // 8, 8, cols), axis=0)


def nt_dot(a, b):
    return lax.dot_general(a, b, (((1,), (1,)), ((), ())), preferred_element_type=F32)


def add_up(values):
    return functools.reduce(jnp.add, values)


def repeat(out_ref):
    for p in range(1, out_ref.shape[0]):
        out_ref[p] = out_ref[0]


def w_loads(w_hbm, w_ref, sems, first=0):
    return [
        pltpu.make_async_copy(
            w_hbm.at[:, (first + k) * WIDE : (first + k + 1) * WIDE],
            w_ref.at[:, k * WIDE : (k + 1) * WIDE],
            sems.at[k],
        )
        for k in range(w_ref.shape[1] // WIDE)
    ]


def stats_kernel(
    t_ref, s_ref, w_hbm, t_exp, s_exp, out_ref, w_ref, unit, logits, top, total, w_sem
):
    chunk = 512
    cols = w_ref.shape[1]
    pieces = [slice(c, c + chunk) for c in range(0, cols, chunk)]
    quarter = out_ref.shape[1] // 4
    outs = (t_exp, s_exp)
    scales = (SCALE_TEACHER, SCALE_STUDENT)
    loads = w_loads(w_hbm, w_ref, w_sem)
    for load in loads:
        load.start()
    for which, ref in enumerate((t_ref, s_ref)):
        unit[which] = unit_rows(ref[...])[0].astype(BF16)
    top[...] = jnp.full(top.shape, -1e30, F32)
    total[...] = jnp.zeros(total.shape, F32)

    def product(which, here):
        values = jnp.dot(unit[which], w_ref[:, here], preferred_element_type=F32) * scales[which]
        top[which] = functools.reduce(jnp.maximum, lane_tiles(values), top[which])
        return values

    def peak(which):
        return jnp.max(top[which], axis=1, keepdims=True)

    def raised(which, here, shift):
        values = jnp.exp2(logits[:, here] - shift)
        outs[which][:, here] = values.astype(BF16)
        total[which] += fold(values)

    for here in pieces:
        if here.start % WIDE == 0:
            loads[here.start // WIDE].wait()
        logits[:, here] = product(0, here)
    peaks = [peak(0)]
    shift = jnp.broadcast_to(peaks[0], (peaks[0].shape[0], chunk))
    for here in pieces:
        values = product(1, here)
        raised(0, here, shift)
        logits[:, here] = values
    peaks.append(peak(1))
    shift = jnp.broadcast_to(peaks[1], (peaks[1].shape[0], chunk))
    for here in pieces:
        raised(1, here, shift)
    for which in range(2):
        sums = jnp.sum(total[which], axis=1, keepdims=True)
        for k, column in enumerate((peaks[which], sums)):
            first = (2 * which + k) * quarter
            pack_rows(out_ref.at[0, first : first + quarter], column)
    repeat(out_ref)


def merged(stats_ref, which):
    parts, height, _ = stats_ref.shape
    quarter = height // 4
    first = 2 * which * quarter
    tops = [stats_ref[p, first : first + quarter, :] for p in range(parts)]
    top = functools.reduce(jnp.maximum, tops)
    sums = [
        stats_ref[p, first + quarter : first + 2 * quarter, :] * jnp.exp2(tops[p] - top)
        for p in range(parts)
    ]
    return top + jnp.log2(add_up(sums))


def column_pass(exp_ref, weight, out_ref):
    rows, cols = exp_ref.shape
    for a in range(0, cols, WIDE):
        sums = jnp.zeros((8, WIDE), F32)
        for g in range(0, rows, 16):
            shift = weight[g : g + 16, :]
            tiles = lane_tiles(exp_ref[g : g + 16, a : a + WIDE].astype(F32))
            sums = sums + column_sums(jnp.concatenate([tile * shift for tile in tiles], axis=1))
        sums = jnp.sum(sums, axis=0, keepdims=True)
        block = jnp.concatenate(lane_tiles(sums), axis=0)
        for g in range(out_ref.shape[0]):
            out_ref[g, a // LANES : (a + WIDE) // LANES, :] = block


def first_column_kernel(place_ref, stats_ref, exp_ref, *refs):
    factor_ref, out_ref, weight = refs[-3:]
    quarter = stats_ref.shape[1] // 4
    height = out_ref.shape[1] - 8
    own = stats_ref[pl.ds(place_ref[1], 1)][0]
    factor_ref[...] = jnp.zeros(factor_ref.shape, F32)
    logs = jnp.zeros((8, LANES), F32)
    rows = []
    for which in range(2):
        log_sum = merged(stats_ref, which)
        here = slice(which * quarter, (which + 1) * quarter)
        factor_ref[here, :] = jnp.exp2(
            own[2 * which * quarter : (2 * which + 1) * quarter, :] - log_sum
        )
        rows.append(log_sum)
    rows.append(jnp.zeros((8 - 2 * quarter, LANES), F32))
    logs = jnp.concatenate(rows, axis=0)
    for g in range(out_ref.shape[0]):
        out_ref[g, height:, :] = logs
    spread_rows(weight, factor_ref[:quarter, :])
    column_pass(exp_ref, weight, out_ref)


def column_kernel(sums_ref, factor_ref, exp_ref, *refs):
    out_ref, weight = refs[-2:]
    quarter = weight.shape[0] // LANES
    scale = 1.0 / add_up([sums_ref[p, :quarter, :] for p in range(sums_ref.shape[0])])
    spread_rows(weight, scale * factor_ref[:quarter, :])
    column_pass(exp_ref, weight, out_ref)


def column_scales(cols_ref, height):
    return 1.0 / add_up([cols_ref[g, :height, :] for g in range(cols_ref.shape[0])])


def row_sums(ref, scales, step):
    sums = []
    for g in range(0, ref.shape[0], step):
        total = jnp.zeros((step, LANES), F32)
        for t, tile in enumerate(lane_tiles(ref[g : g + step, :].astype(F32))):
            total = total + tile * scales[t : t + 1, :]
        sums.append(jnp.sum(total, axis=1, keepdims=True))
    return jnp.concatenate(sums, axis=0)


def row_kernel(cols_ref, factor_ref, exp_ref, *refs):
    out_ref, scales = refs[-2:]
    scales[...] = column_scales(cols_ref, scales.shape[0])
    quarter = exp_ref.shape[0] // LANES
    out_ref[0] = jnp.zeros(out_ref.shape[1:], F32)
    pack_rows(out_ref.at[0, :quarter], row_sums(exp_ref, scales, 32))
    out_ref[0, :quarter, :] = out_ref[0, :quarter, :] * factor_ref[:quarter, :]
    repeat(out_ref)


def own_back_kernel(protos, factor_ref, exp_ref, w_hbm, back_ref, w_ref, back, w_sem):
    loads = w_loads(w_hbm, w_ref, w_sem)
    for load in loads:
        load.start()
    back[...] = jnp.zeros(back.shape, F32)
    for k, load in enumerate(loads):
        load.wait()
        here = slice(k * WIDE, (k + 1) * WIDE)
        back[...] += nt_dot(exp_ref[:, here], w_ref[:, here])
    quarter = back.shape[0] // LANES
    for a in range(quarter):
        here = slice(a * LANES, (a + 1) * LANES)
        factor = to_column(factor_ref[quarter + a : quarter + a + 1, :] * protos)
        back_ref[here, :] = (back[here, :] * factor).astype(BF16)


def relative(place_ref, g, groups):
    return pl.ds(lax.rem(place_ref[0] + g, groups), 1)


def relative_logs(place_ref, logs_ref, lse, which, shift=0.0):
    groups = logs_ref.shape[0]
    own = lse.shape[0] // (groups - 1)
    quarter = own // LANES
    height = logs_ref.shape[1] - 8
    for g in range(1, groups):
        there = logs_ref[relative(place_ref, g, groups)][0]
        first = height + which * quarter
        spread_rows(lse.at[(g - 1) * own : g * own], there[first : first + quarter, :] - shift)


def student_rows_kernel(log_protos, place_ref, logs_ref, factor_ref, own_ref, *refs):
    groups = logs_ref.shape[0]
    raw, (unit_ref, lse_ref, feat_ref, scaled_ref, turned) = refs[: groups - 1], refs[-5:]
    own = own_ref.shape[0]
    quarter, feats = own // LANES, feat_ref.shape[0]
    for g in range(groups):
        half = unit_rows((raw[g - 1] if g else own_ref)[...])[0].astype(BF16)
        if g:
            unit_ref[(g - 1) * own : g * own, :] = half
        half = half.astype(F32)
        for a in range(0, own, LANES):
            first = g * own + a
            turned[:, first : first + LANES] = jnp.transpose(half[a : a + LANES, :]).astype(BF16)
    feat = turned[pl.ds(pl.multiple_of(place_ref[0] * feats, feats), feats), :]
    feat_ref[...] = feat
    for a in range(quarter):
        lanes = slice(a * LANES, (a + 1) * LANES)
        factor = factor_ref[quarter + a : quarter + a + 1, :] * 2.0**log_protos
        scaled_ref[:, lanes] = (feat[:, lanes].astype(F32) * factor).astype(BF16)
    relative_logs(place_ref, logs_ref, lse_ref, 1, log_protos)


def probabilities(unit, own, w, lse, scale, use):
    for g in range(unit.shape[0] // own):
        here = slice(g * own, (g + 1) * own)
        for n in range(0, WIDE, 512):
            logits = jnp.dot(unit[here, :], w[:, n : n + 512], preferred_element_type=F32)
            shift = lse[here, :]
            use(g, n, [jnp.exp2(tile * scale - shift) for tile in lane_tiles(logits)])


def student_kernel(first, count, unit, lse, feat_ref, scaled_ref, exp_ref, w_hbm, *refs):
    grad_ref, token_ref, prob, w_ref, w_sem = refs[-5:]
    own = exp_ref.shape[0]
    loads = w_loads(w_hbm, w_ref, w_sem, first)
    for load in loads:
        load.start()
    token_ref[...] = jnp.zeros(token_ref.shape, F32)
    for k, load in enumerate(loads):
        load.wait()
        here = slice((first + k) * WIDE, (first + k + 1) * WIDE)
        slot = prob.at[k % 2]

        def use(g, n, tiles):
            for t, tile in enumerate(tiles):
                lanes = slice(n + t * LANES, n + (t + 1) * LANES)
                slot[g * own : (g + 1) * own, lanes] = tile.astype(BF16)

        probabilities(unit, own, w_ref.at[:, k * WIDE : (k + 1) * WIDE], lse, SCALE_STUDENT, use)
        grad_ref[:, here] = jnp.dot(
            scaled_ref[...], exp_ref[:, here], preferred_element_type=F32
        ) + jnp.dot(feat_ref[:, own:], slot[...], preferred_element_type=F32)


def as_three(value):
    high = value.astype(BF16)
    rest = value - high.astype(F32)
    middle = rest.astype(BF16)
    return high, middle, (rest - middle.astype(F32)).astype(BF16)


def last_kernel(groups, place_ref, logs_ref, cols_ref, factor_ref, own_ref, student_ref, exp_ref, w_hbm, *refs):
    raw = refs[: groups - 1]
    prob_ref, scale_ref, out_ref, unit, lse, rows, back, scaled, sums, w_ref, w_sem = refs[-11:]
    own, others = exp_ref.shape[0], prob_ref.shape[0]
    tiles = (own + others) // LANES
    quarter = own // LANES
    loads = w_loads(w_hbm, w_ref, w_sem)
    for load in loads:
        load.start()
    scale_ref[...] = column_scales(cols_ref, scale_ref.shape[0])
    rows[...] = jnp.zeros(rows.shape, F32)
    back[...] = jnp.zeros(back.shape, F32)
    relative_logs(place_ref, logs_ref, lse, 0)
    for g in range(groups - 1):
        unit[g * own : (g + 1) * own, :] = unit_rows(raw[g][...])[0].astype(BF16)

    @pl.loop(0, len(loads))
    def _(k):
        here = pl.ds(pl.multiple_of(k * WIDE, WIDE), WIDE)
        pltpu.make_async_copy(w_hbm.at[:, here], w_ref.at[:, here], w_sem.at[k]).wait()
        scales = scale_ref[pl.ds(pl.multiple_of(k * (WIDE // LANES), 8), WIDE // LANES), :]

        def use(g, n, tiles):
            first = n // LANES
            for t, tile in enumerate(tiles):
                lanes = pl.ds(pl.multiple_of(k * WIDE + n + t * LANES, LANES), LANES)
                prob_ref[g * own : (g + 1) * own, lanes] = tile.astype(BF16)
            tiles = [
                tile * scales[first + t : first + t + 1, :] for t, tile in enumerate(tiles)
            ]
            rows[g * own : (g + 1) * own, :] += add_up(tiles)
            if g == groups // 2 - 1:
                for t, tile in enumerate(tiles):
                    scaled[:, n + t * LANES : n + (t + 1) * LANES] = tile.astype(BF16)

        probabilities(unit, own, w_ref.at[:, here], lse, SCALE_TEACHER, use)
        back[...] += nt_dot(scaled[...], w_ref[:, here])

    sums[...] = jnp.zeros(sums.shape, F32)
    pack_rows(sums.at[:quarter], row_sums(exp_ref, scale_ref, 32))
    sums[:quarter, :] = sums[:quarter, :] * factor_ref[:quarter, :]
    pack_rows(sums.at[quarter:tiles], jnp.sum(rows[...], axis=1, keepdims=True))
    half = unit_rows(own_ref[...])[0].astype(BF16).astype(F32)
    inner = jnp.sum(half * back[...], axis=1, keepdims=True)
    pack_rows(sums.at[tiles : tiles + quarter], inner)
    parts = out_ref.shape[0]
    share = own // parts
    terms = list(as_three(sums[...]))
    terms.append(jnp.zeros((sums.shape[0], out_ref.shape[2] - 3 * LANES), BF16))
    terms = jnp.concatenate(terms, axis=1)
    for p in range(parts):
        here = slice(p * share, (p + 1) * share)
        out_ref[p] = jnp.concatenate(
            [student_ref[here, :], back[here, :].astype(BF16), terms], axis=0
        )


def total_sums(message_ref, first):
    parts = message_ref.shape[0]
    each = [
        add_up([t.astype(F32) for t in lane_tiles(message_ref[p, first:, : 3 * LANES])[::-1]])
        for p in range(parts)
    ]
    return add_up(each)


def rows_kernel(tiles, protos, place_ref, s_ref, message_ref, logs_ref, *refs):
    out_ref, loss_ref, sums_ref, weight = refs[-4:]
    parts = message_ref.shape[0]
    share, own = out_ref.shape[1], weight.shape[0]
    quarter = own // LANES
    first = tiles // 2
    totals = total_sums(message_ref, 2 * share)
    sums_ref[...] = totals
    scale = 1.0 / totals[first : first + quarter, :]
    spread_rows(weight, scale)
    mine = pl.ds(pl.multiple_of(place_ref[1] * share, share), share)
    total = add_up([message_ref[p, :share, :].astype(F32) for p in range(parts)])
    paired = add_up([message_ref[p, share : 2 * share, :].astype(F32) for p in range(parts)])
    total = total - paired * (weight[mine, :1] * protos)
    unit, length = unit_rows(s_ref[mine, :])
    out_ref[0] = (total - unit * jnp.sum(unit * total, axis=-1, keepdims=True)) / length
    repeat(out_ref)
    height = logs_ref.shape[1] - 8
    logs = logs_ref[pl.ds(place_ref[0], 1)][0][height + quarter : height + 2 * quarter, :]
    terms = logs / LOG2E - totals[tiles : tiles + quarter, :] * scale / TEMP_STUDENT
    loss_ref[...] = jnp.broadcast_to(jnp.sum(terms), loss_ref.shape)


def grad_kernel(protos, exp_ref, prob_ref, feat_ref, part_ref, scale_ref, sums_ref, factor_ref, out_hbm, scaled, out, sem):
    own = exp_ref.shape[0]
    tiles = (own + prob_ref.shape[0]) // LANES
    rows = protos / sums_ref[:tiles, :]
    for a in range(tiles):
        other = (a + tiles // 2) % tiles
        feat = feat_ref[:, other * LANES : (other + 1) * LANES].astype(F32)
        row = rows[a : a + 1, :]
        if a < own // LANES:
            row = row * factor_ref[a : a + 1, :]
        scaled[:, a * LANES : (a + 1) * LANES] = (feat * row).astype(BF16)
    copies = []
    for k in range(out.shape[1] // WIDE):
        here = slice(k * WIDE, (k + 1) * WIDE)
        paired = jnp.dot(scaled[:, :own], exp_ref[:, here], preferred_element_type=F32)
        paired = paired + jnp.dot(scaled[:, own:], prob_ref[:, here], preferred_element_type=F32)
        for t, tile in enumerate(lane_tiles(paired)):
            lanes = slice(k * WIDE + t * LANES, k * WIDE + (t + 1) * LANES)
            scale = scale_ref[lanes.start // LANES : lanes.stop // LANES, :]
            out[:, lanes] = (part_ref[:, lanes] - tile * scale).astype(BF16)
        copies.append(pltpu.make_async_copy(out.at[:, here], out_hbm.at[:, here], sem.at[k]))
        copies[-1].start()
    for copy in copies:
        copy.wait()


SMEM = pl.BlockSpec(memory_space=pltpu.SMEM)
VMEM = pl.BlockSpec(memory_space=pltpu.VMEM)
ANY = pl.BlockSpec(memory_space=pl.ANY)


def params(nbytes):
    return pltpu.CompilerParams(vmem_limit_bytes=int(nbytes) + 8 * 2**20)


def cost(flops, nbytes, exps=0):
    return pl.CostEstimate(flops=int(flops), bytes_accessed=int(nbytes), transcendentals=int(exps))


def exchange(value, axis):
    return lax.all_to_all(value, axis, 0, 0)


def following(value, axis):
    n = lax.axis_size(axis)
    return [lax.ppermute(value, axis, [(i, (i - s) % n) for i in range(n)]) for s in range(1, n)]


def tree_sum(value, axis):
    n = lax.axis_size(axis)
    values = [value] + [
        lax.ppermute(value, axis, [(i, i ^ s) for i in range(n)]) for s in range(1, n)
    ]
    while len(values) > 1:
        values = [a + b for a, b in zip(values[::2], values[1::2])]
    return values[0]


def local(teacher_feats, student_feats, proto_weight):
    parts, groups = lax.axis_size("proto"), lax.axis_size("batch")
    own, width = teacher_feats.shape
    local_protos = proto_weight.shape[1]
    rows = own * groups
    others = rows - own
    protos = local_protos * parts
    feats = width // groups
    share = own // parts
    tiles = rows // LANES
    height = local_protos // LANES
    chunks = local_protos // WIDE
    place = jnp.stack([lax.axis_index("batch"), lax.axis_index("proto")]).astype(jnp.int32)
    struct = jax.ShapeDtypeStruct
    weight_bytes = 2 * width * local_protos
    exp_bytes = 2 * own * local_protos
    others_bytes = 2 * others * local_protos
    spread = pltpu.VMEM((own, LANES), F32)
    w_buffer = pltpu.VMEM((width, local_protos), BF16)
    w_sems = pltpu.SemaphoreType.DMA((chunks,))
    weight_here = pltpu.with_memory_space_constraint(proto_weight, pltpu.HBM)
    token = struct((8, LANES), F32)

    s_all = following(student_feats, "batch")
    t_all = following(teacher_feats, "batch")

    exps = pltpu.VMEM((own, local_protos), BF16)
    t_exp, s_exp, stats = pl.pallas_call(
        stats_kernel,
        in_specs=[VMEM, VMEM, ANY],
        out_specs=[VMEM, VMEM, VMEM],
        out_shape=[exps, exps, struct((parts, 4 * own // LANES, LANES), F32)],
        scratch_shapes=[
            w_buffer,
            pltpu.VMEM((2, own, width), BF16),
            pltpu.VMEM((own, local_protos), F32),
            pltpu.VMEM((2, own, LANES), F32),
            pltpu.VMEM((2, own, LANES), F32),
            w_sems,
        ],
        compiler_params=params(weight_bytes + 2 * exp_bytes),
        cost_estimate=cost(4 * own * width * local_protos, weight_bytes),
        name="own_rows",
    )(teacher_feats, student_feats, weight_here)
    stats = exchange(stats, "proto")

    def pinned(value):
        return pltpu.with_memory_space_constraint(value, pltpu.VMEM)

    first_shape = (groups, height + 8, LANES)
    factor, cols = pl.pallas_call(
        first_column_kernel,
        in_specs=[SMEM, VMEM, VMEM] + [ANY] * (groups - 1),
        out_specs=[VMEM, VMEM],
        out_shape=[token, struct(first_shape, F32)],
        scratch_shapes=[spread],
        compiler_params=params(0),
        cost_estimate=cost(2 * own * local_protos, exp_bytes),
        name="first_columns",
    )(place, stats, pinned(t_exp), *s_all)

    back_student = pl.pallas_call(
        functools.partial(own_back_kernel, float(protos)),
        in_specs=[VMEM, VMEM, ANY],
        out_specs=VMEM,
        out_shape=struct((own, width), BF16),
        scratch_shapes=[w_buffer, pltpu.VMEM((own, width), F32), w_sems],
        compiler_params=params(weight_bytes),
        cost_estimate=cost(2 * own * width * local_protos, weight_bytes),
        name="own_back",
    )(factor, pinned(s_exp), weight_here)
    cols = exchange(cols, "batch")
    logs = cols

    done = [back_student]
    counts = [1, 2, 1, 2, 2]
    grad_part, first = None, 0
    unit = lse = feat = scaled = None
    for turn in range(SWEEPS - 1):
        sums = pl.pallas_call(
            row_kernel,
            in_specs=[VMEM] * 3 + [ANY] * len(done),
            out_specs=VMEM,
            out_shape=struct((parts, 8, LANES), F32),
            scratch_shapes=[pltpu.VMEM((height, LANES), F32)],
            compiler_params=params(0),
            cost_estimate=cost(2 * own * local_protos, exp_bytes),
            name="rows",
        )(cols, factor, pinned(t_exp), *done)
        if turn == 0:
            unit, lse, feat, scaled = pl.pallas_call(
                functools.partial(student_rows_kernel, math.log2(protos)),
                in_specs=[SMEM, VMEM, VMEM, VMEM] + [VMEM] * (groups - 1) + [ANY],
                out_specs=[VMEM] * 4,
                out_shape=[
                    struct((others, width), BF16),
                    struct((others, LANES), F32),
                    struct((feats, rows), BF16),
                    struct((feats, own), BF16),
                ],
                scratch_shapes=[pltpu.VMEM((width, rows), BF16)],
                compiler_params=params(2 * rows * width),
                cost_estimate=cost(8 * rows * width, 2 * rows * width),
                name="student_rows",
            )(place, logs, factor, student_feats, *s_all, sums)

        def student_piece(turn, before):
            nonlocal grad_part, first
            count = counts[turn] * chunks // 8
            if turn == 2 * (SWEEPS - 1):
                count = chunks - first
            prior = [] if grad_part is None else [pinned(grad_part)]
            grad_part, token_out = pl.pallas_call(
                functools.partial(student_kernel, first, count),
                in_specs=[VMEM] * 5 + [ANY] + [ANY] + [VMEM] * len(prior),
                out_specs=[VMEM, VMEM],
                out_shape=[pltpu.VMEM((feats, local_protos), F32), token],
                scratch_shapes=[
                    pltpu.VMEM((2, others, WIDE), BF16),
                    pltpu.VMEM((width, count * WIDE), BF16),
                    pltpu.SemaphoreType.DMA((count,)),
                ],
                input_output_aliases={7: 0} if prior else {},
                compiler_params=params(8 * 2**20),
                cost_estimate=cost(
                    2.5 * rows * width * WIDE * count, 2 * width * WIDE * count
                ),
                name="student_side",
            )(unit, lse, feat, scaled, pinned(s_exp), weight_here, before, *prior)
            first += count
            return token_out

        done = [student_piece(2 * turn, sums)]
        sums = exchange(sums, "proto")
        late = t_all if turn == 0 else []
        cols = pl.pallas_call(
            column_kernel,
            in_specs=[VMEM] * 3 + [ANY] * (len(done) + len(late)),
            out_specs=VMEM,
            out_shape=struct((groups, height, LANES), F32),
            scratch_shapes=[spread],
            compiler_params=params(0),
            cost_estimate=cost(2 * own * local_protos, exp_bytes),
            name="columns",
        )(sums, factor, pinned(t_exp), *done, *late)
        done = [student_piece(2 * turn + 1, cols)]
        cols = exchange(cols, "batch")

    sum_rows = -(-(tiles + own // LANES) // 16) * 16
    message_shape = (parts, 2 * share + sum_rows, width)
    prob, col_scale, message = pl.pallas_call(
        functools.partial(last_kernel, groups),
        in_specs=[SMEM] + [VMEM] * 6 + [ANY] + [VMEM] * (groups - 1) + [ANY] * len(done),
        out_specs=[VMEM] * 3,
        out_shape=[
            pltpu.VMEM((others, local_protos), BF16),
            struct((height, LANES), F32),
            struct(message_shape, BF16),
        ],
        scratch_shapes=[
            pltpu.VMEM((others, width), BF16),
            pltpu.VMEM((others, LANES), F32),
            pltpu.VMEM((others, LANES), F32),
            pltpu.VMEM((own, width), F32),
            pltpu.VMEM((own, WIDE), BF16),
            pltpu.VMEM((sum_rows, LANES), F32),
            w_buffer,
            w_sems,
        ],
        compiler_params=params(weight_bytes),
        cost_estimate=cost(2 * rows * width * local_protos, others_bytes),
        name="last_rows",
    )(
        place, logs, cols, factor, student_feats, back_student, pinned(t_exp), weight_here,
        *t_all, *done,
    )
    done = [student_piece(2 * (SWEEPS - 1), message)]
    message = exchange(message, "proto")

    grad_rows, loss_part, sums = pl.pallas_call(
        functools.partial(rows_kernel, tiles, float(protos)),
        in_specs=[SMEM] + [VMEM] * 3 + [ANY] * len(done),
        out_specs=[VMEM] * 3,
        out_shape=[struct((parts, share, width), F32), token, struct((sum_rows, LANES), F32)],
        scratch_shapes=[spread],
        compiler_params=params(0),
        name="row_grads",
    )(place, student_feats, message, logs, *done)
    grad_rows = exchange(grad_rows, "proto").reshape(own, width)
    loss = tree_sum(loss_part, "batch")[0, 0] / rows

    grad_weight = pl.pallas_call(
        functools.partial(grad_kernel, float(protos)),
        in_specs=[VMEM] * 7,
        out_specs=ANY,
        out_shape=struct((feats, local_protos), BF16),
        scratch_shapes=[
            pltpu.VMEM((feats, rows), BF16), pltpu.VMEM((feats, local_protos), BF16), w_sems,
        ],
        compiler_params=params(2 * feats * local_protos),
        cost_estimate=cost(2 * feats * rows * local_protos, others_bytes),
        name="weight_grads",
    )(pinned(t_exp), pinned(prob), feat, pinned(grad_part), col_scale, sums, factor)
    return grad_weight, grad_rows, loss


def solution(mesh):
    return jax.shard_map(
        local,
        mesh=mesh,
        in_specs=(P("batch", None), P("batch", None), P(None, "proto")),
        out_specs=(P("batch", "proto"), P("batch", None), P()),
        check_vma=False,
    )
```

```python
import functools
import math

import jax
import jax.numpy as jnp
from jax import lax
from jax.experimental import pallas as pl
from jax.experimental.pallas import tpu as pltpu
from jax.sharding import PartitionSpec as P

SWEEPS = 3
TEMP_TEACHER = 0.04
TEMP_STUDENT = 0.1
LOG2E = math.log2(math.e)
SCALE_TEACHER = LOG2E / TEMP_TEACHER
SCALE_STUDENT = LOG2E / TEMP_STUDENT
LANES = 128
WIDE = 1024
F32 = jnp.float32
BF16 = jnp.bfloat16


def unit_rows(values):
    wide = values.astype(F32)
    length = jnp.sqrt(jnp.sum(wide * wide, axis=-1, keepdims=True) + 1e-06)
    return wide / length, length


def diagonal():
    shape = (LANES, LANES)
    return lax.broadcasted_iota(jnp.int32, shape, 0) == lax.broadcasted_iota(jnp.int32, shape, 1)


def to_column(row):
    spread = jnp.where(diagonal(), jnp.broadcast_to(row, (LANES, LANES)), 0.0)
    return jnp.sum(spread, axis=1, keepdims=True)


def to_row(column):
    spread = jnp.where(diagonal(), jnp.broadcast_to(column, (LANES, LANES)), 0.0)
    return jnp.sum(spread, axis=0, keepdims=True)


def spread_rows(ref, rows):
    for a in range(rows.shape[0]):
        ref[a * LANES : (a + 1) * LANES, :] = jnp.broadcast_to(
            to_column(rows[a : a + 1, :]), (LANES, LANES)
        )


def pack_rows(ref, columns):
    for a in range(columns.shape[0] // LANES):
        ref[a : a + 1, :] = to_row(columns[a * LANES : (a + 1) * LANES, :])


def lane_tiles(values):
    return [values[:, t * LANES : (t + 1) * LANES] for t in range(values.shape[1] // LANES)]


def fold(values):
    return functools.reduce(jnp.add, lane_tiles(values))


def column_sums(values):
    rows, cols = values.shape
    return jnp.sum(values.reshape(rows // 8, 8, cols), axis=0)


def nt_dot(a, b):
    return lax.dot_general(a, b, (((1,), (1,)), ((), ())), preferred_element_type=F32)


def add_up(values):
    return functools.reduce(jnp.add, values)


def repeat(out_ref):
    for p in range(1, out_ref.shape[0]):
        out_ref[p] = out_ref[0]


def chunk_copies(source, target, sems, first=0, back=0):
    count = min(source.shape[1], target.shape[1]) // WIDE
    return [
        pltpu.make_async_copy(
            source.at[:, (first + k) * WIDE : (first + k + 1) * WIDE],
            target.at[:, (back + k) * WIDE : (back + k + 1) * WIDE],
            sems.at[k],
        )
        for k in range(count)
    ]


def start(*copies):
    for each in zip(*copies):
        for copy in each:
            copy.start()


def chunk(k):
    return slice(k * WIDE, (k + 1) * WIDE)


def stats_kernel(
    t_ref, s_ref, w_hbm, t_out, s_out, out_ref,
    w_ref, unit, exps, logits, top, total, w_sem, t_sem, s_sem,
):
    piece = 512
    cols = w_ref.shape[1]
    pieces = [slice(c, c + piece) for c in range(0, cols, piece)]
    quarter = out_ref.shape[1] // 4
    scales = (SCALE_TEACHER, SCALE_STUDENT)
    loads = chunk_copies(w_hbm, w_ref, w_sem)
    start(loads)
    stores = [
        chunk_copies(exps.at[0], t_out, t_sem), chunk_copies(exps.at[1], s_out, s_sem),
    ]
    for which, ref in enumerate((t_ref, s_ref)):
        unit[which] = unit_rows(ref[...])[0].astype(BF16)
    top[...] = jnp.full(top.shape, -1e30, F32)
    total[...] = jnp.zeros(total.shape, F32)

    def product(which, here):
        values = jnp.dot(unit[which], w_ref[:, here], preferred_element_type=F32) * scales[which]
        top[which] = functools.reduce(jnp.maximum, lane_tiles(values), top[which])
        return values

    def peak(which):
        return jnp.max(top[which], axis=1, keepdims=True)

    def raised(which, here, shift):
        values = jnp.exp2(logits[:, here] - shift)
        exps[which, :, here] = values.astype(BF16)
        total[which] += fold(values)
        if here.stop % WIDE == 0:
            stores[which][here.stop // WIDE - 1].start()

    for here in pieces:
        if here.start % WIDE == 0:
            loads[here.start // WIDE].wait()
        logits[:, here] = product(0, here)
    peaks = [peak(0)]
    shift = jnp.broadcast_to(peaks[0], (peaks[0].shape[0], piece))
    for here in pieces:
        values = product(1, here)
        raised(0, here, shift)
        logits[:, here] = values
    peaks.append(peak(1))
    shift = jnp.broadcast_to(peaks[1], (peaks[1].shape[0], piece))
    for here in pieces:
        raised(1, here, shift)
    for which in range(2):
        sums = jnp.sum(total[which], axis=1, keepdims=True)
        for k, column in enumerate((peaks[which], sums)):
            first = (2 * which + k) * quarter
            pack_rows(out_ref.at[0, first : first + quarter], column)
    repeat(out_ref)
    for copy in stores[0] + stores[1]:
        copy.wait()


def merged(stats_ref, which):
    parts, height, _ = stats_ref.shape
    quarter = height // 4
    first = 2 * which * quarter
    tops = [stats_ref[p, first : first + quarter, :] for p in range(parts)]
    top = functools.reduce(jnp.maximum, tops)
    sums = [
        stats_ref[p, first + quarter : first + 2 * quarter, :] * jnp.exp2(tops[p] - top)
        for p in range(parts)
    ]
    return top + jnp.log2(add_up(sums))


def column_pass(loads, exp_ref, weight, out_ref):
    for k, load in enumerate(loads):
        load.wait()
        sums = jnp.zeros((8, WIDE), F32)
        for g in range(0, exp_ref.shape[0], 16):
            shift = weight[g : g + 16, :]
            tiles = lane_tiles(exp_ref[g : g + 16, chunk(k)].astype(F32))
            sums = sums + column_sums(jnp.concatenate([tile * shift for tile in tiles], axis=1))
        sums = jnp.sum(sums, axis=0, keepdims=True)
        block = jnp.concatenate(lane_tiles(sums), axis=0)
        for g in range(out_ref.shape[0]):
            out_ref[g, k * (WIDE // LANES) : (k + 1) * (WIDE // LANES), :] = block


def first_column_kernel(place_ref, stats_ref, exp_hbm, *refs):
    factor_ref, out_ref, weight, exp_ref, sem = refs[-5:]
    loads = chunk_copies(exp_hbm, exp_ref, sem)
    start(loads)
    quarter = stats_ref.shape[1] // 4
    height = out_ref.shape[1] - 8
    own = stats_ref[pl.ds(place_ref[1], 1)][0]
    factor_ref[...] = jnp.zeros(factor_ref.shape, F32)
    rows = []
    for which in range(2):
        log_sum = merged(stats_ref, which)
        here = slice(which * quarter, (which + 1) * quarter)
        factor_ref[here, :] = jnp.exp2(
            own[2 * which * quarter : (2 * which + 1) * quarter, :] - log_sum
        )
        rows.append(log_sum)
    rows.append(jnp.zeros((8 - 2 * quarter, LANES), F32))
    logs = jnp.concatenate(rows, axis=0)
    for g in range(out_ref.shape[0]):
        out_ref[g, height:, :] = logs
    spread_rows(weight, factor_ref[:quarter, :])
    column_pass(loads, exp_ref, weight, out_ref)


def column_kernel(sums_ref, factor_ref, exp_hbm, *refs):
    out_ref, weight, exp_ref, sem = refs[-4:]
    loads = chunk_copies(exp_hbm, exp_ref, sem)
    start(loads)
    quarter = weight.shape[0] // LANES
    scale = 1.0 / add_up([sums_ref[p, :quarter, :] for p in range(sums_ref.shape[0])])
    spread_rows(weight, scale * factor_ref[:quarter, :])
    column_pass(loads, exp_ref, weight, out_ref)


def column_scales(cols_ref, height):
    return 1.0 / add_up([cols_ref[g, :height, :] for g in range(cols_ref.shape[0])])


def add_row_sums(rows, ref, scales, k):
    for g in range(0, ref.shape[0], 32):
        total = rows[g : g + 32, :]
        for t, tile in enumerate(lane_tiles(ref[g : g + 32, chunk(k)].astype(F32))):
            first = k * (WIDE // LANES) + t
            total = total + tile * scales[first : first + 1, :]
        rows[g : g + 32, :] = total


def row_kernel(cols_ref, factor_ref, exp_hbm, *refs):
    out_ref, scales, rows, exp_ref, sem = refs[-5:]
    loads = chunk_copies(exp_hbm, exp_ref, sem)
    start(loads)
    scales[...] = column_scales(cols_ref, scales.shape[0])
    rows[...] = jnp.zeros(rows.shape, F32)
    quarter = rows.shape[0] // LANES
    out_ref[0] = jnp.zeros(out_ref.shape[1:], F32)
    for k, load in enumerate(loads):
        load.wait()
        add_row_sums(rows, exp_ref, scales, k)
    pack_rows(out_ref.at[0, :quarter], jnp.sum(rows[...], axis=1, keepdims=True))
    out_ref[0, :quarter, :] = out_ref[0, :quarter, :] * factor_ref[:quarter, :]
    repeat(out_ref)


def own_back_kernel(before_ref, exp_hbm, w_hbm, back_ref, exp_ref, w_ref, exp_sem, w_sem):
    exp_loads = chunk_copies(exp_hbm, exp_ref, exp_sem)
    w_loads = chunk_copies(w_hbm, w_ref, w_sem)
    start(exp_loads, w_loads)
    back_ref[...] = jnp.zeros(back_ref.shape, F32)
    for k in range(len(w_loads)):
        exp_loads[k].wait()
        w_loads[k].wait()
        back_ref[...] += nt_dot(exp_ref[:, chunk(k)], w_ref[:, chunk(k)])


def relative(place_ref, g, groups):
    return pl.ds(lax.rem(place_ref[0] + g, groups), 1)


def relative_logs(place_ref, logs_ref, lse, which, shift=0.0):
    groups = logs_ref.shape[0]
    own = lse.shape[0] // (groups - 1)
    quarter = own // LANES
    height = logs_ref.shape[1] - 8
    for g in range(1, groups):
        there = logs_ref[relative(place_ref, g, groups)][0]
        first = height + which * quarter
        spread_rows(lse.at[(g - 1) * own : g * own], there[first : first + quarter, :] - shift)


def student_rows_kernel(log_protos, place_ref, factor_ref, own_ref, *refs):
    unit_ref, feat_ref, scaled_ref, turned = refs[-4:]
    own = own_ref.shape[0]
    groups = turned.shape[1] // own
    raw = refs[: groups - 1]
    quarter, feats = own // LANES, feat_ref.shape[0]
    for g in range(groups):
        half = unit_rows((raw[g - 1] if g else own_ref)[...])[0].astype(BF16)
        if g:
            unit_ref[(g - 1) * own : g * own, :] = half
        half = half.astype(F32)
        for a in range(0, own, LANES):
            first = g * own + a
            turned[:, first : first + LANES] = jnp.transpose(half[a : a + LANES, :]).astype(BF16)
    feat = turned[pl.ds(pl.multiple_of(place_ref[0] * feats, feats), feats), :]
    feat_ref[...] = feat
    for a in range(quarter):
        lanes = slice(a * LANES, (a + 1) * LANES)
        factor = factor_ref[quarter + a : quarter + a + 1, :] * 2.0**log_protos
        scaled_ref[:, lanes] = (feat[:, lanes].astype(F32) * factor).astype(BF16)


def probabilities(unit, own, w, lse, scale, use):
    blocks = [(g, n) for g in range(unit.shape[0] // own) for n in range(0, WIDE, 512)]

    def product(g, n):
        return jnp.dot(
            unit[g * own : (g + 1) * own, :], w[:, n : n + 512], preferred_element_type=F32
        )

    logits = product(*blocks[0])
    for i, (g, n) in enumerate(blocks):
        later = product(*blocks[i + 1]) if i + 1 < len(blocks) else None
        shift = lse[g * own : (g + 1) * own, :]
        use(g, n, [jnp.exp2(tile * scale - shift) for tile in lane_tiles(logits)])
        logits = later


def student_kernel(
    log_protos, first, place_ref, logs_ref, unit, feat_ref, scaled_ref, exp_hbm, w_hbm, *refs
):
    grad_hbm, token_ref, lse, prob, exp_ref, w_ref, grad, exp_sem, w_sem, grad_sem = refs[-10:]
    own = exp_ref.shape[0]
    exp_loads = chunk_copies(exp_hbm, exp_ref, exp_sem, first)
    w_loads = chunk_copies(w_hbm, w_ref, w_sem, first)
    stores = chunk_copies(grad, grad_hbm, grad_sem)
    start(w_loads, exp_loads)
    token_ref[...] = jnp.zeros(token_ref.shape, F32)
    relative_logs(place_ref, logs_ref, lse, 1, log_protos)
    for k in range(len(w_loads)):
        w_loads[k].wait()
        slot = prob.at[k % 2]

        def use(g, n, tiles):
            for t, tile in enumerate(tiles):
                lanes = slice(n + t * LANES, n + (t + 1) * LANES)
                slot[g * own : (g + 1) * own, lanes] = tile.astype(BF16)

        probabilities(unit, own, w_ref.at[:, chunk(k)], lse, SCALE_STUDENT, use)
        exp_loads[k].wait()
        grad[:, chunk(k)] = jnp.dot(
            scaled_ref[...], exp_ref[:, chunk(k)], preferred_element_type=F32
        ) + jnp.dot(feat_ref[:, own:], slot[...], preferred_element_type=F32)
        stores[k].start()
    for store in stores:
        store.wait()


def as_three(value):
    high = value.astype(BF16)
    rest = value - high.astype(F32)
    middle = rest.astype(BF16)
    return high, middle, (rest - middle.astype(F32)).astype(BF16)


def last_kernel(groups, place_ref, logs_ref, cols_ref, factor_ref, own_ref, student_ref, exp_hbm, w_hbm, *refs):
    raw = refs[: groups - 1]
    (
        prob_hbm, scale_ref, out_ref, unit, lse, rows, own_rows, back, scaled, sums,
        exp_ref, w_ref, prob_ref, exp_sem, w_sem, prob_sem,
    ) = refs[-16:]
    own, others = exp_ref.shape[0], prob_ref.shape[0]
    tiles = (own + others) // LANES
    quarter = own // LANES
    loads = chunk_copies(w_hbm, w_ref, w_sem)
    exp_loads = chunk_copies(exp_hbm, exp_ref, exp_sem)
    start(loads)
    start(exp_loads)
    scale_ref[...] = column_scales(cols_ref, scale_ref.shape[0])
    rows[...] = jnp.zeros(rows.shape, F32)
    back[...] = jnp.zeros(back.shape, F32)
    relative_logs(place_ref, logs_ref, lse, 0)
    for g in range(groups - 1):
        unit[g * own : (g + 1) * own, :] = unit_rows(raw[g][...])[0].astype(BF16)

    @pl.loop(0, len(loads))
    def _(k):
        here = pl.ds(pl.multiple_of(k * WIDE, WIDE), WIDE)
        pltpu.make_async_copy(w_hbm.at[:, here], w_ref.at[:, here], w_sem.at[k]).wait()
        scales = scale_ref[pl.ds(pl.multiple_of(k * (WIDE // LANES), 8), WIDE // LANES), :]

        def use(g, n, tiles):
            first = n // LANES
            for t, tile in enumerate(tiles):
                lanes = pl.ds(pl.multiple_of(k * WIDE + n + t * LANES, LANES), LANES)
                prob_ref[g * own : (g + 1) * own, lanes] = tile.astype(BF16)
            tiles = [
                tile * scales[first + t : first + t + 1, :] for t, tile in enumerate(tiles)
            ]
            rows[g * own : (g + 1) * own, :] += add_up(tiles)
            if g == groups // 2 - 1:
                for t, tile in enumerate(tiles):
                    scaled[:, n + t * LANES : n + (t + 1) * LANES] = tile.astype(BF16)

        probabilities(unit, own, w_ref.at[:, here], lse, SCALE_TEACHER, use)
        pltpu.make_async_copy(prob_ref.at[:, here], prob_hbm.at[:, here], prob_sem.at[k]).start()
        back[...] += nt_dot(scaled[...], w_ref[:, here])

    sums[...] = jnp.zeros(sums.shape, F32)
    own_rows[...] = jnp.zeros(own_rows.shape, F32)
    for k, load in enumerate(exp_loads):
        load.wait()
        add_row_sums(own_rows, exp_ref, scale_ref, k)
    pack_rows(sums.at[:quarter], jnp.sum(own_rows[...], axis=1, keepdims=True))
    sums[:quarter, :] = sums[:quarter, :] * factor_ref[:quarter, :]
    pack_rows(sums.at[quarter:tiles], jnp.sum(rows[...], axis=1, keepdims=True))
    half = unit_rows(own_ref[...])[0].astype(BF16).astype(F32)
    inner = jnp.sum(half * back[...], axis=1, keepdims=True)
    pack_rows(sums.at[tiles : tiles + quarter], inner)
    parts = out_ref.shape[0]
    share = own // parts
    protos = 1.0 * out_ref.shape[0] * w_ref.shape[1]
    student = []
    for a in range(quarter):
        factor = to_column(factor_ref[quarter + a : quarter + a + 1, :] * protos)
        student.append(student_ref[a * LANES : (a + 1) * LANES, :] * factor)
    student = jnp.concatenate(student, axis=0).astype(BF16)
    terms = list(as_three(sums[...]))
    terms.append(jnp.zeros((sums.shape[0], out_ref.shape[2] - 3 * LANES), BF16))
    terms = jnp.concatenate(terms, axis=1)
    for p in range(parts):
        here = slice(p * share, (p + 1) * share)
        out_ref[p] = jnp.concatenate(
            [student[here, :], back[here, :].astype(BF16), terms], axis=0
        )
    for store in chunk_copies(prob_ref, prob_hbm, prob_sem):
        store.wait()


def total_sums(message_ref, first):
    parts = message_ref.shape[0]
    each = [
        add_up([t.astype(F32) for t in lane_tiles(message_ref[p, first:, : 3 * LANES])[::-1]])
        for p in range(parts)
    ]
    return add_up(each)


def rows_kernel(tiles, protos, place_ref, s_ref, message_ref, logs_ref, *refs):
    out_ref, loss_ref, sums_ref, weight = refs[-4:]
    parts = message_ref.shape[0]
    share, own = out_ref.shape[1], weight.shape[0]
    quarter = own // LANES
    first = tiles // 2
    totals = total_sums(message_ref, 2 * share)
    sums_ref[...] = totals
    scale = 1.0 / totals[first : first + quarter, :]
    spread_rows(weight, scale)
    mine = pl.ds(pl.multiple_of(place_ref[1] * share, share), share)
    total = add_up([message_ref[p, :share, :].astype(F32) for p in range(parts)])
    paired = add_up([message_ref[p, share : 2 * share, :].astype(F32) for p in range(parts)])
    total = total - paired * (weight[mine, :1] * protos)
    unit, length = unit_rows(s_ref[mine, :])
    out_ref[0] = (total - unit * jnp.sum(unit * total, axis=-1, keepdims=True)) / length
    repeat(out_ref)
    height = logs_ref.shape[1] - 8
    logs = logs_ref[pl.ds(place_ref[0], 1)][0][height + quarter : height + 2 * quarter, :]
    terms = logs / LOG2E - totals[tiles : tiles + quarter, :] * scale / TEMP_STUDENT
    loss_ref[...] = jnp.broadcast_to(jnp.sum(terms), loss_ref.shape)


def grad_kernel(counts, protos, exp_hbm, prob_hbm, feat_ref, scale_ref, sums_ref, factor_ref, *refs):
    parts = refs[: len(counts)]
    out_hbm, scaled, exp_ref, prob_ref, part_ref, out, exp_sem, prob_sem, part_sem, sem = refs[-10:]
    exp_loads = chunk_copies(exp_hbm, exp_ref, exp_sem)
    prob_loads = chunk_copies(prob_hbm, prob_ref, prob_sem)
    part_loads, first = [], 0
    for count, part in zip(counts, parts):
        part_loads += chunk_copies(part, part_ref, part_sem.at[first : first + count], 0, first)
        first += count
    start(exp_loads, prob_loads, part_loads)
    own = exp_ref.shape[0]
    tiles = (own + prob_ref.shape[0]) // LANES
    rows = protos / sums_ref[:tiles, :]
    for a in range(tiles):
        other = (a + tiles // 2) % tiles
        feat = feat_ref[:, other * LANES : (other + 1) * LANES].astype(F32)
        row = rows[a : a + 1, :]
        if a < own // LANES:
            row = row * factor_ref[a : a + 1, :]
        scaled[:, a * LANES : (a + 1) * LANES] = (feat * row).astype(BF16)
    stores = chunk_copies(out, out_hbm, sem)
    for k, store in enumerate(stores):
        exp_loads[k].wait()
        prob_loads[k].wait()
        paired = jnp.dot(scaled[:, :own], exp_ref[:, chunk(k)], preferred_element_type=F32)
        paired = paired + jnp.dot(
            scaled[:, own:], prob_ref[:, chunk(k)], preferred_element_type=F32
        )
        part_loads[k].wait()
        for t, tile in enumerate(lane_tiles(paired)):
            lanes = slice(k * WIDE + t * LANES, k * WIDE + (t + 1) * LANES)
            scale = scale_ref[lanes.start // LANES : lanes.stop // LANES, :]
            out[:, lanes] = (part_ref[:, lanes] - tile * scale).astype(BF16)
        store.start()
    for store in stores:
        store.wait()


SMEM = pl.BlockSpec(memory_space=pltpu.SMEM)
VMEM = pl.BlockSpec(memory_space=pltpu.VMEM)
ANY = pl.BlockSpec(memory_space=pl.ANY)


def params(nbytes):
    return pltpu.CompilerParams(vmem_limit_bytes=int(nbytes) + 8 * 2**20)


def cost(flops, nbytes, exps=0):
    return pl.CostEstimate(flops=int(flops), bytes_accessed=int(nbytes), transcendentals=int(exps))


def exchange(value, axis):
    return lax.all_to_all(value, axis, 0, 0)


def following(value, axis):
    n = lax.axis_size(axis)
    return [lax.ppermute(value, axis, [(i, (i - s) % n) for i in range(n)]) for s in range(1, n)]


def tree_sum(value, axis):
    n = lax.axis_size(axis)
    values = [value] + [
        lax.ppermute(value, axis, [(i, i ^ s) for i in range(n)]) for s in range(1, n)
    ]
    while len(values) > 1:
        values = [a + b for a, b in zip(values[::2], values[1::2])]
    return values[0]


def local(teacher_feats, student_feats, proto_weight):
    parts, groups = lax.axis_size("proto"), lax.axis_size("batch")
    own, width = teacher_feats.shape
    local_protos = proto_weight.shape[1]
    rows = own * groups
    others = rows - own
    protos = local_protos * parts
    feats = width // groups
    share = own // parts
    tiles = rows // LANES
    height = local_protos // LANES
    chunks = local_protos // WIDE
    place = jnp.stack([lax.axis_index("batch"), lax.axis_index("proto")]).astype(jnp.int32)
    struct = jax.ShapeDtypeStruct
    weight_bytes = 2 * width * local_protos
    exp_bytes = 2 * own * local_protos
    others_bytes = 2 * others * local_protos
    spread = pltpu.VMEM((own, LANES), F32)
    w_buffer = pltpu.VMEM((width, local_protos), BF16)
    exp_buffer = pltpu.VMEM((own, local_protos), BF16)
    sems = pltpu.SemaphoreType.DMA((chunks,))
    log_protos = math.log2(protos)
    token = struct((8, LANES), F32)

    def far(value):
        return pltpu.with_memory_space_constraint(value, pltpu.HBM)

    weight = far(proto_weight)
    s_all = following(student_feats, "batch")
    t_all = following(teacher_feats, "batch")

    exps = pltpu.HBM((own, local_protos), BF16)
    t_exp, s_exp, stats = pl.pallas_call(
        stats_kernel,
        in_specs=[VMEM, VMEM, ANY],
        out_specs=[ANY, ANY, VMEM],
        out_shape=[exps, exps, struct((parts, 4 * own // LANES, LANES), F32)],
        scratch_shapes=[
            w_buffer,
            pltpu.VMEM((2, own, width), BF16),
            pltpu.VMEM((2, own, local_protos), BF16),
            pltpu.VMEM((own, local_protos), F32),
            pltpu.VMEM((2, own, LANES), F32),
            pltpu.VMEM((2, own, LANES), F32),
            sems, sems, sems,
        ],
        compiler_params=params(weight_bytes + 4 * exp_bytes),
        cost_estimate=cost(4 * own * width * local_protos, weight_bytes),
        name="own_rows",
    )(teacher_feats, student_feats, weight)
    t_exp, s_exp = far(t_exp), far(s_exp)

    back_student = pl.pallas_call(
        own_back_kernel,
        in_specs=[ANY] * 3,
        out_specs=VMEM,
        out_shape=struct((own, width), F32),
        scratch_shapes=[exp_buffer, w_buffer, sems, sems],
        compiler_params=params(weight_bytes + exp_bytes),
        cost_estimate=cost(2 * own * width * local_protos, weight_bytes),
        name="own_back",
    )(stats, s_exp, weight)
    stats = exchange(stats, "proto")

    first_shape = (groups, height + 8, LANES)
    factor, cols = pl.pallas_call(
        first_column_kernel,
        in_specs=[SMEM, VMEM, ANY, ANY] + [ANY] * (groups - 1),
        out_specs=[VMEM, VMEM],
        out_shape=[token, struct(first_shape, F32)],
        scratch_shapes=[spread, exp_buffer, sems],
        compiler_params=params(exp_bytes),
        cost_estimate=cost(2 * own * local_protos, exp_bytes),
        name="first_columns",
    )(place, stats, t_exp, back_student, *s_all)

    unit, feat, scaled = pl.pallas_call(
        functools.partial(student_rows_kernel, log_protos),
        in_specs=[SMEM, VMEM, VMEM] + [VMEM] * (groups - 1) + [ANY],
        out_specs=[VMEM] * 3,
        out_shape=[
            struct((others, width), BF16), struct((feats, rows), BF16), struct((feats, own), BF16),
        ],
        scratch_shapes=[pltpu.VMEM((width, rows), BF16)],
        compiler_params=params(2 * rows * width),
        cost_estimate=cost(8 * rows * width, 2 * rows * width),
        name="student_rows",
    )(place, factor, student_feats, *s_all, cols)
    cols = exchange(cols, "batch")
    logs = cols

    counts = [c * chunks // 8 for c in (1, 2, 1, 2, 2)]
    grad_parts = []

    def student_piece(before):
        turn = len(grad_parts)
        first, count = sum(counts[:turn]), counts[turn]
        grad_part, done = pl.pallas_call(
            functools.partial(student_kernel, log_protos, first),
            in_specs=[SMEM] + [VMEM] * 4 + [ANY] * 3,
            out_specs=[ANY, VMEM],
            out_shape=[pltpu.HBM((feats, count * WIDE), F32), token],
            scratch_shapes=[
                pltpu.VMEM((others, LANES), F32),
                pltpu.VMEM((2, others, WIDE), BF16),
                pltpu.VMEM((own, count * WIDE), BF16),
                pltpu.VMEM((width, count * WIDE), BF16),
                pltpu.VMEM((feats, count * WIDE), F32),
            ]
            + [pltpu.SemaphoreType.DMA((count,))] * 3,
            compiler_params=params(8 * 2**20),
            cost_estimate=cost(2.5 * rows * width * WIDE * count, 2 * width * WIDE * count),
            name="student_side",
        )(place, logs, unit, feat, scaled, s_exp, weight, before)
        grad_parts.append(far(grad_part))
        return done

    done = unit
    for turn in range(SWEEPS - 1):
        sums = pl.pallas_call(
            row_kernel,
            in_specs=[VMEM, VMEM, ANY, ANY],
            out_specs=VMEM,
            out_shape=struct((parts, 8, LANES), F32),
            scratch_shapes=[pltpu.VMEM((height, LANES), F32), spread, exp_buffer, sems],
            compiler_params=params(exp_bytes),
            cost_estimate=cost(2 * own * local_protos, exp_bytes),
            name="rows",
        )(cols, factor, t_exp, done)
        done = student_piece(sums)
        sums = exchange(sums, "proto")
        late = t_all if turn == 0 else []
        cols = pl.pallas_call(
            column_kernel,
            in_specs=[VMEM, VMEM, ANY, ANY] + [ANY] * len(late),
            out_specs=VMEM,
            out_shape=struct((groups, height, LANES), F32),
            scratch_shapes=[spread, exp_buffer, sems],
            compiler_params=params(exp_bytes),
            cost_estimate=cost(2 * own * local_protos, exp_bytes),
            name="columns",
        )(sums, factor, t_exp, done, *late)
        done = student_piece(cols)
        cols = exchange(cols, "batch")

    sum_rows = -(-(tiles + own // LANES) // 16) * 16
    message_shape = (parts, 2 * share + sum_rows, width)
    prob, col_scale, message = pl.pallas_call(
        functools.partial(last_kernel, groups),
        in_specs=[SMEM] + [VMEM] * 5 + [ANY] * 2 + [VMEM] * (groups - 1) + [ANY],
        out_specs=[ANY, VMEM, VMEM],
        out_shape=[
            pltpu.HBM((others, local_protos), BF16),
            struct((height, LANES), F32),
            struct(message_shape, BF16),
        ],
        scratch_shapes=[
            pltpu.VMEM((others, width), BF16),
            pltpu.VMEM((others, LANES), F32),
            pltpu.VMEM((others, LANES), F32),
            spread,
            pltpu.VMEM((own, width), F32),
            pltpu.VMEM((own, WIDE), BF16),
            pltpu.VMEM((sum_rows, LANES), F32),
            exp_buffer,
            w_buffer,
            pltpu.VMEM((others, local_protos), BF16),
            sems, sems, sems,
        ],
        compiler_params=params(weight_bytes + exp_bytes + others_bytes),
        cost_estimate=cost(2 * rows * width * local_protos, others_bytes),
        name="last_rows",
    )(
        place, logs, cols, factor, student_feats, back_student, t_exp, weight, *t_all, done,
    )
    done = student_piece(message)
    message = exchange(message, "proto")

    grad_rows, loss_part, sums = pl.pallas_call(
        functools.partial(rows_kernel, tiles, float(protos)),
        in_specs=[SMEM] + [VMEM] * 3 + [ANY],
        out_specs=[VMEM] * 3,
        out_shape=[struct((parts, share, width), F32), token, struct((sum_rows, LANES), F32)],
        scratch_shapes=[spread],
        compiler_params=params(0),
        name="row_grads",
    )(place, student_feats, message, logs, done)
    grad_rows = exchange(grad_rows, "proto").reshape(own, width)
    loss = tree_sum(loss_part, "batch")[0, 0] / rows

    grad_weight = pl.pallas_call(
        functools.partial(grad_kernel, counts, float(protos)),
        in_specs=[ANY] * 2 + [VMEM] * 4 + [ANY] * len(counts),
        out_specs=ANY,
        out_shape=struct((feats, local_protos), BF16),
        scratch_shapes=[
            pltpu.VMEM((feats, rows), BF16),
            exp_buffer,
            pltpu.VMEM((others, local_protos), BF16),
            pltpu.VMEM((feats, local_protos), F32),
            pltpu.VMEM((feats, local_protos), BF16),
            sems, sems, sems, sems,
        ],
        compiler_params=params(exp_bytes + others_bytes + 6 * feats * local_protos),
        cost_estimate=cost(2 * feats * rows * local_protos, others_bytes),
        name="weight_grads",
    )(t_exp, far(prob), feat, col_scale, sums, factor, *grad_parts)
    return grad_weight, grad_rows, loss


def solution(mesh):
    return jax.shard_map(
        local,
        mesh=mesh,
        in_specs=(P("batch", None), P("batch", None), P(None, "proto")),
        out_specs=(P("batch", "proto"), P("batch", None), P()),
        check_vma=False,
    )
```

```python
import functools
import math

import jax
import jax.numpy as jnp
from jax import lax
from jax.experimental import pallas as pl
from jax.experimental.pallas import tpu as pltpu
from jax.sharding import PartitionSpec as P

SWEEPS = 3
TEMP_TEACHER = 0.04
TEMP_STUDENT = 0.1
LOG2E = math.log2(math.e)
SCALE_TEACHER = LOG2E / TEMP_TEACHER
SCALE_STUDENT = LOG2E / TEMP_STUDENT
LANES = 128
WIDE = 1024
F32 = jnp.float32
BF16 = jnp.bfloat16


def unit_rows(values):
    wide = values.astype(F32)
    length = jnp.sqrt(jnp.sum(wide * wide, axis=-1, keepdims=True) + 1e-06)
    return wide / length, length


def diagonal():
    shape = (LANES, LANES)
    return lax.broadcasted_iota(jnp.int32, shape, 0) == lax.broadcasted_iota(jnp.int32, shape, 1)


def to_column(row):
    spread = jnp.where(diagonal(), jnp.broadcast_to(row, (LANES, LANES)), 0.0)
    return jnp.sum(spread, axis=1, keepdims=True)


def to_row(column):
    spread = jnp.where(diagonal(), jnp.broadcast_to(column, (LANES, LANES)), 0.0)
    return jnp.sum(spread, axis=0, keepdims=True)


def spread_rows(ref, rows):
    for a in range(rows.shape[0]):
        ref[a * LANES : (a + 1) * LANES, :] = jnp.broadcast_to(
            to_column(rows[a : a + 1, :]), (LANES, LANES)
        )


def pack_rows(ref, columns):
    for a in range(columns.shape[0] // LANES):
        ref[a : a + 1, :] = to_row(columns[a * LANES : (a + 1) * LANES, :])


def lane_tiles(values):
    return [values[:, t * LANES : (t + 1) * LANES] for t in range(values.shape[1] // LANES)]


def fold(values):
    return functools.reduce(jnp.add, lane_tiles(values))


def column_sums(values):
    rows, cols = values.shape
    return jnp.sum(values.reshape(rows // 8, 8, cols), axis=0)


def nt_dot(a, b):
    return lax.dot_general(a, b, (((1,), (1,)), ((), ())), preferred_element_type=F32)


def add_up(values):
    return functools.reduce(jnp.add, values)


def repeat(out_ref):
    for p in range(1, out_ref.shape[0]):
        out_ref[p] = out_ref[0]


def chunk(k):
    return slice(k * WIDE, (k + 1) * WIDE)


def copies(source, target, sems, first=0, back=0, count=None):
    def part(ref, k):
        return ref.at[k] if len(ref.shape) == 3 else ref.at[:, chunk(k)]

    def chunks(ref):
        return ref.shape[0] if len(ref.shape) == 3 else ref.shape[1] // WIDE

    count = count or min(chunks(source), chunks(target))
    return [
        pltpu.make_async_copy(part(source, first + k), part(target, back + k), sems.at[k])
        for k in range(count)
    ]


def start(*lists):
    for each in zip(*lists):
        for copy in each:
            copy.start()


def wait(*lists):
    for each in lists:
        for copy in each:
            copy.wait()


def stats_kernel(
    t_ref, s_ref, w_hbm, t_out, s_out, t_unit, out_ref,
    w_ref, unit, exps, logits, top, total, w_sem, t_sem, s_sem,
):
    piece = 512
    pieces = [slice(c, c + piece) for c in range(0, w_ref.shape[1], piece)]
    quarter = out_ref.shape[1] // 4
    scales = (SCALE_TEACHER, SCALE_STUDENT)
    loads = copies(w_hbm, w_ref, w_sem)
    start(loads)
    stores = [copies(exps.at[0], t_out, t_sem), copies(exps.at[1], s_out, s_sem)]
    for which, ref in enumerate((t_ref, s_ref)):
        unit[which] = unit_rows(ref[...])[0].astype(BF16)
    t_unit[...] = unit[0]
    top[...] = jnp.full(top.shape, -1e30, F32)
    total[...] = jnp.zeros(total.shape, F32)

    for here in pieces:
        if here.start % WIDE == 0:
            loads[here.start // WIDE].wait()
        for which in range(2):
            values = jnp.dot(unit[which], w_ref[:, here], preferred_element_type=F32)
            values = values * scales[which]
            logits[which, :, here] = values
            top[which] = functools.reduce(jnp.maximum, lane_tiles(values), top[which])
    peaks = [jnp.max(top[which], axis=1, keepdims=True) for which in range(2)]
    for which in range(2):
        shift = jnp.broadcast_to(peaks[which], (peaks[which].shape[0], LANES))
        for here in pieces:
            tiles = [jnp.exp2(t - shift) for t in lane_tiles(logits[which, :, here])]
            k, first = here.start // WIDE, here.start % WIDE
            for t, tile in enumerate(tiles):
                lanes = slice(first + t * LANES, first + (t + 1) * LANES)
                exps[which, k, :, lanes] = tile.astype(BF16)
            total[which] += add_up(tiles)
            if here.stop % WIDE == 0:
                stores[which][k].start()
        sums = jnp.sum(total[which], axis=1, keepdims=True)
        for k, column in enumerate((peaks[which], sums)):
            first = (2 * which + k) * quarter
            pack_rows(out_ref.at[0, first : first + quarter], column)
    repeat(out_ref)
    wait(*stores)


def merged(stats_ref, which):
    parts, height, _ = stats_ref.shape
    quarter = height // 4
    first = 2 * which * quarter
    tops = [stats_ref[p, first : first + quarter, :] for p in range(parts)]
    top = functools.reduce(jnp.maximum, tops)
    sums = [
        stats_ref[p, first + quarter : first + 2 * quarter, :] * jnp.exp2(tops[p] - top)
        for p in range(parts)
    ]
    return top + jnp.log2(add_up(sums))


def column_pass(exp_ref, weight, out_ref):
    for k in range(exp_ref.shape[0]):
        sums = jnp.zeros((8, WIDE), F32)
        for g in range(0, exp_ref.shape[1], 16):
            shift = weight[g : g + 16, :]
            tiles = lane_tiles(exp_ref[k, g : g + 16, :].astype(F32))
            sums = sums + column_sums(jnp.concatenate([tile * shift for tile in tiles], axis=1))
        sums = jnp.sum(sums, axis=0, keepdims=True)
        block = jnp.concatenate(lane_tiles(sums), axis=0)
        for g in range(out_ref.shape[0]):
            out_ref[g, k * (WIDE // LANES) : (k + 1) * (WIDE // LANES), :] = block


def first_column_kernel(place_ref, stats_ref, exp_ref, *refs):
    factor_ref, out_ref, weight = refs[-3:]
    quarter = stats_ref.shape[1] // 4
    height = out_ref.shape[1] - 8
    own = stats_ref[pl.ds(place_ref[1], 1)][0]
    factor_ref[...] = jnp.zeros(factor_ref.shape, F32)
    rows = []
    for which in range(2):
        log_sum = merged(stats_ref, which)
        here = slice(which * quarter, (which + 1) * quarter)
        factor_ref[here, :] = jnp.exp2(
            own[2 * which * quarter : (2 * which + 1) * quarter, :] - log_sum
        )
        rows.append(log_sum)
    rows.append(jnp.zeros((8 - 2 * quarter, LANES), F32))
    logs = jnp.concatenate(rows, axis=0)
    for g in range(out_ref.shape[0]):
        out_ref[g, height:, :] = logs
    spread_rows(weight, factor_ref[:quarter, :])
    column_pass(exp_ref, weight, out_ref)


def column_kernel(sums_ref, factor_ref, exp_ref, *refs):
    out_ref, weight = refs[-2:]
    quarter = weight.shape[0] // LANES
    scale = 1.0 / add_up([sums_ref[p, :quarter, :] for p in range(sums_ref.shape[0])])
    spread_rows(weight, scale * factor_ref[:quarter, :])
    column_pass(exp_ref, weight, out_ref)


def column_scales(cols_ref, height):
    return 1.0 / add_up([cols_ref[g, :height, :] for g in range(cols_ref.shape[0])])


def add_row_sums(rows, values, scales, k):
    for g in range(0, values.shape[0], 32):
        total = rows[g : g + 32, :]
        for t, tile in enumerate(lane_tiles(values[g : g + 32, :].astype(F32))):
            first = k * (WIDE // LANES) + t
            total = total + tile * scales[first : first + 1, :]
        rows[g : g + 32, :] = total


def row_kernel(cols_ref, factor_ref, exp_ref, *refs):
    out_ref, scales, rows = refs[-3:]
    scales[...] = column_scales(cols_ref, scales.shape[0])
    rows[...] = jnp.zeros(rows.shape, F32)
    quarter = rows.shape[0] // LANES
    out_ref[0] = jnp.zeros(out_ref.shape[1:], F32)
    for k in range(exp_ref.shape[0]):
        add_row_sums(rows, exp_ref.at[k], scales, k)
    pack_rows(out_ref.at[0, :quarter], jnp.sum(rows[...], axis=1, keepdims=True))
    out_ref[0, :quarter, :] = out_ref[0, :quarter, :] * factor_ref[:quarter, :]
    repeat(out_ref)


def own_back_kernel(
    before_ref, exp_hbm, w_hbm, t_hbm, back_ref, t_near, exp_ref, w_ref, exp_sem, w_sem, t_sem
):
    exp_loads, w_loads = copies(exp_hbm, exp_ref, exp_sem), copies(w_hbm, w_ref, w_sem)
    t_loads = copies(t_hbm, t_near, t_sem)
    start(exp_loads, w_loads)
    start(t_loads)
    back_ref[...] = jnp.zeros(back_ref.shape, F32)
    for k in range(len(w_loads)):
        exp_loads[k].wait()
        w_loads[k].wait()
        back_ref[...] += nt_dot(exp_ref[k], w_ref[:, chunk(k)])
    wait(t_loads)


def relative(place_ref, g, groups):
    return pl.ds(lax.rem(place_ref[0] + g, groups), 1)


def relative_logs(place_ref, logs_ref, lse, which, shift=0.0):
    groups = logs_ref.shape[0]
    own = lse.shape[0] // (groups - 1)
    quarter = own // LANES
    height = logs_ref.shape[1] - 8
    for g in range(1, groups):
        there = logs_ref[relative(place_ref, g, groups)][0]
        first = height + which * quarter
        spread_rows(lse.at[(g - 1) * own : g * own], there[first : first + quarter, :] - shift)


def student_rows_kernel(log_protos, place_ref, factor_ref, own_ref, t_hbm, *refs):
    unit_ref, feat_ref, scaled_ref, t_near, turned, t_sem = refs[-6:]
    t_loads = copies(t_hbm, t_near, t_sem)
    start(t_loads)
    own = own_ref.shape[0]
    groups = turned.shape[1] // own
    raw = refs[: groups - 1]
    quarter, feats = own // LANES, feat_ref.shape[0]
    for g in range(groups):
        half = unit_rows((raw[g - 1] if g else own_ref)[...])[0].astype(BF16)
        if g:
            unit_ref[(g - 1) * own : g * own, :] = half
        half = half.astype(F32)
        for a in range(0, own, LANES):
            first = g * own + a
            turned[:, first : first + LANES] = jnp.transpose(half[a : a + LANES, :]).astype(BF16)
    feat = turned[pl.ds(pl.multiple_of(place_ref[0] * feats, feats), feats), :]
    feat_ref[...] = feat
    for a in range(quarter):
        lanes = slice(a * LANES, (a + 1) * LANES)
        factor = factor_ref[quarter + a : quarter + a + 1, :] * 2.0**log_protos
        scaled_ref[:, lanes] = (feat[:, lanes].astype(F32) * factor).astype(BF16)
    wait(t_loads)


def probabilities(unit, own, chunks, weights, lse, scale, use, after):
    blocks = [
        (k, g, n)
        for k in range(chunks)
        for g in range(unit.shape[0] // own)
        for n in range(0, WIDE, 512)
    ]

    def product(k, g, n):
        w = weights(k, g == 0 and n == 0)
        return jnp.dot(
            unit[g * own : (g + 1) * own, :], w[:, n : n + 512], preferred_element_type=F32
        )

    logits = product(*blocks[0])
    for i, (k, g, n) in enumerate(blocks):
        later = product(*blocks[i + 1]) if i + 1 < len(blocks) else None
        shift = lse[g * own : (g + 1) * own, :]
        use(k, g, n, [jnp.exp2(tile * scale - shift) for tile in lane_tiles(logits)])
        if i + 1 == len(blocks) or blocks[i + 1][0] != k:
            after(k)
        logits = later


def student_kernel(
    log_protos, first, near, place_ref, logs_ref, unit, feat_ref, scaled_ref, exp_hbm, w_hbm, *refs
):
    far_refs, refs = refs[1 : 1 + near], refs[1 + near :]
    grad_hbm, token_ref, *refs = refs
    near_refs, refs = refs[:near], refs[near:]
    lse, prob, exp_ref, w_ref, grad, exp_sem, w_sem, grad_sem, *near_sems = refs
    own, count = exp_ref.shape[1], exp_ref.shape[0]
    exp_loads = copies(exp_hbm, exp_ref, exp_sem, first, 0, count)
    w_loads = copies(w_hbm, w_ref, w_sem, first, 0, count)
    near_loads = [copies(a, b, c) for a, b, c in zip(far_refs, near_refs, near_sems)]
    stores = copies(grad, grad_hbm, grad_sem)
    start(w_loads, exp_loads)
    for loads in near_loads:
        start(loads)
    token_ref[...] = jnp.zeros(token_ref.shape, F32)
    relative_logs(place_ref, logs_ref, lse, 1, log_protos)

    def weights(k, fresh):
        if fresh:
            w_loads[k].wait()
        return w_ref.at[:, chunk(k)]

    def use(k, g, n, tiles):
        for t, tile in enumerate(tiles):
            lanes = slice(n + t * LANES, n + (t + 1) * LANES)
            prob[k % 2, g * own : (g + 1) * own, lanes] = tile.astype(BF16)

    def after(k):
        exp_loads[k].wait()
        values = jnp.dot(scaled_ref[...], exp_ref[k], preferred_element_type=F32)
        values = values + jnp.dot(feat_ref[:, own:], prob[k % 2], preferred_element_type=F32)
        grad[:, chunk(k)] = values.astype(BF16)
        stores[k].start()

    probabilities(unit, own, count, weights, lse, SCALE_STUDENT, use, after)
    wait(stores, *near_loads)


def as_three(value):
    high = value.astype(BF16)
    rest = value - high.astype(F32)
    middle = rest.astype(BF16)
    return high, middle, (rest - middle.astype(F32)).astype(BF16)


def last_kernel(groups, place_ref, logs_ref, cols_ref, factor_ref, own_ref, student_ref, exp_ref, w_ref, *refs):
    units = refs[: groups - 1]
    (
        prob_hbm, scale_ref, out_ref, unit, lse, rows, own_rows, back, scaled, sums, prob_ref, prob_sem,
    ) = refs[-12:]
    slots, others, _ = prob_ref.shape
    own, chunks = exp_ref.shape[1], exp_ref.shape[0]
    tiles = (own + others) // LANES
    quarter = own // LANES
    scale_ref[...] = column_scales(cols_ref, scale_ref.shape[0])
    rows[...] = jnp.zeros(rows.shape, F32)
    own_rows[...] = jnp.zeros(own_rows.shape, F32)
    back[...] = jnp.zeros(back.shape, F32)
    relative_logs(place_ref, logs_ref, lse, 0)
    for g in range(groups - 1):
        unit[g * own : (g + 1) * own, :] = units[g][...]
    stores = [
        pltpu.make_async_copy(prob_ref.at[k % slots], prob_hbm.at[k], prob_sem.at[k])
        for k in range(chunks)
    ]

    def use(k, g, n, tiles):
        if g == 0 and n == 0 and k >= slots:
            stores[k - slots].wait()
        here = slice(g * own, (g + 1) * own)
        for t, tile in enumerate(tiles):
            prob_ref[k % slots, here, n + t * LANES : n + (t + 1) * LANES] = tile.astype(BF16)
        first = k * (WIDE // LANES) + n // LANES
        tiles = [tile * scale_ref[first + t : first + t + 1, :] for t, tile in enumerate(tiles)]
        rows[here, :] += add_up(tiles)
        if g == groups // 2 - 1:
            for t, tile in enumerate(tiles):
                scaled[k % 2, :, n + t * LANES : n + (t + 1) * LANES] = tile.astype(BF16)

    def after(k):
        stores[k].start()
        back[...] += nt_dot(scaled[k % 2], w_ref[:, chunk(k)])
        add_row_sums(own_rows, exp_ref.at[k], scale_ref, k)

    def weights(k, fresh):
        return w_ref.at[:, chunk(k)]

    probabilities(unit, own, chunks, weights, lse, SCALE_TEACHER, use, after)

    sums[...] = jnp.zeros(sums.shape, F32)
    pack_rows(sums.at[:quarter], jnp.sum(own_rows[...], axis=1, keepdims=True))
    sums[:quarter, :] = sums[:quarter, :] * factor_ref[:quarter, :]
    pack_rows(sums.at[quarter:tiles], jnp.sum(rows[...], axis=1, keepdims=True))
    half = unit_rows(own_ref[...])[0].astype(BF16).astype(F32)
    inner = jnp.sum(half * back[...], axis=1, keepdims=True)
    pack_rows(sums.at[tiles : tiles + quarter], inner)
    parts = out_ref.shape[0]
    share = own // parts
    protos = 1.0 * out_ref.shape[0] * w_ref.shape[1]
    student = []
    for a in range(quarter):
        factor = to_column(factor_ref[quarter + a : quarter + a + 1, :] * protos)
        student.append(student_ref[a * LANES : (a + 1) * LANES, :] * factor)
    student = jnp.concatenate(student, axis=0).astype(BF16)
    terms = list(as_three(sums[...]))
    terms.append(jnp.zeros((sums.shape[0], out_ref.shape[2] - 3 * LANES), BF16))
    terms = jnp.concatenate(terms, axis=1)
    for p in range(parts):
        here = slice(p * share, (p + 1) * share)
        out_ref[p] = jnp.concatenate(
            [student[here, :], back[here, :].astype(BF16), terms], axis=0
        )
    wait(stores[max(0, chunks - slots) :])


def total_sums(message_ref, first):
    parts = message_ref.shape[0]
    each = [
        add_up([t.astype(F32) for t in lane_tiles(message_ref[p, first:, : 3 * LANES])[::-1]])
        for p in range(parts)
    ]
    return add_up(each)


def rows_kernel(tiles, protos, place_ref, s_ref, message_ref, logs_ref, *refs):
    out_ref, loss_ref, sums_ref, weight = refs[-4:]
    parts = message_ref.shape[0]
    share, own = out_ref.shape[1], weight.shape[0]
    quarter = own // LANES
    first = tiles // 2
    totals = total_sums(message_ref, 2 * share)
    sums_ref[...] = totals
    scale = 1.0 / totals[first : first + quarter, :]
    spread_rows(weight, scale)
    mine = pl.ds(pl.multiple_of(place_ref[1] * share, share), share)
    total = add_up([message_ref[p, :share, :].astype(F32) for p in range(parts)])
    paired = add_up([message_ref[p, share : 2 * share, :].astype(F32) for p in range(parts)])
    total = total - paired * (weight[mine, :1] * protos)
    unit, length = unit_rows(s_ref[mine, :])
    out_ref[0] = (total - unit * jnp.sum(unit * total, axis=-1, keepdims=True)) / length
    repeat(out_ref)
    height = logs_ref.shape[1] - 8
    logs = logs_ref[pl.ds(place_ref[0], 1)][0][height + quarter : height + 2 * quarter, :]
    terms = logs / LOG2E - totals[tiles : tiles + quarter, :] * scale / TEMP_STUDENT
    loss_ref[...] = jnp.broadcast_to(jnp.sum(terms), loss_ref.shape)


def grad_kernel(counts, protos, exp_hbm, prob_hbm, feat_ref, scale_ref, sums_ref, factor_ref, *refs):
    parts = refs[: len(counts)]
    out_hbm, scaled, exp_ref, prob_ref, part_ref, out, exp_sem, prob_sem, part_sem, sem = refs[-10:]
    exp_loads = copies(exp_hbm, exp_ref, exp_sem)
    prob_loads = copies(prob_hbm, prob_ref, prob_sem)
    part_loads, first = [], 0
    for count, part in zip(counts, parts):
        part_loads += copies(part, part_ref, part_sem.at[first : first + count], 0, first)
        first += count
    start(exp_loads, prob_loads, part_loads)
    own = exp_ref.shape[1]
    tiles = (own + prob_ref.shape[1]) // LANES
    rows = protos / sums_ref[:tiles, :]
    for a in range(tiles):
        other = (a + tiles // 2) % tiles
        feat = feat_ref[:, other * LANES : (other + 1) * LANES].astype(F32)
        row = rows[a : a + 1, :]
        if a < own // LANES:
            row = row * factor_ref[a : a + 1, :]
        scaled[:, a * LANES : (a + 1) * LANES] = (feat * row).astype(BF16)
    stores = copies(out, out_hbm, sem)
    for k, store in enumerate(stores):
        exp_loads[k].wait()
        prob_loads[k].wait()
        paired = jnp.dot(scaled[:, :own], exp_ref[k], preferred_element_type=F32)
        paired = paired + jnp.dot(
            scaled[:, own:], prob_ref[k], preferred_element_type=F32
        )
        part_loads[k].wait()
        for t, tile in enumerate(lane_tiles(paired)):
            lanes = slice(k * WIDE + t * LANES, k * WIDE + (t + 1) * LANES)
            scale = scale_ref[lanes.start // LANES : lanes.stop // LANES, :]
            out[:, lanes] = (part_ref[:, lanes].astype(F32) - tile * scale).astype(BF16)
        store.start()
    for store in stores:
        store.wait()


SMEM = pl.BlockSpec(memory_space=pltpu.SMEM)
VMEM = pl.BlockSpec(memory_space=pltpu.VMEM)
ANY = pl.BlockSpec(memory_space=pl.ANY)


def params(nbytes):
    return pltpu.CompilerParams(vmem_limit_bytes=int(nbytes) + 8 * 2**20)


def cost(flops, nbytes, exps=0):
    return pl.CostEstimate(flops=int(flops), bytes_accessed=int(nbytes), transcendentals=int(exps))


def exchange(value, axis):
    return lax.all_to_all(value, axis, 0, 0)


def following(value, axis):
    n = lax.axis_size(axis)
    return [lax.ppermute(value, axis, [(i, (i - s) % n) for i in range(n)]) for s in range(1, n)]


def tree_sum(value, axis):
    n = lax.axis_size(axis)
    values = [value] + [
        lax.ppermute(value, axis, [(i, i ^ s) for i in range(n)]) for s in range(1, n)
    ]
    while len(values) > 1:
        values = [a + b for a, b in zip(values[::2], values[1::2])]
    return values[0]


def local(teacher_feats, student_feats, proto_weight):
    parts, groups = lax.axis_size("proto"), lax.axis_size("batch")
    own, width = teacher_feats.shape
    local_protos = proto_weight.shape[1]
    rows = own * groups
    others = rows - own
    protos = local_protos * parts
    feats = width // groups
    share = own // parts
    tiles = rows // LANES
    height = local_protos // LANES
    chunks = local_protos // WIDE
    place = jnp.stack([lax.axis_index("batch"), lax.axis_index("proto")]).astype(jnp.int32)
    struct = jax.ShapeDtypeStruct
    weight_bytes = 2 * width * local_protos
    exp_bytes = 2 * own * local_protos
    others_bytes = 2 * others * local_protos
    spread = pltpu.VMEM((own, LANES), F32)
    w_buffer = pltpu.VMEM((width, local_protos), BF16)
    exp_buffer = pltpu.VMEM((chunks, own, WIDE), BF16)
    near_exp = pltpu.VMEM((chunks, own, WIDE), BF16)
    sems = pltpu.SemaphoreType.DMA((chunks,))
    log_protos = math.log2(protos)
    token = struct((8, LANES), F32)

    def far(value):
        return pltpu.with_memory_space_constraint(value, pltpu.HBM)

    def near(value):
        return pltpu.with_memory_space_constraint(value, pltpu.VMEM)

    weight = far(proto_weight)
    s_all = following(student_feats, "batch")

    exps = pltpu.HBM((chunks, own, WIDE), BF16)
    t_exp, s_exp, t_unit, stats = pl.pallas_call(
        stats_kernel,
        in_specs=[VMEM, VMEM, ANY],
        out_specs=[ANY, ANY, VMEM, VMEM],
        out_shape=[exps, exps, struct((own, width), BF16), struct((parts, 4 * own // LANES, LANES), F32)],
        scratch_shapes=[
            w_buffer,
            pltpu.VMEM((2, own, width), BF16),
            pltpu.VMEM((2, chunks, own, WIDE), BF16),
            pltpu.VMEM((2, own, local_protos), F32),
            pltpu.VMEM((2, own, LANES), F32),
            pltpu.VMEM((2, own, LANES), F32),
            sems, sems, sems,
        ],
        compiler_params=params(weight_bytes + 6 * exp_bytes),
        cost_estimate=cost(4 * own * width * local_protos, weight_bytes),
        name="own_rows",
    )(teacher_feats, student_feats, weight)
    t_exp, s_exp = far(t_exp), far(s_exp)
    t_all = following(t_unit, "batch")

    back_student, t_near = pl.pallas_call(
        own_back_kernel,
        in_specs=[ANY] * 4,
        out_specs=[VMEM, VMEM],
        out_shape=[struct((own, width), F32), near_exp],
        scratch_shapes=[exp_buffer, w_buffer, sems, sems, sems],
        compiler_params=params(weight_bytes + exp_bytes),
        cost_estimate=cost(2 * own * width * local_protos, weight_bytes),
        name="own_back",
    )(stats, s_exp, weight, t_exp)
    stats = exchange(stats, "proto")

    first_shape = (groups, height + 8, LANES)
    factor, cols = pl.pallas_call(
        first_column_kernel,
        in_specs=[SMEM, VMEM, VMEM, ANY] + [ANY] * (groups - 1),
        out_specs=[VMEM, VMEM],
        out_shape=[token, struct(first_shape, F32)],
        scratch_shapes=[spread],
        compiler_params=params(0),
        cost_estimate=cost(2 * own * local_protos, exp_bytes),
        name="first_columns",
    )(place, stats, near(t_near), back_student, *s_all)

    unit, feat, scaled, t_near = pl.pallas_call(
        functools.partial(student_rows_kernel, log_protos),
        in_specs=[SMEM, VMEM, VMEM, ANY] + [VMEM] * (groups - 1) + [ANY],
        out_specs=[VMEM] * 4,
        out_shape=[
            struct((others, width), BF16), struct((feats, rows), BF16), struct((feats, own), BF16),
            near_exp,
        ],
        scratch_shapes=[pltpu.VMEM((width, rows), BF16), sems],
        compiler_params=params(2 * rows * width),
        cost_estimate=cost(8 * rows * width, 2 * rows * width),
        name="student_rows",
    )(place, factor, student_feats, t_exp, *s_all, cols)
    cols = exchange(cols, "batch")
    logs = cols

    counts = [c * chunks // 8 for c in (1, 1, 1, 1, 4)]
    grad_parts = []

    def student_piece(before, *wanted):
        turn = len(grad_parts)
        first, count = sum(counts[:turn]), counts[turn]
        grad_part, done, *fetched = pl.pallas_call(
            functools.partial(student_kernel, log_protos, first, len(wanted)),
            in_specs=[SMEM] + [VMEM] * 4 + [ANY] * (3 + len(wanted)),
            out_specs=[ANY, VMEM] + [VMEM] * len(wanted),
            out_shape=[pltpu.HBM((feats, count * WIDE), BF16), token]
            + [pltpu.VMEM(x.shape, x.dtype) for x in wanted],
            scratch_shapes=[
                pltpu.VMEM((others, LANES), F32),
                pltpu.VMEM((2, others, WIDE), BF16),
                pltpu.VMEM((count, own, WIDE), BF16),
                pltpu.VMEM((width, count * WIDE), BF16),
                pltpu.VMEM((feats, count * WIDE), BF16),
            ]
            + [pltpu.SemaphoreType.DMA((count,))] * 3
            + [sems] * len(wanted),
            compiler_params=params(16 * 2**20),
            cost_estimate=cost(2.5 * rows * width * WIDE * count, 2 * width * WIDE * count),
            name="student_side",
        )(place, logs, unit, feat, scaled, s_exp, weight, before, *wanted)
        grad_parts.append(far(grad_part))
        return done, *[near(x) for x in fetched]

    done = unit
    for turn in range(SWEEPS - 1):
        late = t_all if turn == 1 else []
        sums = pl.pallas_call(
            row_kernel,
            in_specs=[VMEM, VMEM, VMEM, ANY] + [ANY] * len(late),
            out_specs=VMEM,
            out_shape=struct((parts, 8, LANES), F32),
            scratch_shapes=[pltpu.VMEM((height, LANES), F32), spread],
            compiler_params=params(0),
            cost_estimate=cost(2 * own * local_protos, exp_bytes),
            name="rows",
        )(cols, factor, near(t_near), done, *late)
        done, t_near = student_piece(sums, t_exp)
        sums = exchange(sums, "proto")
        cols = pl.pallas_call(
            column_kernel,
            in_specs=[VMEM, VMEM, VMEM, ANY],
            out_specs=VMEM,
            out_shape=struct((groups, height, LANES), F32),
            scratch_shapes=[spread],
            compiler_params=params(0),
            cost_estimate=cost(2 * own * local_protos, exp_bytes),
            name="columns",
        )(sums, factor, near(t_near), done)
        if turn < SWEEPS - 2:
            done, t_near = student_piece(cols, t_exp)
        else:
            done, t_near, w_near = student_piece(cols, t_exp, weight)
        cols = exchange(cols, "batch")

    sum_rows = -(-(tiles + own // LANES) // 16) * 16
    message_shape = (parts, 2 * share + sum_rows, width)
    prob, col_scale, message = pl.pallas_call(
        functools.partial(last_kernel, groups),
        in_specs=[SMEM] + [VMEM] * 7 + [VMEM] * (groups - 1) + [ANY],
        out_specs=[ANY, VMEM, VMEM],
        out_shape=[
            pltpu.HBM((chunks, others, WIDE), BF16),
            struct((height, LANES), F32),
            struct(message_shape, BF16),
        ],
        scratch_shapes=[
            pltpu.VMEM((others, width), BF16),
            pltpu.VMEM((others, LANES), F32),
            pltpu.VMEM((others, LANES), F32),
            spread,
            pltpu.VMEM((own, width), F32),
            pltpu.VMEM((2, own, WIDE), BF16),
            pltpu.VMEM((sum_rows, LANES), F32),
            pltpu.VMEM((min(chunks, 3), others, WIDE), BF16),
            sems,
        ],
        compiler_params=params(20 * 2**20),
        cost_estimate=cost(2 * rows * width * local_protos, others_bytes),
        name="last_rows",
    )(
        place, logs, cols, factor, student_feats, back_student, t_near, w_near, *t_all, done,
    )
    (done,) = student_piece(message)
    message = exchange(message, "proto")

    grad_rows, loss_part, sums = pl.pallas_call(
        functools.partial(rows_kernel, tiles, float(protos)),
        in_specs=[SMEM] + [VMEM] * 3 + [ANY],
        out_specs=[VMEM] * 3,
        out_shape=[struct((parts, share, width), F32), token, struct((sum_rows, LANES), F32)],
        scratch_shapes=[spread],
        compiler_params=params(0),
        name="row_grads",
    )(place, student_feats, message, logs, done)
    grad_rows = exchange(grad_rows, "proto").reshape(own, width)
    loss = tree_sum(loss_part, "batch")[0, 0] / rows

    grad_weight = pl.pallas_call(
        functools.partial(grad_kernel, counts, float(protos)),
        in_specs=[ANY] * 2 + [VMEM] * 4 + [ANY] * len(counts),
        out_specs=ANY,
        out_shape=struct((feats, local_protos), BF16),
        scratch_shapes=[
            pltpu.VMEM((feats, rows), BF16),
            exp_buffer,
            pltpu.VMEM((chunks, others, WIDE), BF16),
            pltpu.VMEM((feats, local_protos), BF16),
            pltpu.VMEM((feats, local_protos), BF16),
            sems, sems, sems, sems,
        ],
        compiler_params=params(exp_bytes + others_bytes + 4 * feats * local_protos),
        cost_estimate=cost(2 * feats * rows * local_protos, others_bytes),
        name="weight_grads",
    )(t_exp, far(prob), feat, col_scale, sums, factor, *grad_parts)
    return grad_weight, grad_rows, loss


def solution(mesh):
    return jax.shard_map(
        local,
        mesh=mesh,
        in_specs=(P("batch", None), P("batch", None), P(None, "proto")),
        out_specs=(P("batch", "proto"), P("batch", None), P()),
        check_vma=False,
    )
```

```python
import functools
import math

import jax
import jax.numpy as jnp
from jax import lax
from jax.experimental import pallas as pl
from jax.experimental.pallas import tpu as pltpu
from jax.sharding import PartitionSpec as P

SWEEPS = 3
TEMP_TEACHER = 0.04
TEMP_STUDENT = 0.1
LOG2E = math.log2(math.e)
LN2 = math.log(2.0)
SCALE_TEACHER = LOG2E / TEMP_TEACHER
SCALE_STUDENT = LOG2E / TEMP_STUDENT
LANES = 128
WIDE = 1024
F32 = jnp.float32
BF16 = jnp.bfloat16


def unit_rows(values):
    wide = values.astype(F32)
    length = jnp.sqrt(jnp.sum(wide * wide, axis=-1, keepdims=True) + 1e-06)
    return wide / length, length


def diagonal():
    shape = (LANES, LANES)
    return lax.broadcasted_iota(jnp.int32, shape, 0) == lax.broadcasted_iota(jnp.int32, shape, 1)


def to_column(row):
    spread = jnp.where(diagonal(), jnp.broadcast_to(row, (LANES, LANES)), 0.0)
    return jnp.sum(spread, axis=1, keepdims=True)


def to_row(column):
    spread = jnp.where(diagonal(), jnp.broadcast_to(column, (LANES, LANES)), 0.0)
    return jnp.sum(spread, axis=0, keepdims=True)


def spread_rows(ref, rows):
    for a in range(rows.shape[0]):
        ref[a * LANES : (a + 1) * LANES, :] = jnp.broadcast_to(
            to_column(rows[a : a + 1, :]), (LANES, LANES)
        )


def pack_rows(ref, columns):
    for a in range(columns.shape[0] // LANES):
        ref[a : a + 1, :] = to_row(columns[a * LANES : (a + 1) * LANES, :])


def lane_tiles(values):
    return [values[:, t * LANES : (t + 1) * LANES] for t in range(values.shape[1] // LANES)]


def fold(values):
    return functools.reduce(jnp.add, lane_tiles(values))


def column_sums(values):
    rows, cols = values.shape
    return jnp.sum(values.reshape(rows // 8, 8, cols), axis=0)


def nt_dot(a, b):
    return lax.dot_general(a, b, (((1,), (1,)), ((), ())), preferred_element_type=F32)


def exp2_half(x):
    high = x.astype(BF16)
    rest = (x - high.astype(F32)).astype(BF16)
    series = rest * (rest * BF16(0.5 * LN2**2) + BF16(LN2)) + BF16(1.0)
    return jnp.exp2(high) * series


def add_up(values):
    return functools.reduce(jnp.add, values)


def repeat(out_ref):
    for p in range(1, out_ref.shape[0]):
        out_ref[p] = out_ref[0]


def chunk(k):
    return slice(k * WIDE, (k + 1) * WIDE)


def copies(source, target, sems, first=0, back=0, count=None):
    def part(ref, k):
        return ref.at[k] if len(ref.shape) == 3 else ref.at[:, chunk(k)]

    def chunks(ref):
        return ref.shape[0] if len(ref.shape) == 3 else ref.shape[1] // WIDE

    count = count or min(chunks(source), chunks(target))
    return [
        pltpu.make_async_copy(part(source, first + k), part(target, back + k), sems.at[k])
        for k in range(count)
    ]


def start(*lists):
    for each in zip(*lists):
        for copy in each:
            copy.start()


def wait(*lists):
    for each in lists:
        for copy in each:
            copy.wait()


def stats_kernel(
    t_ref, s_ref, w_hbm, t_out, s_out, t_unit, out_ref,
    w_ref, unit, exps, logits, top, total, w_sem, t_sem, s_sem,
):
    piece = 512
    pieces = [slice(c, c + piece) for c in range(0, w_ref.shape[1], piece)]
    quarter = out_ref.shape[1] // 4
    scales = (SCALE_TEACHER, SCALE_STUDENT)
    loads = copies(w_hbm, w_ref, w_sem)
    start(loads)
    stores = [copies(exps.at[0], t_out, t_sem), copies(exps.at[1], s_out, s_sem)]
    for which, ref in enumerate((t_ref, s_ref)):
        unit[which] = unit_rows(ref[...])[0].astype(BF16)
    t_unit[...] = unit[0]
    top[...] = jnp.full(top.shape, -1e30, F32)
    total[...] = jnp.zeros(total.shape, F32)

    for here in pieces:
        if here.start % WIDE == 0:
            loads[here.start // WIDE].wait()
        for which in range(2):
            values = jnp.dot(unit[which], w_ref[:, here], preferred_element_type=F32)
            values = values * scales[which]
            logits[which, :, here] = values
            top[which] = functools.reduce(jnp.maximum, lane_tiles(values), top[which])
    peaks = [jnp.max(top[which], axis=1, keepdims=True) for which in range(2)]
    for which in range(2):
        shift = jnp.broadcast_to(peaks[which], (peaks[which].shape[0], LANES))
        for here in pieces:
            tiles = [exp2_half(t - shift) for t in lane_tiles(logits[which, :, here])]
            k, first = here.start // WIDE, here.start % WIDE
            for t, tile in enumerate(tiles):
                lanes = slice(first + t * LANES, first + (t + 1) * LANES)
                exps[which, k, :, lanes] = tile
            total[which] += add_up([tile.astype(F32) for tile in tiles])
            if here.stop % WIDE == 0:
                stores[which][k].start()
        sums = jnp.sum(total[which], axis=1, keepdims=True)
        for k, column in enumerate((peaks[which], sums)):
            first = (2 * which + k) * quarter
            pack_rows(out_ref.at[0, first : first + quarter], column)
    repeat(out_ref)
    wait(*stores)


def merged(stats_ref, which):
    parts, height, _ = stats_ref.shape
    quarter = height // 4
    first = 2 * which * quarter
    tops = [stats_ref[p, first : first + quarter, :] for p in range(parts)]
    top = functools.reduce(jnp.maximum, tops)
    sums = [
        stats_ref[p, first + quarter : first + 2 * quarter, :] * jnp.exp2(tops[p] - top)
        for p in range(parts)
    ]
    return top + jnp.log2(add_up(sums))


def column_pass(loads, exp_ref, weight, out_ref):
    for k, load in enumerate(loads):
        load.wait()
        sums = jnp.zeros((8, WIDE), F32)
        for g in range(0, exp_ref.shape[1], 16):
            shift = weight[g : g + 16, :]
            tiles = lane_tiles(exp_ref[k, g : g + 16, :].astype(F32))
            sums = sums + column_sums(jnp.concatenate([tile * shift for tile in tiles], axis=1))
        sums = jnp.sum(sums, axis=0, keepdims=True)
        block = jnp.concatenate(lane_tiles(sums), axis=0)
        for g in range(out_ref.shape[0]):
            out_ref[g, k * (WIDE // LANES) : (k + 1) * (WIDE // LANES), :] = block


def first_column_kernel(place_ref, stats_ref, exp_hbm, *refs):
    factor_ref, out_ref, weight, exp_ref, sem = refs[-5:]
    loads = copies(exp_hbm, exp_ref, sem)
    start(loads)
    quarter = stats_ref.shape[1] // 4
    height = out_ref.shape[1] - 8
    own = stats_ref[pl.ds(place_ref[1], 1)][0]
    factor_ref[...] = jnp.zeros(factor_ref.shape, F32)
    rows = []
    for which in range(2):
        log_sum = merged(stats_ref, which)
        here = slice(which * quarter, (which + 1) * quarter)
        factor_ref[here, :] = jnp.exp2(
            own[2 * which * quarter : (2 * which + 1) * quarter, :] - log_sum
        )
        rows.append(log_sum)
    rows.append(jnp.zeros((8 - 2 * quarter, LANES), F32))
    logs = jnp.concatenate(rows, axis=0)
    for g in range(out_ref.shape[0]):
        out_ref[g, height:, :] = logs
    spread_rows(weight, factor_ref[:quarter, :])
    column_pass(loads, exp_ref, weight, out_ref)


def column_kernel(sums_ref, factor_ref, exp_hbm, *refs):
    out_ref, weight, exp_ref, sem = refs[-4:]
    loads = copies(exp_hbm, exp_ref, sem)
    start(loads)
    quarter = weight.shape[0] // LANES
    scale = 1.0 / add_up([sums_ref[p, :quarter, :] for p in range(sums_ref.shape[0])])
    spread_rows(weight, scale * factor_ref[:quarter, :])
    column_pass(loads, exp_ref, weight, out_ref)


def column_scales(cols_ref, height):
    return 1.0 / add_up([cols_ref[g, :height, :] for g in range(cols_ref.shape[0])])


def add_row_sums(rows, values, scales, k):
    for g in range(0, values.shape[0], 32):
        total = rows[g : g + 32, :]
        for t, tile in enumerate(lane_tiles(values[g : g + 32, :].astype(F32))):
            first = k * (WIDE // LANES) + t
            total = total + tile * scales[first : first + 1, :]
        rows[g : g + 32, :] = total


def row_kernel(cols_ref, factor_ref, exp_hbm, *refs):
    out_ref, scales, rows, exp_ref, sem = refs[-5:]
    loads = copies(exp_hbm, exp_ref, sem)
    start(loads)
    scales[...] = column_scales(cols_ref, scales.shape[0])
    rows[...] = jnp.zeros(rows.shape, F32)
    quarter = rows.shape[0] // LANES
    out_ref[0] = jnp.zeros(out_ref.shape[1:], F32)
    for k, load in enumerate(loads):
        load.wait()
        add_row_sums(rows, exp_ref.at[k], scales, k)
    pack_rows(out_ref.at[0, :quarter], jnp.sum(rows[...], axis=1, keepdims=True))
    out_ref[0, :quarter, :] = out_ref[0, :quarter, :] * factor_ref[:quarter, :]
    repeat(out_ref)


def own_back_kernel(
    before_ref, exp_hbm, w_hbm, back_ref, exp_ref, w_ref, exp_sem, w_sem
):
    exp_loads, w_loads = copies(exp_hbm, exp_ref, exp_sem), copies(w_hbm, w_ref, w_sem)
    start(exp_loads, w_loads)
    back_ref[...] = jnp.zeros(back_ref.shape, F32)
    for k in range(len(w_loads)):
        exp_loads[k].wait()
        w_loads[k].wait()
        back_ref[...] += nt_dot(exp_ref[k], w_ref[:, chunk(k)])


def relative(place_ref, g, groups):
    return pl.ds(lax.rem(place_ref[0] + g, groups), 1)


def relative_logs(place_ref, logs_ref, lse, which, shift=0.0):
    groups = logs_ref.shape[0]
    own = lse.shape[0] // (groups - 1)
    quarter = own // LANES
    height = logs_ref.shape[1] - 8
    for g in range(1, groups):
        there = logs_ref[relative(place_ref, g, groups)][0]
        first = height + which * quarter
        spread_rows(lse.at[(g - 1) * own : g * own], there[first : first + quarter, :] - shift)


def student_rows_kernel(log_protos, place_ref, factor_ref, own_ref, *refs):
    unit_ref, feat_ref, scaled_ref, turned = refs[-4:]
    own = own_ref.shape[0]
    groups = turned.shape[1] // own
    raw = refs[: groups - 1]
    quarter, feats = own // LANES, feat_ref.shape[0]
    for g in range(groups):
        half = unit_rows((raw[g - 1] if g else own_ref)[...])[0].astype(BF16)
        if g:
            unit_ref[(g - 1) * own : g * own, :] = half
        half = half.astype(F32)
        for a in range(0, own, LANES):
            first = g * own + a
            turned[:, first : first + LANES] = jnp.transpose(half[a : a + LANES, :]).astype(BF16)
    feat = turned[pl.ds(pl.multiple_of(place_ref[0] * feats, feats), feats), :]
    feat_ref[...] = feat
    for a in range(quarter):
        lanes = slice(a * LANES, (a + 1) * LANES)
        factor = factor_ref[quarter + a : quarter + a + 1, :] * 2.0**log_protos
        scaled_ref[:, lanes] = (feat[:, lanes].astype(F32) * factor).astype(BF16)


def probabilities(unit, own, chunks, weights, lse, scale, use, after):
    blocks = [
        (k, g, n)
        for k in range(chunks)
        for g in range(unit.shape[0] // own)
        for n in range(0, WIDE, 512)
    ]

    def product(k, g, n):
        w = weights(k, g == 0 and n == 0)
        return jnp.dot(
            unit[g * own : (g + 1) * own, :], w[:, n : n + 512], preferred_element_type=F32
        )

    logits = product(*blocks[0])
    for i, (k, g, n) in enumerate(blocks):
        later = product(*blocks[i + 1]) if i + 1 < len(blocks) else None
        shift = lse[g * own : (g + 1) * own, :]
        use(k, g, n, [exp2_half(tile * scale - shift) for tile in lane_tiles(logits)])
        if i + 1 == len(blocks) or blocks[i + 1][0] != k:
            after(k)
        logits = later


def student_kernel(
    log_protos, first, place_ref, logs_ref, unit, feat_ref, scaled_ref, exp_hbm, w_hbm, *refs
):
    grad_hbm, token_ref, lse, prob, exp_ref, w_ref, grad, exp_sem, w_sem, grad_sem = refs[-10:]
    own, count = exp_ref.shape[1], exp_ref.shape[0]
    exp_loads = copies(exp_hbm, exp_ref, exp_sem, first, 0, count)
    w_loads = copies(w_hbm, w_ref, w_sem, first, 0, count)
    stores = copies(grad, grad_hbm, grad_sem)
    start(w_loads, exp_loads)
    token_ref[...] = jnp.zeros(token_ref.shape, F32)
    relative_logs(place_ref, logs_ref, lse, 1, log_protos)

    def weights(k, fresh):
        if fresh:
            w_loads[k].wait()
        return w_ref.at[:, chunk(k)]

    def use(k, g, n, tiles):
        for t, tile in enumerate(tiles):
            lanes = slice(n + t * LANES, n + (t + 1) * LANES)
            prob[k % 2, g * own : (g + 1) * own, lanes] = tile

    def after(k):
        exp_loads[k].wait()
        values = jnp.dot(scaled_ref[...], exp_ref[k], preferred_element_type=F32)
        values = values + jnp.dot(feat_ref[:, own:], prob[k % 2], preferred_element_type=F32)
        grad[:, chunk(k)] = values.astype(BF16)
        stores[k].start()

    probabilities(unit, own, count, weights, lse, SCALE_STUDENT, use, after)
    wait(stores)


def as_three(value):
    high = value.astype(BF16)
    rest = value - high.astype(F32)
    middle = rest.astype(BF16)
    return high, middle, (rest - middle.astype(F32)).astype(BF16)


def last_kernel(groups, place_ref, logs_ref, cols_ref, factor_ref, own_ref, student_ref, exp_hbm, w_hbm, *refs):
    units = refs[: groups - 1]
    (
        prob_hbm, scale_ref, out_ref, unit, lse, rows, own_rows, back, scaled, sums, prob_ref,
        exp_ref, w_ref, prob_sem, exp_sem, w_sem,
    ) = refs[-16:]
    w_loads, exp_loads = copies(w_hbm, w_ref, w_sem), copies(exp_hbm, exp_ref, exp_sem)
    start(w_loads, exp_loads)
    slots, others, _ = prob_ref.shape
    own, chunks = exp_ref.shape[1], exp_ref.shape[0]
    tiles = (own + others) // LANES
    quarter = own // LANES
    scale_ref[...] = column_scales(cols_ref, scale_ref.shape[0])
    rows[...] = jnp.zeros(rows.shape, F32)
    own_rows[...] = jnp.zeros(own_rows.shape, F32)
    back[...] = jnp.zeros(back.shape, F32)
    relative_logs(place_ref, logs_ref, lse, 0)
    for g in range(groups - 1):
        unit[g * own : (g + 1) * own, :] = units[g][...]
    stores = [
        pltpu.make_async_copy(prob_ref.at[k % slots], prob_hbm.at[k], prob_sem.at[k])
        for k in range(chunks)
    ]

    def use(k, g, n, tiles):
        if g == 0 and n == 0 and k >= slots:
            stores[k - slots].wait()
        here = slice(g * own, (g + 1) * own)
        for t, tile in enumerate(tiles):
            prob_ref[k % slots, here, n + t * LANES : n + (t + 1) * LANES] = tile
        first = k * (WIDE // LANES) + n // LANES
        tiles = [
            tile.astype(F32) * scale_ref[first + t : first + t + 1, :]
            for t, tile in enumerate(tiles)
        ]
        rows[here, :] += add_up(tiles)
        if g == groups // 2 - 1:
            for t, tile in enumerate(tiles):
                scaled[k % 2, :, n + t * LANES : n + (t + 1) * LANES] = tile.astype(BF16)

    def after(k):
        stores[k].start()
        back[...] += nt_dot(scaled[k % 2], w_ref[:, chunk(k)])
        exp_loads[k].wait()
        add_row_sums(own_rows, exp_ref.at[k], scale_ref, k)

    def weights(k, fresh):
        if fresh:
            w_loads[k].wait()
        return w_ref.at[:, chunk(k)]

    probabilities(unit, own, chunks, weights, lse, SCALE_TEACHER, use, after)

    sums[...] = jnp.zeros(sums.shape, F32)
    pack_rows(sums.at[:quarter], jnp.sum(own_rows[...], axis=1, keepdims=True))
    sums[:quarter, :] = sums[:quarter, :] * factor_ref[:quarter, :]
    pack_rows(sums.at[quarter:tiles], jnp.sum(rows[...], axis=1, keepdims=True))
    half = unit_rows(own_ref[...])[0].astype(BF16).astype(F32)
    inner = jnp.sum(half * back[...], axis=1, keepdims=True)
    pack_rows(sums.at[tiles : tiles + quarter], inner)
    parts = out_ref.shape[0]
    share = own // parts
    protos = 1.0 * out_ref.shape[0] * w_ref.shape[1]
    student = []
    for a in range(quarter):
        factor = to_column(factor_ref[quarter + a : quarter + a + 1, :] * protos)
        student.append(student_ref[a * LANES : (a + 1) * LANES, :] * factor)
    student = jnp.concatenate(student, axis=0).astype(BF16)
    terms = list(as_three(sums[...]))
    terms.append(jnp.zeros((sums.shape[0], out_ref.shape[2] - 3 * LANES), BF16))
    terms = jnp.concatenate(terms, axis=1)
    for p in range(parts):
        here = slice(p * share, (p + 1) * share)
        out_ref[p] = jnp.concatenate(
            [student[here, :], back[here, :].astype(BF16), terms], axis=0
        )
    wait(stores[max(0, chunks - slots) :])


def total_sums(message_ref, first):
    parts = message_ref.shape[0]
    each = [
        add_up([t.astype(F32) for t in lane_tiles(message_ref[p, first:, : 3 * LANES])[::-1]])
        for p in range(parts)
    ]
    return add_up(each)


def rows_kernel(tiles, protos, place_ref, s_ref, message_ref, logs_ref, *refs):
    out_ref, loss_ref, sums_ref, weight = refs[-4:]
    parts = message_ref.shape[0]
    share, own = out_ref.shape[1], weight.shape[0]
    quarter = own // LANES
    first = tiles // 2
    totals = total_sums(message_ref, 2 * share)
    sums_ref[...] = totals
    scale = 1.0 / totals[first : first + quarter, :]
    spread_rows(weight, scale)
    mine = pl.ds(pl.multiple_of(place_ref[1] * share, share), share)
    total = add_up([message_ref[p, :share, :].astype(F32) for p in range(parts)])
    paired = add_up([message_ref[p, share : 2 * share, :].astype(F32) for p in range(parts)])
    total = total - paired * (weight[mine, :1] * protos)
    unit, length = unit_rows(s_ref[mine, :])
    out_ref[0] = (total - unit * jnp.sum(unit * total, axis=-1, keepdims=True)) / length
    repeat(out_ref)
    height = logs_ref.shape[1] - 8
    logs = logs_ref[pl.ds(place_ref[0], 1)][0][height + quarter : height + 2 * quarter, :]
    terms = logs / LOG2E - totals[tiles : tiles + quarter, :] * scale / TEMP_STUDENT
    loss_ref[...] = jnp.broadcast_to(jnp.sum(terms), loss_ref.shape)


def grad_kernel(counts, protos, exp_hbm, prob_hbm, feat_ref, scale_ref, sums_ref, factor_ref, *refs):
    parts = refs[: len(counts)]
    out_hbm, scaled, exp_ref, prob_ref, part_ref, out, exp_sem, prob_sem, part_sem, sem = refs[-10:]
    exp_loads = copies(exp_hbm, exp_ref, exp_sem)
    prob_loads = copies(prob_hbm, prob_ref, prob_sem)
    part_loads, first = [], 0
    for count, part in zip(counts, parts):
        part_loads += copies(part, part_ref, part_sem.at[first : first + count], 0, first)
        first += count
    start(exp_loads, prob_loads, part_loads)
    own = exp_ref.shape[1]
    tiles = (own + prob_ref.shape[1]) // LANES
    rows = protos / sums_ref[:tiles, :]
    for a in range(tiles):
        other = (a + tiles // 2) % tiles
        feat = feat_ref[:, other * LANES : (other + 1) * LANES].astype(F32)
        row = rows[a : a + 1, :]
        if a < own // LANES:
            row = row * factor_ref[a : a + 1, :]
        scaled[:, a * LANES : (a + 1) * LANES] = (feat * row).astype(BF16)
    stores = copies(out, out_hbm, sem)
    for k, store in enumerate(stores):
        exp_loads[k].wait()
        prob_loads[k].wait()
        paired = jnp.dot(scaled[:, :own], exp_ref[k], preferred_element_type=F32)
        paired = paired + jnp.dot(
            scaled[:, own:], prob_ref[k], preferred_element_type=F32
        )
        part_loads[k].wait()
        for t, tile in enumerate(lane_tiles(paired)):
            lanes = slice(k * WIDE + t * LANES, k * WIDE + (t + 1) * LANES)
            scale = scale_ref[lanes.start // LANES : lanes.stop // LANES, :]
            out[:, lanes] = (part_ref[:, lanes].astype(F32) - tile * scale).astype(BF16)
        store.start()
    for store in stores:
        store.wait()


SMEM = pl.BlockSpec(memory_space=pltpu.SMEM)
VMEM = pl.BlockSpec(memory_space=pltpu.VMEM)
ANY = pl.BlockSpec(memory_space=pl.ANY)


def params(nbytes):
    return pltpu.CompilerParams(vmem_limit_bytes=int(nbytes) + 8 * 2**20)


def cost(flops, nbytes, exps=0):
    return pl.CostEstimate(flops=int(flops), bytes_accessed=int(nbytes), transcendentals=int(exps))


def exchange(value, axis):
    return lax.all_to_all(value, axis, 0, 0)


def following(value, axis):
    n = lax.axis_size(axis)
    return [lax.ppermute(value, axis, [(i, (i - s) % n) for i in range(n)]) for s in range(1, n)]


def tree_sum(value, axis):
    n = lax.axis_size(axis)
    values = [value] + [
        lax.ppermute(value, axis, [(i, i ^ s) for i in range(n)]) for s in range(1, n)
    ]
    while len(values) > 1:
        values = [a + b for a, b in zip(values[::2], values[1::2])]
    return values[0]


def local(teacher_feats, student_feats, proto_weight):
    parts, groups = lax.axis_size("proto"), lax.axis_size("batch")
    own, width = teacher_feats.shape
    local_protos = proto_weight.shape[1]
    rows = own * groups
    others = rows - own
    protos = local_protos * parts
    feats = width // groups
    share = own // parts
    tiles = rows // LANES
    height = local_protos // LANES
    chunks = local_protos // WIDE
    place = jnp.stack([lax.axis_index("batch"), lax.axis_index("proto")]).astype(jnp.int32)
    struct = jax.ShapeDtypeStruct
    weight_bytes = 2 * width * local_protos
    exp_bytes = 2 * own * local_protos
    others_bytes = 2 * others * local_protos
    spread = pltpu.VMEM((own, LANES), F32)
    w_buffer = pltpu.VMEM((width, local_protos), BF16)
    exp_buffer = pltpu.VMEM((chunks, own, WIDE), BF16)
    sems = pltpu.SemaphoreType.DMA((chunks,))
    log_protos = math.log2(protos)
    token = struct((8, LANES), F32)

    def far(value):
        return pltpu.with_memory_space_constraint(value, pltpu.HBM)

    weight = far(proto_weight)
    s_all = following(student_feats, "batch")

    exps = pltpu.HBM((chunks, own, WIDE), BF16)
    t_exp, s_exp, t_unit, stats = pl.pallas_call(
        stats_kernel,
        in_specs=[VMEM, VMEM, ANY],
        out_specs=[ANY, ANY, VMEM, VMEM],
        out_shape=[exps, exps, struct((own, width), BF16), struct((parts, 4 * own // LANES, LANES), F32)],
        scratch_shapes=[
            w_buffer,
            pltpu.VMEM((2, own, width), BF16),
            pltpu.VMEM((2, chunks, own, WIDE), BF16),
            pltpu.VMEM((2, own, local_protos), F32),
            pltpu.VMEM((2, own, LANES), F32),
            pltpu.VMEM((2, own, LANES), F32),
            sems, sems, sems,
        ],
        compiler_params=params(weight_bytes + 6 * exp_bytes),
        cost_estimate=cost(4 * own * width * local_protos, weight_bytes),
        name="own_rows",
    )(teacher_feats, student_feats, weight)
    t_exp, s_exp = far(t_exp), far(s_exp)
    t_all = following(t_unit, "batch")

    back_student = pl.pallas_call(
        own_back_kernel,
        in_specs=[ANY] * 3,
        out_specs=VMEM,
        out_shape=struct((own, width), F32),
        scratch_shapes=[exp_buffer, w_buffer, sems, sems],
        compiler_params=params(weight_bytes + exp_bytes),
        cost_estimate=cost(2 * own * width * local_protos, weight_bytes),
        name="own_back",
    )(stats, s_exp, weight)
    stats = exchange(stats, "proto")

    first_shape = (groups, height + 8, LANES)
    factor, cols = pl.pallas_call(
        first_column_kernel,
        in_specs=[SMEM, VMEM, ANY, ANY] + [ANY] * (groups - 1),
        out_specs=[VMEM, VMEM],
        out_shape=[token, struct(first_shape, F32)],
        scratch_shapes=[spread, exp_buffer, sems],
        compiler_params=params(exp_bytes),
        cost_estimate=cost(2 * own * local_protos, exp_bytes),
        name="first_columns",
    )(place, stats, t_exp, back_student, *s_all)

    unit, feat, scaled = pl.pallas_call(
        functools.partial(student_rows_kernel, log_protos),
        in_specs=[SMEM, VMEM, VMEM] + [VMEM] * (groups - 1) + [ANY],
        out_specs=[VMEM] * 3,
        out_shape=[
            struct((others, width), BF16), struct((feats, rows), BF16), struct((feats, own), BF16),
        ],
        scratch_shapes=[pltpu.VMEM((width, rows), BF16)],
        compiler_params=params(2 * rows * width),
        cost_estimate=cost(8 * rows * width, 2 * rows * width),
        name="student_rows",
    )(place, factor, student_feats, *s_all, cols)
    cols = exchange(cols, "batch")
    logs = cols

    counts = [c * chunks // 8 for c in (1, 1, 1, 1, 4)]
    grad_parts = []

    def student_piece(before):
        turn = len(grad_parts)
        first, count = sum(counts[:turn]), counts[turn]
        grad_part, done = pl.pallas_call(
            functools.partial(student_kernel, log_protos, first),
            in_specs=[SMEM] + [VMEM] * 4 + [ANY] * 3,
            out_specs=[ANY, VMEM],
            out_shape=[pltpu.HBM((feats, count * WIDE), BF16), token],
            scratch_shapes=[
                pltpu.VMEM((others, LANES), F32),
                pltpu.VMEM((2, others, WIDE), BF16),
                pltpu.VMEM((count, own, WIDE), BF16),
                pltpu.VMEM((width, count * WIDE), BF16),
                pltpu.VMEM((feats, count * WIDE), BF16),
            ]
            + [pltpu.SemaphoreType.DMA((count,))] * 3,
            compiler_params=params(16 * 2**20),
            cost_estimate=cost(2.5 * rows * width * WIDE * count, 2 * width * WIDE * count),
            name="student_side",
        )(place, logs, unit, feat, scaled, s_exp, weight, before)
        grad_parts.append(far(grad_part))
        return done

    done = unit
    for turn in range(SWEEPS - 1):
        late = t_all if turn == 0 else []
        sums = pl.pallas_call(
            row_kernel,
            in_specs=[VMEM, VMEM, ANY, ANY] + [ANY] * len(late),
            out_specs=VMEM,
            out_shape=struct((parts, 8, LANES), F32),
            scratch_shapes=[pltpu.VMEM((height, LANES), F32), spread, exp_buffer, sems],
            compiler_params=params(exp_bytes),
            cost_estimate=cost(2 * own * local_protos, exp_bytes),
            name="rows",
        )(cols, factor, t_exp, done, *late)
        done = student_piece(sums)
        sums = exchange(sums, "proto")
        cols = pl.pallas_call(
            column_kernel,
            in_specs=[VMEM, VMEM, ANY, ANY],
            out_specs=VMEM,
            out_shape=struct((groups, height, LANES), F32),
            scratch_shapes=[spread, exp_buffer, sems],
            compiler_params=params(exp_bytes),
            cost_estimate=cost(2 * own * local_protos, exp_bytes),
            name="columns",
        )(sums, factor, t_exp, done)
        done = student_piece(cols)
        cols = exchange(cols, "batch")

    sum_rows = -(-(tiles + own // LANES) // 16) * 16
    message_shape = (parts, 2 * share + sum_rows, width)
    prob, col_scale, message = pl.pallas_call(
        functools.partial(last_kernel, groups),
        in_specs=[SMEM] + [VMEM] * 5 + [ANY] * 2 + [VMEM] * (groups - 1) + [ANY],
        out_specs=[ANY, VMEM, VMEM],
        out_shape=[
            pltpu.HBM((chunks, others, WIDE), BF16),
            struct((height, LANES), F32),
            struct(message_shape, BF16),
        ],
        scratch_shapes=[
            pltpu.VMEM((others, width), BF16),
            pltpu.VMEM((others, LANES), F32),
            pltpu.VMEM((others, LANES), F32),
            spread,
            pltpu.VMEM((own, width), F32),
            pltpu.VMEM((2, own, WIDE), BF16),
            pltpu.VMEM((sum_rows, LANES), F32),
            pltpu.VMEM((min(chunks, 3), others, WIDE), BF16),
            exp_buffer,
            w_buffer,
            sems, sems, sems,
        ],
        compiler_params=params(20 * 2**20 + weight_bytes + exp_bytes),
        cost_estimate=cost(2 * rows * width * local_protos, others_bytes),
        name="last_rows",
    )(
        place, logs, cols, factor, student_feats, back_student, t_exp, weight, *t_all, done,
    )
    done = student_piece(message)
    message = exchange(message, "proto")

    grad_rows, loss_part, sums = pl.pallas_call(
        functools.partial(rows_kernel, tiles, float(protos)),
        in_specs=[SMEM] + [VMEM] * 3 + [ANY],
        out_specs=[VMEM] * 3,
        out_shape=[struct((parts, share, width), F32), token, struct((sum_rows, LANES), F32)],
        scratch_shapes=[spread],
        compiler_params=params(0),
        name="row_grads",
    )(place, student_feats, message, logs, done)
    grad_rows = exchange(grad_rows, "proto").reshape(own, width)
    loss = tree_sum(loss_part, "batch")[0, 0] / rows

    grad_weight = pl.pallas_call(
        functools.partial(grad_kernel, counts, float(protos)),
        in_specs=[ANY] * 2 + [VMEM] * 4 + [ANY] * len(counts),
        out_specs=ANY,
        out_shape=struct((feats, local_protos), BF16),
        scratch_shapes=[
            pltpu.VMEM((feats, rows), BF16),
            exp_buffer,
            pltpu.VMEM((chunks, others, WIDE), BF16),
            pltpu.VMEM((feats, local_protos), BF16),
            pltpu.VMEM((feats, local_protos), BF16),
            sems, sems, sems, sems,
        ],
        compiler_params=params(exp_bytes + others_bytes + 4 * feats * local_protos),
        cost_estimate=cost(2 * feats * rows * local_protos, others_bytes),
        name="weight_grads",
    )(t_exp, far(prob), feat, col_scale, sums, factor, *grad_parts)
    return grad_weight, grad_rows, loss


def solution(mesh):
    return jax.shard_map(
        local,
        mesh=mesh,
        in_specs=(P("batch", None), P("batch", None), P(None, "proto")),
        out_specs=(P("batch", "proto"), P("batch", None), P()),
        check_vma=False,
    )
```

```python
import functools
import math

import jax
import jax.numpy as jnp
from jax import lax
from jax.experimental import pallas as pl
from jax.experimental.pallas import tpu as pltpu
from jax.sharding import PartitionSpec as P

SWEEPS = 3
TEMP_TEACHER = 0.04
TEMP_STUDENT = 0.1
LANES = 128
WIDE = 1024
F32 = jnp.float32
BF16 = jnp.bfloat16


def unit_rows(values):
    wide = values.astype(F32)
    length = jnp.sqrt(jnp.sum(wide * wide, axis=-1, keepdims=True) + 1e-06)
    return wide / length, length


def diagonal():
    shape = (LANES, LANES)
    return lax.broadcasted_iota(jnp.int32, shape, 0) == lax.broadcasted_iota(jnp.int32, shape, 1)


def to_column(row):
    spread = jnp.where(diagonal(), jnp.broadcast_to(row, (LANES, LANES)), 0.0)
    return jnp.sum(spread, axis=1, keepdims=True)


def to_row(column):
    spread = jnp.where(diagonal(), jnp.broadcast_to(column, (LANES, LANES)), 0.0)
    return jnp.sum(spread, axis=0, keepdims=True)


def spread_rows(ref, rows):
    for a in range(rows.shape[0]):
        ref[a * LANES : (a + 1) * LANES, :] = jnp.broadcast_to(
            to_column(rows[a : a + 1, :]), (LANES, LANES)
        )


def pack_rows(ref, columns):
    for a in range(columns.shape[0] // LANES):
        ref[a : a + 1, :] = to_row(columns[a * LANES : (a + 1) * LANES, :])


def lane_tiles(values):
    return [values[:, t * LANES : (t + 1) * LANES] for t in range(values.shape[1] // LANES)]


def fold(values):
    return functools.reduce(jnp.add, lane_tiles(values))


def column_sums(values):
    rows, cols = values.shape
    return jnp.sum(values.reshape(rows // 8, 8, cols), axis=0)


def nt_dot(a, b):
    return lax.dot_general(a, b, (((1,), (1,)), ((), ())), preferred_element_type=F32)


def add_up(values):
    return functools.reduce(jnp.add, values)


def repeat(out_ref):
    for p in range(1, out_ref.shape[0]):
        out_ref[p] = out_ref[0]


def chunk(k):
    return slice(k * WIDE, (k + 1) * WIDE)


def copies(source, target, sems, first=0, back=0, count=None):
    def part(ref, k):
        return ref.at[k] if len(ref.shape) == 3 else ref.at[:, chunk(k)]

    def chunks(ref):
        return ref.shape[0] if len(ref.shape) == 3 else ref.shape[1] // WIDE

    count = count or min(chunks(source), chunks(target))
    return [
        pltpu.make_async_copy(part(source, first + k), part(target, back + k), sems.at[k])
        for k in range(count)
    ]


def start(*lists):
    for each in zip(*lists):
        for copy in each:
            copy.start()


def wait(*lists):
    for each in lists:
        for copy in each:
            copy.wait()


def stats_kernel(
    t_hbm, s_hbm, w_hbm, t_out, s_out, t_unit, out_ref, back_ref,
    raw, w_ref, unit, exps, logits, top, total, raw_sem, w_sem, t_sem, s_sem,
):
    piece = 512
    pieces = [slice(c, c + piece) for c in range(0, w_ref.shape[1], piece)]
    quarter = out_ref.shape[1] // 4
    scales = (1.0 / TEMP_TEACHER, 1.0 / TEMP_STUDENT)
    loads = copies(w_hbm, w_ref, w_sem)
    raw_loads = [
        pltpu.make_async_copy(ref, raw.at[which], raw_sem.at[which])
        for which, ref in enumerate((t_hbm, s_hbm))
    ]
    start(raw_loads, loads[:2])
    start(loads[2:])
    stores = [copies(exps.at[0], t_out, t_sem), copies(exps.at[1], s_out, s_sem)]
    back_ref[...] = jnp.zeros(back_ref.shape, F32)
    wait(raw_loads)
    for which in range(2):
        unit[which] = unit_rows(raw[which])[0].astype(BF16)
    t_unit[...] = unit[0]
    top[...] = jnp.full(top.shape, -1e30, F32)
    total[...] = jnp.zeros(total.shape, F32)

    for here in pieces:
        if here.start % WIDE == 0:
            loads[here.start // WIDE].wait()
        for which in range(2):
            values = jnp.dot(unit[which], w_ref[:, here], preferred_element_type=F32)
            values = values * scales[which]
            logits[which, :, here] = values
            top[which] = functools.reduce(jnp.maximum, lane_tiles(values), top[which])
    peaks = [jnp.max(top[which], axis=1, keepdims=True) for which in range(2)]
    for which in range(2):
        shift = jnp.broadcast_to(peaks[which], (peaks[which].shape[0], LANES))
        for here in pieces:
            tiles = [jnp.exp(t - shift) for t in lane_tiles(logits[which, :, here])]
            k, first = here.start // WIDE, here.start % WIDE
            for t, tile in enumerate(tiles):
                lanes = slice(first + t * LANES, first + (t + 1) * LANES)
                exps[which, k, :, lanes] = tile.astype(BF16)
            total[which] += add_up(tiles)
            if here.stop % WIDE == 0:
                stores[which][k].start()
                if which:
                    back_ref[...] += nt_dot(exps[which, k], w_ref[:, chunk(k)])
        sums = jnp.sum(total[which], axis=1, keepdims=True)
        for k, column in enumerate((peaks[which], sums)):
            first = (2 * which + k) * quarter
            pack_rows(out_ref.at[0, first : first + quarter], column)
    repeat(out_ref)
    wait(*stores)


def merged(stats_ref, which):
    parts, height, _ = stats_ref.shape
    quarter = height // 4
    first = 2 * which * quarter
    tops = [stats_ref[p, first : first + quarter, :] for p in range(parts)]
    top = functools.reduce(jnp.maximum, tops)
    sums = [
        stats_ref[p, first + quarter : first + 2 * quarter, :] * jnp.exp(tops[p] - top)
        for p in range(parts)
    ]
    return top + jnp.log(add_up(sums))


def column_pass(loads, exp_ref, weight, out_ref):
    for k, load in enumerate(loads):
        load.wait()
        sums = jnp.zeros((8, WIDE), F32)
        for g in range(0, exp_ref.shape[1], 16):
            shift = weight[g : g + 16, :]
            tiles = lane_tiles(exp_ref[k, g : g + 16, :].astype(F32))
            sums = sums + column_sums(jnp.concatenate([tile * shift for tile in tiles], axis=1))
        sums = jnp.sum(sums, axis=0, keepdims=True)
        block = jnp.concatenate(lane_tiles(sums), axis=0)
        for g in range(out_ref.shape[0]):
            out_ref[g, k * (WIDE // LANES) : (k + 1) * (WIDE // LANES), :] = block


def first_column_kernel(place_ref, stats_ref, exp_hbm, *refs):
    factor_ref, out_ref, weight, exp_ref, sem = refs[-5:]
    loads = copies(exp_hbm, exp_ref, sem)
    start(loads)
    quarter = stats_ref.shape[1] // 4
    height = out_ref.shape[1] - 8
    own = stats_ref[pl.ds(place_ref[1], 1)][0]
    factor_ref[...] = jnp.zeros(factor_ref.shape, F32)
    rows = []
    for which in range(2):
        log_sum = merged(stats_ref, which)
        here = slice(which * quarter, (which + 1) * quarter)
        factor_ref[here, :] = jnp.exp(
            own[2 * which * quarter : (2 * which + 1) * quarter, :] - log_sum
        )
        rows.append(log_sum)
    rows.append(jnp.zeros((8 - 2 * quarter, LANES), F32))
    logs = jnp.concatenate(rows, axis=0)
    for g in range(out_ref.shape[0]):
        out_ref[g, height:, :] = logs
    spread_rows(weight, factor_ref[:quarter, :])
    column_pass(loads, exp_ref, weight, out_ref)


def column_kernel(sums_ref, factor_ref, exp_hbm, *refs):
    out_ref, weight, exp_ref, sem = refs[-4:]
    loads = copies(exp_hbm, exp_ref, sem)
    start(loads)
    quarter = weight.shape[0] // LANES
    scale = 1.0 / add_up([sums_ref[p, :quarter, :] for p in range(sums_ref.shape[0])])
    spread_rows(weight, scale * factor_ref[:quarter, :])
    column_pass(loads, exp_ref, weight, out_ref)


def column_scales(cols_ref, height):
    return 1.0 / add_up([cols_ref[g, :height, :] for g in range(cols_ref.shape[0])])


def add_row_sums(rows, values, scales, k):
    for g in range(0, values.shape[0], 32):
        total = rows[g : g + 32, :]
        for t, tile in enumerate(lane_tiles(values[g : g + 32, :].astype(F32))):
            first = k * (WIDE // LANES) + t
            total = total + tile * scales[first : first + 1, :]
        rows[g : g + 32, :] = total


def row_kernel(cols_ref, factor_ref, exp_hbm, *refs):
    out_ref, scales, rows, exp_ref, sem = refs[-5:]
    loads = copies(exp_hbm, exp_ref, sem)
    start(loads)
    scales[...] = column_scales(cols_ref, scales.shape[0])
    rows[...] = jnp.zeros(rows.shape, F32)
    quarter = rows.shape[0] // LANES
    out_ref[0] = jnp.zeros(out_ref.shape[1:], F32)
    for k, load in enumerate(loads):
        load.wait()
        add_row_sums(rows, exp_ref.at[k], scales, k)
    pack_rows(out_ref.at[0, :quarter], jnp.sum(rows[...], axis=1, keepdims=True))
    out_ref[0, :quarter, :] = out_ref[0, :quarter, :] * factor_ref[:quarter, :]
    repeat(out_ref)


def relative(place_ref, g, groups):
    return pl.ds(lax.rem(place_ref[0] + g, groups), 1)


def relative_logs(place_ref, logs_ref, lse, which, shift=0.0):
    groups = logs_ref.shape[0]
    own = lse.shape[0] // (groups - 1)
    quarter = own // LANES
    height = logs_ref.shape[1] - 8
    for g in range(1, groups):
        there = logs_ref[relative(place_ref, g, groups)][0]
        first = height + which * quarter
        spread_rows(lse.at[(g - 1) * own : g * own], there[first : first + quarter, :] - shift)


def student_rows_kernel(protos, place_ref, factor_ref, own_ref, *refs):
    unit_ref, feat_ref, scaled_ref, turned = refs[-4:]
    own = own_ref.shape[0]
    groups = turned.shape[1] // own
    raw = refs[: groups - 1]
    quarter, feats = own // LANES, feat_ref.shape[0]
    for g in range(groups):
        half = unit_rows((raw[g - 1] if g else own_ref)[...])[0].astype(BF16)
        if g:
            unit_ref[(g - 1) * own : g * own, :] = half
        half = half.astype(F32)
        for a in range(0, own, LANES):
            first = g * own + a
            turned[:, first : first + LANES] = jnp.transpose(half[a : a + LANES, :]).astype(BF16)
    feat = turned[pl.ds(pl.multiple_of(place_ref[0] * feats, feats), feats), :]
    feat_ref[...] = feat
    for a in range(quarter):
        lanes = slice(a * LANES, (a + 1) * LANES)
        factor = factor_ref[quarter + a : quarter + a + 1, :] * protos
        scaled_ref[:, lanes] = (feat[:, lanes].astype(F32) * factor).astype(BF16)


def probabilities(unit, own, chunks, weights, lse, scale, use, after):
    blocks = [
        (k, g, n)
        for k in range(chunks)
        for g in range(unit.shape[0] // own)
        for n in range(0, WIDE, 512)
    ]

    def product(k, g, n):
        w = weights(k, g == 0 and n == 0)
        return jnp.dot(
            unit[g * own : (g + 1) * own, :], w[:, n : n + 512], preferred_element_type=F32
        )

    logits = product(*blocks[0])
    for i, (k, g, n) in enumerate(blocks):
        later = product(*blocks[i + 1]) if i + 1 < len(blocks) else None
        shift = lse[g * own : (g + 1) * own, :]
        use(k, g, n, [jnp.exp(tile * scale - shift) for tile in lane_tiles(logits)])
        if i + 1 == len(blocks) or blocks[i + 1][0] != k:
            after(k)
        logits = later


def student_kernel(
    log_protos, first, place_ref, logs_ref, unit, feat_ref, scaled_ref, exp_hbm, w_hbm, *refs
):
    grad_hbm, token_ref, lse, prob, exp_ref, w_ref, grad, exp_sem, w_sem, grad_sem = refs[-10:]
    own, count = exp_ref.shape[1], exp_ref.shape[0]
    exp_loads = copies(exp_hbm, exp_ref, exp_sem, first, 0, count)
    w_loads = copies(w_hbm, w_ref, w_sem, first, 0, count)
    stores = copies(grad, grad_hbm, grad_sem)
    start(w_loads, exp_loads)
    token_ref[...] = jnp.zeros(token_ref.shape, F32)
    relative_logs(place_ref, logs_ref, lse, 1, log_protos)

    def weights(k, fresh):
        if fresh:
            w_loads[k].wait()
        return w_ref.at[:, chunk(k)]

    def use(k, g, n, tiles):
        for t, tile in enumerate(tiles):
            lanes = slice(n + t * LANES, n + (t + 1) * LANES)
            prob[k % 2, g * own : (g + 1) * own, lanes] = tile.astype(BF16)

    def after(k):
        exp_loads[k].wait()
        values = jnp.dot(scaled_ref[...], exp_ref[k], preferred_element_type=F32)
        values = values + jnp.dot(feat_ref[:, own:], prob[k % 2], preferred_element_type=F32)
        grad[:, chunk(k)] = values.astype(BF16)
        stores[k].start()

    probabilities(unit, own, count, weights, lse, 1.0 / TEMP_STUDENT, use, after)
    wait(stores)


def as_three(value):
    high = value.astype(BF16)
    rest = value - high.astype(F32)
    middle = rest.astype(BF16)
    return high, middle, (rest - middle.astype(F32)).astype(BF16)


def last_kernel(groups, place_ref, logs_ref, cols_ref, factor_ref, own_ref, student_ref, exp_hbm, w_hbm, *refs):
    units = refs[: groups - 1]
    (
        prob_hbm, scale_ref, out_ref, unit, lse, rows, own_rows, back, scaled, sums, prob_ref,
        exp_ref, w_ref, prob_sem, exp_sem, w_sem,
    ) = refs[-16:]
    w_loads, exp_loads = copies(w_hbm, w_ref, w_sem), copies(exp_hbm, exp_ref, exp_sem)
    start(w_loads, exp_loads)
    slots, others, _ = prob_ref.shape
    own, chunks = exp_ref.shape[1], exp_ref.shape[0]
    tiles = (own + others) // LANES
    quarter = own // LANES
    scale_ref[...] = column_scales(cols_ref, scale_ref.shape[0])
    rows[...] = jnp.zeros(rows.shape, F32)
    own_rows[...] = jnp.zeros(own_rows.shape, F32)
    back[...] = jnp.zeros(back.shape, F32)
    relative_logs(place_ref, logs_ref, lse, 0)
    for g in range(groups - 1):
        unit[g * own : (g + 1) * own, :] = units[g][...]
    stores = [
        pltpu.make_async_copy(prob_ref.at[k % slots], prob_hbm.at[k], prob_sem.at[k])
        for k in range(chunks)
    ]

    def use(k, g, n, tiles):
        if g == 0 and n == 0 and k >= slots:
            stores[k - slots].wait()
        here = slice(g * own, (g + 1) * own)
        for t, tile in enumerate(tiles):
            prob_ref[k % slots, here, n + t * LANES : n + (t + 1) * LANES] = tile.astype(BF16)
        first = k * (WIDE // LANES) + n // LANES
        tiles = [
            tile * scale_ref[first + t : first + t + 1, :]
            for t, tile in enumerate(tiles)
        ]
        rows[here, :] += add_up(tiles)
        if g == groups // 2 - 1:
            for t, tile in enumerate(tiles):
                scaled[k % 2, :, n + t * LANES : n + (t + 1) * LANES] = tile.astype(BF16)

    def after(k):
        stores[k].start()
        back[...] += nt_dot(scaled[k % 2], w_ref[:, chunk(k)])
        exp_loads[k].wait()
        add_row_sums(own_rows, exp_ref.at[k], scale_ref, k)

    def weights(k, fresh):
        if fresh:
            w_loads[k].wait()
        return w_ref.at[:, chunk(k)]

    probabilities(unit, own, chunks, weights, lse, 1.0 / TEMP_TEACHER, use, after)

    sums[...] = jnp.zeros(sums.shape, F32)
    pack_rows(sums.at[:quarter], jnp.sum(own_rows[...], axis=1, keepdims=True))
    sums[:quarter, :] = sums[:quarter, :] * factor_ref[:quarter, :]
    pack_rows(sums.at[quarter:tiles], jnp.sum(rows[...], axis=1, keepdims=True))
    half = unit_rows(own_ref[...])[0].astype(BF16).astype(F32)
    inner = jnp.sum(half * back[...], axis=1, keepdims=True)
    pack_rows(sums.at[tiles : tiles + quarter], inner)
    parts = out_ref.shape[0]
    share = own // parts
    protos = 1.0 * out_ref.shape[0] * w_ref.shape[1]
    student = []
    for a in range(quarter):
        factor = to_column(factor_ref[quarter + a : quarter + a + 1, :] * protos)
        student.append(student_ref[a * LANES : (a + 1) * LANES, :] * factor)
    student = jnp.concatenate(student, axis=0).astype(BF16)
    terms = list(as_three(sums[...]))
    terms.append(jnp.zeros((sums.shape[0], out_ref.shape[2] - 3 * LANES), BF16))
    terms = jnp.concatenate(terms, axis=1)
    for p in range(parts):
        here = slice(p * share, (p + 1) * share)
        out_ref[p] = jnp.concatenate(
            [student[here, :], back[here, :].astype(BF16), terms], axis=0
        )
    wait(stores[max(0, chunks - slots) :])


def total_sums(message_ref, first):
    parts = message_ref.shape[0]
    each = [
        add_up([t.astype(F32) for t in lane_tiles(message_ref[p, first:, : 3 * LANES])[::-1]])
        for p in range(parts)
    ]
    return add_up(each)


def rows_kernel(tiles, protos, place_ref, s_ref, message_ref, logs_ref, *refs):
    out_ref, loss_ref, sums_ref, weight = refs[-4:]
    parts = message_ref.shape[0]
    share, own = out_ref.shape[1], weight.shape[0]
    quarter = own // LANES
    first = tiles // 2
    totals = total_sums(message_ref, 2 * share)
    sums_ref[...] = totals
    scale = 1.0 / totals[first : first + quarter, :]
    spread_rows(weight, scale)
    mine = pl.ds(pl.multiple_of(place_ref[1] * share, share), share)
    total = add_up([message_ref[p, :share, :].astype(F32) for p in range(parts)])
    paired = add_up([message_ref[p, share : 2 * share, :].astype(F32) for p in range(parts)])
    total = total - paired * (weight[mine, :1] * protos)
    unit, length = unit_rows(s_ref[mine, :])
    out_ref[0] = (total - unit * jnp.sum(unit * total, axis=-1, keepdims=True)) / length
    repeat(out_ref)
    height = logs_ref.shape[1] - 8
    logs = logs_ref[pl.ds(place_ref[0], 1)][0][height + quarter : height + 2 * quarter, :]
    terms = logs - totals[tiles : tiles + quarter, :] * scale / TEMP_STUDENT
    loss_ref[...] = jnp.broadcast_to(jnp.sum(terms), loss_ref.shape)


def grad_kernel(counts, protos, exp_hbm, prob_hbm, feat_ref, scale_ref, sums_ref, factor_ref, *refs):
    parts = refs[: len(counts)]
    out_hbm, scaled, exp_ref, prob_ref, part_ref, out, exp_sem, prob_sem, part_sem, sem = refs[-10:]
    exp_loads = copies(exp_hbm, exp_ref, exp_sem)
    prob_loads = copies(prob_hbm, prob_ref, prob_sem)
    part_loads, first = [], 0
    for count, part in zip(counts, parts):
        part_loads += copies(part, part_ref, part_sem.at[first : first + count], 0, first)
        first += count
    start(exp_loads, prob_loads, part_loads)
    own = exp_ref.shape[1]
    tiles = (own + prob_ref.shape[1]) // LANES
    rows = protos / sums_ref[:tiles, :]
    for a in range(tiles):
        other = (a + tiles // 2) % tiles
        feat = feat_ref[:, other * LANES : (other + 1) * LANES].astype(F32)
        row = rows[a : a + 1, :]
        if a < own // LANES:
            row = row * factor_ref[a : a + 1, :]
        scaled[:, a * LANES : (a + 1) * LANES] = (feat * row).astype(BF16)
    stores = copies(out, out_hbm, sem)
    for k, store in enumerate(stores):
        exp_loads[k].wait()
        prob_loads[k].wait()
        paired = jnp.dot(scaled[:, :own], exp_ref[k], preferred_element_type=F32)
        paired = paired + jnp.dot(
            scaled[:, own:], prob_ref[k], preferred_element_type=F32
        )
        part_loads[k].wait()
        for t, tile in enumerate(lane_tiles(paired)):
            lanes = slice(k * WIDE + t * LANES, k * WIDE + (t + 1) * LANES)
            scale = scale_ref[lanes.start // LANES : lanes.stop // LANES, :]
            out[:, lanes] = (part_ref[:, lanes].astype(F32) - tile * scale).astype(BF16)
        store.start()
    for store in stores:
        store.wait()


SMEM = pl.BlockSpec(memory_space=pltpu.SMEM)
VMEM = pl.BlockSpec(memory_space=pltpu.VMEM)
ANY = pl.BlockSpec(memory_space=pl.ANY)


def params(nbytes):
    return pltpu.CompilerParams(vmem_limit_bytes=int(nbytes) + 8 * 2**20)


def cost(flops, nbytes, exps=0):
    return pl.CostEstimate(flops=int(flops), bytes_accessed=int(nbytes), transcendentals=int(exps))


def exchange(value, axis):
    return lax.all_to_all(value, axis, 0, 0)


def following(value, axis):
    n = lax.axis_size(axis)
    return [lax.ppermute(value, axis, [(i, (i - s) % n) for i in range(n)]) for s in range(1, n)]


def tree_sum(value, axis):
    n = lax.axis_size(axis)
    values = [value] + [
        lax.ppermute(value, axis, [(i, i ^ s) for i in range(n)]) for s in range(1, n)
    ]
    while len(values) > 1:
        values = [a + b for a, b in zip(values[::2], values[1::2])]
    return values[0]


def local(teacher_feats, student_feats, proto_weight):
    parts, groups = lax.axis_size("proto"), lax.axis_size("batch")
    own, width = teacher_feats.shape
    local_protos = proto_weight.shape[1]
    rows = own * groups
    others = rows - own
    protos = local_protos * parts
    feats = width // groups
    share = own // parts
    tiles = rows // LANES
    height = local_protos // LANES
    chunks = local_protos // WIDE
    place = jnp.stack([lax.axis_index("batch"), lax.axis_index("proto")]).astype(jnp.int32)
    struct = jax.ShapeDtypeStruct
    weight_bytes = 2 * width * local_protos
    exp_bytes = 2 * own * local_protos
    others_bytes = 2 * others * local_protos
    spread = pltpu.VMEM((own, LANES), F32)
    w_buffer = pltpu.VMEM((width, local_protos), BF16)
    exp_buffer = pltpu.VMEM((chunks, own, WIDE), BF16)
    sems = pltpu.SemaphoreType.DMA((chunks,))
    log_protos = math.log(protos)
    token = struct((8, LANES), F32)

    def far(value):
        return pltpu.with_memory_space_constraint(value, pltpu.HBM)

    weight = far(proto_weight)
    s_all = following(student_feats, "batch")

    exps = pltpu.HBM((chunks, own, WIDE), BF16)
    t_exp, s_exp, t_unit, stats, back_student = pl.pallas_call(
        stats_kernel,
        in_specs=[ANY] * 3,
        out_specs=[ANY, ANY, VMEM, VMEM, VMEM],
        out_shape=[
            exps,
            exps,
            struct((own, width), BF16),
            struct((parts, 4 * own // LANES, LANES), F32),
            struct((own, width), F32),
        ],
        scratch_shapes=[
            pltpu.VMEM((2, own, width), BF16),
            w_buffer,
            pltpu.VMEM((2, own, width), BF16),
            pltpu.VMEM((2, chunks, own, WIDE), BF16),
            pltpu.VMEM((2, own, local_protos), F32),
            pltpu.VMEM((2, own, LANES), F32),
            pltpu.VMEM((2, own, LANES), F32),
            pltpu.SemaphoreType.DMA((2,)),
            sems, sems, sems,
        ],
        compiler_params=params(weight_bytes + 6 * exp_bytes),
        cost_estimate=cost(4 * own * width * local_protos, weight_bytes),
        name="own_rows",
    )(far(teacher_feats), far(student_feats), weight)
    t_exp, s_exp = far(t_exp), far(s_exp)
    t_all = following(t_unit, "batch")

    stats = exchange(stats, "proto")

    first_shape = (groups, height + 8, LANES)
    factor, cols = pl.pallas_call(
        first_column_kernel,
        in_specs=[SMEM, VMEM, ANY] + [ANY] * (groups - 1),
        out_specs=[VMEM, VMEM],
        out_shape=[token, struct(first_shape, F32)],
        scratch_shapes=[spread, exp_buffer, sems],
        compiler_params=params(exp_bytes),
        cost_estimate=cost(2 * own * local_protos, exp_bytes),
        name="first_columns",
    )(place, stats, t_exp, *s_all)

    unit, feat, scaled = pl.pallas_call(
        functools.partial(student_rows_kernel, float(protos)),
        in_specs=[SMEM, VMEM, VMEM] + [VMEM] * (groups - 1) + [ANY],
        out_specs=[VMEM] * 3,
        out_shape=[
            struct((others, width), BF16), struct((feats, rows), BF16), struct((feats, own), BF16),
        ],
        scratch_shapes=[pltpu.VMEM((width, rows), BF16)],
        compiler_params=params(2 * rows * width),
        cost_estimate=cost(8 * rows * width, 2 * rows * width),
        name="student_rows",
    )(place, factor, student_feats, *s_all, cols)
    cols = exchange(cols, "batch")
    logs = cols

    counts = [c * chunks // 8 for c in (1, 1, 1, 1, 4)]
    grad_parts = []

    def student_piece(before):
        turn = len(grad_parts)
        first, count = sum(counts[:turn]), counts[turn]
        grad_part, done = pl.pallas_call(
            functools.partial(student_kernel, log_protos, first),
            in_specs=[SMEM] + [VMEM] * 4 + [ANY] * 3,
            out_specs=[ANY, VMEM],
            out_shape=[pltpu.HBM((feats, count * WIDE), BF16), token],
            scratch_shapes=[
                pltpu.VMEM((others, LANES), F32),
                pltpu.VMEM((2, others, WIDE), BF16),
                pltpu.VMEM((count, own, WIDE), BF16),
                pltpu.VMEM((width, count * WIDE), BF16),
                pltpu.VMEM((feats, count * WIDE), BF16),
            ]
            + [pltpu.SemaphoreType.DMA((count,))] * 3,
            compiler_params=params(16 * 2**20),
            cost_estimate=cost(2.5 * rows * width * WIDE * count, 2 * width * WIDE * count),
            name="student_side",
        )(place, logs, unit, feat, scaled, s_exp, weight, before)
        grad_parts.append(far(grad_part))
        return done

    done = unit
    for turn in range(SWEEPS - 1):
        late = t_all if turn == 0 else []
        sums = pl.pallas_call(
            row_kernel,
            in_specs=[VMEM, VMEM, ANY, ANY] + [ANY] * len(late),
            out_specs=VMEM,
            out_shape=struct((parts, 8, LANES), F32),
            scratch_shapes=[pltpu.VMEM((height, LANES), F32), spread, exp_buffer, sems],
            compiler_params=params(exp_bytes),
            cost_estimate=cost(2 * own * local_protos, exp_bytes),
            name="rows",
        )(cols, factor, t_exp, done, *late)
        done = student_piece(sums)
        sums = exchange(sums, "proto")
        cols = pl.pallas_call(
            column_kernel,
            in_specs=[VMEM, VMEM, ANY, ANY],
            out_specs=VMEM,
            out_shape=struct((groups, height, LANES), F32),
            scratch_shapes=[spread, exp_buffer, sems],
            compiler_params=params(exp_bytes),
            cost_estimate=cost(2 * own * local_protos, exp_bytes),
            name="columns",
        )(sums, factor, t_exp, done)
        done = student_piece(cols)
        cols = exchange(cols, "batch")

    sum_rows = -(-(tiles + own // LANES) // 16) * 16
    message_shape = (parts, 2 * share + sum_rows, width)
    prob, col_scale, message = pl.pallas_call(
        functools.partial(last_kernel, groups),
        in_specs=[SMEM] + [VMEM] * 5 + [ANY] * 2 + [VMEM] * (groups - 1) + [ANY],
        out_specs=[ANY, VMEM, VMEM],
        out_shape=[
            pltpu.HBM((chunks, others, WIDE), BF16),
            struct((height, LANES), F32),
            struct(message_shape, BF16),
        ],
        scratch_shapes=[
            pltpu.VMEM((others, width), BF16),
            pltpu.VMEM((others, LANES), F32),
            pltpu.VMEM((others, LANES), F32),
            spread,
            pltpu.VMEM((own, width), F32),
            pltpu.VMEM((2, own, WIDE), BF16),
            pltpu.VMEM((sum_rows, LANES), F32),
            pltpu.VMEM((min(chunks, 3), others, WIDE), BF16),
            exp_buffer,
            w_buffer,
            sems, sems, sems,
        ],
        compiler_params=params(20 * 2**20 + weight_bytes + exp_bytes),
        cost_estimate=cost(2 * rows * width * local_protos, others_bytes),
        name="last_rows",
    )(
        place, logs, cols, factor, student_feats, back_student, t_exp, weight, *t_all, done,
    )
    done = student_piece(message)
    message = exchange(message, "proto")

    grad_rows, loss_part, sums = pl.pallas_call(
        functools.partial(rows_kernel, tiles, float(protos)),
        in_specs=[SMEM] + [VMEM] * 3 + [ANY],
        out_specs=[VMEM] * 3,
        out_shape=[struct((parts, share, width), F32), token, struct((sum_rows, LANES), F32)],
        scratch_shapes=[spread],
        compiler_params=params(0),
        name="row_grads",
    )(place, student_feats, message, logs, done)
    grad_rows = exchange(grad_rows, "proto").reshape(own, width)
    loss = tree_sum(loss_part, "batch")[0, 0] / rows

    grad_weight = pl.pallas_call(
        functools.partial(grad_kernel, counts, float(protos)),
        in_specs=[ANY] * 2 + [VMEM] * 4 + [ANY] * len(counts),
        out_specs=ANY,
        out_shape=struct((feats, local_protos), BF16),
        scratch_shapes=[
            pltpu.VMEM((feats, rows), BF16),
            exp_buffer,
            pltpu.VMEM((chunks, others, WIDE), BF16),
            pltpu.VMEM((feats, local_protos), BF16),
            pltpu.VMEM((feats, local_protos), BF16),
            sems, sems, sems, sems,
        ],
        compiler_params=params(exp_bytes + others_bytes + 4 * feats * local_protos),
        cost_estimate=cost(2 * feats * rows * local_protos, others_bytes),
        name="weight_grads",
    )(t_exp, far(prob), feat, col_scale, sums, factor, *grad_parts)
    return grad_weight, grad_rows, loss


def solution(mesh):
    return jax.shard_map(
        local,
        mesh=mesh,
        in_specs=(P("batch", None), P("batch", None), P(None, "proto")),
        out_specs=(P("batch", "proto"), P("batch", None), P()),
        check_vma=False,
    )
```

```python
import functools
import math

import jax
import jax.numpy as jnp
from jax import lax
from jax.experimental import pallas as pl
from jax.experimental.pallas import tpu as pltpu
from jax.sharding import PartitionSpec as P

SWEEPS = 3
TEMP_TEACHER = 0.04
TEMP_STUDENT = 0.1
LOG2E = math.log2(math.e)
SCALE_TEACHER = LOG2E / TEMP_TEACHER
SCALE_STUDENT = LOG2E / TEMP_STUDENT
LANES = 128
WIDE = 1024
TILE = 256
F32 = jnp.float32
BF16 = jnp.bfloat16


def unit_rows(values):
    wide = values.astype(F32)
    length = jnp.sqrt(jnp.sum(wide * wide, axis=-1, keepdims=True) + 1e-06)
    return wide / length, length


def diagonal():
    shape = (LANES, LANES)
    return lax.broadcasted_iota(jnp.int32, shape, 0) == lax.broadcasted_iota(jnp.int32, shape, 1)


def to_column(row):
    spread = jnp.where(diagonal(), jnp.broadcast_to(row, (LANES, LANES)), 0.0)
    return jnp.sum(spread, axis=1, keepdims=True)


def to_row(column):
    spread = jnp.where(diagonal(), jnp.broadcast_to(column, (LANES, LANES)), 0.0)
    return jnp.sum(spread, axis=0, keepdims=True)


def spread_rows(ref, rows):
    for a in range(rows.shape[0]):
        ref[a * LANES : (a + 1) * LANES, :] = jnp.broadcast_to(
            to_column(rows[a : a + 1, :]), (LANES, LANES)
        )


def pack_rows(ref, columns):
    for a in range(columns.shape[0] // LANES):
        ref[a : a + 1, :] = to_row(columns[a * LANES : (a + 1) * LANES, :])


def lane_tiles(values):
    return [values[:, t * LANES : (t + 1) * LANES] for t in range(values.shape[1] // LANES)]


def fold(values):
    return functools.reduce(jnp.add, lane_tiles(values))


def column_sums(values):
    rows, cols = values.shape
    return jnp.sum(values.reshape(rows // 8, 8, cols), axis=0)


def nt_dot(a, b):
    return lax.dot_general(a, b, (((1,), (1,)), ((), ())), preferred_element_type=F32)


def add_up(values):
    return functools.reduce(jnp.add, values)


def repeat(out_ref):
    for p in range(1, out_ref.shape[0]):
        out_ref[p] = out_ref[0]


def chunk(k):
    return slice(k * WIDE, (k + 1) * WIDE)


def copies(source, target, sems, first=0, back=0, count=None):
    def chunks(ref):
        return ref.shape[0] if len(ref.shape) == 3 else ref.shape[1] // WIDE

    count = count or min(chunks(source), chunks(target))
    return [copy_of(source, target, sems, k, first, back) for k in range(count)]


def columns_of(k, first=0, count=WIDE):
    return pl.ds(pl.multiple_of(k * WIDE + first, LANES), count)


def copy_of(source, target, sems, k, first=0, back=0):
    def part(ref, k):
        return ref.at[k] if len(ref.shape) == 3 else ref.at[:, columns_of(k)]

    return pltpu.make_async_copy(part(source, first + k), part(target, back + k), sems.at[k])


def start(*lists):
    for each in zip(*lists):
        for copy in each:
            copy.start()


def wait(*lists):
    for each in lists:
        for copy in each:
            copy.wait()


def stats_kernel(
    t_hbm, s_hbm, w_hbm, t_out, s_out, t_unit, out_ref, back_ref,
    raw, w_ref, unit, exps, logits, top, total, raw_sem, w_sem, t_sem, s_sem,
):
    own = raw.shape[1]
    quarter = out_ref.shape[1] // 4
    chunks = exps.shape[1]
    halves = (slice(0, own), slice(own, 2 * own))
    loads = copies(w_hbm, w_ref, w_sem)
    raw_loads = [
        pltpu.make_async_copy(ref, raw.at[which], raw_sem.at[which])
        for which, ref in enumerate((t_hbm, s_hbm))
    ]
    start(raw_loads, loads[:2])
    start(loads[2:])
    top[...] = jnp.full(top.shape, -1e30, F32)
    total[...] = jnp.zeros(total.shape, F32)
    back_ref[...] = jnp.zeros(back_ref.shape, F32)
    wait(raw_loads)
    for which in range(2):
        unit[halves[which], :] = unit_rows(raw[which])[0].astype(BF16)
    t_unit[...] = unit[halves[0], :]

    @pl.loop(0, chunks)
    def _(k):
        copy_of(w_hbm, w_ref, w_sem, k).wait()
        for n in range(0, WIDE, TILE):
            here = columns_of(k, n, TILE)
            values = jnp.dot(unit[...], w_ref[:, here], preferred_element_type=F32)
            for half, scale in zip(halves, (SCALE_TEACHER, SCALE_STUDENT)):
                part = values[half, :] * scale
                logits[half, here] = part
                top[half, :] = functools.reduce(jnp.maximum, lane_tiles(part), top[half, :])

    peak = jnp.max(top[...], axis=1, keepdims=True)
    top[...] = jnp.broadcast_to(peak, top.shape)

    @pl.loop(0, chunks)
    def _(k):
        for which, (half, out, sem) in enumerate(zip(halves, (t_out, s_out), (t_sem, s_sem))):
            shift = top[half, :]
            for n in range(0, WIDE, TILE):
                tiles = lane_tiles(logits[half, columns_of(k, n, TILE)])
                tiles = [jnp.exp2(tile - shift) for tile in tiles]
                for t, tile in enumerate(tiles):
                    lanes = slice(n + t * LANES, n + (t + 1) * LANES)
                    exps[which, k, :, lanes] = tile.astype(BF16)
                total[half, :] += add_up(tiles)
            copy_of(exps.at[which], out, sem, k).start()
        back_ref[...] += nt_dot(exps[1, k], w_ref[:, columns_of(k)])

    sums = jnp.sum(total[...], axis=1, keepdims=True)
    for which, half in enumerate(halves):
        for k, column in enumerate((peak, sums)):
            first = (2 * which + k) * quarter
            pack_rows(out_ref.at[0, first : first + quarter], column[half, :])
    repeat(out_ref)
    wait(copies(exps.at[0], t_out, t_sem), copies(exps.at[1], s_out, s_sem))


def merged(stats_ref, which):
    parts, height, _ = stats_ref.shape
    quarter = height // 4
    first = 2 * which * quarter
    tops = [stats_ref[p, first : first + quarter, :] for p in range(parts)]
    top = functools.reduce(jnp.maximum, tops)
    sums = [
        stats_ref[p, first + quarter : first + 2 * quarter, :] * jnp.exp2(tops[p] - top)
        for p in range(parts)
    ]
    return top + jnp.log2(add_up(sums))


def column_pass(exp_hbm, exp_ref, sem, weight, out_ref):
    height = WIDE // LANES

    @pl.loop(0, exp_ref.shape[0])
    def _(k):
        copy_of(exp_hbm, exp_ref, sem, k).wait()
        sums = jnp.zeros((8, WIDE), F32)
        for g in range(0, exp_ref.shape[1], 16):
            shift = weight[g : g + 16, :]
            tiles = lane_tiles(exp_ref[k, g : g + 16, :].astype(F32))
            sums = sums + column_sums(jnp.concatenate([tile * shift for tile in tiles], axis=1))
        sums = jnp.sum(sums, axis=0, keepdims=True)
        block = jnp.concatenate(lane_tiles(sums), axis=0)
        for g in range(out_ref.shape[0]):
            out_ref[g, pl.ds(pl.multiple_of(k * height, height), height), :] = block


def first_column_kernel(place_ref, stats_ref, exp_hbm, *refs):
    factor_ref, out_ref, weight, exp_ref, sem = refs[-5:]
    start(copies(exp_hbm, exp_ref, sem))
    quarter = stats_ref.shape[1] // 4
    height = out_ref.shape[1] - 8
    own = stats_ref[pl.ds(place_ref[1], 1)][0]
    factor_ref[...] = jnp.zeros(factor_ref.shape, F32)
    rows = []
    for which in range(2):
        log_sum = merged(stats_ref, which)
        here = slice(which * quarter, (which + 1) * quarter)
        factor_ref[here, :] = jnp.exp2(
            own[2 * which * quarter : (2 * which + 1) * quarter, :] - log_sum
        )
        rows.append(log_sum)
    rows.append(jnp.zeros((8 - 2 * quarter, LANES), F32))
    logs = jnp.concatenate(rows, axis=0)
    for g in range(out_ref.shape[0]):
        out_ref[g, height:, :] = logs
    spread_rows(weight, factor_ref[:quarter, :])
    column_pass(exp_hbm, exp_ref, sem, weight, out_ref)


def column_kernel(sums_ref, factor_ref, exp_hbm, *refs):
    out_ref, weight, exp_ref, sem = refs[-4:]
    start(copies(exp_hbm, exp_ref, sem))
    quarter = weight.shape[0] // LANES
    scale = 1.0 / add_up([sums_ref[p, :quarter, :] for p in range(sums_ref.shape[0])])
    spread_rows(weight, scale * factor_ref[:quarter, :])
    column_pass(exp_hbm, exp_ref, sem, weight, out_ref)


def column_scales(cols_ref, height):
    return 1.0 / add_up([cols_ref[g, :height, :] for g in range(cols_ref.shape[0])])


def chunk_scales(scales, k):
    height = WIDE // LANES
    return scales[pl.ds(pl.multiple_of(k * height, height), height), :]


def add_row_sums(rows, values, scale):
    for g in range(0, values.shape[0], 32):
        total = rows[g : g + 32, :]
        for t, tile in enumerate(lane_tiles(values[g : g + 32, :].astype(F32))):
            total = total + tile * scale[t : t + 1, :]
        rows[g : g + 32, :] = total


def row_kernel(cols_ref, factor_ref, exp_hbm, *refs):
    out_ref, scales, rows, exp_ref, sem = refs[-5:]
    start(copies(exp_hbm, exp_ref, sem))
    scales[...] = column_scales(cols_ref, scales.shape[0])
    rows[...] = jnp.zeros(rows.shape, F32)
    quarter = rows.shape[0] // LANES
    out_ref[0] = jnp.zeros(out_ref.shape[1:], F32)

    @pl.loop(0, exp_ref.shape[0])
    def _(k):
        copy_of(exp_hbm, exp_ref, sem, k).wait()
        add_row_sums(rows, exp_ref.at[k], chunk_scales(scales, k))

    pack_rows(out_ref.at[0, :quarter], jnp.sum(rows[...], axis=1, keepdims=True))
    out_ref[0, :quarter, :] = out_ref[0, :quarter, :] * factor_ref[:quarter, :]
    repeat(out_ref)


def relative(place_ref, g, groups):
    return pl.ds(lax.rem(place_ref[0] + g, groups), 1)


def relative_logs(place_ref, logs_ref, lse, which, shift=0.0):
    groups = logs_ref.shape[0]
    own = lse.shape[0] // (groups - 1)
    quarter = own // LANES
    height = logs_ref.shape[1] - 8
    for g in range(1, groups):
        there = logs_ref[relative(place_ref, g, groups)][0]
        first = height + which * quarter
        spread_rows(lse.at[(g - 1) * own : g * own], there[first : first + quarter, :] - shift)


def student_rows_kernel(protos, place_ref, factor_ref, own_ref, *refs):
    unit_ref, feat_ref, scaled_ref, turned = refs[-4:]
    own = own_ref.shape[0]
    groups = turned.shape[1] // own
    raw = refs[: groups - 1]
    quarter, feats = own // LANES, feat_ref.shape[0]
    for g in range(groups):
        half = unit_rows((raw[g - 1] if g else own_ref)[...])[0].astype(BF16)
        if g:
            unit_ref[(g - 1) * own : g * own, :] = half
        half = half.astype(F32)
        for a in range(0, own, LANES):
            first = g * own + a
            turned[:, first : first + LANES] = jnp.transpose(half[a : a + LANES, :]).astype(BF16)
    feat = turned[pl.ds(pl.multiple_of(place_ref[0] * feats, feats), feats), :]
    feat_ref[...] = feat
    for a in range(quarter):
        lanes = slice(a * LANES, (a + 1) * LANES)
        factor = factor_ref[quarter + a : quarter + a + 1, :] * protos
        scaled_ref[:, lanes] = (feat[:, lanes].astype(F32) * factor).astype(BF16)


def probabilities(unit, w_ref, k, lse, scale, use):
    for n in range(0, WIDE, TILE):
        logits = jnp.dot(
            unit[...], w_ref[:, columns_of(k, n, TILE)], preferred_element_type=F32
        )
        shift = lse[...]
        use(n, [jnp.exp2(tile * scale - shift) for tile in lane_tiles(logits)])


def student_kernel(
    log_protos, first, place_ref, logs_ref, unit, feat_ref, scaled_ref, exp_hbm, w_hbm, *refs
):
    grad_hbm, token_ref, lse, prob, exp_ref, w_ref, grad, exp_sem, w_sem, grad_sem = refs[-10:]
    own, count = exp_ref.shape[1], exp_ref.shape[0]
    exp_loads = copies(exp_hbm, exp_ref, exp_sem, first, 0, count)
    w_loads = copies(w_hbm, w_ref, w_sem, first, 0, count)
    start(w_loads, exp_loads)
    token_ref[...] = jnp.zeros(token_ref.shape, F32)
    relative_logs(place_ref, logs_ref, lse, 1, log_protos)

    @pl.loop(0, count)
    def _(k):
        copy_of(w_hbm, w_ref, w_sem, k, first).wait()

        def use(n, tiles):
            for t, tile in enumerate(tiles):
                prob[:, n + t * LANES : n + (t + 1) * LANES] = tile.astype(BF16)

        probabilities(unit, w_ref, k, lse, SCALE_STUDENT, use)
        copy_of(exp_hbm, exp_ref, exp_sem, k, first).wait()
        values = jnp.dot(scaled_ref[...], exp_ref[k], preferred_element_type=F32)
        values = values + jnp.dot(feat_ref[:, own:], prob[...], preferred_element_type=F32)
        grad[:, columns_of(k)] = values.astype(BF16)
        copy_of(grad, grad_hbm, grad_sem, k).start()

    wait(copies(grad, grad_hbm, grad_sem))


def as_three(value):
    high = value.astype(BF16)
    rest = value - high.astype(F32)
    middle = rest.astype(BF16)
    return high, middle, (rest - middle.astype(F32)).astype(BF16)


def last_kernel(groups, place_ref, logs_ref, cols_ref, factor_ref, own_ref, student_ref, exp_hbm, w_hbm, *refs):
    units = refs[: groups - 1]
    (
        prob_hbm, scale_ref, out_ref, unit, lse, rows, own_rows, back, scaled, sums, prob_ref,
        exp_ref, w_ref, prob_sem, exp_sem, w_sem,
    ) = refs[-16:]
    w_loads, exp_loads = copies(w_hbm, w_ref, w_sem), copies(exp_hbm, exp_ref, exp_sem)
    start(w_loads, exp_loads)
    slots, others, _ = prob_ref.shape
    own, chunks = exp_ref.shape[1], exp_ref.shape[0]
    tiles = (own + others) // LANES
    quarter = own // LANES
    scale_ref[...] = column_scales(cols_ref, scale_ref.shape[0])
    rows[...] = jnp.zeros(rows.shape, F32)
    own_rows[...] = jnp.zeros(own_rows.shape, F32)
    back[...] = jnp.zeros(back.shape, F32)
    relative_logs(place_ref, logs_ref, lse, 0)
    for g in range(groups - 1):
        unit[g * own : (g + 1) * own, :] = units[g][...]
    partner = slice((groups // 2 - 1) * own, groups // 2 * own)

    def store(k):
        return pltpu.make_async_copy(prob_ref.at[lax.rem(k, slots)], prob_hbm.at[k], prob_sem.at[k])

    @pl.loop(0, chunks)
    def _(k):
        copy_of(w_hbm, w_ref, w_sem, k).wait()
        slot = lax.rem(k, slots)
        scale = chunk_scales(scale_ref, k)

        @pl.when(k >= slots)
        def _():
            store(k - slots).wait()

        def use(n, tiles):
            for t, tile in enumerate(tiles):
                prob_ref[slot, :, n + t * LANES : n + (t + 1) * LANES] = tile.astype(BF16)
            first = n // LANES
            tiles = [tile * scale[first + t : first + t + 1, :] for t, tile in enumerate(tiles)]
            rows[...] += add_up(tiles)
            for t, tile in enumerate(tiles):
                scaled[:, n + t * LANES : n + (t + 1) * LANES] = tile[partner, :].astype(BF16)

        probabilities(unit, w_ref, k, lse, SCALE_TEACHER, use)
        store(k).start()
        back[...] += nt_dot(scaled[...], w_ref[:, columns_of(k)])
        copy_of(exp_hbm, exp_ref, exp_sem, k).wait()
        add_row_sums(own_rows, exp_ref.at[k], scale)

    sums[...] = jnp.zeros(sums.shape, F32)
    pack_rows(sums.at[:quarter], jnp.sum(own_rows[...], axis=1, keepdims=True))
    sums[:quarter, :] = sums[:quarter, :] * factor_ref[:quarter, :]
    pack_rows(sums.at[quarter:tiles], jnp.sum(rows[...], axis=1, keepdims=True))
    half = unit_rows(own_ref[...])[0].astype(BF16).astype(F32)
    inner = jnp.sum(half * back[...], axis=1, keepdims=True)
    pack_rows(sums.at[tiles : tiles + quarter], inner)
    parts = out_ref.shape[0]
    share = own // parts
    protos = 1.0 * out_ref.shape[0] * w_ref.shape[1]
    student = []
    for a in range(quarter):
        factor = to_column(factor_ref[quarter + a : quarter + a + 1, :] * protos)
        student.append(student_ref[a * LANES : (a + 1) * LANES, :] * factor)
    student = jnp.concatenate(student, axis=0).astype(BF16)
    terms = list(as_three(sums[...]))
    terms.append(jnp.zeros((sums.shape[0], out_ref.shape[2] - 3 * LANES), BF16))
    terms = jnp.concatenate(terms, axis=1)
    for p in range(parts):
        here = slice(p * share, (p + 1) * share)
        out_ref[p] = jnp.concatenate(
            [student[here, :], back[here, :].astype(BF16), terms], axis=0
        )
    for k in range(max(0, chunks - slots), chunks):
        store(k).wait()


def total_sums(message_ref, first):
    parts = message_ref.shape[0]
    each = [
        add_up([t.astype(F32) for t in lane_tiles(message_ref[p, first:, : 3 * LANES])[::-1]])
        for p in range(parts)
    ]
    return add_up(each)


def rows_kernel(tiles, protos, place_ref, s_ref, message_ref, logs_ref, *refs):
    out_ref, loss_ref, sums_ref, weight = refs[-4:]
    parts = message_ref.shape[0]
    share, own = out_ref.shape[1], weight.shape[0]
    quarter = own // LANES
    first = tiles // 2
    totals = total_sums(message_ref, 2 * share)
    sums_ref[...] = totals
    scale = 1.0 / totals[first : first + quarter, :]
    spread_rows(weight, scale)
    mine = pl.ds(pl.multiple_of(place_ref[1] * share, share), share)
    total = add_up([message_ref[p, :share, :].astype(F32) for p in range(parts)])
    paired = add_up([message_ref[p, share : 2 * share, :].astype(F32) for p in range(parts)])
    total = total - paired * (weight[mine, :1] * protos)
    unit, length = unit_rows(s_ref[mine, :])
    out_ref[0] = (total - unit * jnp.sum(unit * total, axis=-1, keepdims=True)) / length
    repeat(out_ref)
    height = logs_ref.shape[1] - 8
    logs = logs_ref[pl.ds(place_ref[0], 1)][0][height + quarter : height + 2 * quarter, :]
    terms = logs / LOG2E - totals[tiles : tiles + quarter, :] * scale / TEMP_STUDENT
    loss_ref[...] = jnp.broadcast_to(jnp.sum(terms), loss_ref.shape)


def grad_kernel(counts, protos, exp_hbm, prob_hbm, feat_ref, scale_ref, sums_ref, factor_ref, *refs):
    parts = refs[: len(counts)]
    out_hbm, scaled, exp_ref, prob_ref, part_ref, out, exp_sem, prob_sem, part_sem, sem = refs[-10:]
    exp_loads = copies(exp_hbm, exp_ref, exp_sem)
    prob_loads = copies(prob_hbm, prob_ref, prob_sem)
    part_loads, first = [], 0
    for count, part in zip(counts, parts):
        part_loads += copies(part, part_ref, part_sem.at[first : first + count], 0, first)
        first += count
    start(exp_loads, prob_loads, part_loads)
    own = exp_ref.shape[1]
    tiles = (own + prob_ref.shape[1]) // LANES
    rows = protos / sums_ref[:tiles, :]
    for a in range(tiles):
        other = (a + tiles // 2) % tiles
        feat = feat_ref[:, other * LANES : (other + 1) * LANES].astype(F32)
        row = rows[a : a + 1, :]
        if a < own // LANES:
            row = row * factor_ref[a : a + 1, :]
        scaled[:, a * LANES : (a + 1) * LANES] = (feat * row).astype(BF16)
    stores = copies(out, out_hbm, sem)
    for k, store in enumerate(stores):
        exp_loads[k].wait()
        prob_loads[k].wait()
        paired = jnp.dot(scaled[:, :own], exp_ref[k], preferred_element_type=F32)
        paired = paired + jnp.dot(
            scaled[:, own:], prob_ref[k], preferred_element_type=F32
        )
        part_loads[k].wait()
        for t, tile in enumerate(lane_tiles(paired)):
            lanes = slice(k * WIDE + t * LANES, k * WIDE + (t + 1) * LANES)
            scale = scale_ref[lanes.start // LANES : lanes.stop // LANES, :]
            out[:, lanes] = (part_ref[:, lanes].astype(F32) - tile * scale).astype(BF16)
        store.start()
    for store in stores:
        store.wait()


SMEM = pl.BlockSpec(memory_space=pltpu.SMEM)
VMEM = pl.BlockSpec(memory_space=pltpu.VMEM)
ANY = pl.BlockSpec(memory_space=pl.ANY)


def params(nbytes):
    return pltpu.CompilerParams(vmem_limit_bytes=int(nbytes) + 8 * 2**20)


def cost(flops, nbytes, exps=0):
    return pl.CostEstimate(flops=int(flops), bytes_accessed=int(nbytes), transcendentals=int(exps))


def exchange(value, axis):
    return lax.all_to_all(value, axis, 0, 0)


def following(value, axis):
    n = lax.axis_size(axis)
    return [lax.ppermute(value, axis, [(i, (i - s) % n) for i in range(n)]) for s in range(1, n)]


def tree_sum(value, axis):
    n = lax.axis_size(axis)
    values = [value] + [
        lax.ppermute(value, axis, [(i, i ^ s) for i in range(n)]) for s in range(1, n)
    ]
    while len(values) > 1:
        values = [a + b for a, b in zip(values[::2], values[1::2])]
    return values[0]


def local(teacher_feats, student_feats, proto_weight):
    parts, groups = lax.axis_size("proto"), lax.axis_size("batch")
    own, width = teacher_feats.shape
    local_protos = proto_weight.shape[1]
    rows = own * groups
    others = rows - own
    protos = local_protos * parts
    feats = width // groups
    share = own // parts
    tiles = rows // LANES
    height = local_protos // LANES
    chunks = local_protos // WIDE
    place = jnp.stack([lax.axis_index("batch"), lax.axis_index("proto")]).astype(jnp.int32)
    struct = jax.ShapeDtypeStruct
    weight_bytes = 2 * width * local_protos
    exp_bytes = 2 * own * local_protos
    others_bytes = 2 * others * local_protos
    spread = pltpu.VMEM((own, LANES), F32)
    w_buffer = pltpu.VMEM((width, local_protos), BF16)
    exp_buffer = pltpu.VMEM((chunks, own, WIDE), BF16)
    sems = pltpu.SemaphoreType.DMA((chunks,))
    log_protos = math.log2(protos)
    token = struct((8, LANES), F32)

    def far(value):
        return pltpu.with_memory_space_constraint(value, pltpu.HBM)

    weight = far(proto_weight)
    s_all = following(student_feats, "batch")

    exps = pltpu.HBM((chunks, own, WIDE), BF16)
    t_exp, s_exp, t_unit, stats, back_student = pl.pallas_call(
        stats_kernel,
        in_specs=[ANY] * 3,
        out_specs=[ANY, ANY, VMEM, VMEM, VMEM],
        out_shape=[
            exps,
            exps,
            struct((own, width), BF16),
            struct((parts, 4 * own // LANES, LANES), F32),
            struct((own, width), F32),
        ],
        scratch_shapes=[
            pltpu.VMEM((2, own, width), BF16),
            w_buffer,
            pltpu.VMEM((2 * own, width), BF16),
            pltpu.VMEM((2, chunks, own, WIDE), BF16),
            pltpu.VMEM((2 * own, local_protos), F32),
            pltpu.VMEM((2 * own, LANES), F32),
            pltpu.VMEM((2 * own, LANES), F32),
            pltpu.SemaphoreType.DMA((2,)),
            sems, sems, sems,
        ],
        compiler_params=params(weight_bytes + 6 * exp_bytes),
        cost_estimate=cost(4 * own * width * local_protos, weight_bytes),
        name="own_rows",
    )(far(teacher_feats), far(student_feats), weight)
    t_exp, s_exp = far(t_exp), far(s_exp)
    t_all = following(t_unit, "batch")

    stats = exchange(stats, "proto")

    first_shape = (groups, height + 8, LANES)
    factor, cols = pl.pallas_call(
        first_column_kernel,
        in_specs=[SMEM, VMEM, ANY] + [ANY] * (groups - 1),
        out_specs=[VMEM, VMEM],
        out_shape=[token, struct(first_shape, F32)],
        scratch_shapes=[spread, exp_buffer, sems],
        compiler_params=params(exp_bytes),
        cost_estimate=cost(2 * own * local_protos, exp_bytes),
        name="first_columns",
    )(place, stats, t_exp, *s_all)

    unit, feat, scaled = pl.pallas_call(
        functools.partial(student_rows_kernel, float(protos)),
        in_specs=[SMEM, VMEM, VMEM] + [VMEM] * (groups - 1) + [ANY],
        out_specs=[VMEM] * 3,
        out_shape=[
            struct((others, width), BF16), struct((feats, rows), BF16), struct((feats, own), BF16),
        ],
        scratch_shapes=[pltpu.VMEM((width, rows), BF16)],
        compiler_params=params(2 * rows * width),
        cost_estimate=cost(8 * rows * width, 2 * rows * width),
        name="student_rows",
    )(place, factor, student_feats, *s_all, cols)
    cols = exchange(cols, "batch")
    logs = cols

    counts = [c * chunks // 8 for c in (1, 1, 1, 1, 4)]
    grad_parts = []

    def student_piece(before):
        turn = len(grad_parts)
        first, count = sum(counts[:turn]), counts[turn]
        grad_part, done = pl.pallas_call(
            functools.partial(student_kernel, log_protos, first),
            in_specs=[SMEM] + [VMEM] * 4 + [ANY] * 3,
            out_specs=[ANY, VMEM],
            out_shape=[pltpu.HBM((feats, count * WIDE), BF16), token],
            scratch_shapes=[
                pltpu.VMEM((others, LANES), F32),
                pltpu.VMEM((others, WIDE), BF16),
                pltpu.VMEM((count, own, WIDE), BF16),
                pltpu.VMEM((width, count * WIDE), BF16),
                pltpu.VMEM((feats, count * WIDE), BF16),
            ]
            + [pltpu.SemaphoreType.DMA((count,))] * 3,
            compiler_params=params(16 * 2**20),
            cost_estimate=cost(2.5 * rows * width * WIDE * count, 2 * width * WIDE * count),
            name="student_side",
        )(place, logs, unit, feat, scaled, s_exp, weight, before)
        grad_parts.append(far(grad_part))
        return done

    done = unit
    for turn in range(SWEEPS - 1):
        late = t_all if turn == 0 else []
        sums = pl.pallas_call(
            row_kernel,
            in_specs=[VMEM, VMEM, ANY, ANY],
            out_specs=VMEM,
            out_shape=struct((parts, 8, LANES), F32),
            scratch_shapes=[pltpu.VMEM((height, LANES), F32), spread, exp_buffer, sems],
            compiler_params=params(exp_bytes),
            cost_estimate=cost(2 * own * local_protos, exp_bytes),
            name="rows",
        )(cols, factor, t_exp, done)
        done = student_piece(sums)
        sums = exchange(sums, "proto")
        cols = pl.pallas_call(
            column_kernel,
            in_specs=[VMEM, VMEM, ANY, ANY] + [ANY] * len(late),
            out_specs=VMEM,
            out_shape=struct((groups, height, LANES), F32),
            scratch_shapes=[spread, exp_buffer, sems],
            compiler_params=params(exp_bytes),
            cost_estimate=cost(2 * own * local_protos, exp_bytes),
            name="columns",
        )(sums, factor, t_exp, done, *late)
        done = student_piece(cols)
        cols = exchange(cols, "batch")

    sum_rows = -(-(tiles + own // LANES) // 16) * 16
    message_shape = (parts, 2 * share + sum_rows, width)
    prob, col_scale, message = pl.pallas_call(
        functools.partial(last_kernel, groups),
        in_specs=[SMEM] + [VMEM] * 5 + [ANY] * 2 + [VMEM] * (groups - 1) + [ANY],
        out_specs=[ANY, VMEM, VMEM],
        out_shape=[
            pltpu.HBM((chunks, others, WIDE), BF16),
            struct((height, LANES), F32),
            struct(message_shape, BF16),
        ],
        scratch_shapes=[
            pltpu.VMEM((others, width), BF16),
            pltpu.VMEM((others, LANES), F32),
            pltpu.VMEM((others, LANES), F32),
            spread,
            pltpu.VMEM((own, width), F32),
            pltpu.VMEM((own, WIDE), BF16),
            pltpu.VMEM((sum_rows, LANES), F32),
            pltpu.VMEM((min(chunks, 3), others, WIDE), BF16),
            exp_buffer,
            w_buffer,
            sems, sems, sems,
        ],
        compiler_params=params(20 * 2**20 + weight_bytes + exp_bytes),
        cost_estimate=cost(2 * rows * width * local_protos, others_bytes),
        name="last_rows",
    )(
        place, logs, cols, factor, student_feats, back_student, t_exp, weight, *t_all, done,
    )
    done = student_piece(message)
    message = exchange(message, "proto")

    grad_rows, loss_part, sums = pl.pallas_call(
        functools.partial(rows_kernel, tiles, float(protos)),
        in_specs=[SMEM] + [VMEM] * 3 + [ANY],
        out_specs=[VMEM] * 3,
        out_shape=[struct((parts, share, width), F32), token, struct((sum_rows, LANES), F32)],
        scratch_shapes=[spread],
        compiler_params=params(0),
        name="row_grads",
    )(place, student_feats, message, logs, done)
    grad_rows = exchange(grad_rows, "proto").reshape(own, width)
    loss = tree_sum(loss_part, "batch")[0, 0] / rows

    grad_weight = pl.pallas_call(
        functools.partial(grad_kernel, counts, float(protos)),
        in_specs=[ANY] * 2 + [VMEM] * 4 + [ANY] * len(counts),
        out_specs=ANY,
        out_shape=struct((feats, local_protos), BF16),
        scratch_shapes=[
            pltpu.VMEM((feats, rows), BF16),
            exp_buffer,
            pltpu.VMEM((chunks, others, WIDE), BF16),
            pltpu.VMEM((feats, local_protos), BF16),
            pltpu.VMEM((feats, local_protos), BF16),
            sems, sems, sems, sems,
        ],
        compiler_params=params(exp_bytes + others_bytes + 4 * feats * local_protos),
        cost_estimate=cost(2 * feats * rows * local_protos, others_bytes),
        name="weight_grads",
    )(t_exp, far(prob), feat, col_scale, sums, factor, *grad_parts)
    return grad_weight, grad_rows, loss


def solution(mesh):
    return jax.shard_map(
        local,
        mesh=mesh,
        in_specs=(P("batch", None), P("batch", None), P(None, "proto")),
        out_specs=(P("batch", "proto"), P("batch", None), P()),
        check_vma=False,
    )
```

```python
import functools
import math

import jax
import jax.numpy as jnp
from jax import lax
from jax.experimental import pallas as pl
from jax.experimental.pallas import tpu as pltpu
from jax.sharding import PartitionSpec as P

SWEEPS = 3
TEMP_TEACHER = 0.04
TEMP_STUDENT = 0.1
LOG2E = math.log2(math.e)
SCALE_TEACHER = LOG2E / TEMP_TEACHER
SCALE_STUDENT = LOG2E / TEMP_STUDENT
LANES = 128
WIDE = 1024
TILE = 256
F32 = jnp.float32
BF16 = jnp.bfloat16


def unit_rows(values):
    wide = values.astype(F32)
    length = jnp.sqrt(jnp.sum(wide * wide, axis=-1, keepdims=True) + 1e-06)
    return wide / length, length


def diagonal():
    shape = (LANES, LANES)
    return lax.broadcasted_iota(jnp.int32, shape, 0) == lax.broadcasted_iota(jnp.int32, shape, 1)


def to_column(row):
    spread = jnp.where(diagonal(), jnp.broadcast_to(row, (LANES, LANES)), 0.0)
    return jnp.sum(spread, axis=1, keepdims=True)


def to_row(column):
    spread = jnp.where(diagonal(), jnp.broadcast_to(column, (LANES, LANES)), 0.0)
    return jnp.sum(spread, axis=0, keepdims=True)


def spread_rows(ref, rows):
    for a in range(rows.shape[0]):
        ref[a * LANES : (a + 1) * LANES, :] = jnp.broadcast_to(
            to_column(rows[a : a + 1, :]), (LANES, LANES)
        )


def pack_rows(ref, columns):
    for a in range(columns.shape[0] // LANES):
        ref[a : a + 1, :] = to_row(columns[a * LANES : (a + 1) * LANES, :])


def lane_tiles(values):
    return [values[:, t * LANES : (t + 1) * LANES] for t in range(values.shape[1] // LANES)]


def fold(values):
    return functools.reduce(jnp.add, lane_tiles(values))


def column_sums(values):
    rows, cols = values.shape
    return jnp.sum(values.reshape(rows // 8, 8, cols), axis=0)


def nt_dot(a, b):
    return lax.dot_general(a, b, (((1,), (1,)), ((), ())), preferred_element_type=F32)


def add_up(values):
    return functools.reduce(jnp.add, values)


def repeat(out_ref):
    for p in range(1, out_ref.shape[0]):
        out_ref[p] = out_ref[0]


def chunk(k):
    return slice(k * WIDE, (k + 1) * WIDE)


def copies(source, target, sems, first=0, back=0, count=None):
    def chunks(ref):
        return ref.shape[0] if len(ref.shape) == 3 else ref.shape[1] // WIDE

    count = count or min(chunks(source), chunks(target))
    return [copy_of(source, target, sems, k, first, back) for k in range(count)]


def columns_of(k, first=0, count=WIDE):
    return pl.ds(pl.multiple_of(k * WIDE + first, LANES), count)


def copy_of(source, target, sems, k, first=0, back=0):
    def part(ref, k):
        return ref.at[k] if len(ref.shape) == 3 else ref.at[:, columns_of(k)]

    return pltpu.make_async_copy(part(source, first + k), part(target, back + k), sems.at[k])


def start(*lists):
    for each in zip(*lists):
        for copy in each:
            copy.start()


def wait(*lists):
    for each in lists:
        for copy in each:
            copy.wait()


def stats_kernel(
    t_hbm, s_hbm, w_hbm, t_out, s_out, out_ref,
    raw, w_ref, unit, exps, logits, top, total, raw_sem, w_sem, t_sem, s_sem,
):
    own = raw.shape[1]
    quarter = out_ref.shape[1] // 4
    chunks = exps.shape[1]
    halves = (slice(0, own), slice(own, 2 * own))
    loads = copies(w_hbm, w_ref, w_sem)
    raw_loads = [
        pltpu.make_async_copy(ref, raw.at[which], raw_sem.at[which])
        for which, ref in enumerate((t_hbm, s_hbm))
    ]
    start(raw_loads, loads[:2])
    start(loads[2:])
    top[...] = jnp.full(top.shape, -1e30, F32)
    total[...] = jnp.zeros(total.shape, F32)
    wait(raw_loads)
    for which in range(2):
        unit[halves[which], :] = unit_rows(raw[which])[0].astype(BF16)

    @pl.loop(0, chunks)
    def _(k):
        copy_of(w_hbm, w_ref, w_sem, k).wait()
        for n in range(0, WIDE, TILE):
            here = columns_of(k, n, TILE)
            values = jnp.dot(unit[...], w_ref[:, here], preferred_element_type=F32)
            for half, scale in zip(halves, (SCALE_TEACHER, SCALE_STUDENT)):
                part = values[half, :] * scale
                logits[half, here] = part
                top[half, :] = functools.reduce(jnp.maximum, lane_tiles(part), top[half, :])

    peak = jnp.max(top[...], axis=1, keepdims=True)
    top[...] = jnp.broadcast_to(peak, top.shape)

    @pl.loop(0, chunks)
    def _(k):
        for which, (half, out, sem) in enumerate(zip(halves, (t_out, s_out), (t_sem, s_sem))):
            shift = top[half, :]
            for n in range(0, WIDE, TILE):
                tiles = lane_tiles(logits[half, columns_of(k, n, TILE)])
                tiles = [jnp.exp2(tile - shift) for tile in tiles]
                for t, tile in enumerate(tiles):
                    lanes = slice(n + t * LANES, n + (t + 1) * LANES)
                    exps[which, k, :, lanes] = tile.astype(BF16)
                total[half, :] += add_up(tiles)
            copy_of(exps.at[which], out, sem, k).start()

    sums = jnp.sum(total[...], axis=1, keepdims=True)
    for which, half in enumerate(halves):
        for k, column in enumerate((peak, sums)):
            first = (2 * which + k) * quarter
            pack_rows(out_ref.at[0, first : first + quarter], column[half, :])
    repeat(out_ref)
    wait(copies(exps.at[0], t_out, t_sem), copies(exps.at[1], s_out, s_sem))


def merged(stats_ref, which):
    parts, height, _ = stats_ref.shape
    quarter = height // 4
    first = 2 * which * quarter
    tops = [stats_ref[p, first : first + quarter, :] for p in range(parts)]
    top = functools.reduce(jnp.maximum, tops)
    sums = [
        stats_ref[p, first + quarter : first + 2 * quarter, :] * jnp.exp2(tops[p] - top)
        for p in range(parts)
    ]
    return top + jnp.log2(add_up(sums))


def column_pass(exp_hbm, exp_ref, sem, weight, out_ref):
    height = WIDE // LANES

    @pl.loop(0, exp_ref.shape[0])
    def _(k):
        copy_of(exp_hbm, exp_ref, sem, k).wait()
        sums = jnp.zeros((8, WIDE), F32)
        for g in range(0, exp_ref.shape[1], 16):
            shift = weight[g : g + 16, :]
            tiles = lane_tiles(exp_ref[k, g : g + 16, :].astype(F32))
            sums = sums + column_sums(jnp.concatenate([tile * shift for tile in tiles], axis=1))
        sums = jnp.sum(sums, axis=0, keepdims=True)
        block = jnp.concatenate(lane_tiles(sums), axis=0)
        for g in range(out_ref.shape[0]):
            out_ref[g, pl.ds(pl.multiple_of(k * height, height), height), :] = block


def first_column_kernel(place_ref, stats_ref, exp_hbm, *refs):
    factor_ref, out_ref, weight, exp_ref, sem = refs[-5:]
    start(copies(exp_hbm, exp_ref, sem))
    quarter = stats_ref.shape[1] // 4
    height = out_ref.shape[1] - 8
    own = stats_ref[pl.ds(place_ref[1], 1)][0]
    factor_ref[...] = jnp.zeros(factor_ref.shape, F32)
    rows = []
    for which in range(2):
        log_sum = merged(stats_ref, which)
        here = slice(which * quarter, (which + 1) * quarter)
        factor_ref[here, :] = jnp.exp2(
            own[2 * which * quarter : (2 * which + 1) * quarter, :] - log_sum
        )
        rows.append(log_sum)
    rows.append(jnp.zeros((8 - 2 * quarter, LANES), F32))
    logs = jnp.concatenate(rows, axis=0)
    for g in range(out_ref.shape[0]):
        out_ref[g, height:, :] = logs
    spread_rows(weight, factor_ref[:quarter, :])
    column_pass(exp_hbm, exp_ref, sem, weight, out_ref)


def column_kernel(sums_ref, factor_ref, exp_hbm, *refs):
    out_ref, weight, exp_ref, sem = refs[-4:]
    start(copies(exp_hbm, exp_ref, sem))
    quarter = weight.shape[0] // LANES
    scale = 1.0 / add_up([sums_ref[p, :quarter, :] for p in range(sums_ref.shape[0])])
    spread_rows(weight, scale * factor_ref[:quarter, :])
    column_pass(exp_hbm, exp_ref, sem, weight, out_ref)


def column_scales(cols_ref, height):
    return 1.0 / add_up([cols_ref[g, :height, :] for g in range(cols_ref.shape[0])])


def chunk_scales(scales, k):
    height = WIDE // LANES
    return scales[pl.ds(pl.multiple_of(k * height, height), height), :]


def add_row_sums(rows, values, scale):
    for g in range(0, values.shape[0], 32):
        total = rows[g : g + 32, :]
        for t, tile in enumerate(lane_tiles(values[g : g + 32, :].astype(F32))):
            total = total + tile * scale[t : t + 1, :]
        rows[g : g + 32, :] = total


def row_kernel(cols_ref, factor_ref, exp_hbm, *refs):
    out_ref, scales, rows, exp_ref, sem = refs[-5:]
    start(copies(exp_hbm, exp_ref, sem))
    scales[...] = column_scales(cols_ref, scales.shape[0])
    rows[...] = jnp.zeros(rows.shape, F32)
    quarter = rows.shape[0] // LANES
    out_ref[0] = jnp.zeros(out_ref.shape[1:], F32)

    @pl.loop(0, exp_ref.shape[0])
    def _(k):
        copy_of(exp_hbm, exp_ref, sem, k).wait()
        add_row_sums(rows, exp_ref.at[k], chunk_scales(scales, k))

    pack_rows(out_ref.at[0, :quarter], jnp.sum(rows[...], axis=1, keepdims=True))
    out_ref[0, :quarter, :] = out_ref[0, :quarter, :] * factor_ref[:quarter, :]
    repeat(out_ref)


def own_back_kernel(before_ref, exp_hbm, w_hbm, back_ref, exp_ref, w_ref, exp_sem, w_sem):
    start(copies(exp_hbm, exp_ref, exp_sem), copies(w_hbm, w_ref, w_sem))
    back_ref[...] = jnp.zeros(back_ref.shape, F32)

    @pl.loop(0, exp_ref.shape[0])
    def _(k):
        copy_of(exp_hbm, exp_ref, exp_sem, k).wait()
        copy_of(w_hbm, w_ref, w_sem, k).wait()
        back_ref[...] += nt_dot(exp_ref[k], w_ref[:, columns_of(k)])


def relative(place_ref, g, groups):
    return pl.ds(lax.rem(place_ref[0] + g, groups), 1)


def relative_logs(place_ref, logs_ref, lse, which, shift=0.0):
    groups = logs_ref.shape[0]
    own = lse.shape[0] // (groups - 1)
    quarter = own // LANES
    height = logs_ref.shape[1] - 8
    for g in range(1, groups):
        there = logs_ref[relative(place_ref, g, groups)][0]
        first = height + which * quarter
        spread_rows(lse.at[(g - 1) * own : g * own], there[first : first + quarter, :] - shift)


def student_rows_kernel(protos, place_ref, factor_ref, t_ref, own_ref, *refs):
    unit_ref, feat_ref, scaled_ref, t_unit, turned = refs[-5:]
    t_unit[...] = unit_rows(t_ref[...])[0].astype(BF16)
    own = own_ref.shape[0]
    groups = turned.shape[1] // own
    raw = refs[: groups - 1]
    quarter, feats = own // LANES, feat_ref.shape[0]
    for g in range(groups):
        half = unit_rows((raw[g - 1] if g else own_ref)[...])[0].astype(BF16)
        if g:
            unit_ref[(g - 1) * own : g * own, :] = half
        half = half.astype(F32)
        for a in range(0, own, LANES):
            first = g * own + a
            turned[:, first : first + LANES] = jnp.transpose(half[a : a + LANES, :]).astype(BF16)
    feat = turned[pl.ds(pl.multiple_of(place_ref[0] * feats, feats), feats), :]
    feat_ref[...] = feat
    for a in range(quarter):
        lanes = slice(a * LANES, (a + 1) * LANES)
        factor = factor_ref[quarter + a : quarter + a + 1, :] * protos
        scaled_ref[:, lanes] = (feat[:, lanes].astype(F32) * factor).astype(BF16)


def probabilities(unit, w_ref, k, lse, scale, use):
    for n in range(0, WIDE, TILE):
        logits = jnp.dot(
            unit[...], w_ref[:, columns_of(k, n, TILE)], preferred_element_type=F32
        )
        shift = lse[...]
        use(n, [jnp.exp2(tile * scale - shift) for tile in lane_tiles(logits)])


def student_kernel(
    log_protos, first, place_ref, logs_ref, unit, feat_ref, scaled_ref, exp_hbm, w_hbm, *refs
):
    grad, token_ref, lse, prob, exp_ref, w_ref, exp_sem, w_sem = refs[-8:]
    own, count = exp_ref.shape[1], exp_ref.shape[0]
    exp_loads = copies(exp_hbm, exp_ref, exp_sem, first, 0, count)
    w_loads = copies(w_hbm, w_ref, w_sem, first, 0, count)
    start(w_loads, exp_loads)
    token_ref[...] = jnp.zeros(token_ref.shape, F32)
    relative_logs(place_ref, logs_ref, lse, 1, log_protos)

    @pl.loop(0, count)
    def _(k):
        copy_of(w_hbm, w_ref, w_sem, k, first).wait()

        def use(n, tiles):
            for t, tile in enumerate(tiles):
                prob[:, n + t * LANES : n + (t + 1) * LANES] = tile.astype(BF16)

        probabilities(unit, w_ref, k, lse, SCALE_STUDENT, use)
        copy_of(exp_hbm, exp_ref, exp_sem, k, first).wait()
        values = jnp.dot(scaled_ref[...], exp_ref[k], preferred_element_type=F32)
        values = values + jnp.dot(feat_ref[:, own:], prob[...], preferred_element_type=F32)
        grad[:, columns_of(k)] = values.astype(BF16)


def as_three(value):
    high = value.astype(BF16)
    rest = value - high.astype(F32)
    middle = rest.astype(BF16)
    return high, middle, (rest - middle.astype(F32)).astype(BF16)


def last_kernel(groups, place_ref, logs_ref, cols_ref, factor_ref, own_ref, student_ref, exp_hbm, w_hbm, *refs):
    units = refs[: groups - 1]
    (
        prob_hbm, scale_ref, out_ref, unit, lse, rows, own_rows, back, scaled, sums, prob_ref,
        exp_ref, w_ref, prob_sem, exp_sem, w_sem,
    ) = refs[-16:]
    w_loads, exp_loads = copies(w_hbm, w_ref, w_sem), copies(exp_hbm, exp_ref, exp_sem)
    start(w_loads, exp_loads)
    slots, others, _ = prob_ref.shape
    own, chunks = exp_ref.shape[1], exp_ref.shape[0]
    tiles = (own + others) // LANES
    quarter = own // LANES
    scale_ref[...] = column_scales(cols_ref, scale_ref.shape[0])
    rows[...] = jnp.zeros(rows.shape, F32)
    own_rows[...] = jnp.zeros(own_rows.shape, F32)
    back[...] = jnp.zeros(back.shape, F32)
    relative_logs(place_ref, logs_ref, lse, 0)
    for g in range(groups - 1):
        unit[g * own : (g + 1) * own, :] = units[g][...]
    partner = slice((groups // 2 - 1) * own, groups // 2 * own)

    def store(k):
        return pltpu.make_async_copy(prob_ref.at[lax.rem(k, slots)], prob_hbm.at[k], prob_sem.at[k])

    @pl.loop(0, chunks)
    def _(k):
        copy_of(w_hbm, w_ref, w_sem, k).wait()
        slot = lax.rem(k, slots)
        scale = chunk_scales(scale_ref, k)

        @pl.when(k >= slots)
        def _():
            store(k - slots).wait()

        def use(n, tiles):
            for t, tile in enumerate(tiles):
                prob_ref[slot, :, n + t * LANES : n + (t + 1) * LANES] = tile.astype(BF16)
            first = n // LANES
            tiles = [tile * scale[first + t : first + t + 1, :] for t, tile in enumerate(tiles)]
            rows[...] += add_up(tiles)
            for t, tile in enumerate(tiles):
                scaled[:, n + t * LANES : n + (t + 1) * LANES] = tile[partner, :].astype(BF16)

        probabilities(unit, w_ref, k, lse, SCALE_TEACHER, use)
        store(k).start()
        back[...] += nt_dot(scaled[...], w_ref[:, columns_of(k)])
        copy_of(exp_hbm, exp_ref, exp_sem, k).wait()
        add_row_sums(own_rows, exp_ref.at[k], scale)

    sums[...] = jnp.zeros(sums.shape, F32)
    pack_rows(sums.at[:quarter], jnp.sum(own_rows[...], axis=1, keepdims=True))
    sums[:quarter, :] = sums[:quarter, :] * factor_ref[:quarter, :]
    pack_rows(sums.at[quarter:tiles], jnp.sum(rows[...], axis=1, keepdims=True))
    half = unit_rows(own_ref[...])[0].astype(BF16).astype(F32)
    inner = jnp.sum(half * back[...], axis=1, keepdims=True)
    pack_rows(sums.at[tiles : tiles + quarter], inner)
    parts = out_ref.shape[0]
    share = own // parts
    protos = 1.0 * out_ref.shape[0] * w_ref.shape[1]
    student = []
    for a in range(quarter):
        factor = to_column(factor_ref[quarter + a : quarter + a + 1, :] * protos)
        student.append(student_ref[a * LANES : (a + 1) * LANES, :] * factor)
    student = jnp.concatenate(student, axis=0).astype(BF16)
    terms = list(as_three(sums[...]))
    terms.append(jnp.zeros((sums.shape[0], out_ref.shape[2] - 3 * LANES), BF16))
    terms = jnp.concatenate(terms, axis=1)
    for p in range(parts):
        here = slice(p * share, (p + 1) * share)
        out_ref[p] = jnp.concatenate(
            [student[here, :], back[here, :].astype(BF16), terms], axis=0
        )
    for k in range(max(0, chunks - slots), chunks):
        store(k).wait()


def total_sums(message_ref, first):
    parts = message_ref.shape[0]
    each = [
        add_up([t.astype(F32) for t in lane_tiles(message_ref[p, first:, : 3 * LANES])[::-1]])
        for p in range(parts)
    ]
    return add_up(each)


def rows_kernel(tiles, protos, place_ref, s_ref, message_ref, logs_ref, *refs):
    out_ref, loss_ref, sums_ref, weight = refs[-4:]
    parts = message_ref.shape[0]
    share, own = out_ref.shape[1], weight.shape[0]
    quarter = own // LANES
    first = tiles // 2
    totals = total_sums(message_ref, 2 * share)
    sums_ref[...] = totals
    scale = 1.0 / totals[first : first + quarter, :]
    spread_rows(weight, scale)
    mine = pl.ds(pl.multiple_of(place_ref[1] * share, share), share)
    total = add_up([message_ref[p, :share, :].astype(F32) for p in range(parts)])
    paired = add_up([message_ref[p, share : 2 * share, :].astype(F32) for p in range(parts)])
    total = total - paired * (weight[mine, :1] * protos)
    unit, length = unit_rows(s_ref[mine, :])
    out_ref[0] = (total - unit * jnp.sum(unit * total, axis=-1, keepdims=True)) / length
    repeat(out_ref)
    height = logs_ref.shape[1] - 8
    logs = logs_ref[pl.ds(place_ref[0], 1)][0][height + quarter : height + 2 * quarter, :]
    terms = logs / LOG2E - totals[tiles : tiles + quarter, :] * scale / TEMP_STUDENT
    loss_ref[...] = jnp.broadcast_to(jnp.sum(terms), loss_ref.shape)


def grad_kernel(counts, protos, exp_hbm, prob_hbm, feat_ref, scale_ref, sums_ref, factor_ref, *refs):
    parts = refs[: len(counts)]
    out_hbm, scaled, exp_ref, prob_ref, out, exp_sem, prob_sem, sem = refs[-8:]
    exp_loads = copies(exp_hbm, exp_ref, exp_sem)
    prob_loads = copies(prob_hbm, prob_ref, prob_sem)
    start(exp_loads, prob_loads)
    where = [(part, k) for count, part in zip(counts, parts) for k in range(count)]
    own = exp_ref.shape[1]
    tiles = (own + prob_ref.shape[1]) // LANES
    rows = protos / sums_ref[:tiles, :]
    for a in range(tiles):
        other = (a + tiles // 2) % tiles
        feat = feat_ref[:, other * LANES : (other + 1) * LANES].astype(F32)
        row = rows[a : a + 1, :]
        if a < own // LANES:
            row = row * factor_ref[a : a + 1, :]
        scaled[:, a * LANES : (a + 1) * LANES] = (feat * row).astype(BF16)
    stores = copies(out, out_hbm, sem)
    for k, store in enumerate(stores):
        exp_loads[k].wait()
        prob_loads[k].wait()
        paired = jnp.dot(scaled[:, :own], exp_ref[k], preferred_element_type=F32)
        paired = paired + jnp.dot(
            scaled[:, own:], prob_ref[k], preferred_element_type=F32
        )
        part, there = where[k]
        for t, tile in enumerate(lane_tiles(paired)):
            lanes = slice(k * WIDE + t * LANES, k * WIDE + (t + 1) * LANES)
            scale = scale_ref[lanes.start // LANES : lanes.stop // LANES, :]
            own_part = part[:, there * WIDE + t * LANES : there * WIDE + (t + 1) * LANES]
            out[:, lanes] = (own_part.astype(F32) - tile * scale).astype(BF16)
        store.start()
    for store in stores:
        store.wait()


SMEM = pl.BlockSpec(memory_space=pltpu.SMEM)
VMEM = pl.BlockSpec(memory_space=pltpu.VMEM)
ANY = pl.BlockSpec(memory_space=pl.ANY)


def params(nbytes):
    return pltpu.CompilerParams(vmem_limit_bytes=int(nbytes) + 8 * 2**20)


def cost(flops, nbytes, exps=0):
    return pl.CostEstimate(flops=int(flops), bytes_accessed=int(nbytes), transcendentals=int(exps))


def exchange(value, axis):
    return lax.all_to_all(value, axis, 0, 0)


def following(value, axis):
    n = lax.axis_size(axis)
    return [lax.ppermute(value, axis, [(i, (i - s) % n) for i in range(n)]) for s in range(1, n)]


def tree_sum(value, axis):
    n = lax.axis_size(axis)
    values = [value] + [
        lax.ppermute(value, axis, [(i, i ^ s) for i in range(n)]) for s in range(1, n)
    ]
    while len(values) > 1:
        values = [a + b for a, b in zip(values[::2], values[1::2])]
    return values[0]


def local(teacher_feats, student_feats, proto_weight):
    parts, groups = lax.axis_size("proto"), lax.axis_size("batch")
    own, width = teacher_feats.shape
    local_protos = proto_weight.shape[1]
    rows = own * groups
    others = rows - own
    protos = local_protos * parts
    feats = width // groups
    share = own // parts
    tiles = rows // LANES
    height = local_protos // LANES
    chunks = local_protos // WIDE
    place = jnp.stack([lax.axis_index("batch"), lax.axis_index("proto")]).astype(jnp.int32)
    struct = jax.ShapeDtypeStruct
    weight_bytes = 2 * width * local_protos
    exp_bytes = 2 * own * local_protos
    others_bytes = 2 * others * local_protos
    spread = pltpu.VMEM((own, LANES), F32)
    w_buffer = pltpu.VMEM((width, local_protos), BF16)
    exp_buffer = pltpu.VMEM((chunks, own, WIDE), BF16)
    sems = pltpu.SemaphoreType.DMA((chunks,))
    log_protos = math.log2(protos)
    token = struct((8, LANES), F32)

    def far(value):
        return pltpu.with_memory_space_constraint(value, pltpu.HBM)

    weight = far(proto_weight)
    s_all = following(student_feats, "batch")

    exps = pltpu.HBM((chunks, own, WIDE), BF16)
    t_exp, s_exp, stats = pl.pallas_call(
        stats_kernel,
        in_specs=[ANY] * 3,
        out_specs=[ANY, ANY, VMEM],
        out_shape=[
            exps,
            exps,
            struct((parts, 4 * own // LANES, LANES), F32),
        ],
        scratch_shapes=[
            pltpu.VMEM((2, own, width), BF16),
            w_buffer,
            pltpu.VMEM((2 * own, width), BF16),
            pltpu.VMEM((2, chunks, own, WIDE), BF16),
            pltpu.VMEM((2 * own, local_protos), F32),
            pltpu.VMEM((2 * own, LANES), F32),
            pltpu.VMEM((2 * own, LANES), F32),
            pltpu.SemaphoreType.DMA((2,)),
            sems, sems, sems,
        ],
        compiler_params=params(weight_bytes + 6 * exp_bytes),
        cost_estimate=cost(4 * own * width * local_protos, weight_bytes),
        name="own_rows",
    )(far(teacher_feats), far(student_feats), weight)
    t_exp, s_exp = far(t_exp), far(s_exp)

    back_student = pl.pallas_call(
        own_back_kernel,
        in_specs=[ANY] * 3,
        out_specs=VMEM,
        out_shape=struct((own, width), F32),
        scratch_shapes=[exp_buffer, w_buffer, sems, sems],
        compiler_params=params(weight_bytes + exp_bytes),
        cost_estimate=cost(2 * own * width * local_protos, weight_bytes),
        name="own_back",
    )(stats, s_exp, weight)

    stats = exchange(stats, "proto")

    first_shape = (groups, height + 8, LANES)
    factor, cols = pl.pallas_call(
        first_column_kernel,
        in_specs=[SMEM, VMEM, ANY, ANY] + [ANY] * (groups - 1),
        out_specs=[VMEM, VMEM],
        out_shape=[token, struct(first_shape, F32)],
        scratch_shapes=[spread, exp_buffer, sems],
        compiler_params=params(exp_bytes),
        cost_estimate=cost(2 * own * local_protos, exp_bytes),
        name="first_columns",
    )(place, stats, t_exp, back_student, *s_all)

    unit, feat, scaled, t_unit = pl.pallas_call(
        functools.partial(student_rows_kernel, float(protos)),
        in_specs=[SMEM, VMEM, VMEM, VMEM] + [VMEM] * (groups - 1) + [ANY],
        out_specs=[VMEM] * 4,
        out_shape=[
            struct((others, width), BF16), struct((feats, rows), BF16), struct((feats, own), BF16),
            struct((own, width), BF16),
        ],
        scratch_shapes=[pltpu.VMEM((width, rows), BF16)],
        compiler_params=params(2 * rows * width),
        cost_estimate=cost(8 * rows * width, 2 * rows * width),
        name="student_rows",
    )(place, factor, teacher_feats, student_feats, *s_all, cols)
    t_all = following(t_unit, "batch")
    cols = exchange(cols, "batch")
    logs = cols

    counts = [c * chunks // 8 for c in (1, 1, 1, 1, 4)]
    grad_parts = []

    def student_piece(before):
        turn = len(grad_parts)
        first, count = sum(counts[:turn]), counts[turn]
        grad_part, done = pl.pallas_call(
            functools.partial(student_kernel, log_protos, first),
            in_specs=[SMEM] + [VMEM] * 4 + [ANY] * 3,
            out_specs=[VMEM, VMEM],
            out_shape=[struct((feats, count * WIDE), BF16), token],
            scratch_shapes=[
                pltpu.VMEM((others, LANES), F32),
                pltpu.VMEM((others, WIDE), BF16),
                pltpu.VMEM((count, own, WIDE), BF16),
                pltpu.VMEM((width, count * WIDE), BF16),
            ]
            + [pltpu.SemaphoreType.DMA((count,))] * 2,
            compiler_params=params(16 * 2**20),
            cost_estimate=cost(2.5 * rows * width * WIDE * count, 2 * width * WIDE * count),
            name="student_side",
        )(place, logs, unit, feat, scaled, s_exp, weight, before)
        grad_parts.append(grad_part)
        return done

    done = unit
    for turn in range(SWEEPS - 1):
        late = t_all if turn == 1 else []
        sums = pl.pallas_call(
            row_kernel,
            in_specs=[VMEM, VMEM, ANY, ANY] + [ANY] * len(late),
            out_specs=VMEM,
            out_shape=struct((parts, 8, LANES), F32),
            scratch_shapes=[pltpu.VMEM((height, LANES), F32), spread, exp_buffer, sems],
            compiler_params=params(exp_bytes),
            cost_estimate=cost(2 * own * local_protos, exp_bytes),
            name="rows",
        )(cols, factor, t_exp, done, *late)
        done = student_piece(sums)
        sums = exchange(sums, "proto")
        cols = pl.pallas_call(
            column_kernel,
            in_specs=[VMEM, VMEM, ANY, ANY],
            out_specs=VMEM,
            out_shape=struct((groups, height, LANES), F32),
            scratch_shapes=[spread, exp_buffer, sems],
            compiler_params=params(exp_bytes),
            cost_estimate=cost(2 * own * local_protos, exp_bytes),
            name="columns",
        )(sums, factor, t_exp, done)
        done = student_piece(cols)
        cols = exchange(cols, "batch")

    sum_rows = -(-(tiles + own // LANES) // 16) * 16
    message_shape = (parts, 2 * share + sum_rows, width)
    prob, col_scale, message = pl.pallas_call(
        functools.partial(last_kernel, groups),
        in_specs=[SMEM] + [VMEM] * 5 + [ANY] * 2 + [VMEM] * (groups - 1) + [ANY],
        out_specs=[ANY, VMEM, VMEM],
        out_shape=[
            pltpu.HBM((chunks, others, WIDE), BF16),
            struct((height, LANES), F32),
            struct(message_shape, BF16),
        ],
        scratch_shapes=[
            pltpu.VMEM((others, width), BF16),
            pltpu.VMEM((others, LANES), F32),
            pltpu.VMEM((others, LANES), F32),
            spread,
            pltpu.VMEM((own, width), F32),
            pltpu.VMEM((own, WIDE), BF16),
            pltpu.VMEM((sum_rows, LANES), F32),
            pltpu.VMEM((min(chunks, 3), others, WIDE), BF16),
            exp_buffer,
            w_buffer,
            sems, sems, sems,
        ],
        compiler_params=params(20 * 2**20 + weight_bytes + exp_bytes),
        cost_estimate=cost(2 * rows * width * local_protos, others_bytes),
        name="last_rows",
    )(
        place, logs, cols, factor, student_feats, back_student, t_exp, weight, *t_all, done,
    )
    done = student_piece(message)
    message = exchange(message, "proto")

    grad_rows, loss_part, sums = pl.pallas_call(
        functools.partial(rows_kernel, tiles, float(protos)),
        in_specs=[SMEM] + [VMEM] * 3 + [ANY],
        out_specs=[VMEM] * 3,
        out_shape=[struct((parts, share, width), F32), token, struct((sum_rows, LANES), F32)],
        scratch_shapes=[spread],
        compiler_params=params(0),
        name="row_grads",
    )(place, student_feats, message, logs, done)
    grad_rows = exchange(grad_rows, "proto").reshape(own, width)
    loss = tree_sum(loss_part, "batch")[0, 0] / rows

    grad_weight = pl.pallas_call(
        functools.partial(grad_kernel, counts, float(protos)),
        in_specs=[ANY] * 2 + [VMEM] * (4 + len(counts)),
        out_specs=ANY,
        out_shape=struct((feats, local_protos), BF16),
        scratch_shapes=[
            pltpu.VMEM((feats, rows), BF16),
            exp_buffer,
            pltpu.VMEM((chunks, others, WIDE), BF16),
            pltpu.VMEM((feats, local_protos), BF16),
            sems, sems, sems,
        ],
        compiler_params=params(exp_bytes + others_bytes + 4 * feats * local_protos),
        cost_estimate=cost(2 * feats * rows * local_protos, others_bytes),
        name="weight_grads",
    )(t_exp, far(prob), feat, col_scale, sums, factor, *grad_parts)
    return grad_weight, grad_rows, loss


def solution(mesh):
    return jax.shard_map(
        local,
        mesh=mesh,
        in_specs=(P("batch", None), P("batch", None), P(None, "proto")),
        out_specs=(P("batch", "proto"), P("batch", None), P()),
        check_vma=False,
    )
```

```python
import functools
import math

import jax
import jax.numpy as jnp
from jax import lax
from jax.experimental import pallas as pl
from jax.experimental.pallas import tpu as pltpu
from jax.sharding import PartitionSpec as P

SWEEPS = 3
TEMP_TEACHER = 0.04
TEMP_STUDENT = 0.1
LOG2E = math.log2(math.e)
SCALE_TEACHER = LOG2E / TEMP_TEACHER
SCALE_STUDENT = LOG2E / TEMP_STUDENT
LANES = 128
WIDE = 1024
TILE = 256
F32 = jnp.float32
BF16 = jnp.bfloat16


def unit_rows(values):
    wide = values.astype(F32)
    length = jnp.sqrt(jnp.sum(wide * wide, axis=-1, keepdims=True) + 1e-06)
    return wide / length, length


def diagonal():
    shape = (LANES, LANES)
    return lax.broadcasted_iota(jnp.int32, shape, 0) == lax.broadcasted_iota(jnp.int32, shape, 1)


def to_column(row):
    spread = jnp.where(diagonal(), jnp.broadcast_to(row, (LANES, LANES)), 0.0)
    return jnp.sum(spread, axis=1, keepdims=True)


def to_row(column):
    spread = jnp.where(diagonal(), jnp.broadcast_to(column, (LANES, LANES)), 0.0)
    return jnp.sum(spread, axis=0, keepdims=True)


def spread_rows(ref, rows):
    for a in range(rows.shape[0]):
        ref[a * LANES : (a + 1) * LANES, :] = jnp.broadcast_to(
            to_column(rows[a : a + 1, :]), (LANES, LANES)
        )


def pack_rows(ref, columns):
    for a in range(columns.shape[0] // LANES):
        ref[a : a + 1, :] = to_row(columns[a * LANES : (a + 1) * LANES, :])


def lane_tiles(values):
    return [values[:, t * LANES : (t + 1) * LANES] for t in range(values.shape[1] // LANES)]


def fold(values):
    return functools.reduce(jnp.add, lane_tiles(values))


def column_sums(values):
    rows, cols = values.shape
    return jnp.sum(values.reshape(rows // 8, 8, cols), axis=0)


def nt_dot(a, b):
    return lax.dot_general(a, b, (((1,), (1,)), ((), ())), preferred_element_type=F32)


def add_up(values):
    return functools.reduce(jnp.add, values)


def repeat(out_ref):
    for p in range(1, out_ref.shape[0]):
        out_ref[p] = out_ref[0]


def chunk(k):
    return slice(k * WIDE, (k + 1) * WIDE)


def copies(source, target, sems, first=0, back=0, count=None):
    def chunks(ref):
        return ref.shape[0] if len(ref.shape) == 3 else ref.shape[1] // WIDE

    count = count or min(chunks(source), chunks(target))
    return [copy_of(source, target, sems, k, first, back) for k in range(count)]


def columns_of(k, first=0, count=WIDE):
    return pl.ds(pl.multiple_of(k * WIDE + first, LANES), count)


def copy_of(source, target, sems, k, first=0, back=0):
    def part(ref, k):
        return ref.at[k] if len(ref.shape) == 3 else ref.at[:, columns_of(k)]

    return pltpu.make_async_copy(part(source, first + k), part(target, back + k), sems.at[k])


def start(*lists):
    for each in zip(*lists):
        for copy in each:
            copy.start()


def whole_copies(pairs, sems):
    return [pltpu.make_async_copy(a, b, sems.at[i]) for i, (a, b) in enumerate(pairs)]


def wait(*lists):
    for each in lists:
        for copy in each:
            copy.wait()


def stats_kernel(
    t_hbm, s_hbm, w_hbm, t_out, s_out, out_ref,
    raw, w_ref, unit, exps, logits, top, total, raw_sem, w_sem, t_sem, s_sem,
):
    own = raw.shape[1]
    quarter = out_ref.shape[1] // 4
    chunks = exps.shape[1]
    halves = (slice(0, own), slice(own, 2 * own))
    loads = copies(w_hbm, w_ref, w_sem)
    raw_loads = [
        pltpu.make_async_copy(ref, raw.at[which], raw_sem.at[which])
        for which, ref in enumerate((t_hbm, s_hbm))
    ]
    start(raw_loads, loads[:2])
    start(loads[2:])
    top[...] = jnp.full(top.shape, -1e30, F32)
    total[...] = jnp.zeros(total.shape, F32)
    wait(raw_loads)
    for which in range(2):
        unit[halves[which], :] = unit_rows(raw[which])[0].astype(BF16)

    @pl.loop(0, chunks)
    def _(k):
        copy_of(w_hbm, w_ref, w_sem, k).wait()
        for n in range(0, WIDE, TILE):
            here = columns_of(k, n, TILE)
            values = jnp.dot(unit[...], w_ref[:, here], preferred_element_type=F32)
            for half, scale in zip(halves, (SCALE_TEACHER, SCALE_STUDENT)):
                part = values[half, :] * scale
                logits[half, here] = part
                top[half, :] = functools.reduce(jnp.maximum, lane_tiles(part), top[half, :])

    peak = jnp.max(top[...], axis=1, keepdims=True)
    top[...] = jnp.broadcast_to(peak, top.shape)

    @pl.loop(0, chunks)
    def _(k):
        for which, (half, out, sem) in enumerate(zip(halves, (t_out, s_out), (t_sem, s_sem))):
            shift = top[half, :]
            for n in range(0, WIDE, TILE):
                tiles = lane_tiles(logits[half, columns_of(k, n, TILE)])
                tiles = [jnp.exp2(tile - shift) for tile in tiles]
                for t, tile in enumerate(tiles):
                    lanes = slice(n + t * LANES, n + (t + 1) * LANES)
                    exps[which, k, :, lanes] = tile.astype(BF16)
                total[half, :] += add_up(tiles)
            copy_of(exps.at[which], out, sem, k).start()

    sums = jnp.sum(total[...], axis=1, keepdims=True)
    for which, half in enumerate(halves):
        for k, column in enumerate((peak, sums)):
            first = (2 * which + k) * quarter
            pack_rows(out_ref.at[0, first : first + quarter], column[half, :])
    repeat(out_ref)
    wait(copies(exps.at[0], t_out, t_sem), copies(exps.at[1], s_out, s_sem))


def merged(stats_ref, which):
    parts, height, _ = stats_ref.shape
    quarter = height // 4
    first = 2 * which * quarter
    tops = [stats_ref[p, first : first + quarter, :] for p in range(parts)]
    top = functools.reduce(jnp.maximum, tops)
    sums = [
        stats_ref[p, first + quarter : first + 2 * quarter, :] * jnp.exp2(tops[p] - top)
        for p in range(parts)
    ]
    return top + jnp.log2(add_up(sums))


def column_pass(exp_hbm, exp_ref, sem, weight, out_ref):
    height = WIDE // LANES

    @pl.loop(0, exp_ref.shape[0])
    def _(k):
        copy_of(exp_hbm, exp_ref, sem, k).wait()
        sums = jnp.zeros((8, WIDE), F32)
        for g in range(0, exp_ref.shape[1], 16):
            shift = weight[g : g + 16, :]
            tiles = lane_tiles(exp_ref[k, g : g + 16, :].astype(F32))
            sums = sums + column_sums(jnp.concatenate([tile * shift for tile in tiles], axis=1))
        sums = jnp.sum(sums, axis=0, keepdims=True)
        block = jnp.concatenate(lane_tiles(sums), axis=0)
        for g in range(out_ref.shape[0]):
            out_ref[g, pl.ds(pl.multiple_of(k * height, height), height), :] = block


def first_column_kernel(place_ref, stats_ref, exp_hbm, *refs):
    factor_ref, out_ref, weight, exp_ref, sem = refs[-5:]
    start(copies(exp_hbm, exp_ref, sem))
    quarter = stats_ref.shape[1] // 4
    height = out_ref.shape[1] - 8
    own = stats_ref[pl.ds(place_ref[1], 1)][0]
    factor_ref[...] = jnp.zeros(factor_ref.shape, F32)
    rows = []
    for which in range(2):
        log_sum = merged(stats_ref, which)
        here = slice(which * quarter, (which + 1) * quarter)
        factor_ref[here, :] = jnp.exp2(
            own[2 * which * quarter : (2 * which + 1) * quarter, :] - log_sum
        )
        rows.append(log_sum)
    rows.append(jnp.zeros((8 - 2 * quarter, LANES), F32))
    logs = jnp.concatenate(rows, axis=0)
    for g in range(out_ref.shape[0]):
        out_ref[g, height:, :] = logs
    spread_rows(weight, factor_ref[:quarter, :])
    column_pass(exp_hbm, exp_ref, sem, weight, out_ref)


def column_kernel(sums_ref, factor_ref, exp_hbm, *refs):
    out_ref, weight, exp_ref, sem = refs[-4:]
    start(copies(exp_hbm, exp_ref, sem))
    quarter = weight.shape[0] // LANES
    scale = 1.0 / add_up([sums_ref[p, :quarter, :] for p in range(sums_ref.shape[0])])
    spread_rows(weight, scale * factor_ref[:quarter, :])
    column_pass(exp_hbm, exp_ref, sem, weight, out_ref)


def column_scales(cols_ref, height):
    return 1.0 / add_up([cols_ref[g, :height, :] for g in range(cols_ref.shape[0])])


def chunk_scales(scales, k):
    height = WIDE // LANES
    return scales[pl.ds(pl.multiple_of(k * height, height), height), :]


def add_row_sums(rows, values, scale):
    for g in range(0, values.shape[0], 32):
        total = rows[g : g + 32, :]
        for t, tile in enumerate(lane_tiles(values[g : g + 32, :].astype(F32))):
            total = total + tile * scale[t : t + 1, :]
        rows[g : g + 32, :] = total


def row_kernel(cols_ref, factor_ref, exp_hbm, *refs):
    out_ref, scales, rows, exp_ref, sem = refs[-5:]
    start(copies(exp_hbm, exp_ref, sem))
    scales[...] = column_scales(cols_ref, scales.shape[0])
    rows[...] = jnp.zeros(rows.shape, F32)
    quarter = rows.shape[0] // LANES
    out_ref[0] = jnp.zeros(out_ref.shape[1:], F32)

    @pl.loop(0, exp_ref.shape[0])
    def _(k):
        copy_of(exp_hbm, exp_ref, sem, k).wait()
        add_row_sums(rows, exp_ref.at[k], chunk_scales(scales, k))

    pack_rows(out_ref.at[0, :quarter], jnp.sum(rows[...], axis=1, keepdims=True))
    out_ref[0, :quarter, :] = out_ref[0, :quarter, :] * factor_ref[:quarter, :]
    repeat(out_ref)


def own_back_kernel(before_ref, exp_hbm, w_hbm, back_ref, exp_ref, w_ref, exp_sem, w_sem):
    start(copies(exp_hbm, exp_ref, exp_sem), copies(w_hbm, w_ref, w_sem))
    back_ref[...] = jnp.zeros(back_ref.shape, F32)

    @pl.loop(0, exp_ref.shape[0])
    def _(k):
        copy_of(exp_hbm, exp_ref, exp_sem, k).wait()
        copy_of(w_hbm, w_ref, w_sem, k).wait()
        back_ref[...] += nt_dot(exp_ref[k], w_ref[:, columns_of(k)])


def relative(place_ref, g, groups):
    return pl.ds(lax.rem(place_ref[0] + g, groups), 1)


def relative_logs(place_ref, logs_ref, lse, which, shift=0.0):
    groups = logs_ref.shape[0]
    own = lse.shape[0] // (groups - 1)
    quarter = own // LANES
    height = logs_ref.shape[1] - 8
    for g in range(1, groups):
        there = logs_ref[relative(place_ref, g, groups)][0]
        first = height + which * quarter
        spread_rows(lse.at[(g - 1) * own : g * own], there[first : first + quarter, :] - shift)


def student_rows_kernel(protos, place_ref, factor_ref, t_hbm, own_hbm, *refs):
    unit_ref, feat_ref, scaled_ref, t_unit, turned, t_ref, own_ref, sems = refs[-8:]
    loads = whole_copies([(t_hbm, t_ref), (own_hbm, own_ref)], sems)
    start(loads)
    wait(loads)
    t_unit[...] = unit_rows(t_ref[...])[0].astype(BF16)
    own = own_ref.shape[0]
    groups = turned.shape[1] // own
    raw = refs[: groups - 1]
    quarter, feats = own // LANES, feat_ref.shape[0]
    for g in range(groups):
        half = unit_rows((raw[g - 1] if g else own_ref)[...])[0].astype(BF16)
        if g:
            unit_ref[(g - 1) * own : g * own, :] = half
        half = half.astype(F32)
        for a in range(0, own, LANES):
            first = g * own + a
            turned[:, first : first + LANES] = jnp.transpose(half[a : a + LANES, :]).astype(BF16)
    feat = turned[pl.ds(pl.multiple_of(place_ref[0] * feats, feats), feats), :]
    feat_ref[...] = feat
    for a in range(quarter):
        lanes = slice(a * LANES, (a + 1) * LANES)
        factor = factor_ref[quarter + a : quarter + a + 1, :] * protos
        scaled_ref[:, lanes] = (feat[:, lanes].astype(F32) * factor).astype(BF16)


def probabilities(unit, w_ref, k, lse, scale, use):
    for n in range(0, WIDE, TILE):
        logits = jnp.dot(
            unit[...], w_ref[:, columns_of(k, n, TILE)], preferred_element_type=F32
        )
        shift = lse[...]
        use(n, [jnp.exp2(tile * scale - shift) for tile in lane_tiles(logits)])


def student_kernel(
    log_protos, first, count, place_ref, logs_ref, unit, feat_ref, scaled_ref, exp_hbm, w_hbm, *refs
):
    if count > 1:
        grad_hbm, token_ref, lse, prob, exp_ref, w_ref, exp_sem, w_sem, grad, grad_sem = refs[-10:]
    else:
        grad, token_ref, lse, prob, exp_ref, w_ref, exp_sem, w_sem = refs[-8:]
    own = exp_ref.shape[1]
    exp_loads = copies(exp_hbm, exp_ref, exp_sem, first, 0, count)
    w_loads = copies(w_hbm, w_ref, w_sem, first, 0, count)
    start(w_loads, exp_loads)
    token_ref[...] = jnp.zeros(token_ref.shape, F32)
    relative_logs(place_ref, logs_ref, lse, 1, log_protos)

    @pl.loop(0, count)
    def _(k):
        copy_of(w_hbm, w_ref, w_sem, k, first).wait()

        def use(n, tiles):
            for t, tile in enumerate(tiles):
                prob[:, n + t * LANES : n + (t + 1) * LANES] = tile.astype(BF16)

        probabilities(unit, w_ref, k, lse, SCALE_STUDENT, use)
        copy_of(exp_hbm, exp_ref, exp_sem, k, first).wait()
        values = jnp.dot(scaled_ref[...], exp_ref[k], preferred_element_type=F32)
        values = values + jnp.dot(feat_ref[:, own:], prob[...], preferred_element_type=F32)
        grad[:, columns_of(k)] = values.astype(BF16)
        if count > 1:
            copy_of(grad, grad_hbm, grad_sem, k).start()

    if count > 1:
        wait(copies(grad, grad_hbm, grad_sem))


def as_three(value):
    high = value.astype(BF16)
    rest = value - high.astype(F32)
    middle = rest.astype(BF16)
    return high, middle, (rest - middle.astype(F32)).astype(BF16)


def last_kernel(groups, place_ref, logs_ref, cols_ref, factor_ref, own_hbm, student_hbm, exp_hbm, w_hbm, *refs):
    units = refs[: groups - 1]
    (
        prob_hbm, scale_ref, out_ref, unit, lse, rows, own_rows, back, scaled, sums, prob_ref,
        exp_ref, w_ref, own_ref, student_ref, prob_sem, exp_sem, w_sem, sem,
    ) = refs[-19:]
    own = own_ref.shape[0]
    pairs = [(units[g], unit.at[g * own : (g + 1) * own]) for g in range(groups - 1)]
    loads = whole_copies(pairs + [(own_hbm, own_ref), (student_hbm, student_ref)], sem)
    w_loads, exp_loads = copies(w_hbm, w_ref, w_sem), copies(exp_hbm, exp_ref, exp_sem)
    start(w_loads[:1])
    start(loads)
    start(w_loads[1:])
    start(exp_loads)
    slots, others, _ = prob_ref.shape
    chunks = exp_ref.shape[0]
    tiles = (own + others) // LANES
    quarter = own // LANES
    scale_ref[...] = column_scales(cols_ref, scale_ref.shape[0])
    rows[...] = jnp.zeros(rows.shape, F32)
    own_rows[...] = jnp.zeros(own_rows.shape, F32)
    back[...] = jnp.zeros(back.shape, F32)
    relative_logs(place_ref, logs_ref, lse, 0)
    wait(loads)
    partner = slice((groups // 2 - 1) * own, groups // 2 * own)

    def store(k):
        return pltpu.make_async_copy(prob_ref.at[lax.rem(k, slots)], prob_hbm.at[k], prob_sem.at[k])

    @pl.loop(0, chunks)
    def _(k):
        copy_of(w_hbm, w_ref, w_sem, k).wait()
        slot = lax.rem(k, slots)
        scale = chunk_scales(scale_ref, k)

        @pl.when(k >= slots)
        def _():
            store(k - slots).wait()

        def use(n, tiles):
            for t, tile in enumerate(tiles):
                prob_ref[slot, :, n + t * LANES : n + (t + 1) * LANES] = tile.astype(BF16)
            first = n // LANES
            tiles = [tile * scale[first + t : first + t + 1, :] for t, tile in enumerate(tiles)]
            rows[...] += add_up(tiles)
            for t, tile in enumerate(tiles):
                scaled[:, n + t * LANES : n + (t + 1) * LANES] = tile[partner, :].astype(BF16)

        probabilities(unit, w_ref, k, lse, SCALE_TEACHER, use)
        store(k).start()
        back[...] += nt_dot(scaled[...], w_ref[:, columns_of(k)])
        copy_of(exp_hbm, exp_ref, exp_sem, k).wait()
        add_row_sums(own_rows, exp_ref.at[k], scale)

    sums[...] = jnp.zeros(sums.shape, F32)
    pack_rows(sums.at[:quarter], jnp.sum(own_rows[...], axis=1, keepdims=True))
    sums[:quarter, :] = sums[:quarter, :] * factor_ref[:quarter, :]
    pack_rows(sums.at[quarter:tiles], jnp.sum(rows[...], axis=1, keepdims=True))
    half = unit_rows(own_ref[...])[0].astype(BF16).astype(F32)
    inner = jnp.sum(half * back[...], axis=1, keepdims=True)
    pack_rows(sums.at[tiles : tiles + quarter], inner)
    parts = out_ref.shape[0]
    share = own // parts
    protos = 1.0 * out_ref.shape[0] * w_ref.shape[1]
    student = []
    for a in range(quarter):
        factor = to_column(factor_ref[quarter + a : quarter + a + 1, :] * protos)
        student.append(student_ref[a * LANES : (a + 1) * LANES, :] * factor)
    student = jnp.concatenate(student, axis=0).astype(BF16)
    terms = list(as_three(sums[...]))
    terms.append(jnp.zeros((sums.shape[0], out_ref.shape[2] - 3 * LANES), BF16))
    terms = jnp.concatenate(terms, axis=1)
    for p in range(parts):
        here = slice(p * share, (p + 1) * share)
        out_ref[p] = jnp.concatenate(
            [student[here, :], back[here, :].astype(BF16), terms], axis=0
        )
    for k in range(max(0, chunks - slots), chunks):
        store(k).wait()


def total_sums(message_ref, first):
    parts = message_ref.shape[0]
    each = [
        add_up([t.astype(F32) for t in lane_tiles(message_ref[p, first:, : 3 * LANES])[::-1]])
        for p in range(parts)
    ]
    return add_up(each)


def rows_kernel(tiles, protos, place_ref, s_hbm, message_ref, logs_ref, *refs):
    out_ref, loss_ref, sums_ref, weight, s_ref, sem = refs[-6:]
    parts = message_ref.shape[0]
    share, own = out_ref.shape[1], weight.shape[0]
    mine = pl.ds(pl.multiple_of(place_ref[1] * share, share), share)
    load = pltpu.make_async_copy(s_hbm.at[mine], s_ref, sem)
    load.start()
    quarter = own // LANES
    first = tiles // 2
    totals = total_sums(message_ref, 2 * share)
    sums_ref[...] = totals
    scale = 1.0 / totals[first : first + quarter, :]
    spread_rows(weight, scale)
    total = add_up([message_ref[p, :share, :].astype(F32) for p in range(parts)])
    paired = add_up([message_ref[p, share : 2 * share, :].astype(F32) for p in range(parts)])
    total = total - paired * (weight[mine, :1] * protos)
    load.wait()
    unit, length = unit_rows(s_ref[...])
    out_ref[0] = (total - unit * jnp.sum(unit * total, axis=-1, keepdims=True)) / length
    repeat(out_ref)
    height = logs_ref.shape[1] - 8
    logs = logs_ref[pl.ds(place_ref[0], 1)][0][height + quarter : height + 2 * quarter, :]
    terms = logs / LOG2E - totals[tiles : tiles + quarter, :] * scale / TEMP_STUDENT
    loss_ref[...] = jnp.broadcast_to(jnp.sum(terms), loss_ref.shape)


def grad_kernel(counts, protos, exp_hbm, prob_hbm, feat_ref, scale_ref, sums_ref, factor_ref, *refs):
    parts = refs[: len(counts)]
    out_hbm, scaled, exp_ref, prob_ref, out, last_ref, exp_sem, prob_sem, sem, last_sem = refs[-10:]
    last_load = pltpu.make_async_copy(parts[-1], last_ref, last_sem)
    parts = parts[:-1] + (last_ref,)
    exp_loads = copies(exp_hbm, exp_ref, exp_sem)
    prob_loads = copies(prob_hbm, prob_ref, prob_sem)
    early = sum(counts[:-1])
    start(exp_loads[:early], prob_loads[:early])
    last_load.start()
    start(exp_loads[early:], prob_loads[early:])
    where = [(part, k) for count, part in zip(counts, parts) for k in range(count)]
    own = exp_ref.shape[1]
    tiles = (own + prob_ref.shape[1]) // LANES
    rows = protos / sums_ref[:tiles, :]
    for a in range(tiles):
        other = (a + tiles // 2) % tiles
        feat = feat_ref[:, other * LANES : (other + 1) * LANES].astype(F32)
        row = rows[a : a + 1, :]
        if a < own // LANES:
            row = row * factor_ref[a : a + 1, :]
        scaled[:, a * LANES : (a + 1) * LANES] = (feat * row).astype(BF16)
    stores = copies(out, out_hbm, sem)
    for k, store in enumerate(stores):
        exp_loads[k].wait()
        prob_loads[k].wait()
        paired = jnp.dot(scaled[:, :own], exp_ref[k], preferred_element_type=F32)
        paired = paired + jnp.dot(
            scaled[:, own:], prob_ref[k], preferred_element_type=F32
        )
        part, there = where[k]
        if part is last_ref and there == 0:
            last_load.wait()
        for t, tile in enumerate(lane_tiles(paired)):
            lanes = slice(k * WIDE + t * LANES, k * WIDE + (t + 1) * LANES)
            scale = scale_ref[lanes.start // LANES : lanes.stop // LANES, :]
            own_part = part[:, there * WIDE + t * LANES : there * WIDE + (t + 1) * LANES]
            out[:, lanes] = (own_part.astype(F32) - tile * scale).astype(BF16)
        store.start()
    for store in stores:
        store.wait()


SMEM = pl.BlockSpec(memory_space=pltpu.SMEM)
VMEM = pl.BlockSpec(memory_space=pltpu.VMEM)
ANY = pl.BlockSpec(memory_space=pl.ANY)


def params(nbytes):
    return pltpu.CompilerParams(vmem_limit_bytes=int(nbytes) + 8 * 2**20)


def cost(flops, nbytes, exps=0):
    return pl.CostEstimate(flops=int(flops), bytes_accessed=int(nbytes), transcendentals=int(exps))


def exchange(value, axis):
    return lax.all_to_all(value, axis, 0, 0)


def following(value, axis):
    n = lax.axis_size(axis)
    return [lax.ppermute(value, axis, [(i, (i - s) % n) for i in range(n)]) for s in range(1, n)]


def tree_sum(value, axis):
    n = lax.axis_size(axis)
    values = [value] + [
        lax.ppermute(value, axis, [(i, i ^ s) for i in range(n)]) for s in range(1, n)
    ]
    while len(values) > 1:
        values = [a + b for a, b in zip(values[::2], values[1::2])]
    return values[0]


def local(teacher_feats, student_feats, proto_weight):
    parts, groups = lax.axis_size("proto"), lax.axis_size("batch")
    own, width = teacher_feats.shape
    local_protos = proto_weight.shape[1]
    rows = own * groups
    others = rows - own
    protos = local_protos * parts
    feats = width // groups
    share = own // parts
    tiles = rows // LANES
    height = local_protos // LANES
    chunks = local_protos // WIDE
    place = jnp.stack([lax.axis_index("batch"), lax.axis_index("proto")]).astype(jnp.int32)
    struct = jax.ShapeDtypeStruct
    weight_bytes = 2 * width * local_protos
    exp_bytes = 2 * own * local_protos
    others_bytes = 2 * others * local_protos
    spread = pltpu.VMEM((own, LANES), F32)
    w_buffer = pltpu.VMEM((width, local_protos), BF16)
    exp_buffer = pltpu.VMEM((chunks, own, WIDE), BF16)
    sems = pltpu.SemaphoreType.DMA((chunks,))
    log_protos = math.log2(protos)
    token = struct((8, LANES), F32)

    def far(value):
        return pltpu.with_memory_space_constraint(value, pltpu.HBM)

    weight = far(proto_weight)
    teacher_rows, student_rows = far(teacher_feats), far(student_feats)
    s_all = following(student_feats, "batch")

    exps = pltpu.HBM((chunks, own, WIDE), BF16)
    t_exp, s_exp, stats = pl.pallas_call(
        stats_kernel,
        in_specs=[ANY] * 3,
        out_specs=[ANY, ANY, VMEM],
        out_shape=[
            exps,
            exps,
            struct((parts, 4 * own // LANES, LANES), F32),
        ],
        scratch_shapes=[
            pltpu.VMEM((2, own, width), BF16),
            w_buffer,
            pltpu.VMEM((2 * own, width), BF16),
            pltpu.VMEM((2, chunks, own, WIDE), BF16),
            pltpu.VMEM((2 * own, local_protos), F32),
            pltpu.VMEM((2 * own, LANES), F32),
            pltpu.VMEM((2 * own, LANES), F32),
            pltpu.SemaphoreType.DMA((2,)),
            sems, sems, sems,
        ],
        compiler_params=params(weight_bytes + 6 * exp_bytes),
        cost_estimate=cost(4 * own * width * local_protos, weight_bytes),
        name="own_rows",
    )(teacher_rows, student_rows, weight)
    t_exp, s_exp = far(t_exp), far(s_exp)

    back_student = pl.pallas_call(
        own_back_kernel,
        in_specs=[ANY] * 3,
        out_specs=VMEM,
        out_shape=struct((own, width), F32),
        scratch_shapes=[exp_buffer, w_buffer, sems, sems],
        compiler_params=params(weight_bytes + exp_bytes),
        cost_estimate=cost(2 * own * width * local_protos, weight_bytes),
        name="own_back",
    )(stats, s_exp, weight)

    stats = exchange(stats, "proto")

    first_shape = (groups, height + 8, LANES)
    factor, cols = pl.pallas_call(
        first_column_kernel,
        in_specs=[SMEM, VMEM, ANY, ANY] + [ANY] * (groups - 1),
        out_specs=[VMEM, VMEM],
        out_shape=[token, struct(first_shape, F32)],
        scratch_shapes=[spread, exp_buffer, sems],
        compiler_params=params(exp_bytes),
        cost_estimate=cost(2 * own * local_protos, exp_bytes),
        name="first_columns",
    )(place, stats, t_exp, back_student, *s_all)

    unit, feat, scaled, t_unit = pl.pallas_call(
        functools.partial(student_rows_kernel, float(protos)),
        in_specs=[SMEM, VMEM, ANY, ANY] + [VMEM] * (groups - 1) + [ANY],
        out_specs=[VMEM] * 4,
        out_shape=[
            struct((others, width), BF16), struct((feats, rows), BF16), struct((feats, own), BF16),
            struct((own, width), BF16),
        ],
        scratch_shapes=[
            pltpu.VMEM((width, rows), BF16),
            pltpu.VMEM((own, width), BF16),
            pltpu.VMEM((own, width), BF16),
            pltpu.SemaphoreType.DMA((2,)),
        ],
        compiler_params=params(2 * rows * width),
        cost_estimate=cost(8 * rows * width, 2 * rows * width),
        name="student_rows",
    )(place, factor, teacher_rows, student_rows, *s_all, cols)
    t_all = following(t_unit, "batch")
    cols = exchange(cols, "batch")
    logs = cols

    counts = [c * chunks // 8 for c in (1, 1, 1, 1, 4)]
    grad_parts = []

    def student_piece(before):
        turn = len(grad_parts)
        first, count = sum(counts[:turn]), counts[turn]
        grad_part, done = pl.pallas_call(
            functools.partial(student_kernel, log_protos, first, count),
            in_specs=[SMEM] + [VMEM] * 4 + [ANY] * 3,
            out_specs=[ANY if count > 1 else VMEM, VMEM],
            out_shape=[
                (pltpu.HBM if count > 1 else struct)((feats, count * WIDE), BF16), token,
            ],
            scratch_shapes=[
                pltpu.VMEM((others, LANES), F32),
                pltpu.VMEM((others, WIDE), BF16),
                pltpu.VMEM((count, own, WIDE), BF16),
                pltpu.VMEM((width, count * WIDE), BF16),
            ]
            + [pltpu.SemaphoreType.DMA((count,))] * 2
            + ([pltpu.VMEM((feats, count * WIDE), BF16)] if count > 1 else [])
            + ([pltpu.SemaphoreType.DMA((count,))] if count > 1 else []),
            compiler_params=params(16 * 2**20),
            cost_estimate=cost(2.5 * rows * width * WIDE * count, 2 * width * WIDE * count),
            name="student_side",
        )(place, logs, unit, feat, scaled, s_exp, weight, before)
        grad_parts.append(far(grad_part) if count > 1 else grad_part)
        return done

    done = unit
    for turn in range(SWEEPS - 1):
        late = t_all if turn == 1 else []
        sums = pl.pallas_call(
            row_kernel,
            in_specs=[VMEM, VMEM, ANY, ANY] + [ANY] * len(late),
            out_specs=VMEM,
            out_shape=struct((parts, 8, LANES), F32),
            scratch_shapes=[pltpu.VMEM((height, LANES), F32), spread, exp_buffer, sems],
            compiler_params=params(exp_bytes),
            cost_estimate=cost(2 * own * local_protos, exp_bytes),
            name="rows",
        )(cols, factor, t_exp, done, *late)
        done = student_piece(sums)
        sums = exchange(sums, "proto")
        cols = pl.pallas_call(
            column_kernel,
            in_specs=[VMEM, VMEM, ANY, ANY],
            out_specs=VMEM,
            out_shape=struct((groups, height, LANES), F32),
            scratch_shapes=[spread, exp_buffer, sems],
            compiler_params=params(exp_bytes),
            cost_estimate=cost(2 * own * local_protos, exp_bytes),
            name="columns",
        )(sums, factor, t_exp, done)
        done = student_piece(cols)
        cols = exchange(cols, "batch")

    sum_rows = -(-(tiles + own // LANES) // 16) * 16
    message_shape = (parts, 2 * share + sum_rows, width)
    prob, col_scale, message = pl.pallas_call(
        functools.partial(last_kernel, groups),
        in_specs=[SMEM] + [VMEM] * 3 + [ANY] * (4 + groups),
        out_specs=[ANY, VMEM, VMEM],
        out_shape=[
            pltpu.HBM((chunks, others, WIDE), BF16),
            struct((height, LANES), F32),
            struct(message_shape, BF16),
        ],
        scratch_shapes=[
            pltpu.VMEM((others, width), BF16),
            pltpu.VMEM((others, LANES), F32),
            pltpu.VMEM((others, LANES), F32),
            spread,
            pltpu.VMEM((own, width), F32),
            pltpu.VMEM((own, WIDE), BF16),
            pltpu.VMEM((sum_rows, LANES), F32),
            pltpu.VMEM((min(chunks, 3), others, WIDE), BF16),
            exp_buffer,
            w_buffer,
            pltpu.VMEM((own, width), BF16),
            pltpu.VMEM((own, width), F32),
            sems, sems, sems,
            pltpu.SemaphoreType.DMA((groups + 1,)),
        ],
        compiler_params=params(20 * 2**20 + weight_bytes + exp_bytes),
        cost_estimate=cost(2 * rows * width * local_protos, others_bytes),
        name="last_rows",
    )(
        place, logs, cols, factor, student_rows, far(back_student), t_exp, weight,
        *[far(x) for x in t_all], done,
    )
    done = student_piece(message)
    message = exchange(message, "proto")

    grad_rows, loss_part, sums = pl.pallas_call(
        functools.partial(rows_kernel, tiles, float(protos)),
        in_specs=[SMEM, ANY, VMEM, VMEM, ANY],
        out_specs=[VMEM] * 3,
        out_shape=[struct((parts, share, width), F32), token, struct((sum_rows, LANES), F32)],
        scratch_shapes=[spread, pltpu.VMEM((share, width), BF16), pltpu.SemaphoreType.DMA],
        compiler_params=params(0),
        name="row_grads",
    )(place, student_rows, message, logs, done)
    grad_rows = exchange(grad_rows, "proto").reshape(own, width)
    loss = tree_sum(loss_part, "batch")[0, 0] / rows

    grad_weight = pl.pallas_call(
        functools.partial(grad_kernel, counts, float(protos)),
        in_specs=[ANY] * 2 + [VMEM] * (3 + len(counts)) + [ANY],
        out_specs=ANY,
        out_shape=struct((feats, local_protos), BF16),
        scratch_shapes=[
            pltpu.VMEM((feats, rows), BF16),
            exp_buffer,
            pltpu.VMEM((chunks, others, WIDE), BF16),
            pltpu.VMEM((feats, local_protos), BF16),
            pltpu.VMEM((feats, counts[-1] * WIDE), BF16),
            sems, sems, sems,
            pltpu.SemaphoreType.DMA,
        ],
        compiler_params=params(exp_bytes + others_bytes + 4 * feats * local_protos),
        cost_estimate=cost(2 * feats * rows * local_protos, others_bytes),
        name="weight_grads",
    )(t_exp, far(prob), feat, col_scale, sums, factor, *grad_parts)
    return grad_weight, grad_rows, loss


def solution(mesh):
    return jax.shard_map(
        local,
        mesh=mesh,
        in_specs=(P("batch", None), P("batch", None), P(None, "proto")),
        out_specs=(P("batch", "proto"), P("batch", None), P()),
        check_vma=False,
    )
```

```python
import functools
import math

import jax
import jax.numpy as jnp
from jax import lax
from jax.experimental import pallas as pl
from jax.experimental.pallas import tpu as pltpu
from jax.sharding import PartitionSpec as P

SWEEPS = 3
TEMP_TEACHER = 0.04
TEMP_STUDENT = 0.1
LOG2E = math.log2(math.e)
SCALE_TEACHER = LOG2E / TEMP_TEACHER
SCALE_STUDENT = LOG2E / TEMP_STUDENT
LANES = 128
WIDE = 1024
TILE = 256
F32 = jnp.float32
BF16 = jnp.bfloat16


def unit_rows(values):
    wide = values.astype(F32)
    length = jnp.sqrt(jnp.sum(wide * wide, axis=-1, keepdims=True) + 1e-06)
    return wide / length, length


def diagonal():
    shape = (LANES, LANES)
    return lax.broadcasted_iota(jnp.int32, shape, 0) == lax.broadcasted_iota(jnp.int32, shape, 1)


def to_column(row):
    spread = jnp.where(diagonal(), jnp.broadcast_to(row, (LANES, LANES)), 0.0)
    return jnp.sum(spread, axis=1, keepdims=True)


def to_row(column):
    spread = jnp.where(diagonal(), jnp.broadcast_to(column, (LANES, LANES)), 0.0)
    return jnp.sum(spread, axis=0, keepdims=True)


def spread_rows(ref, rows):
    for a in range(rows.shape[0]):
        ref[a * LANES : (a + 1) * LANES, :] = jnp.broadcast_to(
            to_column(rows[a : a + 1, :]), (LANES, LANES)
        )


def pack_rows(ref, columns):
    for a in range(columns.shape[0] // LANES):
        ref[a : a + 1, :] = to_row(columns[a * LANES : (a + 1) * LANES, :])


def lane_tiles(values):
    return [values[:, t * LANES : (t + 1) * LANES] for t in range(values.shape[1] // LANES)]


def fold(values):
    return functools.reduce(jnp.add, lane_tiles(values))


def column_sums(values):
    rows, cols = values.shape
    return jnp.sum(values.reshape(rows // 8, 8, cols), axis=0)


def nt_dot(a, b):
    return lax.dot_general(a, b, (((1,), (1,)), ((), ())), preferred_element_type=F32)


def add_up(values):
    return functools.reduce(jnp.add, values)


def repeat(out_ref):
    for p in range(1, out_ref.shape[0]):
        out_ref[p] = out_ref[0]


def chunk(k):
    return slice(k * WIDE, (k + 1) * WIDE)


def copies(source, target, sems, first=0, back=0, count=None):
    def chunks(ref):
        return ref.shape[0] if len(ref.shape) == 3 else ref.shape[1] // WIDE

    count = count or min(chunks(source), chunks(target))
    return [copy_of(source, target, sems, k, first, back) for k in range(count)]


def columns_of(k, first=0, count=WIDE):
    return pl.ds(pl.multiple_of(k * WIDE + first, LANES), count)


def copy_of(source, target, sems, k, first=0, back=0):
    def part(ref, k):
        return ref.at[k] if len(ref.shape) == 3 else ref.at[:, columns_of(k)]

    return pltpu.make_async_copy(part(source, first + k), part(target, back + k), sems.at[k])


def start(*lists):
    for each in zip(*lists):
        for copy in each:
            copy.start()


def whole_copies(pairs, sems):
    return [pltpu.make_async_copy(a, b, sems.at[i]) for i, (a, b) in enumerate(pairs)]


def wait(*lists):
    for each in lists:
        for copy in each:
            copy.wait()


def stats_kernel(
    t_hbm, s_hbm, w_hbm, t_out, s_out, out_ref,
    raw, w_ref, unit, exps, logits, top, total, raw_sem, w_sem, t_sem, s_sem,
):
    own = raw.shape[1]
    quarter = out_ref.shape[1] // 4
    chunks = exps.shape[1]
    halves = (slice(0, own), slice(own, 2 * own))
    loads = copies(w_hbm, w_ref, w_sem)
    raw_loads = [
        pltpu.make_async_copy(ref, raw.at[which], raw_sem.at[which])
        for which, ref in enumerate((t_hbm, s_hbm))
    ]
    start(raw_loads, loads[:2])
    start(loads[2:])
    top[...] = jnp.full(top.shape, -1e30, F32)
    total[...] = jnp.zeros(total.shape, F32)
    wait(raw_loads)
    for which in range(2):
        unit[halves[which], :] = unit_rows(raw[which])[0].astype(BF16)

    @pl.loop(0, chunks)
    def _(k):
        copy_of(w_hbm, w_ref, w_sem, k).wait()
        for n in range(0, WIDE, TILE):
            here = columns_of(k, n, TILE)
            values = jnp.dot(unit[...], w_ref[:, here], preferred_element_type=F32)
            for half, scale in zip(halves, (SCALE_TEACHER, SCALE_STUDENT)):
                part = values[half, :] * scale
                logits[half, here] = part
                top[half, :] = functools.reduce(jnp.maximum, lane_tiles(part), top[half, :])

    peak = jnp.max(top[...], axis=1, keepdims=True)
    top[...] = jnp.broadcast_to(peak, top.shape)

    @pl.loop(0, chunks)
    def _(k):
        for which, (half, out, sem) in enumerate(zip(halves, (t_out, s_out), (t_sem, s_sem))):
            shift = top[half, :]
            for n in range(0, WIDE, TILE):
                tiles = lane_tiles(logits[half, columns_of(k, n, TILE)])
                tiles = [jnp.exp2(tile - shift) for tile in tiles]
                for t, tile in enumerate(tiles):
                    lanes = slice(n + t * LANES, n + (t + 1) * LANES)
                    exps[which, k, :, lanes] = tile.astype(BF16)
                total[half, :] += add_up(tiles)
            copy_of(exps.at[which], out, sem, k).start()

    sums = jnp.sum(total[...], axis=1, keepdims=True)
    for which, half in enumerate(halves):
        for k, column in enumerate((peak, sums)):
            first = (2 * which + k) * quarter
            pack_rows(out_ref.at[0, first : first + quarter], column[half, :])
    repeat(out_ref)
    wait(copies(exps.at[0], t_out, t_sem), copies(exps.at[1], s_out, s_sem))


def merged(stats_ref, which):
    parts, height, _ = stats_ref.shape
    quarter = height // 4
    first = 2 * which * quarter
    tops = [stats_ref[p, first : first + quarter, :] for p in range(parts)]
    top = functools.reduce(jnp.maximum, tops)
    sums = [
        stats_ref[p, first + quarter : first + 2 * quarter, :] * jnp.exp2(tops[p] - top)
        for p in range(parts)
    ]
    return top + jnp.log2(add_up(sums))


def column_pass(exp_hbm, exp_ref, sem, weight, out_ref):
    height = WIDE // LANES

    @pl.loop(0, exp_ref.shape[0])
    def _(k):
        copy_of(exp_hbm, exp_ref, sem, k).wait()
        sums = jnp.zeros((8, WIDE), F32)
        for g in range(0, exp_ref.shape[1], 16):
            shift = weight[g : g + 16, :]
            tiles = lane_tiles(exp_ref[k, g : g + 16, :].astype(F32))
            sums = sums + column_sums(jnp.concatenate([tile * shift for tile in tiles], axis=1))
        sums = jnp.sum(sums, axis=0, keepdims=True)
        block = jnp.concatenate(lane_tiles(sums), axis=0)
        for g in range(out_ref.shape[0]):
            out_ref[g, pl.ds(pl.multiple_of(k * height, height), height), :] = block


def first_column_kernel(place_ref, stats_ref, exp_hbm, *refs):
    factor_ref, out_ref, weight, exp_ref, sem = refs[-5:]
    start(copies(exp_hbm, exp_ref, sem))
    quarter = stats_ref.shape[1] // 4
    height = out_ref.shape[1] - 8
    own = stats_ref[pl.ds(place_ref[1], 1)][0]
    factor_ref[...] = jnp.zeros(factor_ref.shape, F32)
    rows = []
    for which in range(2):
        log_sum = merged(stats_ref, which)
        here = slice(which * quarter, (which + 1) * quarter)
        factor_ref[here, :] = jnp.exp2(
            own[2 * which * quarter : (2 * which + 1) * quarter, :] - log_sum
        )
        rows.append(log_sum)
    rows.append(jnp.zeros((8 - 2 * quarter, LANES), F32))
    logs = jnp.concatenate(rows, axis=0)
    for g in range(out_ref.shape[0]):
        out_ref[g, height:, :] = logs
    spread_rows(weight, factor_ref[:quarter, :])
    column_pass(exp_hbm, exp_ref, sem, weight, out_ref)


def column_kernel(sums_ref, factor_ref, exp_hbm, *refs):
    out_ref, weight, exp_ref, sem = refs[-4:]
    start(copies(exp_hbm, exp_ref, sem))
    quarter = weight.shape[0] // LANES
    scale = 1.0 / add_up([sums_ref[p, :quarter, :] for p in range(sums_ref.shape[0])])
    spread_rows(weight, scale * factor_ref[:quarter, :])
    column_pass(exp_hbm, exp_ref, sem, weight, out_ref)


def column_scales(cols, height):
    return 1.0 / add_up([ref[g, :height, :] for ref in cols for g in range(ref.shape[0])])


def chunk_scales(scales, k):
    height = WIDE // LANES
    return scales[pl.ds(pl.multiple_of(k * height, height), height), :]


def add_row_sums(rows, values, scale):
    for g in range(0, values.shape[0], 32):
        total = rows[g : g + 32, :]
        for t, tile in enumerate(lane_tiles(values[g : g + 32, :].astype(F32))):
            total = total + tile * scale[t : t + 1, :]
        rows[g : g + 32, :] = total


def row_kernel(count, *refs):
    cols, (factor_ref, exp_hbm) = refs[:count], refs[count : count + 2]
    out_ref, scales, rows, exp_ref, sem = refs[-5:]
    start(copies(exp_hbm, exp_ref, sem))
    scales[...] = column_scales(cols, scales.shape[0])
    rows[...] = jnp.zeros(rows.shape, F32)
    quarter = rows.shape[0] // LANES
    out_ref[0] = jnp.zeros(out_ref.shape[1:], F32)

    @pl.loop(0, exp_ref.shape[0])
    def _(k):
        copy_of(exp_hbm, exp_ref, sem, k).wait()
        add_row_sums(rows, exp_ref.at[k], chunk_scales(scales, k))

    pack_rows(out_ref.at[0, :quarter], jnp.sum(rows[...], axis=1, keepdims=True))
    out_ref[0, :quarter, :] = out_ref[0, :quarter, :] * factor_ref[:quarter, :]
    repeat(out_ref)


def own_back_kernel(before_ref, exp_hbm, w_hbm, back_ref, exp_ref, w_ref, exp_sem, w_sem):
    start(copies(exp_hbm, exp_ref, exp_sem), copies(w_hbm, w_ref, w_sem))
    back_ref[...] = jnp.zeros(back_ref.shape, F32)

    @pl.loop(0, exp_ref.shape[0])
    def _(k):
        copy_of(exp_hbm, exp_ref, exp_sem, k).wait()
        copy_of(w_hbm, w_ref, w_sem, k).wait()
        back_ref[...] += nt_dot(exp_ref[k], w_ref[:, columns_of(k)])


def relative_logs(logs, lse, which, shift=0.0):
    own = lse.shape[0] // (len(logs) - 1)
    quarter = own // LANES
    for g, ref in enumerate(logs[1:]):
        first = ref.shape[1] - 8 + which * quarter
        spread_rows(lse.at[g * own : (g + 1) * own], ref[0, first : first + quarter, :] - shift)


def student_rows_kernel(protos, place_ref, factor_ref, t_ref, own_ref, *refs):
    unit_ref, feat_ref, scaled_ref, t_unit, turned = refs[-5:]
    t_unit[...] = unit_rows(t_ref[...])[0].astype(BF16)
    own = own_ref.shape[0]
    groups = turned.shape[1] // own
    raw = refs[: groups - 1]
    quarter, feats = own // LANES, feat_ref.shape[0]
    for g in range(groups):
        half = unit_rows((raw[g - 1] if g else own_ref)[...])[0].astype(BF16)
        if g:
            unit_ref[(g - 1) * own : g * own, :] = half
        half = half.astype(F32)
        for a in range(0, own, LANES):
            first = g * own + a
            turned[:, first : first + LANES] = jnp.transpose(half[a : a + LANES, :]).astype(BF16)
    feat = turned[pl.ds(pl.multiple_of(place_ref[0] * feats, feats), feats), :]
    feat_ref[...] = feat
    for a in range(quarter):
        lanes = slice(a * LANES, (a + 1) * LANES)
        factor = factor_ref[quarter + a : quarter + a + 1, :] * protos
        scaled_ref[:, lanes] = (feat[:, lanes].astype(F32) * factor).astype(BF16)


def probabilities(unit, w_ref, k, lse, scale, use):
    for n in range(0, WIDE, TILE):
        logits = jnp.dot(
            unit[...], w_ref[:, columns_of(k, n, TILE)], preferred_element_type=F32
        )
        shift = lse[...]
        use(n, [jnp.exp2(tile * scale - shift) for tile in lane_tiles(logits)])


def student_kernel(
    log_protos, first, groups, unit, feat_ref, scaled_ref, exp_hbm, w_hbm, *refs
):
    logs = refs[:groups]
    grad, token_ref, lse, prob, exp_ref, w_ref, exp_sem, w_sem = refs[-8:]
    own, count = exp_ref.shape[1], exp_ref.shape[0]
    exp_loads = copies(exp_hbm, exp_ref, exp_sem, first, 0, count)
    w_loads = copies(w_hbm, w_ref, w_sem, first, 0, count)
    start(w_loads, exp_loads)
    token_ref[...] = jnp.zeros(token_ref.shape, F32)
    relative_logs(logs, lse, 1, log_protos)

    @pl.loop(0, count)
    def _(k):
        copy_of(w_hbm, w_ref, w_sem, k, first).wait()

        def use(n, tiles):
            for t, tile in enumerate(tiles):
                prob[:, n + t * LANES : n + (t + 1) * LANES] = tile.astype(BF16)

        probabilities(unit, w_ref, k, lse, SCALE_STUDENT, use)
        copy_of(exp_hbm, exp_ref, exp_sem, k, first).wait()
        values = jnp.dot(scaled_ref[...], exp_ref[k], preferred_element_type=F32)
        values = values + jnp.dot(feat_ref[:, own:], prob[...], preferred_element_type=F32)
        grad[:, columns_of(k)] = values.astype(BF16)


def as_three(value):
    high = value.astype(BF16)
    rest = value - high.astype(F32)
    middle = rest.astype(BF16)
    return high, middle, (rest - middle.astype(F32)).astype(BF16)


def last_kernel(groups, factor_ref, own_hbm, student_hbm, exp_hbm, w_hbm, *refs):
    units, refs = refs[: groups - 1], refs[groups - 1 :]
    logs, cols, refs = refs[:groups], refs[groups : 2 * groups], refs[2 * groups :]
    (
        prob_hbm, scale_ref, out_ref, unit, lse, rows, own_rows, back, scaled, sums, prob_ref,
        exp_ref, w_ref, own_ref, student_ref, prob_sem, exp_sem, w_sem, sem,
    ) = refs[-19:]
    w_loads, exp_loads = copies(w_hbm, w_ref, w_sem), copies(exp_hbm, exp_ref, exp_sem)
    late_loads = whole_copies([(own_hbm, own_ref), (student_hbm, student_ref)], sem)
    start(w_loads, exp_loads)
    start(late_loads)
    slots, others, _ = prob_ref.shape
    own, chunks = exp_ref.shape[1], exp_ref.shape[0]
    tiles = (own + others) // LANES
    quarter = own // LANES
    scale_ref[...] = column_scales(cols, scale_ref.shape[0])
    rows[...] = jnp.zeros(rows.shape, F32)
    own_rows[...] = jnp.zeros(own_rows.shape, F32)
    back[...] = jnp.zeros(back.shape, F32)
    relative_logs(logs, lse, 0)
    for g in range(groups - 1):
        unit[g * own : (g + 1) * own, :] = units[g][...]
    partner = slice((groups // 2 - 1) * own, groups // 2 * own)

    def store(k):
        return pltpu.make_async_copy(prob_ref.at[lax.rem(k, slots)], prob_hbm.at[k], prob_sem.at[k])

    @pl.loop(0, chunks)
    def _(k):
        copy_of(w_hbm, w_ref, w_sem, k).wait()
        slot = lax.rem(k, slots)
        scale = chunk_scales(scale_ref, k)

        @pl.when(k >= slots)
        def _():
            store(k - slots).wait()

        def use(n, tiles):
            for t, tile in enumerate(tiles):
                prob_ref[slot, :, n + t * LANES : n + (t + 1) * LANES] = tile.astype(BF16)
            first = n // LANES
            tiles = [tile * scale[first + t : first + t + 1, :] for t, tile in enumerate(tiles)]
            rows[...] += add_up(tiles)
            for t, tile in enumerate(tiles):
                scaled[:, n + t * LANES : n + (t + 1) * LANES] = tile[partner, :].astype(BF16)

        probabilities(unit, w_ref, k, lse, SCALE_TEACHER, use)
        store(k).start()
        back[...] += nt_dot(scaled[...], w_ref[:, columns_of(k)])
        copy_of(exp_hbm, exp_ref, exp_sem, k).wait()
        add_row_sums(own_rows, exp_ref.at[k], scale)

    sums[...] = jnp.zeros(sums.shape, F32)
    pack_rows(sums.at[:quarter], jnp.sum(own_rows[...], axis=1, keepdims=True))
    sums[:quarter, :] = sums[:quarter, :] * factor_ref[:quarter, :]
    pack_rows(sums.at[quarter:tiles], jnp.sum(rows[...], axis=1, keepdims=True))
    wait(late_loads)
    half = unit_rows(own_ref[...])[0].astype(BF16).astype(F32)
    inner = jnp.sum(half * back[...], axis=1, keepdims=True)
    pack_rows(sums.at[tiles : tiles + quarter], inner)
    parts = out_ref.shape[0]
    share = own // parts
    protos = 1.0 * out_ref.shape[0] * w_ref.shape[1]
    student = []
    for a in range(quarter):
        factor = to_column(factor_ref[quarter + a : quarter + a + 1, :] * protos)
        student.append(student_ref[a * LANES : (a + 1) * LANES, :] * factor)
    student = jnp.concatenate(student, axis=0).astype(BF16)
    terms = list(as_three(sums[...]))
    terms.append(jnp.zeros((sums.shape[0], out_ref.shape[2] - 3 * LANES), BF16))
    terms = jnp.concatenate(terms, axis=1)
    for p in range(parts):
        here = slice(p * share, (p + 1) * share)
        out_ref[p] = jnp.concatenate(
            [student[here, :], back[here, :].astype(BF16), terms], axis=0
        )
    for k in range(max(0, chunks - slots), chunks):
        store(k).wait()


def total_sums(message_ref, first):
    parts = message_ref.shape[0]
    each = [
        add_up([t.astype(F32) for t in lane_tiles(message_ref[p, first:, : 3 * LANES])[::-1]])
        for p in range(parts)
    ]
    return add_up(each)


def rows_kernel(tiles, protos, place_ref, s_hbm, message_ref, logs_ref, *refs):
    out_ref, loss_ref, sums_ref, weight, s_ref, sem = refs[-6:]
    parts = message_ref.shape[0]
    share, own = out_ref.shape[1], weight.shape[0]
    mine = pl.ds(pl.multiple_of(place_ref[1] * share, share), share)
    load = pltpu.make_async_copy(s_hbm.at[mine], s_ref, sem)
    load.start()
    quarter = own // LANES
    first = tiles // 2
    totals = total_sums(message_ref, 2 * share)
    sums_ref[...] = totals
    scale = 1.0 / totals[first : first + quarter, :]
    spread_rows(weight, scale)
    total = add_up([message_ref[p, :share, :].astype(F32) for p in range(parts)])
    paired = add_up([message_ref[p, share : 2 * share, :].astype(F32) for p in range(parts)])
    total = total - paired * (weight[mine, :1] * protos)
    load.wait()
    unit, length = unit_rows(s_ref[...])
    out_ref[0] = (total - unit * jnp.sum(unit * total, axis=-1, keepdims=True)) / length
    repeat(out_ref)
    height = logs_ref.shape[1] - 8
    logs = logs_ref[0, height + quarter : height + 2 * quarter, :]
    terms = logs / LOG2E - totals[tiles : tiles + quarter, :] * scale / TEMP_STUDENT
    loss_ref[...] = jnp.broadcast_to(jnp.sum(terms), loss_ref.shape)


def grad_kernel(counts, protos, exp_hbm, prob_hbm, feat_ref, scale_ref, sums_ref, factor_ref, *refs):
    parts = refs[: len(counts)]
    out_hbm, scaled, exp_ref, prob_ref, out, exp_sem, prob_sem, sem = refs[-8:]
    exp_loads = copies(exp_hbm, exp_ref, exp_sem)
    prob_loads = copies(prob_hbm, prob_ref, prob_sem)
    start(exp_loads, prob_loads)
    where = [(part, k) for count, part in zip(counts, parts) for k in range(count)]
    own = exp_ref.shape[1]
    tiles = (own + prob_ref.shape[1]) // LANES
    rows = protos / sums_ref[:tiles, :]
    for a in range(tiles):
        other = (a + tiles // 2) % tiles
        feat = feat_ref[:, other * LANES : (other + 1) * LANES].astype(F32)
        row = rows[a : a + 1, :]
        if a < own // LANES:
            row = row * factor_ref[a : a + 1, :]
        scaled[:, a * LANES : (a + 1) * LANES] = (feat * row).astype(BF16)
    stores = copies(out, out_hbm, sem)
    for k, store in enumerate(stores):
        exp_loads[k].wait()
        prob_loads[k].wait()
        paired = jnp.dot(scaled[:, :own], exp_ref[k], preferred_element_type=F32)
        paired = paired + jnp.dot(
            scaled[:, own:], prob_ref[k], preferred_element_type=F32
        )
        part, there = where[k]
        for t, tile in enumerate(lane_tiles(paired)):
            lanes = slice(k * WIDE + t * LANES, k * WIDE + (t + 1) * LANES)
            scale = scale_ref[lanes.start // LANES : lanes.stop // LANES, :]
            own_part = part[:, there * WIDE + t * LANES : there * WIDE + (t + 1) * LANES]
            out[:, lanes] = (own_part.astype(F32) - tile * scale).astype(BF16)
        store.start()
    for store in stores:
        store.wait()


SMEM = pl.BlockSpec(memory_space=pltpu.SMEM)
VMEM = pl.BlockSpec(memory_space=pltpu.VMEM)
ANY = pl.BlockSpec(memory_space=pl.ANY)


def params(nbytes):
    return pltpu.CompilerParams(vmem_limit_bytes=int(nbytes) + 8 * 2**20)


def cost(flops, nbytes, exps=0):
    return pl.CostEstimate(flops=int(flops), bytes_accessed=int(nbytes), transcendentals=int(exps))


def exchange(value, axis):
    return lax.all_to_all(value, axis, 0, 0)


def following(value, axis):
    n = lax.axis_size(axis)
    return [lax.ppermute(value, axis, [(i, (i - s) % n) for i in range(n)]) for s in range(1, n)]


def tree_sum(value, axis):
    n = lax.axis_size(axis)
    values = [value] + [
        lax.ppermute(value, axis, [(i, i ^ s) for i in range(n)]) for s in range(1, n)
    ]
    while len(values) > 1:
        values = [a + b for a, b in zip(values[::2], values[1::2])]
    return values[0]


def local(teacher_feats, student_feats, proto_weight):
    parts, groups = lax.axis_size("proto"), lax.axis_size("batch")
    own, width = teacher_feats.shape
    local_protos = proto_weight.shape[1]
    rows = own * groups
    others = rows - own
    protos = local_protos * parts
    feats = width // groups
    share = own // parts
    tiles = rows // LANES
    height = local_protos // LANES
    chunks = local_protos // WIDE
    place = jnp.stack([lax.axis_index("batch"), lax.axis_index("proto")]).astype(jnp.int32)
    struct = jax.ShapeDtypeStruct
    weight_bytes = 2 * width * local_protos
    exp_bytes = 2 * own * local_protos
    others_bytes = 2 * others * local_protos
    spread = pltpu.VMEM((own, LANES), F32)
    w_buffer = pltpu.VMEM((width, local_protos), BF16)
    exp_buffer = pltpu.VMEM((chunks, own, WIDE), BF16)
    sems = pltpu.SemaphoreType.DMA((chunks,))
    log_protos = math.log2(protos)
    token = struct((8, LANES), F32)

    def far(value):
        return pltpu.with_memory_space_constraint(value, pltpu.HBM)

    weight = far(proto_weight)
    teacher_rows, student_rows = far(teacher_feats), far(student_feats)
    s_all = following(student_feats, "batch")

    exps = pltpu.HBM((chunks, own, WIDE), BF16)
    t_exp, s_exp, stats = pl.pallas_call(
        stats_kernel,
        in_specs=[ANY] * 3,
        out_specs=[ANY, ANY, VMEM],
        out_shape=[
            exps,
            exps,
            struct((parts, 4 * own // LANES, LANES), F32),
        ],
        scratch_shapes=[
            pltpu.VMEM((2, own, width), BF16),
            w_buffer,
            pltpu.VMEM((2 * own, width), BF16),
            pltpu.VMEM((2, chunks, own, WIDE), BF16),
            pltpu.VMEM((2 * own, local_protos), F32),
            pltpu.VMEM((2 * own, LANES), F32),
            pltpu.VMEM((2 * own, LANES), F32),
            pltpu.SemaphoreType.DMA((2,)),
            sems, sems, sems,
        ],
        compiler_params=params(weight_bytes + 6 * exp_bytes),
        cost_estimate=cost(4 * own * width * local_protos, weight_bytes),
        name="own_rows",
    )(teacher_rows, student_rows, weight)
    t_exp, s_exp = far(t_exp), far(s_exp)

    back_student = pl.pallas_call(
        own_back_kernel,
        in_specs=[ANY] * 3,
        out_specs=VMEM,
        out_shape=struct((own, width), F32),
        scratch_shapes=[exp_buffer, w_buffer, sems, sems],
        compiler_params=params(weight_bytes + exp_bytes),
        cost_estimate=cost(2 * own * width * local_protos, weight_bytes),
        name="own_back",
    )(stats, s_exp, weight)

    stats = exchange(stats, "proto")

    first_shape = (1, height + 8, LANES)
    factor, cols = pl.pallas_call(
        first_column_kernel,
        in_specs=[SMEM, VMEM, ANY, ANY] + [ANY] * (groups - 1),
        out_specs=[VMEM, VMEM],
        out_shape=[token, struct(first_shape, F32)],
        scratch_shapes=[spread, exp_buffer, sems],
        compiler_params=params(exp_bytes),
        cost_estimate=cost(2 * own * local_protos, exp_bytes),
        name="first_columns",
    )(place, stats, t_exp, back_student, *s_all)

    unit, feat, scaled, t_unit = pl.pallas_call(
        functools.partial(student_rows_kernel, float(protos)),
        in_specs=[SMEM, VMEM, VMEM, VMEM] + [VMEM] * (groups - 1) + [ANY],
        out_specs=[VMEM] * 4,
        out_shape=[
            struct((others, width), BF16), struct((feats, rows), BF16), struct((feats, own), BF16),
            struct((own, width), BF16),
        ],
        scratch_shapes=[pltpu.VMEM((width, rows), BF16)],
        compiler_params=params(2 * rows * width),
        cost_estimate=cost(8 * rows * width, 2 * rows * width),
        name="student_rows",
    )(place, factor, teacher_feats, student_feats, *s_all, cols)
    t_all = following(t_unit, "batch")
    cols = [cols] + following(cols, "batch")
    logs = cols

    counts = [c * chunks // 8 for c in (1, 1, 1, 1, 4)]
    grad_parts = []

    def student_piece(before):
        turn = len(grad_parts)
        first, count = sum(counts[:turn]), counts[turn]
        grad_part, done = pl.pallas_call(
            functools.partial(student_kernel, log_protos, first, groups),
            in_specs=[VMEM] * 3 + [ANY] * 2 + [VMEM] * groups + [ANY],
            out_specs=[VMEM, VMEM],
            out_shape=[struct((feats, count * WIDE), BF16), token],
            scratch_shapes=[
                pltpu.VMEM((others, LANES), F32),
                pltpu.VMEM((others, WIDE), BF16),
                pltpu.VMEM((count, own, WIDE), BF16),
                pltpu.VMEM((width, count * WIDE), BF16),
            ]
            + [pltpu.SemaphoreType.DMA((count,))] * 2,
            compiler_params=params(16 * 2**20),
            cost_estimate=cost(2.5 * rows * width * WIDE * count, 2 * width * WIDE * count),
            name="student_side",
        )(unit, feat, scaled, s_exp, weight, *logs, before)
        grad_parts.append(grad_part)
        return done

    done = unit
    for turn in range(SWEEPS - 1):
        late = t_all if turn == 1 else []
        sums = pl.pallas_call(
            functools.partial(row_kernel, len(cols)),
            in_specs=[VMEM] * (len(cols) + 1) + [ANY] * (2 + len(late)),
            out_specs=VMEM,
            out_shape=struct((parts, 8, LANES), F32),
            scratch_shapes=[pltpu.VMEM((height, LANES), F32), spread, exp_buffer, sems],
            compiler_params=params(exp_bytes),
            cost_estimate=cost(2 * own * local_protos, exp_bytes),
            name="rows",
        )(*cols, factor, t_exp, done, *late)
        done = student_piece(sums)
        sums = exchange(sums, "proto")
        middle = turn < SWEEPS - 2
        cols = pl.pallas_call(
            column_kernel,
            in_specs=[VMEM, VMEM, ANY, ANY],
            out_specs=VMEM,
            out_shape=struct((groups if middle else 1, height, LANES), F32),
            scratch_shapes=[spread, exp_buffer, sems],
            compiler_params=params(exp_bytes),
            cost_estimate=cost(2 * own * local_protos, exp_bytes),
            name="columns",
        )(sums, factor, t_exp, done)
        done = student_piece(cols)
        if middle:
            cols = [exchange(cols, "batch")]
        else:
            cols = [cols] + following(cols, "batch")

    sum_rows = -(-(tiles + own // LANES) // 16) * 16
    message_shape = (parts, 2 * share + sum_rows, width)
    prob, col_scale, message = pl.pallas_call(
        functools.partial(last_kernel, groups),
        in_specs=[VMEM] + [ANY] * 4 + [VMEM] * (3 * groups - 1) + [ANY],
        out_specs=[ANY, VMEM, VMEM],
        out_shape=[
            pltpu.HBM((chunks, others, WIDE), BF16),
            struct((height, LANES), F32),
            struct(message_shape, BF16),
        ],
        scratch_shapes=[
            pltpu.VMEM((others, width), BF16),
            pltpu.VMEM((others, LANES), F32),
            pltpu.VMEM((others, LANES), F32),
            spread,
            pltpu.VMEM((own, width), F32),
            pltpu.VMEM((own, WIDE), BF16),
            pltpu.VMEM((sum_rows, LANES), F32),
            pltpu.VMEM((min(chunks, 3), others, WIDE), BF16),
            exp_buffer,
            w_buffer,
            pltpu.VMEM((own, width), BF16),
            pltpu.VMEM((own, width), F32),
            sems, sems, sems,
            pltpu.SemaphoreType.DMA((2,)),
        ],
        compiler_params=params(20 * 2**20 + weight_bytes + exp_bytes),
        cost_estimate=cost(2 * rows * width * local_protos, others_bytes),
        name="last_rows",
    )(
        factor, student_rows, far(back_student), t_exp, weight, *t_all, *logs, *cols, done,
    )
    done = student_piece(message)
    message = exchange(message, "proto")

    grad_rows, loss_part, sums = pl.pallas_call(
        functools.partial(rows_kernel, tiles, float(protos)),
        in_specs=[SMEM, ANY, VMEM, VMEM, ANY],
        out_specs=[VMEM] * 3,
        out_shape=[struct((parts, share, width), F32), token, struct((sum_rows, LANES), F32)],
        scratch_shapes=[spread, pltpu.VMEM((share, width), BF16), pltpu.SemaphoreType.DMA],
        compiler_params=params(0),
        name="row_grads",
    )(place, student_rows, message, logs[0], done)
    grad_rows = exchange(grad_rows, "proto").reshape(own, width)
    loss = tree_sum(loss_part, "batch")[0, 0] / rows

    grad_weight = pl.pallas_call(
        functools.partial(grad_kernel, counts, float(protos)),
        in_specs=[ANY] * 2 + [VMEM] * (4 + len(counts)),
        out_specs=ANY,
        out_shape=struct((feats, local_protos), BF16),
        scratch_shapes=[
            pltpu.VMEM((feats, rows), BF16),
            exp_buffer,
            pltpu.VMEM((chunks, others, WIDE), BF16),
            pltpu.VMEM((feats, local_protos), BF16),
            sems, sems, sems,
        ],
        compiler_params=params(exp_bytes + others_bytes + 4 * feats * local_protos),
        cost_estimate=cost(2 * feats * rows * local_protos, others_bytes),
        name="weight_grads",
    )(t_exp, far(prob), feat, col_scale, sums, factor, *grad_parts)
    return grad_weight, grad_rows, loss


def solution(mesh):
    return jax.shard_map(
        local,
        mesh=mesh,
        in_specs=(P("batch", None), P("batch", None), P(None, "proto")),
        out_specs=(P("batch", "proto"), P("batch", None), P()),
        check_vma=False,
    )
```

```python
import functools
import math

import jax
import jax.numpy as jnp
from jax import lax
from jax.experimental import pallas as pl
from jax.experimental.pallas import tpu as pltpu
from jax.sharding import PartitionSpec as P

SWEEPS = 3
TEMP_TEACHER = 0.04
TEMP_STUDENT = 0.1
LOG2E = math.log2(math.e)
SCALE_TEACHER = LOG2E / TEMP_TEACHER
SCALE_STUDENT = LOG2E / TEMP_STUDENT
LANES = 128
WIDE = 1024
TILE = 256
F32 = jnp.float32
BF16 = jnp.bfloat16


def unit_rows(values):
    wide = values.astype(F32)
    length = jnp.sqrt(jnp.sum(wide * wide, axis=-1, keepdims=True) + 1e-06)
    return wide / length, length


def diagonal():
    shape = (LANES, LANES)
    return lax.broadcasted_iota(jnp.int32, shape, 0) == lax.broadcasted_iota(jnp.int32, shape, 1)


def to_column(row):
    spread = jnp.where(diagonal(), jnp.broadcast_to(row, (LANES, LANES)), 0.0)
    return jnp.sum(spread, axis=1, keepdims=True)


def to_row(column):
    spread = jnp.where(diagonal(), jnp.broadcast_to(column, (LANES, LANES)), 0.0)
    return jnp.sum(spread, axis=0, keepdims=True)


def spread_rows(ref, rows):
    for a in range(rows.shape[0]):
        ref[a * LANES : (a + 1) * LANES, :] = jnp.broadcast_to(
            to_column(rows[a : a + 1, :]), (LANES, LANES)
        )


def pack_rows(ref, columns):
    for a in range(columns.shape[0] // LANES):
        ref[a : a + 1, :] = to_row(columns[a * LANES : (a + 1) * LANES, :])


def lane_tiles(values):
    return [values[:, t * LANES : (t + 1) * LANES] for t in range(values.shape[1] // LANES)]


def fold(values):
    return functools.reduce(jnp.add, lane_tiles(values))


def column_sums(values):
    rows, cols = values.shape
    return jnp.sum(values.reshape(rows // 8, 8, cols), axis=0)


def nt_dot(a, b):
    return lax.dot_general(a, b, (((1,), (1,)), ((), ())), preferred_element_type=F32)


def add_up(values):
    return functools.reduce(jnp.add, values)


def repeat(out_ref):
    for p in range(1, out_ref.shape[0]):
        out_ref[p] = out_ref[0]


def chunk(k):
    return slice(k * WIDE, (k + 1) * WIDE)


def copies(source, target, sems, first=0, back=0, count=None):
    def chunks(ref):
        return ref.shape[0] if len(ref.shape) == 3 else ref.shape[1] // WIDE

    count = count or min(chunks(source), chunks(target))
    return [copy_of(source, target, sems, k, first, back) for k in range(count)]


def columns_of(k, first=0, count=WIDE):
    return pl.ds(pl.multiple_of(k * WIDE + first, LANES), count)


def copy_of(source, target, sems, k, first=0, back=0):
    def part(ref, k):
        return ref.at[k] if len(ref.shape) == 3 else ref.at[:, columns_of(k)]

    return pltpu.make_async_copy(part(source, first + k), part(target, back + k), sems.at[k])


def start(*lists):
    for each in zip(*lists):
        for copy in each:
            copy.start()


def whole_copies(pairs, sems):
    return [pltpu.make_async_copy(a, b, sems.at[i]) for i, (a, b) in enumerate(pairs)]


def wait(*lists):
    for each in lists:
        for copy in each:
            copy.wait()


def stats_kernel(
    t_hbm, s_hbm, w_hbm, t_out, s_out, out_ref,
    raw, w_ref, unit, exps, logits, top, total, raw_sem, w_sem, t_sem, s_sem,
):
    own = raw.shape[1]
    quarter = out_ref.shape[1] // 4
    chunks = exps.shape[1]
    halves = (slice(0, own), slice(own, 2 * own))
    loads = copies(w_hbm, w_ref, w_sem)
    raw_loads = [
        pltpu.make_async_copy(ref, raw.at[which], raw_sem.at[which])
        for which, ref in enumerate((t_hbm, s_hbm))
    ]
    start(raw_loads, loads[:2])
    start(loads[2:])
    top[...] = jnp.full(top.shape, -1e30, F32)
    total[...] = jnp.zeros(total.shape, F32)
    wait(raw_loads)
    for which in range(2):
        unit[halves[which], :] = unit_rows(raw[which])[0].astype(BF16)

    @pl.loop(0, chunks)
    def _(k):
        copy_of(w_hbm, w_ref, w_sem, k).wait()
        for n in range(0, WIDE, TILE):
            here = columns_of(k, n, TILE)
            values = jnp.dot(unit[...], w_ref[:, here], preferred_element_type=F32)
            for half, scale in zip(halves, (SCALE_TEACHER, SCALE_STUDENT)):
                part = values[half, :] * scale
                logits[half, here] = part
                top[half, :] = functools.reduce(jnp.maximum, lane_tiles(part), top[half, :])

    peak = jnp.max(top[...], axis=1, keepdims=True)
    top[...] = jnp.broadcast_to(peak, top.shape)

    @pl.loop(0, chunks)
    def _(k):
        for which, (half, out, sem) in enumerate(zip(halves, (t_out, s_out), (t_sem, s_sem))):
            shift = top[half, :]
            for n in range(0, WIDE, TILE):
                tiles = lane_tiles(logits[half, columns_of(k, n, TILE)])
                tiles = [jnp.exp2(tile - shift) for tile in tiles]
                for t, tile in enumerate(tiles):
                    lanes = slice(n + t * LANES, n + (t + 1) * LANES)
                    exps[which, k, :, lanes] = tile.astype(BF16)
                total[half, :] += add_up(tiles)
            copy_of(exps.at[which], out, sem, k).start()

    sums = jnp.sum(total[...], axis=1, keepdims=True)
    for which, half in enumerate(halves):
        for k, column in enumerate((peak, sums)):
            first = (2 * which + k) * quarter
            pack_rows(out_ref.at[0, first : first + quarter], column[half, :])
    repeat(out_ref)
    wait(copies(exps.at[0], t_out, t_sem), copies(exps.at[1], s_out, s_sem))


def merged(stats_ref, which):
    parts, height, _ = stats_ref.shape
    quarter = height // 4
    first = 2 * which * quarter
    tops = [stats_ref[p, first : first + quarter, :] for p in range(parts)]
    top = functools.reduce(jnp.maximum, tops)
    sums = [
        stats_ref[p, first + quarter : first + 2 * quarter, :] * jnp.exp2(tops[p] - top)
        for p in range(parts)
    ]
    return top + jnp.log2(add_up(sums))


def column_pass(exp_hbm, exp_ref, sem, weight, out_ref):
    height = WIDE // LANES

    @pl.loop(0, exp_ref.shape[0])
    def _(k):
        copy_of(exp_hbm, exp_ref, sem, k).wait()
        sums = jnp.zeros((8, WIDE), F32)
        for g in range(0, exp_ref.shape[1], 16):
            shift = weight[g : g + 16, :]
            tiles = lane_tiles(exp_ref[k, g : g + 16, :].astype(F32))
            sums = sums + column_sums(jnp.concatenate([tile * shift for tile in tiles], axis=1))
        sums = jnp.sum(sums, axis=0, keepdims=True)
        block = jnp.concatenate(lane_tiles(sums), axis=0)
        for g in range(out_ref.shape[0]):
            out_ref[g, pl.ds(pl.multiple_of(k * height, height), height), :] = block


def first_column_kernel(place_ref, stats_ref, exp_hbm, *refs):
    factor_ref, out_ref, weight, exp_ref, sem = refs[-5:]
    start(copies(exp_hbm, exp_ref, sem))
    quarter = stats_ref.shape[1] // 4
    height = out_ref.shape[1] - 8
    own = stats_ref[pl.ds(place_ref[1], 1)][0]
    factor_ref[...] = jnp.zeros(factor_ref.shape, F32)
    rows = []
    for which in range(2):
        log_sum = merged(stats_ref, which)
        here = slice(which * quarter, (which + 1) * quarter)
        factor_ref[here, :] = jnp.exp2(
            own[2 * which * quarter : (2 * which + 1) * quarter, :] - log_sum
        )
        rows.append(log_sum)
    rows.append(jnp.zeros((8 - 2 * quarter, LANES), F32))
    logs = jnp.concatenate(rows, axis=0)
    for g in range(out_ref.shape[0]):
        out_ref[g, height:, :] = logs
    spread_rows(weight, factor_ref[:quarter, :])
    column_pass(exp_hbm, exp_ref, sem, weight, out_ref)


def column_kernel(sums_ref, factor_ref, exp_hbm, *refs):
    out_ref, weight, exp_ref, sem = refs[-4:]
    start(copies(exp_hbm, exp_ref, sem))
    quarter = weight.shape[0] // LANES
    scale = 1.0 / add_up([sums_ref[p, :quarter, :] for p in range(sums_ref.shape[0])])
    spread_rows(weight, scale * factor_ref[:quarter, :])
    column_pass(exp_hbm, exp_ref, sem, weight, out_ref)


def column_scales(cols, height):
    return 1.0 / add_up([ref[g, :height, :] for ref in cols for g in range(ref.shape[0])])


def chunk_scales(scales, k):
    height = WIDE // LANES
    return scales[pl.ds(pl.multiple_of(k * height, height), height), :]


def add_row_sums(rows, values, scale):
    for g in range(0, values.shape[0], 32):
        total = rows[g : g + 32, :]
        for t, tile in enumerate(lane_tiles(values[g : g + 32, :].astype(F32))):
            total = total + tile * scale[t : t + 1, :]
        rows[g : g + 32, :] = total


def row_kernel(count, *refs):
    cols, (factor_ref, exp_hbm) = refs[:count], refs[count : count + 2]
    out_ref, scales, rows, exp_ref, sem = refs[-5:]
    start(copies(exp_hbm, exp_ref, sem))
    scales[...] = column_scales(cols, scales.shape[0])
    rows[...] = jnp.zeros(rows.shape, F32)
    quarter = rows.shape[0] // LANES
    out_ref[0] = jnp.zeros(out_ref.shape[1:], F32)

    @pl.loop(0, exp_ref.shape[0])
    def _(k):
        copy_of(exp_hbm, exp_ref, sem, k).wait()
        add_row_sums(rows, exp_ref.at[k], chunk_scales(scales, k))

    pack_rows(out_ref.at[0, :quarter], jnp.sum(rows[...], axis=1, keepdims=True))
    out_ref[0, :quarter, :] = out_ref[0, :quarter, :] * factor_ref[:quarter, :]
    repeat(out_ref)


def own_back_kernel(before_ref, exp_hbm, w_hbm, back_ref, exp_ref, w_ref, exp_sem, w_sem):
    start(copies(exp_hbm, exp_ref, exp_sem), copies(w_hbm, w_ref, w_sem))
    back_ref[...] = jnp.zeros(back_ref.shape, F32)

    @pl.loop(0, exp_ref.shape[0])
    def _(k):
        copy_of(exp_hbm, exp_ref, exp_sem, k).wait()
        copy_of(w_hbm, w_ref, w_sem, k).wait()
        back_ref[...] += nt_dot(exp_ref[k], w_ref[:, columns_of(k)])


def relative_logs(logs, lse, which, shift=0.0):
    own = lse.shape[0] // (len(logs) - 1)
    quarter = own // LANES
    for g, ref in enumerate(logs[1:]):
        first = ref.shape[1] - 8 + which * quarter
        spread_rows(lse.at[g * own : (g + 1) * own], ref[0, first : first + quarter, :] - shift)


def student_rows_kernel(protos, place_ref, factor_ref, t_ref, own_ref, *refs):
    unit_ref, feat_ref, scaled_ref, t_unit, turned = refs[-5:]
    t_unit[...] = unit_rows(t_ref[...])[0].astype(BF16)
    own = own_ref.shape[0]
    groups = turned.shape[1] // own
    raw = refs[: groups - 1]
    quarter, feats = own // LANES, feat_ref.shape[0]
    for g in range(groups):
        half = unit_rows((raw[g - 1] if g else own_ref)[...])[0].astype(BF16)
        if g:
            unit_ref[(g - 1) * own : g * own, :] = half
        half = half.astype(F32)
        for a in range(0, own, LANES):
            first = g * own + a
            turned[:, first : first + LANES] = jnp.transpose(half[a : a + LANES, :]).astype(BF16)
    feat = turned[pl.ds(pl.multiple_of(place_ref[0] * feats, feats), feats), :]
    feat_ref[...] = feat
    for a in range(quarter):
        lanes = slice(a * LANES, (a + 1) * LANES)
        factor = factor_ref[quarter + a : quarter + a + 1, :] * protos
        scaled_ref[:, lanes] = (feat[:, lanes].astype(F32) * factor).astype(BF16)


def probabilities(unit, w_ref, k, lse, scale, use):
    for n in range(0, WIDE, TILE):
        logits = jnp.dot(
            unit[...], w_ref[:, columns_of(k, n, TILE)], preferred_element_type=F32
        )
        shift = lse[...]
        use(n, [jnp.exp2(tile * scale - shift) for tile in lane_tiles(logits)])


def student_kernel(
    log_protos, first, count, groups, unit, feat_ref, scaled_ref, exp_hbm, w_hbm, *refs
):
    logs = refs[:groups]
    if count > 1:
        grad_hbm, token_ref, lse, prob, exp_ref, w_ref, exp_sem, w_sem, grad, grad_sem = refs[-10:]
    else:
        grad, token_ref, lse, prob, exp_ref, w_ref, exp_sem, w_sem = refs[-8:]
    own = exp_ref.shape[1]
    exp_loads = copies(exp_hbm, exp_ref, exp_sem, first, 0, count)
    w_loads = copies(w_hbm, w_ref, w_sem, first, 0, count)
    start(w_loads, exp_loads)
    token_ref[...] = jnp.zeros(token_ref.shape, F32)
    relative_logs(logs, lse, 1, log_protos)

    @pl.loop(0, count)
    def _(k):
        copy_of(w_hbm, w_ref, w_sem, k, first).wait()

        def use(n, tiles):
            for t, tile in enumerate(tiles):
                prob[:, n + t * LANES : n + (t + 1) * LANES] = tile.astype(BF16)

        probabilities(unit, w_ref, k, lse, SCALE_STUDENT, use)
        copy_of(exp_hbm, exp_ref, exp_sem, k, first).wait()
        values = jnp.dot(scaled_ref[...], exp_ref[k], preferred_element_type=F32)
        values = values + jnp.dot(feat_ref[:, own:], prob[...], preferred_element_type=F32)
        grad[:, columns_of(k)] = values.astype(BF16)
        if count > 1:
            copy_of(grad, grad_hbm, grad_sem, k).start()

    if count > 1:
        wait(copies(grad, grad_hbm, grad_sem))


def as_three(value):
    high = value.astype(BF16)
    rest = value - high.astype(F32)
    middle = rest.astype(BF16)
    return high, middle, (rest - middle.astype(F32)).astype(BF16)


def last_kernel(groups, factor_ref, own_hbm, student_hbm, exp_hbm, w_hbm, *refs):
    units, refs = refs[: groups - 1], refs[groups - 1 :]
    logs, cols, refs = refs[:groups], refs[groups : 2 * groups], refs[2 * groups :]
    (
        prob_hbm, scale_ref, out_ref, unit, lse, rows, own_rows, back, scaled, sums, prob_ref,
        exp_ref, w_ref, own_ref, student_ref, prob_sem, exp_sem, w_sem, sem,
    ) = refs[-19:]
    w_loads, exp_loads = copies(w_hbm, w_ref, w_sem), copies(exp_hbm, exp_ref, exp_sem)
    late_loads = whole_copies([(own_hbm, own_ref), (student_hbm, student_ref)], sem)
    start(w_loads, exp_loads)
    start(late_loads)
    slots, others, _ = prob_ref.shape
    own, chunks = exp_ref.shape[1], exp_ref.shape[0]
    tiles = (own + others) // LANES
    quarter = own // LANES
    scale_ref[...] = column_scales(cols, scale_ref.shape[0])
    rows[...] = jnp.zeros(rows.shape, F32)
    own_rows[...] = jnp.zeros(own_rows.shape, F32)
    back[...] = jnp.zeros(back.shape, F32)
    relative_logs(logs, lse, 0)
    for g in range(groups - 1):
        unit[g * own : (g + 1) * own, :] = units[g][...]
    partner = slice((groups // 2 - 1) * own, groups // 2 * own)

    def store(k):
        return pltpu.make_async_copy(prob_ref.at[lax.rem(k, slots)], prob_hbm.at[k], prob_sem.at[k])

    @pl.loop(0, chunks)
    def _(k):
        copy_of(w_hbm, w_ref, w_sem, k).wait()
        slot = lax.rem(k, slots)
        scale = chunk_scales(scale_ref, k)

        @pl.when(k >= slots)
        def _():
            store(k - slots).wait()

        def use(n, tiles):
            for t, tile in enumerate(tiles):
                prob_ref[slot, :, n + t * LANES : n + (t + 1) * LANES] = tile.astype(BF16)
            first = n // LANES
            tiles = [tile * scale[first + t : first + t + 1, :] for t, tile in enumerate(tiles)]
            rows[...] += add_up(tiles)
            for t, tile in enumerate(tiles):
                scaled[:, n + t * LANES : n + (t + 1) * LANES] = tile[partner, :].astype(BF16)

        probabilities(unit, w_ref, k, lse, SCALE_TEACHER, use)
        store(k).start()
        back[...] += nt_dot(scaled[...], w_ref[:, columns_of(k)])
        copy_of(exp_hbm, exp_ref, exp_sem, k).wait()
        add_row_sums(own_rows, exp_ref.at[k], scale)

    sums[...] = jnp.zeros(sums.shape, F32)
    pack_rows(sums.at[:quarter], jnp.sum(own_rows[...], axis=1, keepdims=True))
    sums[:quarter, :] = sums[:quarter, :] * factor_ref[:quarter, :]
    pack_rows(sums.at[quarter:tiles], jnp.sum(rows[...], axis=1, keepdims=True))
    wait(late_loads)
    half = unit_rows(own_ref[...])[0].astype(BF16).astype(F32)
    inner = jnp.sum(half * back[...], axis=1, keepdims=True)
    pack_rows(sums.at[tiles : tiles + quarter], inner)
    parts = out_ref.shape[0]
    share = own // parts
    protos = 1.0 * out_ref.shape[0] * w_ref.shape[1]
    student = []
    for a in range(quarter):
        factor = to_column(factor_ref[quarter + a : quarter + a + 1, :] * protos)
        student.append(student_ref[a * LANES : (a + 1) * LANES, :] * factor)
    student = jnp.concatenate(student, axis=0).astype(BF16)
    terms = list(as_three(sums[...]))
    terms.append(jnp.zeros((sums.shape[0], out_ref.shape[2] - 3 * LANES), BF16))
    terms = jnp.concatenate(terms, axis=1)
    for p in range(parts):
        here = slice(p * share, (p + 1) * share)
        out_ref[p] = jnp.concatenate(
            [student[here, :], back[here, :].astype(BF16), terms], axis=0
        )
    for k in range(max(0, chunks - slots), chunks):
        store(k).wait()


def total_sums(message_ref, first):
    parts = message_ref.shape[0]
    each = [
        add_up([t.astype(F32) for t in lane_tiles(message_ref[p, first:, : 3 * LANES])[::-1]])
        for p in range(parts)
    ]
    return add_up(each)


def rows_kernel(tiles, protos, place_ref, s_hbm, message_ref, logs_ref, *refs):
    out_ref, loss_ref, sums_ref, weight, s_ref, sem = refs[-6:]
    parts = message_ref.shape[0]
    share, own = out_ref.shape[1], weight.shape[0]
    mine = pl.ds(pl.multiple_of(place_ref[1] * share, share), share)
    load = pltpu.make_async_copy(s_hbm.at[mine], s_ref, sem)
    load.start()
    quarter = own // LANES
    first = tiles // 2
    totals = total_sums(message_ref, 2 * share)
    sums_ref[...] = totals
    scale = 1.0 / totals[first : first + quarter, :]
    spread_rows(weight, scale)
    total = add_up([message_ref[p, :share, :].astype(F32) for p in range(parts)])
    paired = add_up([message_ref[p, share : 2 * share, :].astype(F32) for p in range(parts)])
    total = total - paired * (weight[mine, :1] * protos)
    load.wait()
    unit, length = unit_rows(s_ref[...])
    out_ref[0] = (total - unit * jnp.sum(unit * total, axis=-1, keepdims=True)) / length
    repeat(out_ref)
    height = logs_ref.shape[1] - 8
    logs = logs_ref[0, height + quarter : height + 2 * quarter, :]
    terms = logs / LOG2E - totals[tiles : tiles + quarter, :] * scale / TEMP_STUDENT
    loss_ref[...] = jnp.broadcast_to(jnp.sum(terms), loss_ref.shape)


def grad_kernel(
    counts, protos, rows_all, exp_hbm, prob_hbm, feat_ref, scale_ref, sums_ref, factor_ref, *refs
):
    parts, losses = refs[: len(counts)], refs[len(counts) : -11]
    (
        out_hbm, loss_ref, scaled, exp_ref, prob_ref, out, last_ref, exp_sem, prob_sem, sem, last_sem,
    ) = refs[-11:]
    last_load = pltpu.make_async_copy(parts[-1], last_ref, last_sem)
    parts = (*parts[:-1], last_ref)
    exp_loads = copies(exp_hbm, exp_ref, exp_sem)
    prob_loads = copies(prob_hbm, prob_ref, prob_sem)
    early = sum(counts[:-1])
    start(exp_loads[:early], prob_loads[:early])
    last_load.start()
    start(exp_loads[early:], prob_loads[early:])
    losses = [ref[0:1, 0:1] for ref in losses]
    while len(losses) > 1:
        losses = [a + b for a, b in zip(losses[::2], losses[1::2])]
    loss_ref[...] = losses[0] / rows_all
    where = [(part, k) for count, part in zip(counts, parts) for k in range(count)]
    own = exp_ref.shape[1]
    tiles = (own + prob_ref.shape[1]) // LANES
    rows = protos / sums_ref[:tiles, :]
    for a in range(tiles):
        other = (a + tiles // 2) % tiles
        feat = feat_ref[:, other * LANES : (other + 1) * LANES].astype(F32)
        row = rows[a : a + 1, :]
        if a < own // LANES:
            row = row * factor_ref[a : a + 1, :]
        scaled[:, a * LANES : (a + 1) * LANES] = (feat * row).astype(BF16)
    stores = copies(out, out_hbm, sem)
    for k, store in enumerate(stores):
        exp_loads[k].wait()
        prob_loads[k].wait()
        paired = jnp.dot(scaled[:, :own], exp_ref[k], preferred_element_type=F32)
        paired = paired + jnp.dot(
            scaled[:, own:], prob_ref[k], preferred_element_type=F32
        )
        part, there = where[k]
        if part is last_ref and there == 0:
            last_load.wait()
        for t, tile in enumerate(lane_tiles(paired)):
            lanes = slice(k * WIDE + t * LANES, k * WIDE + (t + 1) * LANES)
            scale = scale_ref[lanes.start // LANES : lanes.stop // LANES, :]
            own_part = part[:, there * WIDE + t * LANES : there * WIDE + (t + 1) * LANES]
            out[:, lanes] = (own_part.astype(F32) - tile * scale).astype(BF16)
        store.start()
    for store in stores:
        store.wait()


SMEM = pl.BlockSpec(memory_space=pltpu.SMEM)
VMEM = pl.BlockSpec(memory_space=pltpu.VMEM)
ANY = pl.BlockSpec(memory_space=pl.ANY)


def params(nbytes):
    return pltpu.CompilerParams(vmem_limit_bytes=int(nbytes) + 8 * 2**20)


def cost(flops, nbytes, exps=0):
    return pl.CostEstimate(flops=int(flops), bytes_accessed=int(nbytes), transcendentals=int(exps))


def exchange(value, axis):
    return lax.all_to_all(value, axis, 0, 0)


def following(value, axis):
    n = lax.axis_size(axis)
    return [lax.ppermute(value, axis, [(i, (i - s) % n) for i in range(n)]) for s in range(1, n)]


def swapped(value, axis):
    n = lax.axis_size(axis)
    return [value] + [
        lax.ppermute(value, axis, [(i, i ^ s) for i in range(n)]) for s in range(1, n)
    ]


def local(teacher_feats, student_feats, proto_weight):
    parts, groups = lax.axis_size("proto"), lax.axis_size("batch")
    own, width = teacher_feats.shape
    local_protos = proto_weight.shape[1]
    rows = own * groups
    others = rows - own
    protos = local_protos * parts
    feats = width // groups
    share = own // parts
    tiles = rows // LANES
    height = local_protos // LANES
    chunks = local_protos // WIDE
    place = jnp.stack([lax.axis_index("batch"), lax.axis_index("proto")]).astype(jnp.int32)
    struct = jax.ShapeDtypeStruct
    weight_bytes = 2 * width * local_protos
    exp_bytes = 2 * own * local_protos
    others_bytes = 2 * others * local_protos
    spread = pltpu.VMEM((own, LANES), F32)
    w_buffer = pltpu.VMEM((width, local_protos), BF16)
    exp_buffer = pltpu.VMEM((chunks, own, WIDE), BF16)
    sems = pltpu.SemaphoreType.DMA((chunks,))
    log_protos = math.log2(protos)
    token = struct((8, LANES), F32)

    def far(value):
        return pltpu.with_memory_space_constraint(value, pltpu.HBM)

    weight = far(proto_weight)
    teacher_rows, student_rows = far(teacher_feats), far(student_feats)
    s_all = following(student_feats, "batch")

    exps = pltpu.HBM((chunks, own, WIDE), BF16)
    t_exp, s_exp, stats = pl.pallas_call(
        stats_kernel,
        in_specs=[ANY] * 3,
        out_specs=[ANY, ANY, VMEM],
        out_shape=[
            exps,
            exps,
            struct((parts, 4 * own // LANES, LANES), F32),
        ],
        scratch_shapes=[
            pltpu.VMEM((2, own, width), BF16),
            w_buffer,
            pltpu.VMEM((2 * own, width), BF16),
            pltpu.VMEM((2, chunks, own, WIDE), BF16),
            pltpu.VMEM((2 * own, local_protos), F32),
            pltpu.VMEM((2 * own, LANES), F32),
            pltpu.VMEM((2 * own, LANES), F32),
            pltpu.SemaphoreType.DMA((2,)),
            sems, sems, sems,
        ],
        compiler_params=params(weight_bytes + 6 * exp_bytes),
        cost_estimate=cost(4 * own * width * local_protos, weight_bytes),
        name="own_rows",
    )(teacher_rows, student_rows, weight)
    t_exp, s_exp = far(t_exp), far(s_exp)

    back_student = pl.pallas_call(
        own_back_kernel,
        in_specs=[ANY] * 3,
        out_specs=VMEM,
        out_shape=struct((own, width), F32),
        scratch_shapes=[exp_buffer, w_buffer, sems, sems],
        compiler_params=params(weight_bytes + exp_bytes),
        cost_estimate=cost(2 * own * width * local_protos, weight_bytes),
        name="own_back",
    )(stats, s_exp, weight)

    stats = exchange(stats, "proto")

    first_shape = (1, height + 8, LANES)
    factor, cols = pl.pallas_call(
        first_column_kernel,
        in_specs=[SMEM, VMEM, ANY, ANY] + [ANY] * (groups - 1),
        out_specs=[VMEM, VMEM],
        out_shape=[token, struct(first_shape, F32)],
        scratch_shapes=[spread, exp_buffer, sems],
        compiler_params=params(exp_bytes),
        cost_estimate=cost(2 * own * local_protos, exp_bytes),
        name="first_columns",
    )(place, stats, t_exp, back_student, *s_all)

    unit, feat, scaled, t_unit = pl.pallas_call(
        functools.partial(student_rows_kernel, float(protos)),
        in_specs=[SMEM, VMEM, VMEM, VMEM] + [VMEM] * (groups - 1) + [ANY],
        out_specs=[VMEM] * 4,
        out_shape=[
            struct((others, width), BF16), struct((feats, rows), BF16), struct((feats, own), BF16),
            struct((own, width), BF16),
        ],
        scratch_shapes=[pltpu.VMEM((width, rows), BF16)],
        compiler_params=params(2 * rows * width),
        cost_estimate=cost(8 * rows * width, 2 * rows * width),
        name="student_rows",
    )(place, factor, teacher_feats, student_feats, *s_all, cols)
    t_all = following(t_unit, "batch")
    cols = [cols] + following(cols, "batch")
    logs = cols

    counts = [c * chunks // 8 for c in (1, 1, 1, 1, 4)]
    grad_parts = []

    def student_piece(before):
        turn = len(grad_parts)
        first, count = sum(counts[:turn]), counts[turn]
        grad_part, done = pl.pallas_call(
            functools.partial(student_kernel, log_protos, first, count, groups),
            in_specs=[VMEM] * 3 + [ANY] * 2 + [VMEM] * groups + [ANY],
            out_specs=[ANY if count > 1 else VMEM, VMEM],
            out_shape=[
                (pltpu.HBM if count > 1 else struct)((feats, count * WIDE), BF16), token,
            ],
            scratch_shapes=[
                pltpu.VMEM((others, LANES), F32),
                pltpu.VMEM((others, WIDE), BF16),
                pltpu.VMEM((count, own, WIDE), BF16),
                pltpu.VMEM((width, count * WIDE), BF16),
            ]
            + [pltpu.SemaphoreType.DMA((count,))] * 2
            + ([pltpu.VMEM((feats, count * WIDE), BF16)] if count > 1 else [])
            + ([pltpu.SemaphoreType.DMA((count,))] if count > 1 else []),
            compiler_params=params(16 * 2**20),
            cost_estimate=cost(2.5 * rows * width * WIDE * count, 2 * width * WIDE * count),
            name="student_side",
        )(unit, feat, scaled, s_exp, weight, *logs, before)
        grad_parts.append(far(grad_part) if count > 1 else grad_part)
        return done

    done = unit
    for turn in range(SWEEPS - 1):
        late = t_all if turn == 1 else []
        sums = pl.pallas_call(
            functools.partial(row_kernel, len(cols)),
            in_specs=[VMEM] * (len(cols) + 1) + [ANY] * (2 + len(late)),
            out_specs=VMEM,
            out_shape=struct((parts, 8, LANES), F32),
            scratch_shapes=[pltpu.VMEM((height, LANES), F32), spread, exp_buffer, sems],
            compiler_params=params(exp_bytes),
            cost_estimate=cost(2 * own * local_protos, exp_bytes),
            name="rows",
        )(*cols, factor, t_exp, done, *late)
        done = student_piece(sums)
        sums = exchange(sums, "proto")
        cols = pl.pallas_call(
            column_kernel,
            in_specs=[VMEM, VMEM, ANY, ANY],
            out_specs=VMEM,
            out_shape=struct((1, height, LANES), F32),
            scratch_shapes=[spread, exp_buffer, sems],
            compiler_params=params(exp_bytes),
            cost_estimate=cost(2 * own * local_protos, exp_bytes),
            name="columns",
        )(sums, factor, t_exp, done)
        done = student_piece(cols)
        cols = [cols] + following(cols, "batch")

    sum_rows = -(-(tiles + own // LANES) // 16) * 16
    message_shape = (parts, 2 * share + sum_rows, width)
    prob, col_scale, message = pl.pallas_call(
        functools.partial(last_kernel, groups),
        in_specs=[VMEM] + [ANY] * 4 + [VMEM] * (3 * groups - 1) + [ANY],
        out_specs=[ANY, VMEM, VMEM],
        out_shape=[
            pltpu.HBM((chunks, others, WIDE), BF16),
            struct((height, LANES), F32),
            struct(message_shape, BF16),
        ],
        scratch_shapes=[
            pltpu.VMEM((others, width), BF16),
            pltpu.VMEM((others, LANES), F32),
            pltpu.VMEM((others, LANES), F32),
            spread,
            pltpu.VMEM((own, width), F32),
            pltpu.VMEM((own, WIDE), BF16),
            pltpu.VMEM((sum_rows, LANES), F32),
            pltpu.VMEM((min(chunks, 3), others, WIDE), BF16),
            exp_buffer,
            w_buffer,
            pltpu.VMEM((own, width), BF16),
            pltpu.VMEM((own, width), F32),
            sems, sems, sems,
            pltpu.SemaphoreType.DMA((2,)),
        ],
        compiler_params=params(20 * 2**20 + weight_bytes + exp_bytes),
        cost_estimate=cost(2 * rows * width * local_protos, others_bytes),
        name="last_rows",
    )(
        factor, student_rows, far(back_student), t_exp, weight, *t_all, *logs, *cols, done,
    )
    done = student_piece(message)
    message = exchange(message, "proto")

    grad_rows, loss_part, sums = pl.pallas_call(
        functools.partial(rows_kernel, tiles, float(protos)),
        in_specs=[SMEM, ANY, VMEM, VMEM, ANY],
        out_specs=[VMEM] * 3,
        out_shape=[struct((parts, share, width), F32), token, struct((sum_rows, LANES), F32)],
        scratch_shapes=[spread, pltpu.VMEM((share, width), BF16), pltpu.SemaphoreType.DMA],
        compiler_params=params(0),
        name="row_grads",
    )(place, student_rows, message, logs[0], done)
    grad_rows = exchange(grad_rows, "proto").reshape(own, width)
    losses = swapped(loss_part, "batch")

    grad_weight, loss = pl.pallas_call(
        functools.partial(grad_kernel, counts, float(protos), float(rows)),
        in_specs=[ANY] * 2 + [VMEM] * (3 + len(counts)) + [ANY] + [VMEM] * groups,
        out_specs=[ANY, VMEM],
        out_shape=[struct((feats, local_protos), BF16), struct((1, 1), F32)],
        scratch_shapes=[
            pltpu.VMEM((feats, rows), BF16),
            exp_buffer,
            pltpu.VMEM((chunks, others, WIDE), BF16),
            pltpu.VMEM((feats, local_protos), BF16),
            pltpu.VMEM((feats, counts[-1] * WIDE), BF16),
            sems, sems, sems,
            pltpu.SemaphoreType.DMA,
        ],
        compiler_params=params(exp_bytes + others_bytes + 4 * feats * local_protos),
        cost_estimate=cost(2 * feats * rows * local_protos, others_bytes),
        name="weight_grads",
    )(t_exp, far(prob), feat, col_scale, sums, factor, *grad_parts, *losses)
    return grad_weight, grad_rows, loss.reshape(())


def solution(mesh):
    return jax.shard_map(
        local,
        mesh=mesh,
        in_specs=(P("batch", None), P("batch", None), P(None, "proto")),
        out_specs=(P("batch", "proto"), P("batch", None), P()),
        check_vma=False,
    )
```

```python
import functools
import math

import jax
import jax.numpy as jnp
from jax import lax
from jax.experimental import pallas as pl
from jax.experimental.pallas import tpu as pltpu
from jax.sharding import PartitionSpec as P

SWEEPS = 3
TEMP_TEACHER = 0.04
TEMP_STUDENT = 0.1
LOG2E = math.log2(math.e)
SCALE_TEACHER = LOG2E / TEMP_TEACHER
SCALE_STUDENT = LOG2E / TEMP_STUDENT
LANES = 128
WIDE = 1024
SERIES = (0.00093768624, 0.0091820806, 0.055269409, 0.24016587, 0.6931408, 0.99999982)
TILE = 256
F32 = jnp.float32
BF16 = jnp.bfloat16


def unit_rows(values):
    wide = values.astype(F32)
    length = jnp.sqrt(jnp.sum(wide * wide, axis=-1, keepdims=True) + 1e-06)
    return wide / length, length


def diagonal():
    shape = (LANES, LANES)
    return lax.broadcasted_iota(jnp.int32, shape, 0) == lax.broadcasted_iota(jnp.int32, shape, 1)


def to_column(row):
    spread = jnp.where(diagonal(), jnp.broadcast_to(row, (LANES, LANES)), 0.0)
    return jnp.sum(spread, axis=1, keepdims=True)


def to_row(column):
    spread = jnp.where(diagonal(), jnp.broadcast_to(column, (LANES, LANES)), 0.0)
    return jnp.sum(spread, axis=0, keepdims=True)


def spread_rows(ref, rows):
    for a in range(rows.shape[0]):
        ref[a * LANES : (a + 1) * LANES, :] = jnp.broadcast_to(
            to_column(rows[a : a + 1, :]), (LANES, LANES)
        )


def pack_rows(ref, columns):
    for a in range(columns.shape[0] // LANES):
        ref[a : a + 1, :] = to_row(columns[a * LANES : (a + 1) * LANES, :])


def lane_tiles(values):
    return [values[:, t * LANES : (t + 1) * LANES] for t in range(values.shape[1] // LANES)]


def fold(values):
    return functools.reduce(jnp.add, lane_tiles(values))


def column_sums(values):
    rows, cols = values.shape
    return jnp.sum(values.reshape(rows // 8, 8, cols), axis=0)


def nt_dot(a, b):
    return lax.dot_general(a, b, (((1,), (1,)), ((), ())), preferred_element_type=F32)


def exp2_by_squares(x):
    y = jnp.maximum(x, -127.0) * (1.0 / 128.0)
    value = SERIES[0]
    for term in SERIES[1:]:
        value = value * y + term
    for _ in range(7):
        value = value * value
    return value


def add_up(values):
    return functools.reduce(jnp.add, values)


def repeat(out_ref):
    for p in range(1, out_ref.shape[0]):
        out_ref[p] = out_ref[0]


def chunk(k):
    return slice(k * WIDE, (k + 1) * WIDE)


def copies(source, target, sems, first=0, back=0, count=None):
    def chunks(ref):
        return ref.shape[0] if len(ref.shape) == 3 else ref.shape[1] // WIDE

    count = count or min(chunks(source), chunks(target))
    return [copy_of(source, target, sems, k, first, back) for k in range(count)]


def columns_of(k, first=0, count=WIDE):
    return pl.ds(pl.multiple_of(k * WIDE + first, LANES), count)


def copy_of(source, target, sems, k, first=0, back=0):
    def part(ref, k):
        return ref.at[k] if len(ref.shape) == 3 else ref.at[:, columns_of(k)]

    return pltpu.make_async_copy(part(source, first + k), part(target, back + k), sems.at[k])


def start(*lists):
    for each in zip(*lists):
        for copy in each:
            copy.start()


def whole_copies(pairs, sems):
    return [pltpu.make_async_copy(a, b, sems.at[i]) for i, (a, b) in enumerate(pairs)]


def wait(*lists):
    for each in lists:
        for copy in each:
            copy.wait()


def stats_kernel(
    t_hbm, s_hbm, w_hbm, t_out, s_out, out_ref,
    raw, w_ref, unit, exps, logits, top, total, raw_sem, w_sem, t_sem, s_sem,
):
    own = raw.shape[1]
    quarter = out_ref.shape[1] // 4
    chunks = exps.shape[1]
    halves = (slice(0, own), slice(own, 2 * own))
    loads = copies(w_hbm, w_ref, w_sem)
    raw_loads = [
        pltpu.make_async_copy(ref, raw.at[which], raw_sem.at[which])
        for which, ref in enumerate((t_hbm, s_hbm))
    ]
    start(raw_loads, loads[:2])
    start(loads[2:])
    top[...] = jnp.full(top.shape, -1e30, F32)
    total[...] = jnp.zeros(total.shape, F32)
    wait(raw_loads)
    for which in range(2):
        unit[halves[which], :] = unit_rows(raw[which])[0].astype(BF16)

    @pl.loop(0, chunks)
    def _(k):
        copy_of(w_hbm, w_ref, w_sem, k).wait()
        for n in range(0, WIDE, TILE):
            here = columns_of(k, n, TILE)
            values = jnp.dot(unit[...], w_ref[:, here], preferred_element_type=F32)
            for half, scale in zip(halves, (SCALE_TEACHER, SCALE_STUDENT)):
                part = values[half, :] * scale
                logits[half, here] = part
                top[half, :] = functools.reduce(jnp.maximum, lane_tiles(part), top[half, :])

    peak = jnp.max(top[...], axis=1, keepdims=True)
    top[...] = jnp.broadcast_to(peak, top.shape)

    @pl.loop(0, chunks)
    def _(k):
        for which, (half, out, sem) in enumerate(zip(halves, (t_out, s_out), (t_sem, s_sem))):
            shift = top[half, :]
            for n in range(0, WIDE, TILE):
                tiles = lane_tiles(logits[half, columns_of(k, n, TILE)])
                tiles = [jnp.exp2(tile - shift) for tile in tiles]
                for t, tile in enumerate(tiles):
                    lanes = slice(n + t * LANES, n + (t + 1) * LANES)
                    exps[which, k, :, lanes] = tile.astype(BF16)
                total[half, :] += add_up(tiles)
            copy_of(exps.at[which], out, sem, k).start()

    sums = jnp.sum(total[...], axis=1, keepdims=True)
    for which, half in enumerate(halves):
        for k, column in enumerate((peak, sums)):
            first = (2 * which + k) * quarter
            pack_rows(out_ref.at[0, first : first + quarter], column[half, :])
    repeat(out_ref)
    wait(copies(exps.at[0], t_out, t_sem), copies(exps.at[1], s_out, s_sem))


def merged(stats_ref, which):
    parts, height, _ = stats_ref.shape
    quarter = height // 4
    first = 2 * which * quarter
    tops = [stats_ref[p, first : first + quarter, :] for p in range(parts)]
    top = functools.reduce(jnp.maximum, tops)
    sums = [
        stats_ref[p, first + quarter : first + 2 * quarter, :] * jnp.exp2(tops[p] - top)
        for p in range(parts)
    ]
    return top + jnp.log2(add_up(sums))


def column_pass(exp_hbm, exp_ref, sem, weight, out_ref):
    height = WIDE // LANES

    @pl.loop(0, exp_ref.shape[0])
    def _(k):
        copy_of(exp_hbm, exp_ref, sem, k).wait()
        sums = jnp.zeros((8, WIDE), F32)
        for g in range(0, exp_ref.shape[1], 16):
            shift = weight[g : g + 16, :]
            tiles = lane_tiles(exp_ref[k, g : g + 16, :].astype(F32))
            sums = sums + column_sums(jnp.concatenate([tile * shift for tile in tiles], axis=1))
        sums = jnp.sum(sums, axis=0, keepdims=True)
        block = jnp.concatenate(lane_tiles(sums), axis=0)
        for g in range(out_ref.shape[0]):
            out_ref[g, pl.ds(pl.multiple_of(k * height, height), height), :] = block


def first_column_kernel(place_ref, stats_ref, exp_hbm, *refs):
    factor_ref, out_ref, weight, exp_ref, sem = refs[-5:]
    start(copies(exp_hbm, exp_ref, sem))
    quarter = stats_ref.shape[1] // 4
    height = out_ref.shape[1] - 8
    own = stats_ref[pl.ds(place_ref[1], 1)][0]
    factor_ref[...] = jnp.zeros(factor_ref.shape, F32)
    rows = []
    for which in range(2):
        log_sum = merged(stats_ref, which)
        here = slice(which * quarter, (which + 1) * quarter)
        factor_ref[here, :] = jnp.exp2(
            own[2 * which * quarter : (2 * which + 1) * quarter, :] - log_sum
        )
        rows.append(log_sum)
    rows.append(jnp.zeros((8 - 2 * quarter, LANES), F32))
    logs = jnp.concatenate(rows, axis=0)
    for g in range(out_ref.shape[0]):
        out_ref[g, height:, :] = logs
    spread_rows(weight, factor_ref[:quarter, :])
    column_pass(exp_hbm, exp_ref, sem, weight, out_ref)


def column_kernel(sums_ref, factor_ref, exp_hbm, *refs):
    out_ref, weight, exp_ref, sem = refs[-4:]
    start(copies(exp_hbm, exp_ref, sem))
    quarter = weight.shape[0] // LANES
    scale = 1.0 / add_up([sums_ref[p, :quarter, :] for p in range(sums_ref.shape[0])])
    spread_rows(weight, scale * factor_ref[:quarter, :])
    column_pass(exp_hbm, exp_ref, sem, weight, out_ref)


def column_scales(cols, height):
    return 1.0 / add_up([ref[g, :height, :] for ref in cols for g in range(ref.shape[0])])


def chunk_scales(scales, k):
    height = WIDE // LANES
    return scales[pl.ds(pl.multiple_of(k * height, height), height), :]


def add_row_sums(rows, values, scale):
    for g in range(0, values.shape[0], 32):
        total = rows[g : g + 32, :]
        for t, tile in enumerate(lane_tiles(values[g : g + 32, :].astype(F32))):
            total = total + tile * scale[t : t + 1, :]
        rows[g : g + 32, :] = total


def row_kernel(count, *refs):
    cols, (factor_ref, exp_hbm) = refs[:count], refs[count : count + 2]
    out_ref, scales, rows, exp_ref, sem = refs[-5:]
    start(copies(exp_hbm, exp_ref, sem))
    scales[...] = column_scales(cols, scales.shape[0])
    rows[...] = jnp.zeros(rows.shape, F32)
    quarter = rows.shape[0] // LANES
    out_ref[0] = jnp.zeros(out_ref.shape[1:], F32)

    @pl.loop(0, exp_ref.shape[0])
    def _(k):
        copy_of(exp_hbm, exp_ref, sem, k).wait()
        add_row_sums(rows, exp_ref.at[k], chunk_scales(scales, k))

    pack_rows(out_ref.at[0, :quarter], jnp.sum(rows[...], axis=1, keepdims=True))
    out_ref[0, :quarter, :] = out_ref[0, :quarter, :] * factor_ref[:quarter, :]
    repeat(out_ref)


def own_back_kernel(before_ref, exp_hbm, w_hbm, back_ref, exp_ref, w_ref, exp_sem, w_sem):
    start(copies(exp_hbm, exp_ref, exp_sem), copies(w_hbm, w_ref, w_sem))
    back_ref[...] = jnp.zeros(back_ref.shape, F32)

    @pl.loop(0, exp_ref.shape[0])
    def _(k):
        copy_of(exp_hbm, exp_ref, exp_sem, k).wait()
        copy_of(w_hbm, w_ref, w_sem, k).wait()
        back_ref[...] += nt_dot(exp_ref[k], w_ref[:, columns_of(k)])


def relative_logs(logs, lse, which, shift=0.0):
    own = lse.shape[0] // (len(logs) - 1)
    quarter = own // LANES
    for g, ref in enumerate(logs[1:]):
        first = ref.shape[1] - 8 + which * quarter
        spread_rows(lse.at[g * own : (g + 1) * own], ref[0, first : first + quarter, :] - shift)


def student_rows_kernel(protos, place_ref, factor_ref, t_ref, own_ref, *refs):
    unit_ref, feat_ref, scaled_ref, t_unit, turned = refs[-5:]
    t_unit[...] = unit_rows(t_ref[...])[0].astype(BF16)
    own = own_ref.shape[0]
    groups = turned.shape[1] // own
    raw = refs[: groups - 1]
    quarter, feats = own // LANES, feat_ref.shape[0]
    for g in range(groups):
        half = unit_rows((raw[g - 1] if g else own_ref)[...])[0].astype(BF16)
        if g:
            unit_ref[(g - 1) * own : g * own, :] = half
        half = half.astype(F32)
        for a in range(0, own, LANES):
            first = g * own + a
            turned[:, first : first + LANES] = jnp.transpose(half[a : a + LANES, :]).astype(BF16)
    feat = turned[pl.ds(pl.multiple_of(place_ref[0] * feats, feats), feats), :]
    feat_ref[...] = feat
    for a in range(quarter):
        lanes = slice(a * LANES, (a + 1) * LANES)
        factor = factor_ref[quarter + a : quarter + a + 1, :] * protos
        scaled_ref[:, lanes] = (feat[:, lanes].astype(F32) * factor).astype(BF16)


def probabilities(unit, w_ref, k, lse, scale, use):
    for n in range(0, WIDE, TILE):
        logits = jnp.dot(
            unit[...], w_ref[:, columns_of(k, n, TILE)], preferred_element_type=F32
        )
        shift = lse[...]
        tiles = [tile * scale - shift for tile in lane_tiles(logits)]
        if n == 0:
            use(n, [exp2_by_squares(tiles[0])] + [jnp.exp2(tile) for tile in tiles[1:]])
        else:
            use(n, [jnp.exp2(tile) for tile in tiles])


def student_kernel(
    log_protos, first, groups, unit, feat_ref, scaled_ref, exp_hbm, w_hbm, *refs
):
    logs = refs[:groups]
    grad, token_ref, lse, prob, exp_ref, w_ref, exp_sem, w_sem = refs[-8:]
    own, count = exp_ref.shape[1], exp_ref.shape[0]
    exp_loads = copies(exp_hbm, exp_ref, exp_sem, first, 0, count)
    w_loads = copies(w_hbm, w_ref, w_sem, first, 0, count)
    start(w_loads, exp_loads)
    token_ref[...] = jnp.zeros(token_ref.shape, F32)
    relative_logs(logs, lse, 1, log_protos)

    @pl.loop(0, count)
    def _(k):
        copy_of(w_hbm, w_ref, w_sem, k, first).wait()

        def use(n, tiles):
            for t, tile in enumerate(tiles):
                prob[:, n + t * LANES : n + (t + 1) * LANES] = tile.astype(BF16)

        probabilities(unit, w_ref, k, lse, SCALE_STUDENT, use)
        copy_of(exp_hbm, exp_ref, exp_sem, k, first).wait()
        values = jnp.dot(scaled_ref[...], exp_ref[k], preferred_element_type=F32)
        values = values + jnp.dot(feat_ref[:, own:], prob[...], preferred_element_type=F32)
        grad[:, columns_of(k)] = values.astype(BF16)


def as_three(value):
    high = value.astype(BF16)
    rest = value - high.astype(F32)
    middle = rest.astype(BF16)
    return high, middle, (rest - middle.astype(F32)).astype(BF16)


def last_kernel(groups, factor_ref, own_hbm, student_hbm, exp_hbm, w_hbm, *refs):
    units, refs = refs[: groups - 1], refs[groups - 1 :]
    logs, cols, refs = refs[:groups], refs[groups : 2 * groups], refs[2 * groups :]
    (
        prob_hbm, scale_ref, out_ref, unit, lse, rows, own_rows, back, scaled, sums, prob_ref,
        exp_ref, w_ref, own_ref, student_ref, prob_sem, exp_sem, w_sem, sem,
    ) = refs[-19:]
    w_loads, exp_loads = copies(w_hbm, w_ref, w_sem), copies(exp_hbm, exp_ref, exp_sem)
    late_loads = whole_copies([(own_hbm, own_ref), (student_hbm, student_ref)], sem)
    start(w_loads, exp_loads)
    start(late_loads)
    slots, others, _ = prob_ref.shape
    own, chunks = exp_ref.shape[1], exp_ref.shape[0]
    tiles = (own + others) // LANES
    quarter = own // LANES
    scale_ref[...] = column_scales(cols, scale_ref.shape[0])
    rows[...] = jnp.zeros(rows.shape, F32)
    own_rows[...] = jnp.zeros(own_rows.shape, F32)
    back[...] = jnp.zeros(back.shape, F32)
    relative_logs(logs, lse, 0)
    for g in range(groups - 1):
        unit[g * own : (g + 1) * own, :] = units[g][...]
    partner = slice((groups // 2 - 1) * own, groups // 2 * own)

    def store(k):
        return pltpu.make_async_copy(prob_ref.at[lax.rem(k, slots)], prob_hbm.at[k], prob_sem.at[k])

    @pl.loop(0, chunks)
    def _(k):
        copy_of(w_hbm, w_ref, w_sem, k).wait()
        slot = lax.rem(k, slots)
        scale = chunk_scales(scale_ref, k)

        @pl.when(k >= slots)
        def _():
            store(k - slots).wait()

        def use(n, tiles):
            for t, tile in enumerate(tiles):
                prob_ref[slot, :, n + t * LANES : n + (t + 1) * LANES] = tile.astype(BF16)
            first = n // LANES
            tiles = [tile * scale[first + t : first + t + 1, :] for t, tile in enumerate(tiles)]
            rows[...] += add_up(tiles)
            for t, tile in enumerate(tiles):
                scaled[:, n + t * LANES : n + (t + 1) * LANES] = tile[partner, :].astype(BF16)

        probabilities(unit, w_ref, k, lse, SCALE_TEACHER, use)
        store(k).start()
        back[...] += nt_dot(scaled[...], w_ref[:, columns_of(k)])
        copy_of(exp_hbm, exp_ref, exp_sem, k).wait()
        add_row_sums(own_rows, exp_ref.at[k], scale)

    sums[...] = jnp.zeros(sums.shape, F32)
    pack_rows(sums.at[:quarter], jnp.sum(own_rows[...], axis=1, keepdims=True))
    sums[:quarter, :] = sums[:quarter, :] * factor_ref[:quarter, :]
    pack_rows(sums.at[quarter:tiles], jnp.sum(rows[...], axis=1, keepdims=True))
    wait(late_loads)
    half = unit_rows(own_ref[...])[0].astype(BF16).astype(F32)
    inner = jnp.sum(half * back[...], axis=1, keepdims=True)
    pack_rows(sums.at[tiles : tiles + quarter], inner)
    parts = out_ref.shape[0]
    share = own // parts
    protos = 1.0 * out_ref.shape[0] * w_ref.shape[1]
    student = []
    for a in range(quarter):
        factor = to_column(factor_ref[quarter + a : quarter + a + 1, :] * protos)
        student.append(student_ref[a * LANES : (a + 1) * LANES, :] * factor)
    student = jnp.concatenate(student, axis=0).astype(BF16)
    terms = list(as_three(sums[...]))
    terms.append(jnp.zeros((sums.shape[0], out_ref.shape[2] - 3 * LANES), BF16))
    terms = jnp.concatenate(terms, axis=1)
    for p in range(parts):
        here = slice(p * share, (p + 1) * share)
        out_ref[p] = jnp.concatenate(
            [student[here, :], back[here, :].astype(BF16), terms], axis=0
        )
    for k in range(max(0, chunks - slots), chunks):
        store(k).wait()


def total_sums(message_ref, first):
    parts = message_ref.shape[0]
    each = [
        add_up([t.astype(F32) for t in lane_tiles(message_ref[p, first:, : 3 * LANES])[::-1]])
        for p in range(parts)
    ]
    return add_up(each)


def rows_kernel(tiles, protos, place_ref, s_hbm, message_ref, logs_ref, *refs):
    out_ref, loss_ref, sums_ref, weight, s_ref, sem = refs[-6:]
    parts = message_ref.shape[0]
    share, own = out_ref.shape[1], weight.shape[0]
    mine = pl.ds(pl.multiple_of(place_ref[1] * share, share), share)
    load = pltpu.make_async_copy(s_hbm.at[mine], s_ref, sem)
    load.start()
    quarter = own // LANES
    first = tiles // 2
    totals = total_sums(message_ref, 2 * share)
    sums_ref[...] = totals
    scale = 1.0 / totals[first : first + quarter, :]
    spread_rows(weight, scale)
    total = add_up([message_ref[p, :share, :].astype(F32) for p in range(parts)])
    paired = add_up([message_ref[p, share : 2 * share, :].astype(F32) for p in range(parts)])
    total = total - paired * (weight[mine, :1] * protos)
    load.wait()
    unit, length = unit_rows(s_ref[...])
    out_ref[0] = (total - unit * jnp.sum(unit * total, axis=-1, keepdims=True)) / length
    repeat(out_ref)
    height = logs_ref.shape[1] - 8
    logs = logs_ref[0, height + quarter : height + 2 * quarter, :]
    terms = logs / LOG2E - totals[tiles : tiles + quarter, :] * scale / TEMP_STUDENT
    loss_ref[...] = jnp.broadcast_to(jnp.sum(terms), loss_ref.shape)


def grad_kernel(counts, protos, exp_hbm, prob_hbm, feat_ref, scale_ref, sums_ref, factor_ref, *refs):
    parts = refs[: len(counts)]
    out_hbm, scaled, exp_ref, prob_ref, out, exp_sem, prob_sem, sem = refs[-8:]
    exp_loads = copies(exp_hbm, exp_ref, exp_sem)
    prob_loads = copies(prob_hbm, prob_ref, prob_sem)
    start(exp_loads, prob_loads)
    where = [(part, k) for count, part in zip(counts, parts) for k in range(count)]
    own = exp_ref.shape[1]
    tiles = (own + prob_ref.shape[1]) // LANES
    rows = protos / sums_ref[:tiles, :]
    for a in range(tiles):
        other = (a + tiles // 2) % tiles
        feat = feat_ref[:, other * LANES : (other + 1) * LANES].astype(F32)
        row = rows[a : a + 1, :]
        if a < own // LANES:
            row = row * factor_ref[a : a + 1, :]
        scaled[:, a * LANES : (a + 1) * LANES] = (feat * row).astype(BF16)
    stores = copies(out, out_hbm, sem)
    for k, store in enumerate(stores):
        exp_loads[k].wait()
        prob_loads[k].wait()
        paired = jnp.dot(scaled[:, :own], exp_ref[k], preferred_element_type=F32)
        paired = paired + jnp.dot(
            scaled[:, own:], prob_ref[k], preferred_element_type=F32
        )
        part, there = where[k]
        for t, tile in enumerate(lane_tiles(paired)):
            lanes = slice(k * WIDE + t * LANES, k * WIDE + (t + 1) * LANES)
            scale = scale_ref[lanes.start // LANES : lanes.stop // LANES, :]
            own_part = part[:, there * WIDE + t * LANES : there * WIDE + (t + 1) * LANES]
            out[:, lanes] = (own_part.astype(F32) - tile * scale).astype(BF16)
        store.start()
    for store in stores:
        store.wait()


SMEM = pl.BlockSpec(memory_space=pltpu.SMEM)
VMEM = pl.BlockSpec(memory_space=pltpu.VMEM)
ANY = pl.BlockSpec(memory_space=pl.ANY)


def params(nbytes):
    return pltpu.CompilerParams(vmem_limit_bytes=int(nbytes) + 8 * 2**20)


def cost(flops, nbytes, exps=0):
    return pl.CostEstimate(flops=int(flops), bytes_accessed=int(nbytes), transcendentals=int(exps))


def exchange(value, axis):
    return lax.all_to_all(value, axis, 0, 0)


def following(value, axis):
    n = lax.axis_size(axis)
    return [lax.ppermute(value, axis, [(i, (i - s) % n) for i in range(n)]) for s in range(1, n)]


def tree_sum(value, axis):
    n = lax.axis_size(axis)
    values = [value] + [
        lax.ppermute(value, axis, [(i, i ^ s) for i in range(n)]) for s in range(1, n)
    ]
    while len(values) > 1:
        values = [a + b for a, b in zip(values[::2], values[1::2])]
    return values[0]


def local(teacher_feats, student_feats, proto_weight):
    parts, groups = lax.axis_size("proto"), lax.axis_size("batch")
    own, width = teacher_feats.shape
    local_protos = proto_weight.shape[1]
    rows = own * groups
    others = rows - own
    protos = local_protos * parts
    feats = width // groups
    share = own // parts
    tiles = rows // LANES
    height = local_protos // LANES
    chunks = local_protos // WIDE
    place = jnp.stack([lax.axis_index("batch"), lax.axis_index("proto")]).astype(jnp.int32)
    struct = jax.ShapeDtypeStruct
    weight_bytes = 2 * width * local_protos
    exp_bytes = 2 * own * local_protos
    others_bytes = 2 * others * local_protos
    spread = pltpu.VMEM((own, LANES), F32)
    w_buffer = pltpu.VMEM((width, local_protos), BF16)
    exp_buffer = pltpu.VMEM((chunks, own, WIDE), BF16)
    sems = pltpu.SemaphoreType.DMA((chunks,))
    log_protos = math.log2(protos)
    token = struct((8, LANES), F32)

    def far(value):
        return pltpu.with_memory_space_constraint(value, pltpu.HBM)

    weight = far(proto_weight)
    teacher_rows, student_rows = far(teacher_feats), far(student_feats)
    s_all = following(student_feats, "batch")

    exps = pltpu.HBM((chunks, own, WIDE), BF16)
    t_exp, s_exp, stats = pl.pallas_call(
        stats_kernel,
        in_specs=[ANY] * 3,
        out_specs=[ANY, ANY, VMEM],
        out_shape=[
            exps,
            exps,
            struct((parts, 4 * own // LANES, LANES), F32),
        ],
        scratch_shapes=[
            pltpu.VMEM((2, own, width), BF16),
            w_buffer,
            pltpu.VMEM((2 * own, width), BF16),
            pltpu.VMEM((2, chunks, own, WIDE), BF16),
            pltpu.VMEM((2 * own, local_protos), F32),
            pltpu.VMEM((2 * own, LANES), F32),
            pltpu.VMEM((2 * own, LANES), F32),
            pltpu.SemaphoreType.DMA((2,)),
            sems, sems, sems,
        ],
        compiler_params=params(weight_bytes + 6 * exp_bytes),
        cost_estimate=cost(4 * own * width * local_protos, weight_bytes),
        name="own_rows",
    )(teacher_rows, student_rows, weight)
    t_exp, s_exp = far(t_exp), far(s_exp)

    back_student = pl.pallas_call(
        own_back_kernel,
        in_specs=[ANY] * 3,
        out_specs=VMEM,
        out_shape=struct((own, width), F32),
        scratch_shapes=[exp_buffer, w_buffer, sems, sems],
        compiler_params=params(weight_bytes + exp_bytes),
        cost_estimate=cost(2 * own * width * local_protos, weight_bytes),
        name="own_back",
    )(stats, s_exp, weight)

    stats = exchange(stats, "proto")

    first_shape = (1, height + 8, LANES)
    factor, cols = pl.pallas_call(
        first_column_kernel,
        in_specs=[SMEM, VMEM, ANY, ANY] + [ANY] * (groups - 1),
        out_specs=[VMEM, VMEM],
        out_shape=[token, struct(first_shape, F32)],
        scratch_shapes=[spread, exp_buffer, sems],
        compiler_params=params(exp_bytes),
        cost_estimate=cost(2 * own * local_protos, exp_bytes),
        name="first_columns",
    )(place, stats, t_exp, back_student, *s_all)

    unit, feat, scaled, t_unit = pl.pallas_call(
        functools.partial(student_rows_kernel, float(protos)),
        in_specs=[SMEM, VMEM, VMEM, VMEM] + [VMEM] * (groups - 1) + [ANY],
        out_specs=[VMEM] * 4,
        out_shape=[
            struct((others, width), BF16), struct((feats, rows), BF16), struct((feats, own), BF16),
            struct((own, width), BF16),
        ],
        scratch_shapes=[pltpu.VMEM((width, rows), BF16)],
        compiler_params=params(2 * rows * width),
        cost_estimate=cost(8 * rows * width, 2 * rows * width),
        name="student_rows",
    )(place, factor, teacher_feats, student_feats, *s_all, cols)
    t_all = following(t_unit, "batch")
    cols = [cols] + following(cols, "batch")
    logs = cols

    counts = [c * chunks // 8 for c in (1, 1, 1, 1, 4)]
    grad_parts = []

    def student_piece(before):
        turn = len(grad_parts)
        first, count = sum(counts[:turn]), counts[turn]
        grad_part, done = pl.pallas_call(
            functools.partial(student_kernel, log_protos, first, groups),
            in_specs=[VMEM] * 3 + [ANY] * 2 + [VMEM] * groups + [ANY],
            out_specs=[VMEM, VMEM],
            out_shape=[struct((feats, count * WIDE), BF16), token],
            scratch_shapes=[
                pltpu.VMEM((others, LANES), F32),
                pltpu.VMEM((others, WIDE), BF16),
                pltpu.VMEM((count, own, WIDE), BF16),
                pltpu.VMEM((width, count * WIDE), BF16),
            ]
            + [pltpu.SemaphoreType.DMA((count,))] * 2,
            compiler_params=params(16 * 2**20),
            cost_estimate=cost(2.5 * rows * width * WIDE * count, 2 * width * WIDE * count),
            name="student_side",
        )(unit, feat, scaled, s_exp, weight, *logs, before)
        grad_parts.append(grad_part)
        return done

    done = unit
    for turn in range(SWEEPS - 1):
        late = t_all if turn == 1 else []
        sums = pl.pallas_call(
            functools.partial(row_kernel, len(cols)),
            in_specs=[VMEM] * (len(cols) + 1) + [ANY] * (2 + len(late)),
            out_specs=VMEM,
            out_shape=struct((parts, 8, LANES), F32),
            scratch_shapes=[pltpu.VMEM((height, LANES), F32), spread, exp_buffer, sems],
            compiler_params=params(exp_bytes),
            cost_estimate=cost(2 * own * local_protos, exp_bytes),
            name="rows",
        )(*cols, factor, t_exp, done, *late)
        done = student_piece(sums)
        sums = exchange(sums, "proto")
        middle = turn < SWEEPS - 2
        cols = pl.pallas_call(
            column_kernel,
            in_specs=[VMEM, VMEM, ANY, ANY],
            out_specs=VMEM,
            out_shape=struct((groups if middle else 1, height, LANES), F32),
            scratch_shapes=[spread, exp_buffer, sems],
            compiler_params=params(exp_bytes),
            cost_estimate=cost(2 * own * local_protos, exp_bytes),
            name="columns",
        )(sums, factor, t_exp, done)
        done = student_piece(cols)
        if middle:
            cols = [exchange(cols, "batch")]
        else:
            cols = [cols] + following(cols, "batch")

    sum_rows = -(-(tiles + own // LANES) // 16) * 16
    message_shape = (parts, 2 * share + sum_rows, width)
    prob, col_scale, message = pl.pallas_call(
        functools.partial(last_kernel, groups),
        in_specs=[VMEM] + [ANY] * 4 + [VMEM] * (3 * groups - 1) + [ANY],
        out_specs=[ANY, VMEM, VMEM],
        out_shape=[
            pltpu.HBM((chunks, others, WIDE), BF16),
            struct((height, LANES), F32),
            struct(message_shape, BF16),
        ],
        scratch_shapes=[
            pltpu.VMEM((others, width), BF16),
            pltpu.VMEM((others, LANES), F32),
            pltpu.VMEM((others, LANES), F32),
            spread,
            pltpu.VMEM((own, width), F32),
            pltpu.VMEM((own, WIDE), BF16),
            pltpu.VMEM((sum_rows, LANES), F32),
            pltpu.VMEM((min(chunks, 3), others, WIDE), BF16),
            exp_buffer,
            w_buffer,
            pltpu.VMEM((own, width), BF16),
            pltpu.VMEM((own, width), F32),
            sems, sems, sems,
            pltpu.SemaphoreType.DMA((2,)),
        ],
        compiler_params=params(20 * 2**20 + weight_bytes + exp_bytes),
        cost_estimate=cost(2 * rows * width * local_protos, others_bytes),
        name="last_rows",
    )(
        factor, student_rows, far(back_student), t_exp, weight, *t_all, *logs, *cols, done,
    )
    done = student_piece(message)
    message = exchange(message, "proto")

    grad_rows, loss_part, sums = pl.pallas_call(
        functools.partial(rows_kernel, tiles, float(protos)),
        in_specs=[SMEM, ANY, VMEM, VMEM, ANY],
        out_specs=[VMEM] * 3,
        out_shape=[struct((parts, share, width), F32), token, struct((sum_rows, LANES), F32)],
        scratch_shapes=[spread, pltpu.VMEM((share, width), BF16), pltpu.SemaphoreType.DMA],
        compiler_params=params(0),
        name="row_grads",
    )(place, student_rows, message, logs[0], done)
    grad_rows = exchange(grad_rows, "proto").reshape(own, width)
    loss = tree_sum(loss_part, "batch")[0, 0] / rows

    grad_weight = pl.pallas_call(
        functools.partial(grad_kernel, counts, float(protos)),
        in_specs=[ANY] * 2 + [VMEM] * (4 + len(counts)),
        out_specs=ANY,
        out_shape=struct((feats, local_protos), BF16),
        scratch_shapes=[
            pltpu.VMEM((feats, rows), BF16),
            exp_buffer,
            pltpu.VMEM((chunks, others, WIDE), BF16),
            pltpu.VMEM((feats, local_protos), BF16),
            sems, sems, sems,
        ],
        compiler_params=params(exp_bytes + others_bytes + 4 * feats * local_protos),
        cost_estimate=cost(2 * feats * rows * local_protos, others_bytes),
        name="weight_grads",
    )(t_exp, far(prob), feat, col_scale, sums, factor, *grad_parts)
    return grad_weight, grad_rows, loss


def solution(mesh):
    return jax.shard_map(
        local,
        mesh=mesh,
        in_specs=(P("batch", None), P("batch", None), P(None, "proto")),
        out_specs=(P("batch", "proto"), P("batch", None), P()),
        check_vma=False,
    )
```

```python
import functools
import math

import jax
import jax.numpy as jnp
from jax import lax
from jax.experimental import pallas as pl
from jax.experimental.pallas import tpu as pltpu
from jax.sharding import PartitionSpec as P

SWEEPS = 3
TEMP_TEACHER = 0.04
TEMP_STUDENT = 0.1
LOG2E = math.log2(math.e)
SCALE_TEACHER = LOG2E / TEMP_TEACHER
SCALE_STUDENT = LOG2E / TEMP_STUDENT
LANES = 128
WIDE = 1024
TILE = 256
FAR = (2, 3)
F32 = jnp.float32
BF16 = jnp.bfloat16


def unit_rows(values):
    wide = values.astype(F32)
    length = jnp.sqrt(jnp.sum(wide * wide, axis=-1, keepdims=True) + 1e-06)
    return wide / length, length


def diagonal():
    shape = (LANES, LANES)
    return lax.broadcasted_iota(jnp.int32, shape, 0) == lax.broadcasted_iota(jnp.int32, shape, 1)


def to_column(row):
    spread = jnp.where(diagonal(), jnp.broadcast_to(row, (LANES, LANES)), 0.0)
    return jnp.sum(spread, axis=1, keepdims=True)


def to_row(column):
    spread = jnp.where(diagonal(), jnp.broadcast_to(column, (LANES, LANES)), 0.0)
    return jnp.sum(spread, axis=0, keepdims=True)


def spread_rows(ref, rows):
    for a in range(rows.shape[0]):
        ref[a * LANES : (a + 1) * LANES, :] = jnp.broadcast_to(
            to_column(rows[a : a + 1, :]), (LANES, LANES)
        )


def pack_rows(ref, columns):
    for a in range(columns.shape[0] // LANES):
        ref[a : a + 1, :] = to_row(columns[a * LANES : (a + 1) * LANES, :])


def lane_tiles(values):
    return [values[:, t * LANES : (t + 1) * LANES] for t in range(values.shape[1] // LANES)]


def fold(values):
    return functools.reduce(jnp.add, lane_tiles(values))


def column_sums(values):
    rows, cols = values.shape
    return jnp.sum(values.reshape(rows // 8, 8, cols), axis=0)


def nt_dot(a, b):
    return lax.dot_general(a, b, (((1,), (1,)), ((), ())), preferred_element_type=F32)


def add_up(values):
    return functools.reduce(jnp.add, values)


def repeat(out_ref):
    for p in range(1, out_ref.shape[0]):
        out_ref[p] = out_ref[0]


def chunk(k):
    return slice(k * WIDE, (k + 1) * WIDE)


def copies(source, target, sems, first=0, back=0, count=None):
    def chunks(ref):
        return ref.shape[0] if len(ref.shape) == 3 else ref.shape[1] // WIDE

    count = count or min(chunks(source), chunks(target))
    return [copy_of(source, target, sems, k, first, back) for k in range(count)]


def columns_of(k, first=0, count=WIDE):
    return pl.ds(pl.multiple_of(k * WIDE + first, LANES), count)


def copy_of(source, target, sems, k, first=0, back=0):
    def part(ref, k):
        return ref.at[k] if len(ref.shape) == 3 else ref.at[:, columns_of(k)]

    return pltpu.make_async_copy(part(source, first + k), part(target, back + k), sems.at[k])


def start(*lists):
    for each in zip(*lists):
        for copy in each:
            copy.start()


def whole_copies(pairs, sems):
    return [pltpu.make_async_copy(a, b, sems.at[i]) for i, (a, b) in enumerate(pairs)]


def wait(*lists):
    for each in lists:
        for copy in each:
            copy.wait()


def stats_kernel(
    t_hbm, s_hbm, w_hbm, t_out, s_out, out_ref,
    raw, w_ref, unit, exps, logits, top, total, raw_sem, w_sem, t_sem, s_sem,
):
    own = raw.shape[1]
    quarter = out_ref.shape[1] // 4
    chunks = exps.shape[1]
    halves = (slice(0, own), slice(own, 2 * own))
    loads = copies(w_hbm, w_ref, w_sem)
    raw_loads = [
        pltpu.make_async_copy(ref, raw.at[which], raw_sem.at[which])
        for which, ref in enumerate((t_hbm, s_hbm))
    ]
    start(raw_loads, loads[:2])
    start(loads[2:])
    top[...] = jnp.full(top.shape, -1e30, F32)
    total[...] = jnp.zeros(total.shape, F32)
    wait(raw_loads)
    for which in range(2):
        unit[halves[which], :] = unit_rows(raw[which])[0].astype(BF16)

    @pl.loop(0, chunks)
    def _(k):
        copy_of(w_hbm, w_ref, w_sem, k).wait()
        for n in range(0, WIDE, TILE):
            here = columns_of(k, n, TILE)
            values = jnp.dot(unit[...], w_ref[:, here], preferred_element_type=F32)
            for half, scale in zip(halves, (SCALE_TEACHER, SCALE_STUDENT)):
                part = values[half, :] * scale
                logits[half, here] = part
                top[half, :] = functools.reduce(jnp.maximum, lane_tiles(part), top[half, :])

    peak = jnp.max(top[...], axis=1, keepdims=True)
    top[...] = jnp.broadcast_to(peak, top.shape)

    @pl.loop(0, chunks)
    def _(k):
        for which, (half, out, sem) in enumerate(zip(halves, (t_out, s_out), (t_sem, s_sem))):
            shift = top[half, :]
            for n in range(0, WIDE, 2 * TILE):
                tiles = lane_tiles(logits[half, columns_of(k, n, 2 * TILE)])
                tiles = [jnp.exp2(tile - shift) for tile in tiles]
                for t, tile in enumerate(tiles):
                    lanes = slice(n + t * LANES, n + (t + 1) * LANES)
                    exps[which, k, :, lanes] = tile.astype(BF16)
                total[half, :] += add_up(tiles)
            copy_of(exps.at[which], out, sem, k).start()

    sums = jnp.sum(total[...], axis=1, keepdims=True)
    for which, half in enumerate(halves):
        for k, column in enumerate((peak, sums)):
            first = (2 * which + k) * quarter
            pack_rows(out_ref.at[0, first : first + quarter], column[half, :])
    repeat(out_ref)
    wait(copies(exps.at[0], t_out, t_sem), copies(exps.at[1], s_out, s_sem))


def merged(stats_ref, which):
    parts, height, _ = stats_ref.shape
    quarter = height // 4
    first = 2 * which * quarter
    tops = [stats_ref[p, first : first + quarter, :] for p in range(parts)]
    top = functools.reduce(jnp.maximum, tops)
    sums = [
        stats_ref[p, first + quarter : first + 2 * quarter, :] * jnp.exp2(tops[p] - top)
        for p in range(parts)
    ]
    return top + jnp.log2(add_up(sums))


def column_pass(exp_hbm, exp_ref, sem, weight, out_ref):
    height = WIDE // LANES

    @pl.loop(0, exp_ref.shape[0])
    def _(k):
        copy_of(exp_hbm, exp_ref, sem, k).wait()
        sums = jnp.zeros((8, WIDE), F32)
        for g in range(0, exp_ref.shape[1], 16):
            shift = weight[g : g + 16, :]
            tiles = lane_tiles(exp_ref[k, g : g + 16, :].astype(F32))
            sums = sums + column_sums(jnp.concatenate([tile * shift for tile in tiles], axis=1))
        sums = jnp.sum(sums, axis=0, keepdims=True)
        block = jnp.concatenate(lane_tiles(sums), axis=0)
        for g in range(out_ref.shape[0]):
            out_ref[g, pl.ds(pl.multiple_of(k * height, height), height), :] = block


def first_column_kernel(place_ref, stats_ref, exp_hbm, *refs):
    factor_ref, out_ref, weight, exp_ref, sem = refs[-5:]
    start(copies(exp_hbm, exp_ref, sem))
    quarter = stats_ref.shape[1] // 4
    height = out_ref.shape[1] - 8
    own = stats_ref[pl.ds(place_ref[1], 1)][0]
    factor_ref[...] = jnp.zeros(factor_ref.shape, F32)
    rows = []
    for which in range(2):
        log_sum = merged(stats_ref, which)
        here = slice(which * quarter, (which + 1) * quarter)
        factor_ref[here, :] = jnp.exp2(
            own[2 * which * quarter : (2 * which + 1) * quarter, :] - log_sum
        )
        rows.append(log_sum)
    rows.append(jnp.zeros((8 - 2 * quarter, LANES), F32))
    logs = jnp.concatenate(rows, axis=0)
    for g in range(out_ref.shape[0]):
        out_ref[g, height:, :] = logs
    spread_rows(weight, factor_ref[:quarter, :])
    column_pass(exp_hbm, exp_ref, sem, weight, out_ref)


def column_kernel(sums_ref, factor_ref, exp_hbm, *refs):
    out_ref, weight, exp_ref, sem = refs[-4:]
    start(copies(exp_hbm, exp_ref, sem))
    quarter = weight.shape[0] // LANES
    scale = 1.0 / add_up([sums_ref[p, :quarter, :] for p in range(sums_ref.shape[0])])
    spread_rows(weight, scale * factor_ref[:quarter, :])
    column_pass(exp_hbm, exp_ref, sem, weight, out_ref)


def column_scales(cols, height):
    return 1.0 / add_up([ref[g, :height, :] for ref in cols for g in range(ref.shape[0])])


def chunk_scales(scales, k):
    height = WIDE // LANES
    return scales[pl.ds(pl.multiple_of(k * height, height), height), :]


def add_row_sums(rows, values, scale):
    for g in range(0, values.shape[0], 32):
        total = rows[g : g + 32, :]
        for t, tile in enumerate(lane_tiles(values[g : g + 32, :].astype(F32))):
            total = total + tile * scale[t : t + 1, :]
        rows[g : g + 32, :] = total


def row_kernel(count, *refs):
    cols, (factor_ref, exp_hbm) = refs[:count], refs[count : count + 2]
    out_ref, scales, rows, exp_ref, sem = refs[-5:]
    start(copies(exp_hbm, exp_ref, sem))
    scales[...] = column_scales(cols, scales.shape[0])
    rows[...] = jnp.zeros(rows.shape, F32)
    quarter = rows.shape[0] // LANES
    out_ref[0] = jnp.zeros(out_ref.shape[1:], F32)

    @pl.loop(0, exp_ref.shape[0])
    def _(k):
        copy_of(exp_hbm, exp_ref, sem, k).wait()
        add_row_sums(rows, exp_ref.at[k], chunk_scales(scales, k))

    pack_rows(out_ref.at[0, :quarter], jnp.sum(rows[...], axis=1, keepdims=True))
    out_ref[0, :quarter, :] = out_ref[0, :quarter, :] * factor_ref[:quarter, :]
    repeat(out_ref)


def own_back_kernel(before_ref, exp_hbm, w_hbm, back_ref, exp_ref, w_ref, exp_sem, w_sem):
    start(copies(exp_hbm, exp_ref, exp_sem), copies(w_hbm, w_ref, w_sem))
    back_ref[...] = jnp.zeros(back_ref.shape, F32)

    @pl.loop(0, exp_ref.shape[0])
    def _(k):
        copy_of(exp_hbm, exp_ref, exp_sem, k).wait()
        copy_of(w_hbm, w_ref, w_sem, k).wait()
        back_ref[...] += nt_dot(exp_ref[k], w_ref[:, columns_of(k)])


def relative_logs(logs, lse, which, shift=0.0):
    own = lse.shape[0] // (len(logs) - 1)
    quarter = own // LANES
    for g, ref in enumerate(logs[1:]):
        first = ref.shape[1] - 8 + which * quarter
        spread_rows(lse.at[g * own : (g + 1) * own], ref[0, first : first + quarter, :] - shift)


def student_rows_kernel(protos, place_ref, factor_ref, t_ref, own_ref, *refs):
    unit_ref, feat_ref, scaled_ref, t_unit, turned = refs[-5:]
    t_unit[...] = unit_rows(t_ref[...])[0].astype(BF16)
    own = own_ref.shape[0]
    groups = turned.shape[1] // own
    raw = refs[: groups - 1]
    quarter, feats = own // LANES, feat_ref.shape[0]
    for g in range(groups):
        half = unit_rows((raw[g - 1] if g else own_ref)[...])[0].astype(BF16)
        if g:
            unit_ref[(g - 1) * own : g * own, :] = half
        half = half.astype(F32)
        for a in range(0, own, LANES):
            first = g * own + a
            turned[:, first : first + LANES] = jnp.transpose(half[a : a + LANES, :]).astype(BF16)
    feat = turned[pl.ds(pl.multiple_of(place_ref[0] * feats, feats), feats), :]
    feat_ref[...] = feat
    for a in range(quarter):
        lanes = slice(a * LANES, (a + 1) * LANES)
        factor = factor_ref[quarter + a : quarter + a + 1, :] * protos
        scaled_ref[:, lanes] = (feat[:, lanes].astype(F32) * factor).astype(BF16)


def probabilities(unit, w_ref, k, lse, scale, use):
    for n in range(0, WIDE, TILE):
        logits = jnp.dot(
            unit[...], w_ref[:, columns_of(k, n, TILE)], preferred_element_type=F32
        )
        shift = lse[...]
        use(n, [jnp.exp2(tile * scale - shift) for tile in lane_tiles(logits)])


def student_kernel(
    log_protos, first, groups, unit, feat_ref, scaled_ref, exp_hbm, w_hbm, *refs
):
    logs = refs[:groups]
    grad, token_ref, lse, prob, exp_ref, w_ref, exp_sem, w_sem = refs[-8:]
    own, count = exp_ref.shape[1], exp_ref.shape[0]
    exp_loads = copies(exp_hbm, exp_ref, exp_sem, first, 0, count)
    w_loads = copies(w_hbm, w_ref, w_sem, first, 0, count)
    start(w_loads, exp_loads)
    token_ref[...] = jnp.zeros(token_ref.shape, F32)
    relative_logs(logs, lse, 1, log_protos)

    @pl.loop(0, count)
    def _(k):
        copy_of(w_hbm, w_ref, w_sem, k, first).wait()

        def use(n, tiles):
            for t, tile in enumerate(tiles):
                prob[:, n + t * LANES : n + (t + 1) * LANES] = tile.astype(BF16)

        probabilities(unit, w_ref, k, lse, SCALE_STUDENT, use)
        copy_of(exp_hbm, exp_ref, exp_sem, k, first).wait()
        values = jnp.dot(scaled_ref[...], exp_ref[k], preferred_element_type=F32)
        values = values + jnp.dot(feat_ref[:, own:], prob[...], preferred_element_type=F32)
        grad[:, columns_of(k)] = values.astype(BF16)


def as_three(value):
    high = value.astype(BF16)
    rest = value - high.astype(F32)
    middle = rest.astype(BF16)
    return high, middle, (rest - middle.astype(F32)).astype(BF16)


def last_kernel(groups, factor_ref, own_hbm, student_hbm, exp_hbm, w_hbm, *refs):
    units, refs = refs[: groups - 1], refs[groups - 1 :]
    logs, cols, refs = refs[:groups], refs[groups : 2 * groups], refs[2 * groups :]
    (
        prob_hbm, scale_ref, out_ref, unit, lse, rows, own_rows, back, scaled, sums, prob_ref,
        exp_ref, w_ref, own_ref, student_ref, prob_sem, exp_sem, w_sem, sem,
    ) = refs[-19:]
    w_loads, exp_loads = copies(w_hbm, w_ref, w_sem), copies(exp_hbm, exp_ref, exp_sem)
    late_loads = whole_copies([(own_hbm, own_ref), (student_hbm, student_ref)], sem)
    start(w_loads, exp_loads)
    start(late_loads)
    slots, others, _ = prob_ref.shape
    own, chunks = exp_ref.shape[1], exp_ref.shape[0]
    tiles = (own + others) // LANES
    quarter = own // LANES
    scale_ref[...] = column_scales(cols, scale_ref.shape[0])
    rows[...] = jnp.zeros(rows.shape, F32)
    own_rows[...] = jnp.zeros(own_rows.shape, F32)
    back[...] = jnp.zeros(back.shape, F32)
    relative_logs(logs, lse, 0)
    for g in range(groups - 1):
        unit[g * own : (g + 1) * own, :] = units[g][...]
    partner = slice((groups // 2 - 1) * own, groups // 2 * own)

    def store(k):
        return pltpu.make_async_copy(prob_ref.at[lax.rem(k, slots)], prob_hbm.at[k], prob_sem.at[k])

    @pl.loop(0, chunks)
    def _(k):
        copy_of(w_hbm, w_ref, w_sem, k).wait()
        slot = lax.rem(k, slots)
        scale = chunk_scales(scale_ref, k)

        @pl.when(k >= slots)
        def _():
            store(k - slots).wait()

        def use(n, tiles):
            for t, tile in enumerate(tiles):
                prob_ref[slot, :, n + t * LANES : n + (t + 1) * LANES] = tile.astype(BF16)
            first = n // LANES
            tiles = [tile * scale[first + t : first + t + 1, :] for t, tile in enumerate(tiles)]
            rows[...] += add_up(tiles)
            for t, tile in enumerate(tiles):
                scaled[:, n + t * LANES : n + (t + 1) * LANES] = tile[partner, :].astype(BF16)

        probabilities(unit, w_ref, k, lse, SCALE_TEACHER, use)
        store(k).start()
        back[...] += nt_dot(scaled[...], w_ref[:, columns_of(k)])
        copy_of(exp_hbm, exp_ref, exp_sem, k).wait()
        add_row_sums(own_rows, exp_ref.at[k], scale)

    sums[...] = jnp.zeros(sums.shape, F32)
    pack_rows(sums.at[:quarter], jnp.sum(own_rows[...], axis=1, keepdims=True))
    sums[:quarter, :] = sums[:quarter, :] * factor_ref[:quarter, :]
    pack_rows(sums.at[quarter:tiles], jnp.sum(rows[...], axis=1, keepdims=True))
    wait(late_loads)
    half = unit_rows(own_ref[...])[0].astype(BF16).astype(F32)
    inner = jnp.sum(half * back[...], axis=1, keepdims=True)
    pack_rows(sums.at[tiles : tiles + quarter], inner)
    parts = out_ref.shape[0]
    share = own // parts
    protos = 1.0 * out_ref.shape[0] * w_ref.shape[1]
    student = []
    for a in range(quarter):
        factor = to_column(factor_ref[quarter + a : quarter + a + 1, :] * protos)
        student.append(student_ref[a * LANES : (a + 1) * LANES, :] * factor)
    student = jnp.concatenate(student, axis=0).astype(BF16)
    terms = list(as_three(sums[...]))
    terms.append(jnp.zeros((sums.shape[0], out_ref.shape[2] - 3 * LANES), BF16))
    terms = jnp.concatenate(terms, axis=1)
    for p in range(parts):
        here = slice(p * share, (p + 1) * share)
        out_ref[p] = jnp.concatenate(
            [student[here, :], back[here, :].astype(BF16), terms], axis=0
        )
    for k in range(max(0, chunks - slots), chunks):
        store(k).wait()


def total_sums(message_ref, first):
    parts = message_ref.shape[0]
    each = [
        add_up([t.astype(F32) for t in lane_tiles(message_ref[p, first:, : 3 * LANES])[::-1]])
        for p in range(parts)
    ]
    return add_up(each)


def rows_kernel(tiles, protos, place_ref, s_hbm, message_ref, logs_ref, *refs):
    out_ref, loss_ref, sums_ref, weight, s_ref, sem = refs[-6:]
    parts = message_ref.shape[0]
    share, own = out_ref.shape[1], weight.shape[0]
    mine = pl.ds(pl.multiple_of(place_ref[1] * share, share), share)
    load = pltpu.make_async_copy(s_hbm.at[mine], s_ref, sem)
    load.start()
    quarter = own // LANES
    first = tiles // 2
    totals = total_sums(message_ref, 2 * share)
    sums_ref[...] = totals
    scale = 1.0 / totals[first : first + quarter, :]
    spread_rows(weight, scale)
    total = add_up([message_ref[p, :share, :].astype(F32) for p in range(parts)])
    paired = add_up([message_ref[p, share : 2 * share, :].astype(F32) for p in range(parts)])
    total = total - paired * (weight[mine, :1] * protos)
    load.wait()
    unit, length = unit_rows(s_ref[...])
    total = (total - unit * jnp.sum(unit * total, axis=-1, keepdims=True)) / length
    out_ref[0] = total.astype(BF16)
    repeat(out_ref)
    height = logs_ref.shape[1] - 8
    logs = logs_ref[0, height + quarter : height + 2 * quarter, :]
    terms = logs / LOG2E - totals[tiles : tiles + quarter, :] * scale / TEMP_STUDENT
    loss_ref[...] = jnp.broadcast_to(jnp.sum(terms) / (tiles * LANES), loss_ref.shape)


def grad_kernel(counts, protos, exp_hbm, prob_hbm, feat_ref, scale_ref, sums_ref, factor_ref, *refs):
    parts = refs[: len(counts)]
    out_hbm, scaled, exp_ref, prob_ref, out, part_ref, exp_sem, prob_sem, sem, part_sem = refs[-10:]
    part_loads, where = {}, []
    for i, (count, part) in enumerate(zip(counts, parts)):
        for k in range(count):
            if i in FAR:
                slot = len(part_loads)
                part_loads[len(where)] = copy_of(part, part_ref, part_sem, slot, k - slot)
                where.append((part_ref, slot))
            else:
                where.append((part, k))
    exp_loads = copies(exp_hbm, exp_ref, exp_sem)
    prob_loads = copies(prob_hbm, prob_ref, prob_sem)
    start(exp_loads[:2], prob_loads[:2])
    start(list(part_loads.values()))
    start(exp_loads[2:], prob_loads[2:])
    own = exp_ref.shape[1]
    tiles = (own + prob_ref.shape[1]) // LANES
    rows = protos / sums_ref[:tiles, :]
    for a in range(tiles):
        other = (a + tiles // 2) % tiles
        feat = feat_ref[:, other * LANES : (other + 1) * LANES].astype(F32)
        row = rows[a : a + 1, :]
        if a < own // LANES:
            row = row * factor_ref[a : a + 1, :]
        scaled[:, a * LANES : (a + 1) * LANES] = (feat * row).astype(BF16)
    stores = copies(out, out_hbm, sem)
    for k, store in enumerate(stores):
        exp_loads[k].wait()
        prob_loads[k].wait()
        paired = jnp.dot(scaled[:, :own], exp_ref[k], preferred_element_type=F32)
        paired = paired + jnp.dot(
            scaled[:, own:], prob_ref[k], preferred_element_type=F32
        )
        part, there = where[k]
        if k in part_loads:
            part_loads[k].wait()
        for t, tile in enumerate(lane_tiles(paired)):
            lanes = slice(k * WIDE + t * LANES, k * WIDE + (t + 1) * LANES)
            scale = scale_ref[lanes.start // LANES : lanes.stop // LANES, :]
            own_part = part[:, there * WIDE + t * LANES : there * WIDE + (t + 1) * LANES]
            out[:, lanes] = (own_part.astype(F32) - tile * scale).astype(BF16)
        store.start()
    for store in stores:
        store.wait()


SMEM = pl.BlockSpec(memory_space=pltpu.SMEM)
VMEM = pl.BlockSpec(memory_space=pltpu.VMEM)
ANY = pl.BlockSpec(memory_space=pl.ANY)


def params(nbytes):
    return pltpu.CompilerParams(vmem_limit_bytes=int(nbytes) + 8 * 2**20)


def cost(flops, nbytes, exps=0):
    return pl.CostEstimate(flops=int(flops), bytes_accessed=int(nbytes), transcendentals=int(exps))


def exchange(value, axis):
    return lax.all_to_all(value, axis, 0, 0)


def following(value, axis):
    n = lax.axis_size(axis)
    return [lax.ppermute(value, axis, [(i, (i - s) % n) for i in range(n)]) for s in range(1, n)]


def tree_sum(value, axis):
    n = lax.axis_size(axis)
    values = [value] + [
        lax.ppermute(value, axis, [(i, i ^ s) for i in range(n)]) for s in range(1, n)
    ]
    while len(values) > 1:
        values = [a + b for a, b in zip(values[::2], values[1::2])]
    return values[0]


def local(teacher_feats, student_feats, proto_weight):
    parts, groups = lax.axis_size("proto"), lax.axis_size("batch")
    own, width = teacher_feats.shape
    local_protos = proto_weight.shape[1]
    rows = own * groups
    others = rows - own
    protos = local_protos * parts
    feats = width // groups
    share = own // parts
    tiles = rows // LANES
    height = local_protos // LANES
    chunks = local_protos // WIDE
    place = jnp.stack([lax.axis_index("batch"), lax.axis_index("proto")]).astype(jnp.int32)
    struct = jax.ShapeDtypeStruct
    weight_bytes = 2 * width * local_protos
    exp_bytes = 2 * own * local_protos
    others_bytes = 2 * others * local_protos
    spread = pltpu.VMEM((own, LANES), F32)
    w_buffer = pltpu.VMEM((width, local_protos), BF16)
    exp_buffer = pltpu.VMEM((chunks, own, WIDE), BF16)
    sems = pltpu.SemaphoreType.DMA((chunks,))
    log_protos = math.log2(protos)
    token = struct((8, LANES), F32)

    def far(value):
        return pltpu.with_memory_space_constraint(value, pltpu.HBM)

    weight = far(proto_weight)
    teacher_rows, student_rows = far(teacher_feats), far(student_feats)
    s_all = following(student_feats, "batch")

    exps = pltpu.HBM((chunks, own, WIDE), BF16)
    t_exp, s_exp, stats = pl.pallas_call(
        stats_kernel,
        in_specs=[ANY] * 3,
        out_specs=[ANY, ANY, VMEM],
        out_shape=[
            exps,
            exps,
            struct((parts, 4 * own // LANES, LANES), F32),
        ],
        scratch_shapes=[
            pltpu.VMEM((2, own, width), BF16),
            w_buffer,
            pltpu.VMEM((2 * own, width), BF16),
            pltpu.VMEM((2, chunks, own, WIDE), BF16),
            pltpu.VMEM((2 * own, local_protos), F32),
            pltpu.VMEM((2 * own, LANES), F32),
            pltpu.VMEM((2 * own, LANES), F32),
            pltpu.SemaphoreType.DMA((2,)),
            sems, sems, sems,
        ],
        compiler_params=params(weight_bytes + 6 * exp_bytes),
        cost_estimate=cost(4 * own * width * local_protos, weight_bytes),
        name="own_rows",
    )(teacher_rows, student_rows, weight)
    t_exp, s_exp = far(t_exp), far(s_exp)

    back_student = pl.pallas_call(
        own_back_kernel,
        in_specs=[ANY] * 3,
        out_specs=VMEM,
        out_shape=struct((own, width), F32),
        scratch_shapes=[exp_buffer, w_buffer, sems, sems],
        compiler_params=params(weight_bytes + exp_bytes),
        cost_estimate=cost(2 * own * width * local_protos, weight_bytes),
        name="own_back",
    )(stats, s_exp, weight)

    stats = exchange(stats, "proto")

    first_shape = (1, height + 8, LANES)
    factor, cols = pl.pallas_call(
        first_column_kernel,
        in_specs=[SMEM, VMEM, ANY, ANY] + [ANY] * (groups - 1),
        out_specs=[VMEM, VMEM],
        out_shape=[token, struct(first_shape, F32)],
        scratch_shapes=[spread, exp_buffer, sems],
        compiler_params=params(exp_bytes),
        cost_estimate=cost(2 * own * local_protos, exp_bytes),
        name="first_columns",
    )(place, stats, t_exp, back_student, *s_all)

    unit, feat, scaled, t_unit = pl.pallas_call(
        functools.partial(student_rows_kernel, float(protos)),
        in_specs=[SMEM, VMEM, VMEM, VMEM] + [VMEM] * (groups - 1) + [ANY],
        out_specs=[VMEM] * 4,
        out_shape=[
            struct((others, width), BF16), struct((feats, rows), BF16), struct((feats, own), BF16),
            struct((own, width), BF16),
        ],
        scratch_shapes=[pltpu.VMEM((width, rows), BF16)],
        compiler_params=params(2 * rows * width),
        cost_estimate=cost(8 * rows * width, 2 * rows * width),
        name="student_rows",
    )(place, factor, teacher_feats, student_feats, *s_all, cols)
    t_all = following(t_unit, "batch")
    cols = [cols] + following(cols, "batch")
    logs = cols

    counts = [c * chunks // 8 for c in (1, 1, 1, 1, 4)]
    grad_parts = []

    def student_piece(before):
        turn = len(grad_parts)
        first, count = sum(counts[:turn]), counts[turn]
        grad_part, done = pl.pallas_call(
            functools.partial(student_kernel, log_protos, first, groups),
            in_specs=[VMEM] * 3 + [ANY] * 2 + [VMEM] * groups + [ANY],
            out_specs=[VMEM, VMEM],
            out_shape=[struct((feats, count * WIDE), BF16), token],
            scratch_shapes=[
                pltpu.VMEM((others, LANES), F32),
                pltpu.VMEM((others, WIDE), BF16),
                pltpu.VMEM((count, own, WIDE), BF16),
                pltpu.VMEM((width, count * WIDE), BF16),
            ]
            + [pltpu.SemaphoreType.DMA((count,))] * 2,
            compiler_params=params(16 * 2**20),
            cost_estimate=cost(2.5 * rows * width * WIDE * count, 2 * width * WIDE * count),
            name="student_side",
        )(unit, feat, scaled, s_exp, weight, *logs, before)
        grad_parts.append(grad_part)
        return done

    done = unit
    for turn in range(SWEEPS - 1):
        late = t_all if turn == 1 else []
        sums = pl.pallas_call(
            functools.partial(row_kernel, len(cols)),
            in_specs=[VMEM] * (len(cols) + 1) + [ANY] * (2 + len(late)),
            out_specs=VMEM,
            out_shape=struct((parts, 8, LANES), F32),
            scratch_shapes=[pltpu.VMEM((height, LANES), F32), spread, exp_buffer, sems],
            compiler_params=params(exp_bytes),
            cost_estimate=cost(2 * own * local_protos, exp_bytes),
            name="rows",
        )(*cols, factor, t_exp, done, *late)
        done = student_piece(sums)
        sums = exchange(sums, "proto")
        middle = turn < SWEEPS - 2
        cols = pl.pallas_call(
            column_kernel,
            in_specs=[VMEM, VMEM, ANY, ANY],
            out_specs=VMEM,
            out_shape=struct((groups if middle else 1, height, LANES), F32),
            scratch_shapes=[spread, exp_buffer, sems],
            compiler_params=params(exp_bytes),
            cost_estimate=cost(2 * own * local_protos, exp_bytes),
            name="columns",
        )(sums, factor, t_exp, done)
        done = student_piece(cols)
        if middle:
            cols = [exchange(cols, "batch")]
        else:
            cols = [cols] + following(cols, "batch")

    sum_rows = -(-(tiles + own // LANES) // 16) * 16
    message_shape = (parts, 2 * share + sum_rows, width)
    prob, col_scale, message = pl.pallas_call(
        functools.partial(last_kernel, groups),
        in_specs=[VMEM] + [ANY] * 4 + [VMEM] * (3 * groups - 1) + [ANY],
        out_specs=[ANY, VMEM, VMEM],
        out_shape=[
            pltpu.HBM((chunks, others, WIDE), BF16),
            struct((height, LANES), F32),
            struct(message_shape, BF16),
        ],
        scratch_shapes=[
            pltpu.VMEM((others, width), BF16),
            pltpu.VMEM((others, LANES), F32),
            pltpu.VMEM((others, LANES), F32),
            spread,
            pltpu.VMEM((own, width), F32),
            pltpu.VMEM((own, WIDE), BF16),
            pltpu.VMEM((sum_rows, LANES), F32),
            pltpu.VMEM((min(chunks, 3), others, WIDE), BF16),
            exp_buffer,
            w_buffer,
            pltpu.VMEM((own, width), BF16),
            pltpu.VMEM((own, width), F32),
            sems, sems, sems,
            pltpu.SemaphoreType.DMA((2,)),
        ],
        compiler_params=params(20 * 2**20 + weight_bytes + exp_bytes),
        cost_estimate=cost(2 * rows * width * local_protos, others_bytes),
        name="last_rows",
    )(
        factor, student_rows, far(back_student), t_exp, weight, *t_all, *logs, *cols, done,
    )
    done = student_piece(message)
    message = exchange(message, "proto")

    grad_rows, loss_part, sums = pl.pallas_call(
        functools.partial(rows_kernel, tiles, float(protos)),
        in_specs=[SMEM, ANY, VMEM, VMEM, ANY],
        out_specs=[VMEM] * 3,
        out_shape=[struct((parts, share, width), BF16), token, struct((sum_rows, LANES), F32)],
        scratch_shapes=[spread, pltpu.VMEM((share, width), BF16), pltpu.SemaphoreType.DMA],
        compiler_params=params(0),
        name="row_grads",
    )(place, student_rows, message, logs[0], done)
    grad_rows = exchange(grad_rows, "proto").reshape(own, width).astype(F32)
    loss = tree_sum(loss_part, "batch")[0, 0]

    grad_weight = pl.pallas_call(
        functools.partial(grad_kernel, counts, float(protos)),
        in_specs=[ANY] * 2
        + [VMEM] * 4
        + [ANY if i in FAR else VMEM for i in range(len(counts))],
        out_specs=ANY,
        out_shape=struct((feats, local_protos), BF16),
        scratch_shapes=[
            pltpu.VMEM((feats, rows), BF16),
            exp_buffer,
            pltpu.VMEM((chunks, others, WIDE), BF16),
            pltpu.VMEM((feats, local_protos), BF16),
            pltpu.VMEM((feats, sum(counts[i] for i in FAR) * WIDE), BF16),
            sems, sems, sems, sems,
        ],
        compiler_params=params(exp_bytes + others_bytes + 4 * feats * local_protos),
        cost_estimate=cost(2 * feats * rows * local_protos, others_bytes),
        name="weight_grads",
    )(t_exp, far(prob), feat, col_scale, sums, factor, *[far(x) if i in FAR else x for i, x in enumerate(grad_parts)])
    return grad_weight, grad_rows, loss


def solution(mesh):
    return jax.shard_map(
        local,
        mesh=mesh,
        in_specs=(P("batch", None), P("batch", None), P(None, "proto")),
        out_specs=(P("batch", "proto"), P("batch", None), P()),
        check_vma=False,
    )
```

```python
import functools
import math

import jax
import jax.numpy as jnp
from jax import lax
from jax.experimental import pallas as pl
from jax.experimental.pallas import tpu as pltpu
from jax.sharding import PartitionSpec as P

SWEEPS = 3
TEMP_TEACHER = 0.04
TEMP_STUDENT = 0.1
LOG2E = math.log2(math.e)
SCALE_TEACHER = LOG2E / TEMP_TEACHER
SCALE_STUDENT = LOG2E / TEMP_STUDENT
LANES = 128
WIDE = 1024
TILE = 256
FAR = (2, 3)
F32 = jnp.float32
BF16 = jnp.bfloat16


def unit_rows(values):
    wide = values.astype(F32)
    length = jnp.sqrt(jnp.sum(wide * wide, axis=-1, keepdims=True) + 1e-06)
    return wide / length, length


def diagonal():
    shape = (LANES, LANES)
    return lax.broadcasted_iota(jnp.int32, shape, 0) == lax.broadcasted_iota(jnp.int32, shape, 1)


def to_column(row):
    spread = jnp.where(diagonal(), jnp.broadcast_to(row, (LANES, LANES)), 0.0)
    return jnp.sum(spread, axis=1, keepdims=True)


def to_row(column):
    spread = jnp.where(diagonal(), jnp.broadcast_to(column, (LANES, LANES)), 0.0)
    return jnp.sum(spread, axis=0, keepdims=True)


def spread_rows(ref, rows):
    for a in range(rows.shape[0]):
        ref[a * LANES : (a + 1) * LANES, :] = jnp.broadcast_to(
            to_column(rows[a : a + 1, :]), (LANES, LANES)
        )


def pack_rows(ref, columns):
    for a in range(columns.shape[0] // LANES):
        ref[a : a + 1, :] = to_row(columns[a * LANES : (a + 1) * LANES, :])


def lane_tiles(values):
    return [values[:, t * LANES : (t + 1) * LANES] for t in range(values.shape[1] // LANES)]


def fold(values):
    return functools.reduce(jnp.add, lane_tiles(values))


def column_sums(values):
    rows, cols = values.shape
    return jnp.sum(values.reshape(rows // 8, 8, cols), axis=0)


def nt_dot(a, b):
    return lax.dot_general(a, b, (((1,), (1,)), ((), ())), preferred_element_type=F32)


def add_up(values):
    return functools.reduce(jnp.add, values)


def repeat(out_ref):
    for p in range(1, out_ref.shape[0]):
        out_ref[p] = out_ref[0]


def chunk(k):
    return slice(k * WIDE, (k + 1) * WIDE)


def copies(source, target, sems, first=0, back=0, count=None):
    def chunks(ref):
        return ref.shape[0] if len(ref.shape) == 3 else ref.shape[1] // WIDE

    count = count or min(chunks(source), chunks(target))
    return [copy_of(source, target, sems, k, first, back) for k in range(count)]


def columns_of(k, first=0, count=WIDE):
    return pl.ds(pl.multiple_of(k * WIDE + first, LANES), count)


def copy_of(source, target, sems, k, first=0, back=0):
    def part(ref, k):
        return ref.at[k] if len(ref.shape) == 3 else ref.at[:, columns_of(k)]

    return pltpu.make_async_copy(part(source, first + k), part(target, back + k), sems.at[k])


def start(*lists):
    for each in zip(*lists):
        for copy in each:
            copy.start()


def whole_copies(pairs, sems):
    return [pltpu.make_async_copy(a, b, sems.at[i]) for i, (a, b) in enumerate(pairs)]


def wait(*lists):
    for each in lists:
        for copy in each:
            copy.wait()


def stats_kernel(
    t_hbm, s_hbm, w_hbm, t_out, s_out, out_ref,
    raw, w_ref, unit, exps, logits, top, total, raw_sem, w_sem, t_sem, s_sem,
):
    own = raw.shape[1]
    quarter = out_ref.shape[1] // 4
    chunks = exps.shape[1]
    halves = (slice(0, own), slice(own, 2 * own))
    loads = copies(w_hbm, w_ref, w_sem)
    raw_loads = [
        pltpu.make_async_copy(ref, raw.at[which], raw_sem.at[which])
        for which, ref in enumerate((t_hbm, s_hbm))
    ]
    start(raw_loads, loads[:2])
    start(loads[2:])
    top[...] = jnp.full(top.shape, -1e30, F32)
    total[...] = jnp.zeros(total.shape, F32)
    wait(raw_loads)
    for which in range(2):
        unit[halves[which], :] = unit_rows(raw[which])[0].astype(BF16)

    @pl.loop(0, chunks)
    def _(k):
        copy_of(w_hbm, w_ref, w_sem, k).wait()
        for n in range(0, WIDE, TILE):
            here = columns_of(k, n, TILE)
            values = jnp.dot(unit[...], w_ref[:, here], preferred_element_type=F32)
            for half, scale in zip(halves, (SCALE_TEACHER, SCALE_STUDENT)):
                part = values[half, :] * scale
                logits[half, here] = part
                top[half, :] = functools.reduce(jnp.maximum, lane_tiles(part), top[half, :])

    peak = jnp.max(top[...], axis=1, keepdims=True)
    top[...] = jnp.broadcast_to(peak, top.shape)

    @pl.loop(0, chunks)
    def _(k):
        for which, (half, out, sem) in enumerate(zip(halves, (t_out, s_out), (t_sem, s_sem))):
            shift = top[half, :]
            for n in range(0, WIDE, 2 * TILE):
                tiles = lane_tiles(logits[half, columns_of(k, n, 2 * TILE)])
                tiles = [jnp.exp2(tile - shift) for tile in tiles]
                for t, tile in enumerate(tiles):
                    lanes = slice(n + t * LANES, n + (t + 1) * LANES)
                    exps[which, k, :, lanes] = tile.astype(BF16)
                total[half, :] += add_up(tiles)
            copy_of(exps.at[which], out, sem, k).start()

    sums = jnp.sum(total[...], axis=1, keepdims=True)
    for which, half in enumerate(halves):
        for k, column in enumerate((peak, sums)):
            first = (2 * which + k) * quarter
            pack_rows(out_ref.at[0, first : first + quarter], column[half, :])
    repeat(out_ref)
    wait(copies(exps.at[0], t_out, t_sem), copies(exps.at[1], s_out, s_sem))


def merged(stats_ref, which):
    parts, height, _ = stats_ref.shape
    quarter = height // 4
    first = 2 * which * quarter
    tops = [stats_ref[p, first : first + quarter, :] for p in range(parts)]
    top = functools.reduce(jnp.maximum, tops)
    sums = [
        stats_ref[p, first + quarter : first + 2 * quarter, :] * jnp.exp2(tops[p] - top)
        for p in range(parts)
    ]
    return top + jnp.log2(add_up(sums))


def column_pass(exp_hbm, exp_ref, sem, weight, out_ref):
    height = WIDE // LANES

    @pl.loop(0, exp_ref.shape[0])
    def _(k):
        copy_of(exp_hbm, exp_ref, sem, k).wait()
        sums = jnp.zeros((8, WIDE), F32)
        for g in range(0, exp_ref.shape[1], 16):
            shift = weight[g : g + 16, :]
            tiles = lane_tiles(exp_ref[k, g : g + 16, :].astype(F32))
            sums = sums + column_sums(jnp.concatenate([tile * shift for tile in tiles], axis=1))
        sums = jnp.sum(sums, axis=0, keepdims=True)
        block = jnp.concatenate(lane_tiles(sums), axis=0)
        for g in range(out_ref.shape[0]):
            out_ref[g, pl.ds(pl.multiple_of(k * height, height), height), :] = block


def first_column_kernel(place_ref, stats_ref, exp_hbm, *refs):
    factor_ref, out_ref, weight, exp_ref, sem = refs[-5:]
    start(copies(exp_hbm, exp_ref, sem))
    quarter = stats_ref.shape[1] // 4
    height = out_ref.shape[1] - 8
    own = stats_ref[pl.ds(place_ref[1], 1)][0]
    factor_ref[...] = jnp.zeros(factor_ref.shape, F32)
    rows = []
    for which in range(2):
        log_sum = merged(stats_ref, which)
        here = slice(which * quarter, (which + 1) * quarter)
        factor_ref[here, :] = jnp.exp2(
            own[2 * which * quarter : (2 * which + 1) * quarter, :] - log_sum
        )
        rows.append(log_sum)
    rows.append(jnp.zeros((8 - 2 * quarter, LANES), F32))
    logs = jnp.concatenate(rows, axis=0)
    for g in range(out_ref.shape[0]):
        out_ref[g, height:, :] = logs
    spread_rows(weight, factor_ref[:quarter, :])
    column_pass(exp_hbm, exp_ref, sem, weight, out_ref)


def column_kernel(sums_ref, factor_ref, exp_hbm, *refs):
    out_ref, weight, exp_ref, sem = refs[-4:]
    start(copies(exp_hbm, exp_ref, sem))
    quarter = weight.shape[0] // LANES
    scale = 1.0 / add_up([sums_ref[p, :quarter, :] for p in range(sums_ref.shape[0])])
    spread_rows(weight, scale * factor_ref[:quarter, :])
    column_pass(exp_hbm, exp_ref, sem, weight, out_ref)


def column_scales(cols, height):
    return 1.0 / add_up([ref[g, :height, :] for ref in cols for g in range(ref.shape[0])])


def chunk_scales(scales, k):
    height = WIDE // LANES
    return scales[pl.ds(pl.multiple_of(k * height, height), height), :]


def add_row_sums(rows, values, scale):
    for g in range(0, values.shape[0], 32):
        total = rows[g : g + 32, :]
        for t, tile in enumerate(lane_tiles(values[g : g + 32, :].astype(F32))):
            total = total + tile * scale[t : t + 1, :]
        rows[g : g + 32, :] = total


def row_kernel(count, *refs):
    cols, (factor_ref, exp_hbm) = refs[:count], refs[count : count + 2]
    out_ref, scales, rows, exp_ref, sem = refs[-5:]
    start(copies(exp_hbm, exp_ref, sem))
    scales[...] = column_scales(cols, scales.shape[0])
    rows[...] = jnp.zeros(rows.shape, F32)
    quarter = rows.shape[0] // LANES
    out_ref[0] = jnp.zeros(out_ref.shape[1:], F32)

    @pl.loop(0, exp_ref.shape[0])
    def _(k):
        copy_of(exp_hbm, exp_ref, sem, k).wait()
        add_row_sums(rows, exp_ref.at[k], chunk_scales(scales, k))

    pack_rows(out_ref.at[0, :quarter], jnp.sum(rows[...], axis=1, keepdims=True))
    out_ref[0, :quarter, :] = out_ref[0, :quarter, :] * factor_ref[:quarter, :]
    repeat(out_ref)


def own_back_kernel(before_ref, exp_hbm, w_hbm, back_ref, exp_ref, w_ref, exp_sem, w_sem):
    start(copies(exp_hbm, exp_ref, exp_sem), copies(w_hbm, w_ref, w_sem))
    back_ref[...] = jnp.zeros(back_ref.shape, F32)

    @pl.loop(0, exp_ref.shape[0])
    def _(k):
        copy_of(exp_hbm, exp_ref, exp_sem, k).wait()
        copy_of(w_hbm, w_ref, w_sem, k).wait()
        back_ref[...] += nt_dot(exp_ref[k], w_ref[:, columns_of(k)])


def relative_logs(logs, lse, which, shift=0.0):
    own = lse.shape[0] // (len(logs) - 1)
    quarter = own // LANES
    for g, ref in enumerate(logs[1:]):
        first = ref.shape[1] - 8 + which * quarter
        spread_rows(lse.at[g * own : (g + 1) * own], ref[0, first : first + quarter, :] - shift)


def student_rows_kernel(protos, place_ref, factor_ref, t_ref, own_ref, *refs):
    unit_ref, feat_ref, scaled_ref, t_unit, turned = refs[-5:]
    t_unit[...] = unit_rows(t_ref[...])[0].astype(BF16)
    own = own_ref.shape[0]
    groups = turned.shape[1] // own
    raw = refs[: groups - 1]
    quarter, feats = own // LANES, feat_ref.shape[0]
    for g in range(groups):
        half = unit_rows((raw[g - 1] if g else own_ref)[...])[0].astype(BF16)
        if g:
            unit_ref[(g - 1) * own : g * own, :] = half
        half = half.astype(F32)
        for a in range(0, own, LANES):
            first = g * own + a
            turned[:, first : first + LANES] = jnp.transpose(half[a : a + LANES, :]).astype(BF16)
    feat = turned[pl.ds(pl.multiple_of(place_ref[0] * feats, feats), feats), :]
    feat_ref[...] = feat
    for a in range(quarter):
        lanes = slice(a * LANES, (a + 1) * LANES)
        factor = factor_ref[quarter + a : quarter + a + 1, :] * protos
        scaled_ref[:, lanes] = (feat[:, lanes].astype(F32) * factor).astype(BF16)


def probabilities(unit, w_ref, k, lse, scale, use):
    for n in range(0, WIDE, TILE):
        logits = jnp.dot(
            unit[...], w_ref[:, columns_of(k, n, TILE)], preferred_element_type=F32
        )
        shift = lse[...]
        use(n, [jnp.exp2(tile * scale - shift) for tile in lane_tiles(logits)])


def student_kernel(
    log_protos, first, groups, unit, feat_ref, scaled_ref, exp_hbm, w_hbm, *refs
):
    logs = refs[:groups]
    grad, token_ref, lse, prob, exp_ref, w_ref, exp_sem, w_sem = refs[-8:]
    own, count = exp_ref.shape[1], exp_ref.shape[0]
    exp_loads = copies(exp_hbm, exp_ref, exp_sem, first, 0, count)
    w_loads = copies(w_hbm, w_ref, w_sem, first, 0, count)
    start(w_loads, exp_loads)
    token_ref[...] = jnp.zeros(token_ref.shape, F32)
    relative_logs(logs, lse, 1, log_protos)

    @pl.loop(0, count)
    def _(k):
        copy_of(w_hbm, w_ref, w_sem, k, first).wait()

        def use(n, tiles):
            for t, tile in enumerate(tiles):
                prob[:, n + t * LANES : n + (t + 1) * LANES] = tile.astype(BF16)

        probabilities(unit, w_ref, k, lse, SCALE_STUDENT, use)
        copy_of(exp_hbm, exp_ref, exp_sem, k, first).wait()
        values = jnp.dot(scaled_ref[...], exp_ref[k], preferred_element_type=F32)
        values = values + jnp.dot(feat_ref[:, own:], prob[...], preferred_element_type=F32)
        grad[:, columns_of(k)] = values.astype(BF16)


def as_three(value):
    high = value.astype(BF16)
    rest = value - high.astype(F32)
    middle = rest.astype(BF16)
    return high, middle, (rest - middle.astype(F32)).astype(BF16)


def last_kernel(groups, factor_ref, own_hbm, student_hbm, exp_hbm, w_hbm, s_hbm, *refs):
    units, refs = refs[: groups - 1], refs[groups - 1 :]
    logs, cols, refs = refs[:groups], refs[groups : 2 * groups], refs[2 * groups :]
    (
        prob_hbm, scale_ref, out_ref, unit, lse, rows, own_rows, back, scaled, sums, prob_ref,
        exp_ref, w_ref, own_ref, student_ref, s_ref, prob_sem, exp_sem, w_sem, sem, s_sem,
    ) = refs[-21:]
    w_loads, exp_loads = copies(w_hbm, w_ref, w_sem), copies(exp_hbm, exp_ref, exp_sem)
    late_loads = whole_copies([(own_hbm, own_ref), (student_hbm, student_ref)], sem)
    half_chunks = s_ref.shape[0]
    start(w_loads, exp_loads)
    start(late_loads)
    start(copies(s_hbm, s_ref, s_sem, exp_ref.shape[0] - half_chunks, 0, half_chunks))
    slots, others, _ = prob_ref.shape
    own, chunks = exp_ref.shape[1], exp_ref.shape[0]
    tiles = (own + others) // LANES
    quarter = own // LANES
    scale_ref[...] = column_scales(cols, scale_ref.shape[0])
    rows[...] = jnp.zeros(rows.shape, F32)
    own_rows[...] = jnp.zeros(own_rows.shape, F32)
    back[...] = jnp.zeros(back.shape, F32)
    relative_logs(logs, lse, 0)
    for g in range(groups - 1):
        unit[g * own : (g + 1) * own, :] = units[g][...]
    partner = slice((groups // 2 - 1) * own, groups // 2 * own)

    def store(k):
        return pltpu.make_async_copy(prob_ref.at[lax.rem(k, slots)], prob_hbm.at[k], prob_sem.at[k])

    def one_chunk(k):
        copy_of(w_hbm, w_ref, w_sem, k).wait()
        slot = lax.rem(k, slots)
        scale = chunk_scales(scale_ref, k)

        @pl.when(k >= slots)
        def _():
            store(k - slots).wait()

        def use(n, tiles):
            for t, tile in enumerate(tiles):
                prob_ref[slot, :, n + t * LANES : n + (t + 1) * LANES] = tile.astype(BF16)
            first = n // LANES
            tiles = [tile * scale[first + t : first + t + 1, :] for t, tile in enumerate(tiles)]
            rows[...] += add_up(tiles)
            for t, tile in enumerate(tiles):
                scaled[:, n + t * LANES : n + (t + 1) * LANES] = tile[partner, :].astype(BF16)

        probabilities(unit, w_ref, k, lse, SCALE_TEACHER, use)
        store(k).start()
        back[...] += nt_dot(scaled[...], w_ref[:, columns_of(k)])
        copy_of(exp_hbm, exp_ref, exp_sem, k).wait()
        add_row_sums(own_rows, exp_ref.at[k], scale)

    @pl.loop(0, chunks - half_chunks)
    def _(k):
        one_chunk(k)

    wait(late_loads)

    @pl.loop(chunks - half_chunks, chunks)
    def _(k):
        one_chunk(k)
        j = k - (chunks - half_chunks)
        copy_of(s_hbm, s_ref, s_sem, j, chunks - half_chunks).wait()
        student_ref[...] += nt_dot(s_ref[j], w_ref[:, columns_of(k)])

    sums[...] = jnp.zeros(sums.shape, F32)
    pack_rows(sums.at[:quarter], jnp.sum(own_rows[...], axis=1, keepdims=True))
    sums[:quarter, :] = sums[:quarter, :] * factor_ref[:quarter, :]
    pack_rows(sums.at[quarter:tiles], jnp.sum(rows[...], axis=1, keepdims=True))
    half = unit_rows(own_ref[...])[0].astype(BF16).astype(F32)
    inner = jnp.sum(half * back[...], axis=1, keepdims=True)
    pack_rows(sums.at[tiles : tiles + quarter], inner)
    parts = out_ref.shape[0]
    share = own // parts
    protos = 1.0 * out_ref.shape[0] * w_ref.shape[1]
    student = []
    for a in range(quarter):
        factor = to_column(factor_ref[quarter + a : quarter + a + 1, :] * protos)
        student.append(student_ref[a * LANES : (a + 1) * LANES, :] * factor)
    student = jnp.concatenate(student, axis=0).astype(BF16)
    terms = list(as_three(sums[...]))
    terms.append(jnp.zeros((sums.shape[0], out_ref.shape[2] - 3 * LANES), BF16))
    terms = jnp.concatenate(terms, axis=1)
    for p in range(parts):
        here = slice(p * share, (p + 1) * share)
        out_ref[p] = jnp.concatenate(
            [student[here, :], back[here, :].astype(BF16), terms], axis=0
        )
    for k in range(max(0, chunks - slots), chunks):
        store(k).wait()


def total_sums(message_ref, first):
    parts = message_ref.shape[0]
    each = [
        add_up([t.astype(F32) for t in lane_tiles(message_ref[p, first:, : 3 * LANES])[::-1]])
        for p in range(parts)
    ]
    return add_up(each)


def rows_kernel(tiles, protos, place_ref, s_hbm, message_ref, logs_ref, *refs):
    out_ref, loss_ref, sums_ref, weight, s_ref, sem = refs[-6:]
    parts = message_ref.shape[0]
    share, own = out_ref.shape[1], weight.shape[0]
    mine = pl.ds(pl.multiple_of(place_ref[1] * share, share), share)
    load = pltpu.make_async_copy(s_hbm.at[mine], s_ref, sem)
    load.start()
    quarter = own // LANES
    first = tiles // 2
    totals = total_sums(message_ref, 2 * share)
    sums_ref[...] = totals
    scale = 1.0 / totals[first : first + quarter, :]
    spread_rows(weight, scale)
    total = add_up([message_ref[p, :share, :].astype(F32) for p in range(parts)])
    paired = add_up([message_ref[p, share : 2 * share, :].astype(F32) for p in range(parts)])
    total = total - paired * (weight[mine, :1] * protos)
    load.wait()
    unit, length = unit_rows(s_ref[...])
    total = (total - unit * jnp.sum(unit * total, axis=-1, keepdims=True)) / length
    out_ref[0] = total.astype(BF16)
    repeat(out_ref)
    height = logs_ref.shape[1] - 8
    logs = logs_ref[0, height + quarter : height + 2 * quarter, :]
    terms = logs / LOG2E - totals[tiles : tiles + quarter, :] * scale / TEMP_STUDENT
    loss_ref[...] = jnp.broadcast_to(jnp.sum(terms) / (tiles * LANES), loss_ref.shape)


def grad_kernel(counts, protos, exp_hbm, prob_hbm, feat_ref, scale_ref, sums_ref, factor_ref, *refs):
    parts = refs[: len(counts)]
    out_hbm, scaled, exp_ref, prob_ref, out, part_ref, exp_sem, prob_sem, sem, part_sem = refs[-10:]
    part_loads, where = {}, []
    for i, (count, part) in enumerate(zip(counts, parts)):
        for k in range(count):
            if i in FAR:
                slot = len(part_loads)
                part_loads[len(where)] = copy_of(part, part_ref, part_sem, slot, k - slot)
                where.append((part_ref, slot))
            else:
                where.append((part, k))
    exp_loads = copies(exp_hbm, exp_ref, exp_sem)
    prob_loads = copies(prob_hbm, prob_ref, prob_sem)
    start(exp_loads[:2], prob_loads[:2])
    start(list(part_loads.values()))
    start(exp_loads[2:], prob_loads[2:])
    own = exp_ref.shape[1]
    tiles = (own + prob_ref.shape[1]) // LANES
    rows = protos / sums_ref[:tiles, :]
    for a in range(tiles):
        other = (a + tiles // 2) % tiles
        feat = feat_ref[:, other * LANES : (other + 1) * LANES].astype(F32)
        row = rows[a : a + 1, :]
        if a < own // LANES:
            row = row * factor_ref[a : a + 1, :]
        scaled[:, a * LANES : (a + 1) * LANES] = (feat * row).astype(BF16)
    stores = copies(out, out_hbm, sem)
    for k, store in enumerate(stores):
        exp_loads[k].wait()
        prob_loads[k].wait()
        paired = jnp.dot(scaled[:, :own], exp_ref[k], preferred_element_type=F32)
        paired = paired + jnp.dot(
            scaled[:, own:], prob_ref[k], preferred_element_type=F32
        )
        part, there = where[k]
        if k in part_loads:
            part_loads[k].wait()
        for t, tile in enumerate(lane_tiles(paired)):
            lanes = slice(k * WIDE + t * LANES, k * WIDE + (t + 1) * LANES)
            scale = scale_ref[lanes.start // LANES : lanes.stop // LANES, :]
            own_part = part[:, there * WIDE + t * LANES : there * WIDE + (t + 1) * LANES]
            out[:, lanes] = (own_part.astype(F32) - tile * scale).astype(BF16)
        store.start()
    for store in stores:
        store.wait()


SMEM = pl.BlockSpec(memory_space=pltpu.SMEM)
VMEM = pl.BlockSpec(memory_space=pltpu.VMEM)
ANY = pl.BlockSpec(memory_space=pl.ANY)


def params(nbytes):
    return pltpu.CompilerParams(vmem_limit_bytes=int(nbytes) + 8 * 2**20)


def cost(flops, nbytes, exps=0):
    return pl.CostEstimate(flops=int(flops), bytes_accessed=int(nbytes), transcendentals=int(exps))


def exchange(value, axis):
    return lax.all_to_all(value, axis, 0, 0)


def following(value, axis):
    n = lax.axis_size(axis)
    return [lax.ppermute(value, axis, [(i, (i - s) % n) for i in range(n)]) for s in range(1, n)]


def tree_sum(value, axis):
    n = lax.axis_size(axis)
    values = [value] + [
        lax.ppermute(value, axis, [(i, i ^ s) for i in range(n)]) for s in range(1, n)
    ]
    while len(values) > 1:
        values = [a + b for a, b in zip(values[::2], values[1::2])]
    return values[0]


def local(teacher_feats, student_feats, proto_weight):
    parts, groups = lax.axis_size("proto"), lax.axis_size("batch")
    own, width = teacher_feats.shape
    local_protos = proto_weight.shape[1]
    rows = own * groups
    others = rows - own
    protos = local_protos * parts
    feats = width // groups
    share = own // parts
    tiles = rows // LANES
    height = local_protos // LANES
    chunks = local_protos // WIDE
    place = jnp.stack([lax.axis_index("batch"), lax.axis_index("proto")]).astype(jnp.int32)
    struct = jax.ShapeDtypeStruct
    weight_bytes = 2 * width * local_protos
    exp_bytes = 2 * own * local_protos
    others_bytes = 2 * others * local_protos
    spread = pltpu.VMEM((own, LANES), F32)
    w_buffer = pltpu.VMEM((width, local_protos), BF16)
    exp_buffer = pltpu.VMEM((chunks, own, WIDE), BF16)
    sems = pltpu.SemaphoreType.DMA((chunks,))
    half_chunks = chunks // 2
    log_protos = math.log2(protos)
    token = struct((8, LANES), F32)

    def far(value):
        return pltpu.with_memory_space_constraint(value, pltpu.HBM)

    weight = far(proto_weight)
    teacher_rows, student_rows = far(teacher_feats), far(student_feats)
    s_all = following(student_feats, "batch")

    exps = pltpu.HBM((chunks, own, WIDE), BF16)
    t_exp, s_exp, stats = pl.pallas_call(
        stats_kernel,
        in_specs=[ANY] * 3,
        out_specs=[ANY, ANY, VMEM],
        out_shape=[
            exps,
            exps,
            struct((parts, 4 * own // LANES, LANES), F32),
        ],
        scratch_shapes=[
            pltpu.VMEM((2, own, width), BF16),
            w_buffer,
            pltpu.VMEM((2 * own, width), BF16),
            pltpu.VMEM((2, chunks, own, WIDE), BF16),
            pltpu.VMEM((2 * own, local_protos), F32),
            pltpu.VMEM((2 * own, LANES), F32),
            pltpu.VMEM((2 * own, LANES), F32),
            pltpu.SemaphoreType.DMA((2,)),
            sems, sems, sems,
        ],
        compiler_params=params(weight_bytes + 6 * exp_bytes),
        cost_estimate=cost(4 * own * width * local_protos, weight_bytes),
        name="own_rows",
    )(teacher_rows, student_rows, weight)
    t_exp, s_exp = far(t_exp), far(s_exp)

    back_student = pl.pallas_call(
        own_back_kernel,
        in_specs=[ANY] * 3,
        out_specs=VMEM,
        out_shape=struct((own, width), F32),
        scratch_shapes=[
            pltpu.VMEM((half_chunks, own, WIDE), BF16),
            pltpu.VMEM((width, half_chunks * WIDE), BF16),
            sems, sems,
        ],
        compiler_params=params(weight_bytes + exp_bytes),
        cost_estimate=cost(2 * own * width * local_protos, weight_bytes),
        name="own_back",
    )(stats, s_exp, weight)

    stats = exchange(stats, "proto")

    first_shape = (1, height + 8, LANES)
    factor, cols = pl.pallas_call(
        first_column_kernel,
        in_specs=[SMEM, VMEM, ANY, ANY] + [ANY] * (groups - 1),
        out_specs=[VMEM, VMEM],
        out_shape=[token, struct(first_shape, F32)],
        scratch_shapes=[spread, exp_buffer, sems],
        compiler_params=params(exp_bytes),
        cost_estimate=cost(2 * own * local_protos, exp_bytes),
        name="first_columns",
    )(place, stats, t_exp, back_student, *s_all)

    unit, feat, scaled, t_unit = pl.pallas_call(
        functools.partial(student_rows_kernel, float(protos)),
        in_specs=[SMEM, VMEM, VMEM, VMEM] + [VMEM] * (groups - 1) + [ANY],
        out_specs=[VMEM] * 4,
        out_shape=[
            struct((others, width), BF16), struct((feats, rows), BF16), struct((feats, own), BF16),
            struct((own, width), BF16),
        ],
        scratch_shapes=[pltpu.VMEM((width, rows), BF16)],
        compiler_params=params(2 * rows * width),
        cost_estimate=cost(8 * rows * width, 2 * rows * width),
        name="student_rows",
    )(place, factor, teacher_feats, student_feats, *s_all, cols)
    t_all = following(t_unit, "batch")
    cols = [cols] + following(cols, "batch")
    logs = cols

    counts = [c * chunks // 8 for c in (1, 1, 1, 1, 4)]
    grad_parts = []

    def student_piece(before):
        turn = len(grad_parts)
        first, count = sum(counts[:turn]), counts[turn]
        grad_part, done = pl.pallas_call(
            functools.partial(student_kernel, log_protos, first, groups),
            in_specs=[VMEM] * 3 + [ANY] * 2 + [VMEM] * groups + [ANY],
            out_specs=[VMEM, VMEM],
            out_shape=[struct((feats, count * WIDE), BF16), token],
            scratch_shapes=[
                pltpu.VMEM((others, LANES), F32),
                pltpu.VMEM((others, WIDE), BF16),
                pltpu.VMEM((count, own, WIDE), BF16),
                pltpu.VMEM((width, count * WIDE), BF16),
            ]
            + [pltpu.SemaphoreType.DMA((count,))] * 2,
            compiler_params=params(16 * 2**20),
            cost_estimate=cost(2.5 * rows * width * WIDE * count, 2 * width * WIDE * count),
            name="student_side",
        )(unit, feat, scaled, s_exp, weight, *logs, before)
        grad_parts.append(grad_part)
        return done

    done = unit
    for turn in range(SWEEPS - 1):
        late = t_all if turn == 1 else []
        sums = pl.pallas_call(
            functools.partial(row_kernel, len(cols)),
            in_specs=[VMEM] * (len(cols) + 1) + [ANY] * (2 + len(late)),
            out_specs=VMEM,
            out_shape=struct((parts, 8, LANES), F32),
            scratch_shapes=[pltpu.VMEM((height, LANES), F32), spread, exp_buffer, sems],
            compiler_params=params(exp_bytes),
            cost_estimate=cost(2 * own * local_protos, exp_bytes),
            name="rows",
        )(*cols, factor, t_exp, done, *late)
        done = student_piece(sums)
        sums = exchange(sums, "proto")
        middle = turn < SWEEPS - 2
        cols = pl.pallas_call(
            column_kernel,
            in_specs=[VMEM, VMEM, ANY, ANY],
            out_specs=VMEM,
            out_shape=struct((groups if middle else 1, height, LANES), F32),
            scratch_shapes=[spread, exp_buffer, sems],
            compiler_params=params(exp_bytes),
            cost_estimate=cost(2 * own * local_protos, exp_bytes),
            name="columns",
        )(sums, factor, t_exp, done)
        done = student_piece(cols)
        if middle:
            cols = [exchange(cols, "batch")]
        else:
            cols = [cols] + following(cols, "batch")

    sum_rows = -(-(tiles + own // LANES) // 16) * 16
    message_shape = (parts, 2 * share + sum_rows, width)
    prob, col_scale, message = pl.pallas_call(
        functools.partial(last_kernel, groups),
        in_specs=[VMEM] + [ANY] * 5 + [VMEM] * (3 * groups - 1) + [ANY],
        out_specs=[ANY, VMEM, VMEM],
        out_shape=[
            pltpu.HBM((chunks, others, WIDE), BF16),
            struct((height, LANES), F32),
            struct(message_shape, BF16),
        ],
        scratch_shapes=[
            pltpu.VMEM((others, width), BF16),
            pltpu.VMEM((others, LANES), F32),
            pltpu.VMEM((others, LANES), F32),
            spread,
            pltpu.VMEM((own, width), F32),
            pltpu.VMEM((own, WIDE), BF16),
            pltpu.VMEM((sum_rows, LANES), F32),
            pltpu.VMEM((min(chunks, 3), others, WIDE), BF16),
            exp_buffer,
            w_buffer,
            pltpu.VMEM((own, width), BF16),
            pltpu.VMEM((own, width), F32),
            pltpu.VMEM((chunks - half_chunks, own, WIDE), BF16),
            sems, sems, sems,
            pltpu.SemaphoreType.DMA((2,)),
            sems,
        ],
        compiler_params=params(20 * 2**20 + weight_bytes + 2 * exp_bytes),
        cost_estimate=cost(2 * rows * width * local_protos, others_bytes),
        name="last_rows",
    )(
        factor, student_rows, far(back_student), t_exp, weight, s_exp, *t_all, *logs, *cols, done,
    )
    done = student_piece(message)
    message = exchange(message, "proto")

    grad_rows, loss_part, sums = pl.pallas_call(
        functools.partial(rows_kernel, tiles, float(protos)),
        in_specs=[SMEM, ANY, VMEM, VMEM, ANY],
        out_specs=[VMEM] * 3,
        out_shape=[struct((parts, share, width), BF16), token, struct((sum_rows, LANES), F32)],
        scratch_shapes=[spread, pltpu.VMEM((share, width), BF16), pltpu.SemaphoreType.DMA],
        compiler_params=params(0),
        name="row_grads",
    )(place, student_rows, message, logs[0], done)
    grad_rows = exchange(grad_rows, "proto").reshape(own, width).astype(F32)
    loss = tree_sum(loss_part, "batch")[0, 0]

    grad_weight = pl.pallas_call(
        functools.partial(grad_kernel, counts, float(protos)),
        in_specs=[ANY] * 2
        + [VMEM] * 4
        + [ANY if i in FAR else VMEM for i in range(len(counts))],
        out_specs=ANY,
        out_shape=struct((feats, local_protos), BF16),
        scratch_shapes=[
            pltpu.VMEM((feats, rows), BF16),
            exp_buffer,
            pltpu.VMEM((chunks, others, WIDE), BF16),
            pltpu.VMEM((feats, local_protos), BF16),
            pltpu.VMEM((feats, sum(counts[i] for i in FAR) * WIDE), BF16),
            sems, sems, sems, sems,
        ],
        compiler_params=params(exp_bytes + others_bytes + 4 * feats * local_protos),
        cost_estimate=cost(2 * feats * rows * local_protos, others_bytes),
        name="weight_grads",
    )(t_exp, far(prob), feat, col_scale, sums, factor, *[far(x) if i in FAR else x for i, x in enumerate(grad_parts)])
    return grad_weight, grad_rows, loss


def solution(mesh):
    return jax.shard_map(
        local,
        mesh=mesh,
        in_specs=(P("batch", None), P("batch", None), P(None, "proto")),
        out_specs=(P("batch", "proto"), P("batch", None), P()),
        check_vma=False,
    )
```

```python
import functools
import math

import jax
import jax.numpy as jnp
from jax import lax
from jax.experimental import pallas as pl
from jax.experimental.pallas import tpu as pltpu
from jax.sharding import PartitionSpec as P

SWEEPS = 3
TEMP_TEACHER = 0.04
TEMP_STUDENT = 0.1
LOG2E = math.log2(math.e)
SCALE_TEACHER = LOG2E / TEMP_TEACHER
SCALE_STUDENT = LOG2E / TEMP_STUDENT
LANES = 128
WIDE = 1024
TILE = 256
FAR = (2,)
F32 = jnp.float32
BF16 = jnp.bfloat16


def unit_rows(values):
    wide = values.astype(F32)
    length = jnp.sqrt(jnp.sum(wide * wide, axis=-1, keepdims=True) + 1e-06)
    return wide / length, length


def diagonal():
    shape = (LANES, LANES)
    return lax.broadcasted_iota(jnp.int32, shape, 0) == lax.broadcasted_iota(jnp.int32, shape, 1)


def to_column(row):
    spread = jnp.where(diagonal(), jnp.broadcast_to(row, (LANES, LANES)), 0.0)
    return jnp.sum(spread, axis=1, keepdims=True)


def to_row(column):
    spread = jnp.where(diagonal(), jnp.broadcast_to(column, (LANES, LANES)), 0.0)
    return jnp.sum(spread, axis=0, keepdims=True)


def spread_rows(ref, rows):
    for a in range(rows.shape[0]):
        ref[a * LANES : (a + 1) * LANES, :] = jnp.broadcast_to(
            to_column(rows[a : a + 1, :]), (LANES, LANES)
        )


def pack_rows(ref, columns):
    for a in range(columns.shape[0] // LANES):
        ref[a : a + 1, :] = to_row(columns[a * LANES : (a + 1) * LANES, :])


def lane_tiles(values):
    return [values[:, t * LANES : (t + 1) * LANES] for t in range(values.shape[1] // LANES)]


def fold(values):
    return functools.reduce(jnp.add, lane_tiles(values))


def column_sums(values):
    rows, cols = values.shape
    return jnp.sum(values.reshape(rows // 8, 8, cols), axis=0)


def nt_dot(a, b):
    return lax.dot_general(a, b, (((1,), (1,)), ((), ())), preferred_element_type=F32)


def add_up(values):
    return functools.reduce(jnp.add, values)


def repeat(out_ref):
    for p in range(1, out_ref.shape[0]):
        out_ref[p] = out_ref[0]


def chunk(k):
    return slice(k * WIDE, (k + 1) * WIDE)


def copies(source, target, sems, first=0, back=0, count=None):
    def chunks(ref):
        return ref.shape[0] if len(ref.shape) == 3 else ref.shape[1] // WIDE

    count = count or min(chunks(source), chunks(target))
    return [copy_of(source, target, sems, k, first, back) for k in range(count)]


def columns_of(k, first=0, count=WIDE):
    return pl.ds(pl.multiple_of(k * WIDE + first, LANES), count)


def copy_of(source, target, sems, k, first=0, back=0):
    def part(ref, k):
        return ref.at[k] if len(ref.shape) == 3 else ref.at[:, columns_of(k)]

    return pltpu.make_async_copy(part(source, first + k), part(target, back + k), sems.at[k])


def start(*lists):
    for each in zip(*lists):
        for copy in each:
            copy.start()


def whole_copies(pairs, sems):
    return [pltpu.make_async_copy(a, b, sems.at[i]) for i, (a, b) in enumerate(pairs)]


def wait(*lists):
    for each in lists:
        for copy in each:
            copy.wait()


def stats_kernel(
    t_hbm, s_hbm, w_hbm, t_out, s_out, out_ref,
    raw, w_ref, unit, exps, logits, top, total, raw_sem, w_sem, t_sem, s_sem,
):
    own = raw.shape[1]
    quarter = out_ref.shape[1] // 4
    chunks = exps.shape[1]
    halves = (slice(0, own), slice(own, 2 * own))
    loads = copies(w_hbm, w_ref, w_sem)
    raw_loads = [
        pltpu.make_async_copy(ref, raw.at[which], raw_sem.at[which])
        for which, ref in enumerate((t_hbm, s_hbm))
    ]
    start(raw_loads, loads[:2])
    start(loads[2:])
    top[...] = jnp.full(top.shape, -1e30, F32)
    total[...] = jnp.zeros(total.shape, F32)
    wait(raw_loads)
    for which in range(2):
        unit[halves[which], :] = unit_rows(raw[which])[0].astype(BF16)

    @pl.loop(0, chunks)
    def _(k):
        copy_of(w_hbm, w_ref, w_sem, k).wait()
        for n in range(0, WIDE, TILE):
            here = columns_of(k, n, TILE)
            values = jnp.dot(unit[...], w_ref[:, here], preferred_element_type=F32)
            for half, scale in zip(halves, (SCALE_TEACHER, SCALE_STUDENT)):
                part = values[half, :] * scale
                logits[half, here] = part
                top[half, :] = functools.reduce(jnp.maximum, lane_tiles(part), top[half, :])

    peak = jnp.max(top[...], axis=1, keepdims=True)
    top[...] = jnp.broadcast_to(peak, top.shape)

    @pl.loop(0, chunks)
    def _(k):
        for which, (half, out, sem) in enumerate(zip(halves, (t_out, s_out), (t_sem, s_sem))):
            shift = top[half, :]
            for n in range(0, WIDE, 2 * TILE):
                tiles = lane_tiles(logits[half, columns_of(k, n, 2 * TILE)])
                tiles = [jnp.exp2(tile - shift) for tile in tiles]
                for t, tile in enumerate(tiles):
                    lanes = slice(n + t * LANES, n + (t + 1) * LANES)
                    exps[which, k, :, lanes] = tile.astype(BF16)
                total[half, :] += add_up(tiles)
            copy_of(exps.at[which], out, sem, k).start()

    sums = jnp.sum(total[...], axis=1, keepdims=True)
    for which, half in enumerate(halves):
        for k, column in enumerate((peak, sums)):
            first = (2 * which + k) * quarter
            pack_rows(out_ref.at[0, first : first + quarter], column[half, :])
    repeat(out_ref)
    wait(copies(exps.at[0], t_out, t_sem), copies(exps.at[1], s_out, s_sem))


def merged(stats_ref, which):
    parts, height, _ = stats_ref.shape
    quarter = height // 4
    first = 2 * which * quarter
    tops = [stats_ref[p, first : first + quarter, :] for p in range(parts)]
    top = functools.reduce(jnp.maximum, tops)
    sums = [
        stats_ref[p, first + quarter : first + 2 * quarter, :] * jnp.exp2(tops[p] - top)
        for p in range(parts)
    ]
    return top + jnp.log2(add_up(sums))


def column_pass(exp_hbm, exp_ref, sem, weight, out_ref):
    height = WIDE // LANES

    @pl.loop(0, exp_ref.shape[0])
    def _(k):
        copy_of(exp_hbm, exp_ref, sem, k).wait()
        sums = jnp.zeros((8, WIDE), F32)
        for g in range(0, exp_ref.shape[1], 16):
            shift = weight[g : g + 16, :]
            tiles = lane_tiles(exp_ref[k, g : g + 16, :].astype(F32))
            sums = sums + column_sums(jnp.concatenate([tile * shift for tile in tiles], axis=1))
        sums = jnp.sum(sums, axis=0, keepdims=True)
        block = jnp.concatenate(lane_tiles(sums), axis=0)
        for g in range(out_ref.shape[0]):
            out_ref[g, pl.ds(pl.multiple_of(k * height, height), height), :] = block


def first_column_kernel(place_ref, stats_ref, exp_hbm, *refs):
    factor_ref, out_ref, weight, exp_ref, sem = refs[-5:]
    start(copies(exp_hbm, exp_ref, sem))
    quarter = stats_ref.shape[1] // 4
    height = out_ref.shape[1] - 8
    own = stats_ref[pl.ds(place_ref[1], 1)][0]
    factor_ref[...] = jnp.zeros(factor_ref.shape, F32)
    rows = []
    for which in range(2):
        log_sum = merged(stats_ref, which)
        here = slice(which * quarter, (which + 1) * quarter)
        factor_ref[here, :] = jnp.exp2(
            own[2 * which * quarter : (2 * which + 1) * quarter, :] - log_sum
        )
        rows.append(log_sum)
    rows.append(jnp.zeros((8 - 2 * quarter, LANES), F32))
    logs = jnp.concatenate(rows, axis=0)
    for g in range(out_ref.shape[0]):
        out_ref[g, height:, :] = logs
    spread_rows(weight, factor_ref[:quarter, :])
    column_pass(exp_hbm, exp_ref, sem, weight, out_ref)


def column_kernel(sums_ref, factor_ref, exp_hbm, *refs):
    out_ref, weight, exp_ref, sem = refs[-4:]
    start(copies(exp_hbm, exp_ref, sem))
    quarter = weight.shape[0] // LANES
    scale = 1.0 / add_up([sums_ref[p, :quarter, :] for p in range(sums_ref.shape[0])])
    spread_rows(weight, scale * factor_ref[:quarter, :])
    column_pass(exp_hbm, exp_ref, sem, weight, out_ref)


def column_scales(cols, height):
    return 1.0 / add_up([ref[g, :height, :] for ref in cols for g in range(ref.shape[0])])


def chunk_scales(scales, k):
    height = WIDE // LANES
    return scales[pl.ds(pl.multiple_of(k * height, height), height), :]


def add_row_sums(rows, values, scale):
    for g in range(0, values.shape[0], 32):
        total = rows[g : g + 32, :]
        for t, tile in enumerate(lane_tiles(values[g : g + 32, :].astype(F32))):
            total = total + tile * scale[t : t + 1, :]
        rows[g : g + 32, :] = total


def row_kernel(count, *refs):
    cols, (factor_ref, exp_hbm) = refs[:count], refs[count : count + 2]
    out_ref, scales, rows, exp_ref, sem = refs[-5:]
    start(copies(exp_hbm, exp_ref, sem))
    scales[...] = column_scales(cols, scales.shape[0])
    rows[...] = jnp.zeros(rows.shape, F32)
    quarter = rows.shape[0] // LANES
    out_ref[0] = jnp.zeros(out_ref.shape[1:], F32)

    @pl.loop(0, exp_ref.shape[0])
    def _(k):
        copy_of(exp_hbm, exp_ref, sem, k).wait()
        add_row_sums(rows, exp_ref.at[k], chunk_scales(scales, k))

    pack_rows(out_ref.at[0, :quarter], jnp.sum(rows[...], axis=1, keepdims=True))
    out_ref[0, :quarter, :] = out_ref[0, :quarter, :] * factor_ref[:quarter, :]
    repeat(out_ref)


def own_back_kernel(before_ref, exp_hbm, w_hbm, back_ref, exp_ref, w_ref, exp_sem, w_sem):
    start(copies(exp_hbm, exp_ref, exp_sem), copies(w_hbm, w_ref, w_sem))
    back_ref[...] = jnp.zeros(back_ref.shape, F32)

    @pl.loop(0, exp_ref.shape[0])
    def _(k):
        copy_of(exp_hbm, exp_ref, exp_sem, k).wait()
        copy_of(w_hbm, w_ref, w_sem, k).wait()
        back_ref[...] += nt_dot(exp_ref[k], w_ref[:, columns_of(k)])


def relative_logs(logs, lse, which, shift=0.0):
    own = lse.shape[0] // (len(logs) - 1)
    quarter = own // LANES
    for g, ref in enumerate(logs[1:]):
        first = ref.shape[1] - 8 + which * quarter
        spread_rows(lse.at[g * own : (g + 1) * own], ref[0, first : first + quarter, :] - shift)


def student_rows_kernel(protos, place_ref, factor_ref, t_ref, own_ref, *refs):
    unit_ref, feat_ref, scaled_ref, t_unit, turned = refs[-5:]
    t_unit[...] = unit_rows(t_ref[...])[0].astype(BF16)
    own = own_ref.shape[0]
    groups = turned.shape[1] // own
    raw = refs[: groups - 1]
    quarter, feats = own // LANES, feat_ref.shape[0]
    for g in range(groups):
        half = unit_rows((raw[g - 1] if g else own_ref)[...])[0].astype(BF16)
        if g:
            unit_ref[(g - 1) * own : g * own, :] = half
        half = half.astype(F32)
        for a in range(0, own, LANES):
            first = g * own + a
            turned[:, first : first + LANES] = jnp.transpose(half[a : a + LANES, :]).astype(BF16)
    feat = turned[pl.ds(pl.multiple_of(place_ref[0] * feats, feats), feats), :]
    feat_ref[...] = feat
    for a in range(quarter):
        lanes = slice(a * LANES, (a + 1) * LANES)
        factor = factor_ref[quarter + a : quarter + a + 1, :] * protos
        scaled_ref[:, lanes] = (feat[:, lanes].astype(F32) * factor).astype(BF16)


def probabilities(unit, w_ref, k, lse, scale, use):
    for n in range(0, WIDE, TILE):
        logits = jnp.dot(
            unit[...], w_ref[:, columns_of(k, n, TILE)], preferred_element_type=F32
        )
        shift = lse[...]
        use(n, [jnp.exp2(tile * scale - shift) for tile in lane_tiles(logits)])


def student_kernel(
    log_protos, first, groups, unit, feat_ref, scaled_ref, exp_hbm, w_hbm, *refs
):
    logs = refs[:groups]
    grad, token_ref, lse, prob, exp_ref, w_ref, exp_sem, w_sem = refs[-8:]
    own, count = exp_ref.shape[1], exp_ref.shape[0]
    exp_loads = copies(exp_hbm, exp_ref, exp_sem, first, 0, count)
    w_loads = copies(w_hbm, w_ref, w_sem, first, 0, count)
    start(w_loads, exp_loads)
    token_ref[...] = jnp.zeros(token_ref.shape, F32)
    relative_logs(logs, lse, 1, log_protos)

    @pl.loop(0, count)
    def _(k):
        copy_of(w_hbm, w_ref, w_sem, k, first).wait()

        def use(n, tiles):
            for t, tile in enumerate(tiles):
                prob[:, n + t * LANES : n + (t + 1) * LANES] = tile.astype(BF16)

        probabilities(unit, w_ref, k, lse, SCALE_STUDENT, use)
        copy_of(exp_hbm, exp_ref, exp_sem, k, first).wait()
        values = jnp.dot(scaled_ref[...], exp_ref[k], preferred_element_type=F32)
        values = values + jnp.dot(feat_ref[:, own:], prob[...], preferred_element_type=F32)
        grad[:, columns_of(k)] = values.astype(BF16)


def as_three(value):
    high = value.astype(BF16)
    rest = value - high.astype(F32)
    middle = rest.astype(BF16)
    return high, middle, (rest - middle.astype(F32)).astype(BF16)


def last_kernel(groups, factor_ref, own_hbm, student_hbm, exp_hbm, w_hbm, *refs):
    units, refs = refs[: groups - 1], refs[groups - 1 :]
    logs, cols, refs = refs[:groups], refs[groups : 2 * groups], refs[2 * groups :]
    (
        prob_hbm, scale_ref, out_ref, unit, lse, rows, own_rows, back, scaled, sums, prob_ref,
        exp_ref, w_ref, own_ref, student_ref, prob_sem, exp_sem, w_sem, sem,
    ) = refs[-19:]
    w_loads, exp_loads = copies(w_hbm, w_ref, w_sem), copies(exp_hbm, exp_ref, exp_sem)
    late_loads = whole_copies([(own_hbm, own_ref), (student_hbm, student_ref)], sem)
    start(w_loads, exp_loads)
    start(late_loads)
    slots, others, _ = prob_ref.shape
    own, chunks = exp_ref.shape[1], exp_ref.shape[0]
    tiles = (own + others) // LANES
    quarter = own // LANES
    scale_ref[...] = column_scales(cols, scale_ref.shape[0])
    rows[...] = jnp.zeros(rows.shape, F32)
    own_rows[...] = jnp.zeros(own_rows.shape, F32)
    back[...] = jnp.zeros(back.shape, F32)
    relative_logs(logs, lse, 0)
    for g in range(groups - 1):
        unit[g * own : (g + 1) * own, :] = units[g][...]
    partner = slice((groups // 2 - 1) * own, groups // 2 * own)

    def store(k):
        return pltpu.make_async_copy(prob_ref.at[lax.rem(k, slots)], prob_hbm.at[k], prob_sem.at[k])

    @pl.loop(0, chunks)
    def _(k):
        copy_of(w_hbm, w_ref, w_sem, k).wait()
        slot = lax.rem(k, slots)
        scale = chunk_scales(scale_ref, k)

        @pl.when(k >= slots)
        def _():
            store(k - slots).wait()

        def use(n, tiles):
            for t, tile in enumerate(tiles):
                prob_ref[slot, :, n + t * LANES : n + (t + 1) * LANES] = tile.astype(BF16)
            first = n // LANES
            tiles = [tile * scale[first + t : first + t + 1, :] for t, tile in enumerate(tiles)]
            rows[...] += add_up(tiles)
            for t, tile in enumerate(tiles):
                scaled[:, n + t * LANES : n + (t + 1) * LANES] = tile[partner, :].astype(BF16)

        probabilities(unit, w_ref, k, lse, SCALE_TEACHER, use)
        store(k).start()
        back[...] += nt_dot(scaled[...], w_ref[:, columns_of(k)])
        copy_of(exp_hbm, exp_ref, exp_sem, k).wait()
        add_row_sums(own_rows, exp_ref.at[k], scale)

    sums[...] = jnp.zeros(sums.shape, F32)
    pack_rows(sums.at[:quarter], jnp.sum(own_rows[...], axis=1, keepdims=True))
    sums[:quarter, :] = sums[:quarter, :] * factor_ref[:quarter, :]
    pack_rows(sums.at[quarter:tiles], jnp.sum(rows[...], axis=1, keepdims=True))
    wait(late_loads)
    half = unit_rows(own_ref[...])[0].astype(BF16).astype(F32)
    inner = jnp.sum(half * back[...], axis=1, keepdims=True)
    pack_rows(sums.at[tiles : tiles + quarter], inner)
    parts = out_ref.shape[0]
    share = own // parts
    protos = 1.0 * out_ref.shape[0] * w_ref.shape[1]
    student = []
    for a in range(quarter):
        factor = to_column(factor_ref[quarter + a : quarter + a + 1, :] * protos)
        student.append(student_ref[a * LANES : (a + 1) * LANES, :] * factor)
    student = jnp.concatenate(student, axis=0).astype(BF16)
    terms = list(as_three(sums[...]))
    terms.append(jnp.zeros((sums.shape[0], out_ref.shape[2] - 3 * LANES), BF16))
    terms = jnp.concatenate(terms, axis=1)
    for p in range(parts):
        here = slice(p * share, (p + 1) * share)
        out_ref[p] = jnp.concatenate(
            [student[here, :], back[here, :].astype(BF16), terms], axis=0
        )
    for k in range(max(0, chunks - slots), chunks):
        store(k).wait()


def total_sums(message_ref, first):
    parts = message_ref.shape[0]
    each = [
        add_up([t.astype(F32) for t in lane_tiles(message_ref[p, first:, : 3 * LANES])[::-1]])
        for p in range(parts)
    ]
    return add_up(each)


def rows_kernel(tiles, protos, place_ref, s_hbm, message_ref, logs_ref, *refs):
    out_ref, loss_ref, sums_ref, weight, s_ref, sem = refs[-6:]
    parts = message_ref.shape[0]
    share, own = out_ref.shape[1], weight.shape[0]
    mine = pl.ds(pl.multiple_of(place_ref[1] * share, share), share)
    load = pltpu.make_async_copy(s_hbm.at[mine], s_ref, sem)
    load.start()
    quarter = own // LANES
    first = tiles // 2
    totals = total_sums(message_ref, 2 * share)
    sums_ref[...] = totals
    scale = 1.0 / totals[first : first + quarter, :]
    spread_rows(weight, scale)
    total = add_up([message_ref[p, :share, :].astype(F32) for p in range(parts)])
    paired = add_up([message_ref[p, share : 2 * share, :].astype(F32) for p in range(parts)])
    total = total - paired * (weight[mine, :1] * protos)
    load.wait()
    unit, length = unit_rows(s_ref[...])
    total = (total - unit * jnp.sum(unit * total, axis=-1, keepdims=True)) / length
    out_ref[0] = total.astype(BF16)
    repeat(out_ref)
    height = logs_ref.shape[1] - 8
    logs = logs_ref[0, height + quarter : height + 2 * quarter, :]
    terms = logs / LOG2E - totals[tiles : tiles + quarter, :] * scale / TEMP_STUDENT
    loss_ref[...] = jnp.broadcast_to(jnp.sum(terms) / (tiles * LANES), loss_ref.shape)


def grad_kernel(counts, protos, exp_hbm, prob_hbm, feat_ref, scale_ref, sums_ref, factor_ref, *refs):
    parts = refs[: len(counts)]
    out_hbm, scaled, exp_ref, prob_ref, out, part_ref, exp_sem, prob_sem, sem, part_sem = refs[-10:]
    part_loads, where = {}, []
    for i, (count, part) in enumerate(zip(counts, parts)):
        for k in range(count):
            if i in FAR:
                slot = len(part_loads)
                part_loads[len(where)] = copy_of(part, part_ref, part_sem, slot, k - slot)
                where.append((part_ref, slot))
            else:
                where.append((part, k))
    exp_loads = copies(exp_hbm, exp_ref, exp_sem)
    prob_loads = copies(prob_hbm, prob_ref, prob_sem)
    start(exp_loads[:2], prob_loads[:2])
    start(list(part_loads.values()))
    start(exp_loads[2:], prob_loads[2:])
    own = exp_ref.shape[1]
    tiles = (own + prob_ref.shape[1]) // LANES
    rows = protos / sums_ref[:tiles, :]
    for a in range(tiles):
        other = (a + tiles // 2) % tiles
        feat = feat_ref[:, other * LANES : (other + 1) * LANES].astype(F32)
        row = rows[a : a + 1, :]
        if a < own // LANES:
            row = row * factor_ref[a : a + 1, :]
        scaled[:, a * LANES : (a + 1) * LANES] = (feat * row).astype(BF16)
    stores = copies(out, out_hbm, sem)
    for k, store in enumerate(stores):
        exp_loads[k].wait()
        prob_loads[k].wait()
        paired = jnp.dot(scaled[:, :own], exp_ref[k], preferred_element_type=F32)
        paired = paired + jnp.dot(
            scaled[:, own:], prob_ref[k], preferred_element_type=F32
        )
        part, there = where[k]
        if k in part_loads:
            part_loads[k].wait()
        for t, tile in enumerate(lane_tiles(paired)):
            lanes = slice(k * WIDE + t * LANES, k * WIDE + (t + 1) * LANES)
            scale = scale_ref[lanes.start // LANES : lanes.stop // LANES, :]
            own_part = part[:, there * WIDE + t * LANES : there * WIDE + (t + 1) * LANES]
            out[:, lanes] = (own_part.astype(F32) - tile * scale).astype(BF16)
        store.start()
    for store in stores:
        store.wait()


SMEM = pl.BlockSpec(memory_space=pltpu.SMEM)
VMEM = pl.BlockSpec(memory_space=pltpu.VMEM)
ANY = pl.BlockSpec(memory_space=pl.ANY)


def params(nbytes):
    return pltpu.CompilerParams(vmem_limit_bytes=int(nbytes) + 8 * 2**20)


def cost(flops, nbytes, exps=0):
    return pl.CostEstimate(flops=int(flops), bytes_accessed=int(nbytes), transcendentals=int(exps))


def exchange(value, axis):
    return lax.all_to_all(value, axis, 0, 0)


def following(value, axis):
    n = lax.axis_size(axis)
    return [lax.ppermute(value, axis, [(i, (i - s) % n) for i in range(n)]) for s in range(1, n)]


def tree_sum(value, axis):
    n = lax.axis_size(axis)
    values = [value] + [
        lax.ppermute(value, axis, [(i, i ^ s) for i in range(n)]) for s in range(1, n)
    ]
    while len(values) > 1:
        values = [a + b for a, b in zip(values[::2], values[1::2])]
    return values[0]


def local(teacher_feats, student_feats, proto_weight):
    parts, groups = lax.axis_size("proto"), lax.axis_size("batch")
    own, width = teacher_feats.shape
    local_protos = proto_weight.shape[1]
    rows = own * groups
    others = rows - own
    protos = local_protos * parts
    feats = width // groups
    share = own // parts
    tiles = rows // LANES
    height = local_protos // LANES
    chunks = local_protos // WIDE
    place = jnp.stack([lax.axis_index("batch"), lax.axis_index("proto")]).astype(jnp.int32)
    struct = jax.ShapeDtypeStruct
    weight_bytes = 2 * width * local_protos
    exp_bytes = 2 * own * local_protos
    others_bytes = 2 * others * local_protos
    spread = pltpu.VMEM((own, LANES), F32)
    w_buffer = pltpu.VMEM((width, local_protos), BF16)
    exp_buffer = pltpu.VMEM((chunks, own, WIDE), BF16)
    sems = pltpu.SemaphoreType.DMA((chunks,))
    log_protos = math.log2(protos)
    token = struct((8, LANES), F32)

    def far(value):
        return pltpu.with_memory_space_constraint(value, pltpu.HBM)

    weight = far(proto_weight)
    teacher_rows, student_rows = far(teacher_feats), far(student_feats)
    s_all = following(student_feats, "batch")

    exps = pltpu.HBM((chunks, own, WIDE), BF16)
    t_exp, s_exp, stats = pl.pallas_call(
        stats_kernel,
        in_specs=[ANY] * 3,
        out_specs=[ANY, ANY, VMEM],
        out_shape=[
            exps,
            exps,
            struct((parts, 4 * own // LANES, LANES), F32),
        ],
        scratch_shapes=[
            pltpu.VMEM((2, own, width), BF16),
            w_buffer,
            pltpu.VMEM((2 * own, width), BF16),
            pltpu.VMEM((2, chunks, own, WIDE), BF16),
            pltpu.VMEM((2 * own, local_protos), F32),
            pltpu.VMEM((2 * own, LANES), F32),
            pltpu.VMEM((2 * own, LANES), F32),
            pltpu.SemaphoreType.DMA((2,)),
            sems, sems, sems,
        ],
        compiler_params=params(weight_bytes + 6 * exp_bytes),
        cost_estimate=cost(4 * own * width * local_protos, weight_bytes),
        name="own_rows",
    )(teacher_rows, student_rows, weight)
    t_exp, s_exp = far(t_exp), far(s_exp)

    back_student = pl.pallas_call(
        own_back_kernel,
        in_specs=[ANY] * 3,
        out_specs=VMEM,
        out_shape=struct((own, width), F32),
        scratch_shapes=[exp_buffer, w_buffer, sems, sems],
        compiler_params=params(weight_bytes + exp_bytes),
        cost_estimate=cost(2 * own * width * local_protos, weight_bytes),
        name="own_back",
    )(stats, s_exp, weight)

    stats = exchange(stats, "proto")

    first_shape = (1, height + 8, LANES)
    factor, cols = pl.pallas_call(
        first_column_kernel,
        in_specs=[SMEM, VMEM, ANY, ANY] + [ANY] * (groups - 1),
        out_specs=[VMEM, VMEM],
        out_shape=[token, struct(first_shape, F32)],
        scratch_shapes=[spread, exp_buffer, sems],
        compiler_params=params(exp_bytes),
        cost_estimate=cost(2 * own * local_protos, exp_bytes),
        name="first_columns",
    )(place, stats, t_exp, back_student, *s_all)

    unit, feat, scaled, t_unit = pl.pallas_call(
        functools.partial(student_rows_kernel, float(protos)),
        in_specs=[SMEM, VMEM, VMEM, VMEM] + [VMEM] * (groups - 1) + [ANY],
        out_specs=[VMEM] * 4,
        out_shape=[
            struct((others, width), BF16), struct((feats, rows), BF16), struct((feats, own), BF16),
            struct((own, width), BF16),
        ],
        scratch_shapes=[pltpu.VMEM((width, rows), BF16)],
        compiler_params=params(2 * rows * width),
        cost_estimate=cost(8 * rows * width, 2 * rows * width),
        name="student_rows",
    )(place, factor, teacher_feats, student_feats, *s_all, cols)
    t_all = following(t_unit, "batch")
    cols = [cols] + following(cols, "batch")
    logs = cols

    counts = [c * chunks // 8 for c in (1, 1, 1, 5)]
    grad_parts = []

    def student_piece(before):
        turn = len(grad_parts)
        first, count = sum(counts[:turn]), counts[turn]
        grad_part, done = pl.pallas_call(
            functools.partial(student_kernel, log_protos, first, groups),
            in_specs=[VMEM] * 3 + [ANY] * 2 + [VMEM] * groups + [ANY],
            out_specs=[VMEM, VMEM],
            out_shape=[struct((feats, count * WIDE), BF16), token],
            scratch_shapes=[
                pltpu.VMEM((others, LANES), F32),
                pltpu.VMEM((others, WIDE), BF16),
                pltpu.VMEM((count, own, WIDE), BF16),
                pltpu.VMEM((width, count * WIDE), BF16),
            ]
            + [pltpu.SemaphoreType.DMA((count,))] * 2,
            compiler_params=params(16 * 2**20),
            cost_estimate=cost(2.5 * rows * width * WIDE * count, 2 * width * WIDE * count),
            name="student_side",
        )(unit, feat, scaled, s_exp, weight, *logs, before)
        grad_parts.append(grad_part)
        return done

    done = unit
    for turn in range(SWEEPS - 1):
        late = t_all if turn == 1 else []
        sums = pl.pallas_call(
            functools.partial(row_kernel, len(cols)),
            in_specs=[VMEM] * (len(cols) + 1) + [ANY] * (2 + len(late)),
            out_specs=VMEM,
            out_shape=struct((parts, 8, LANES), F32),
            scratch_shapes=[pltpu.VMEM((height, LANES), F32), spread, exp_buffer, sems],
            compiler_params=params(exp_bytes),
            cost_estimate=cost(2 * own * local_protos, exp_bytes),
            name="rows",
        )(*cols, factor, t_exp, done, *late)
        done = student_piece(sums)
        sums = exchange(sums, "proto")
        middle = turn < SWEEPS - 2
        cols = pl.pallas_call(
            column_kernel,
            in_specs=[VMEM, VMEM, ANY, ANY],
            out_specs=VMEM,
            out_shape=struct((groups if middle else 1, height, LANES), F32),
            scratch_shapes=[spread, exp_buffer, sems],
            compiler_params=params(exp_bytes),
            cost_estimate=cost(2 * own * local_protos, exp_bytes),
            name="columns",
        )(sums, factor, t_exp, done)
        if turn < SWEEPS - 2:
            done = student_piece(cols)
        if middle:
            cols = [exchange(cols, "batch")]
        else:
            cols = [cols] + following(cols, "batch")

    sum_rows = -(-(tiles + own // LANES) // 16) * 16
    message_shape = (parts, 2 * share + sum_rows, width)
    prob, col_scale, message = pl.pallas_call(
        functools.partial(last_kernel, groups),
        in_specs=[VMEM] + [ANY] * 4 + [VMEM] * (3 * groups - 1) + [ANY],
        out_specs=[ANY, VMEM, VMEM],
        out_shape=[
            pltpu.HBM((chunks, others, WIDE), BF16),
            struct((height, LANES), F32),
            struct(message_shape, BF16),
        ],
        scratch_shapes=[
            pltpu.VMEM((others, width), BF16),
            pltpu.VMEM((others, LANES), F32),
            pltpu.VMEM((others, LANES), F32),
            spread,
            pltpu.VMEM((own, width), F32),
            pltpu.VMEM((own, WIDE), BF16),
            pltpu.VMEM((sum_rows, LANES), F32),
            pltpu.VMEM((min(chunks, 3), others, WIDE), BF16),
            exp_buffer,
            w_buffer,
            pltpu.VMEM((own, width), BF16),
            pltpu.VMEM((own, width), F32),
            sems, sems, sems,
            pltpu.SemaphoreType.DMA((2,)),
        ],
        compiler_params=params(20 * 2**20 + weight_bytes + exp_bytes),
        cost_estimate=cost(2 * rows * width * local_protos, others_bytes),
        name="last_rows",
    )(
        factor, student_rows, far(back_student), t_exp, weight, *t_all, *logs, *cols, done,
    )
    done = student_piece(message)
    message = exchange(message, "proto")

    grad_rows, loss_part, sums = pl.pallas_call(
        functools.partial(rows_kernel, tiles, float(protos)),
        in_specs=[SMEM, ANY, VMEM, VMEM, ANY],
        out_specs=[VMEM] * 3,
        out_shape=[struct((parts, share, width), BF16), token, struct((sum_rows, LANES), F32)],
        scratch_shapes=[spread, pltpu.VMEM((share, width), BF16), pltpu.SemaphoreType.DMA],
        compiler_params=params(0),
        name="row_grads",
    )(place, student_rows, message, logs[0], done)
    grad_rows = exchange(grad_rows, "proto").reshape(own, width).astype(F32)
    loss = tree_sum(loss_part, "batch")[0, 0]

    grad_weight = pl.pallas_call(
        functools.partial(grad_kernel, counts, float(protos)),
        in_specs=[ANY] * 2
        + [VMEM] * 4
        + [ANY if i in FAR else VMEM for i in range(len(counts))],
        out_specs=ANY,
        out_shape=struct((feats, local_protos), BF16),
        scratch_shapes=[
            pltpu.VMEM((feats, rows), BF16),
            exp_buffer,
            pltpu.VMEM((chunks, others, WIDE), BF16),
            pltpu.VMEM((feats, local_protos), BF16),
            pltpu.VMEM((feats, sum(counts[i] for i in FAR) * WIDE), BF16),
            sems, sems, sems, sems,
        ],
        compiler_params=params(exp_bytes + others_bytes + 4 * feats * local_protos),
        cost_estimate=cost(2 * feats * rows * local_protos, others_bytes),
        name="weight_grads",
    )(t_exp, far(prob), feat, col_scale, sums, factor, *[far(x) if i in FAR else x for i, x in enumerate(grad_parts)])
    return grad_weight, grad_rows, loss


def solution(mesh):
    return jax.shard_map(
        local,
        mesh=mesh,
        in_specs=(P("batch", None), P("batch", None), P(None, "proto")),
        out_specs=(P("batch", "proto"), P("batch", None), P()),
        check_vma=False,
    )
```

```python
import functools
import math

import jax
import jax.numpy as jnp
from jax import lax
from jax.experimental import pallas as pl
from jax.experimental.pallas import tpu as pltpu
from jax.sharding import PartitionSpec as P

SWEEPS = 3
TEMP_TEACHER = 0.04
TEMP_STUDENT = 0.1
LOG2E = math.log2(math.e)
SCALE_TEACHER = LOG2E / TEMP_TEACHER
SCALE_STUDENT = LOG2E / TEMP_STUDENT
LANES = 128
WIDE = 1024
TILE = 256
FAR = (0, 1, 2)
F32 = jnp.float32
BF16 = jnp.bfloat16


def unit_rows(values):
    wide = values.astype(F32)
    length = jnp.sqrt(jnp.sum(wide * wide, axis=-1, keepdims=True) + 1e-06)
    return wide / length, length


def diagonal():
    shape = (LANES, LANES)
    return lax.broadcasted_iota(jnp.int32, shape, 0) == lax.broadcasted_iota(jnp.int32, shape, 1)


def to_column(row):
    spread = jnp.where(diagonal(), jnp.broadcast_to(row, (LANES, LANES)), 0.0)
    return jnp.sum(spread, axis=1, keepdims=True)


def to_row(column):
    spread = jnp.where(diagonal(), jnp.broadcast_to(column, (LANES, LANES)), 0.0)
    return jnp.sum(spread, axis=0, keepdims=True)


def spread_rows(ref, rows):
    for a in range(rows.shape[0]):
        ref[a * LANES : (a + 1) * LANES, :] = jnp.broadcast_to(
            to_column(rows[a : a + 1, :]), (LANES, LANES)
        )


def pack_rows(ref, columns):
    for a in range(columns.shape[0] // LANES):
        ref[a : a + 1, :] = to_row(columns[a * LANES : (a + 1) * LANES, :])


def lane_tiles(values):
    return [values[:, t * LANES : (t + 1) * LANES] for t in range(values.shape[1] // LANES)]


def fold(values):
    return functools.reduce(jnp.add, lane_tiles(values))


def column_sums(values):
    rows, cols = values.shape
    return jnp.sum(values.reshape(rows // 8, 8, cols), axis=0)


def nt_dot(a, b):
    return lax.dot_general(a, b, (((1,), (1,)), ((), ())), preferred_element_type=F32)


def add_up(values):
    return functools.reduce(jnp.add, values)


def repeat(out_ref):
    for p in range(1, out_ref.shape[0]):
        out_ref[p] = out_ref[0]


def chunk(k):
    return slice(k * WIDE, (k + 1) * WIDE)


def copies(source, target, sems, first=0, back=0, count=None):
    def chunks(ref):
        return ref.shape[0] if len(ref.shape) == 3 else ref.shape[1] // WIDE

    count = count or min(chunks(source), chunks(target))
    return [copy_of(source, target, sems, k, first, back) for k in range(count)]


def columns_of(k, first=0, count=WIDE):
    return pl.ds(pl.multiple_of(k * WIDE + first, LANES), count)


def copy_of(source, target, sems, k, first=0, back=0):
    def part(ref, k):
        return ref.at[k] if len(ref.shape) == 3 else ref.at[:, columns_of(k)]

    return pltpu.make_async_copy(part(source, first + k), part(target, back + k), sems.at[k])


def start(*lists):
    for each in zip(*lists):
        for copy in each:
            copy.start()


def whole_copies(pairs, sems):
    return [pltpu.make_async_copy(a, b, sems.at[i]) for i, (a, b) in enumerate(pairs)]


def wait(*lists):
    for each in lists:
        for copy in each:
            copy.wait()


def stats_kernel(
    t_hbm, s_hbm, w_hbm, t_out, s_out, out_ref,
    raw, w_ref, unit, exps, logits, top, total, raw_sem, w_sem, t_sem, s_sem,
):
    own = raw.shape[1]
    quarter = out_ref.shape[1] // 4
    chunks = exps.shape[1]
    halves = (slice(0, own), slice(own, 2 * own))
    loads = copies(w_hbm, w_ref, w_sem)
    raw_loads = [
        pltpu.make_async_copy(ref, raw.at[which], raw_sem.at[which])
        for which, ref in enumerate((t_hbm, s_hbm))
    ]
    start(raw_loads, loads[:2])
    start(loads[2:])
    top[...] = jnp.full(top.shape, -1e30, F32)
    total[...] = jnp.zeros(total.shape, F32)
    wait(raw_loads)
    for which in range(2):
        unit[halves[which], :] = unit_rows(raw[which])[0].astype(BF16)

    @pl.loop(0, chunks)
    def _(k):
        copy_of(w_hbm, w_ref, w_sem, k).wait()
        for n in range(0, WIDE, TILE):
            here = columns_of(k, n, TILE)
            values = jnp.dot(unit[...], w_ref[:, here], preferred_element_type=F32)
            for half, scale in zip(halves, (SCALE_TEACHER, SCALE_STUDENT)):
                part = values[half, :] * scale
                logits[half, here] = part
                top[half, :] = functools.reduce(jnp.maximum, lane_tiles(part), top[half, :])

    peak = jnp.max(top[...], axis=1, keepdims=True)
    top[...] = jnp.broadcast_to(peak, top.shape)

    @pl.loop(0, chunks)
    def _(k):
        for which, (half, out, sem) in enumerate(zip(halves, (t_out, s_out), (t_sem, s_sem))):
            shift = top[half, :]
            for n in range(0, WIDE, 2 * TILE):
                tiles = lane_tiles(logits[half, columns_of(k, n, 2 * TILE)])
                tiles = [jnp.exp2(tile - shift) for tile in tiles]
                for t, tile in enumerate(tiles):
                    lanes = slice(n + t * LANES, n + (t + 1) * LANES)
                    exps[which, k, :, lanes] = tile.astype(BF16)
                total[half, :] += add_up(tiles)
            copy_of(exps.at[which], out, sem, k).start()

    sums = jnp.sum(total[...], axis=1, keepdims=True)
    for which, half in enumerate(halves):
        for k, column in enumerate((peak, sums)):
            first = (2 * which + k) * quarter
            pack_rows(out_ref.at[0, first : first + quarter], column[half, :])
    repeat(out_ref)
    wait(copies(exps.at[0], t_out, t_sem), copies(exps.at[1], s_out, s_sem))


def merged(stats_ref, which):
    parts, height, _ = stats_ref.shape
    quarter = height // 4
    first = 2 * which * quarter
    tops = [stats_ref[p, first : first + quarter, :] for p in range(parts)]
    top = functools.reduce(jnp.maximum, tops)
    sums = [
        stats_ref[p, first + quarter : first + 2 * quarter, :] * jnp.exp2(tops[p] - top)
        for p in range(parts)
    ]
    return top + jnp.log2(add_up(sums))


def column_pass(exp_hbm, exp_ref, sem, weight, out_ref):
    height = WIDE // LANES

    @pl.loop(0, exp_ref.shape[0])
    def _(k):
        copy_of(exp_hbm, exp_ref, sem, k).wait()
        sums = jnp.zeros((8, WIDE), F32)
        for g in range(0, exp_ref.shape[1], 16):
            shift = weight[g : g + 16, :]
            tiles = lane_tiles(exp_ref[k, g : g + 16, :].astype(F32))
            sums = sums + column_sums(jnp.concatenate([tile * shift for tile in tiles], axis=1))
        sums = jnp.sum(sums, axis=0, keepdims=True)
        block = jnp.concatenate(lane_tiles(sums), axis=0)
        for g in range(out_ref.shape[0]):
            out_ref[g, pl.ds(pl.multiple_of(k * height, height), height), :] = block


def first_column_kernel(place_ref, stats_ref, exp_hbm, *refs):
    factor_ref, out_ref, weight, exp_ref, sem = refs[-5:]
    start(copies(exp_hbm, exp_ref, sem))
    quarter = stats_ref.shape[1] // 4
    height = out_ref.shape[1] - 8
    own = stats_ref[pl.ds(place_ref[1], 1)][0]
    factor_ref[...] = jnp.zeros(factor_ref.shape, F32)
    rows = []
    for which in range(2):
        log_sum = merged(stats_ref, which)
        here = slice(which * quarter, (which + 1) * quarter)
        factor_ref[here, :] = jnp.exp2(
            own[2 * which * quarter : (2 * which + 1) * quarter, :] - log_sum
        )
        rows.append(log_sum)
    rows.append(jnp.zeros((8 - 2 * quarter, LANES), F32))
    logs = jnp.concatenate(rows, axis=0)
    for g in range(out_ref.shape[0]):
        out_ref[g, height:, :] = logs
    spread_rows(weight, factor_ref[:quarter, :])
    column_pass(exp_hbm, exp_ref, sem, weight, out_ref)


def column_kernel(sums_ref, factor_ref, exp_hbm, *refs):
    out_ref, weight, exp_ref, sem = refs[-4:]
    start(copies(exp_hbm, exp_ref, sem))
    quarter = weight.shape[0] // LANES
    scale = 1.0 / add_up([sums_ref[p, :quarter, :] for p in range(sums_ref.shape[0])])
    spread_rows(weight, scale * factor_ref[:quarter, :])
    column_pass(exp_hbm, exp_ref, sem, weight, out_ref)


def column_scales(cols, height):
    return 1.0 / add_up([ref[g, :height, :] for ref in cols for g in range(ref.shape[0])])


def chunk_scales(scales, k):
    height = WIDE // LANES
    return scales[pl.ds(pl.multiple_of(k * height, height), height), :]


def add_row_sums(rows, values, scale):
    for g in range(0, values.shape[0], 32):
        total = rows[g : g + 32, :]
        for t, tile in enumerate(lane_tiles(values[g : g + 32, :].astype(F32))):
            total = total + tile * scale[t : t + 1, :]
        rows[g : g + 32, :] = total


def row_kernel(count, *refs):
    cols, (factor_ref, exp_hbm) = refs[:count], refs[count : count + 2]
    out_ref, scales, rows, exp_ref, sem = refs[-5:]
    start(copies(exp_hbm, exp_ref, sem))
    scales[...] = column_scales(cols, scales.shape[0])
    rows[...] = jnp.zeros(rows.shape, F32)
    quarter = rows.shape[0] // LANES
    out_ref[0] = jnp.zeros(out_ref.shape[1:], F32)

    @pl.loop(0, exp_ref.shape[0])
    def _(k):
        copy_of(exp_hbm, exp_ref, sem, k).wait()
        add_row_sums(rows, exp_ref.at[k], chunk_scales(scales, k))

    pack_rows(out_ref.at[0, :quarter], jnp.sum(rows[...], axis=1, keepdims=True))
    out_ref[0, :quarter, :] = out_ref[0, :quarter, :] * factor_ref[:quarter, :]
    repeat(out_ref)


def own_back_kernel(before_ref, exp_hbm, w_hbm, back_ref, exp_ref, w_ref, exp_sem, w_sem):
    start(copies(exp_hbm, exp_ref, exp_sem), copies(w_hbm, w_ref, w_sem))
    back_ref[...] = jnp.zeros(back_ref.shape, F32)

    @pl.loop(0, exp_ref.shape[0])
    def _(k):
        copy_of(exp_hbm, exp_ref, exp_sem, k).wait()
        copy_of(w_hbm, w_ref, w_sem, k).wait()
        back_ref[...] += nt_dot(exp_ref[k], w_ref[:, columns_of(k)])


def relative_logs(logs, lse, which, shift=0.0):
    own = lse.shape[0] // (len(logs) - 1)
    quarter = own // LANES
    for g, ref in enumerate(logs[1:]):
        first = ref.shape[1] - 8 + which * quarter
        spread_rows(lse.at[g * own : (g + 1) * own], ref[0, first : first + quarter, :] - shift)


def student_rows_kernel(protos, place_ref, factor_ref, t_ref, own_ref, *refs):
    unit_ref, feat_ref, scaled_ref, t_unit, turned = refs[-5:]
    t_unit[...] = unit_rows(t_ref[...])[0].astype(BF16)
    own = own_ref.shape[0]
    groups = turned.shape[1] // own
    raw = refs[: groups - 1]
    quarter, feats = own // LANES, feat_ref.shape[0]
    for g in range(groups):
        half = unit_rows((raw[g - 1] if g else own_ref)[...])[0].astype(BF16)
        if g:
            unit_ref[(g - 1) * own : g * own, :] = half
        half = half.astype(F32)
        for a in range(0, own, LANES):
            first = g * own + a
            turned[:, first : first + LANES] = jnp.transpose(half[a : a + LANES, :]).astype(BF16)
    feat = turned[pl.ds(pl.multiple_of(place_ref[0] * feats, feats), feats), :]
    feat_ref[...] = feat
    for a in range(quarter):
        lanes = slice(a * LANES, (a + 1) * LANES)
        factor = factor_ref[quarter + a : quarter + a + 1, :] * protos
        scaled_ref[:, lanes] = (feat[:, lanes].astype(F32) * factor).astype(BF16)


def probabilities(unit, w_ref, k, lse, scale, use):
    for n in range(0, WIDE, TILE):
        logits = jnp.dot(
            unit[...], w_ref[:, columns_of(k, n, TILE)], preferred_element_type=F32
        )
        shift = lse[...]
        use(n, [jnp.exp2(tile * scale - shift) for tile in lane_tiles(logits)])


def student_kernel(
    log_protos, first, groups, unit, feat_ref, scaled_ref, exp_hbm, w_hbm, *refs
):
    logs = refs[:groups]
    grad, token_ref, lse, prob, exp_ref, w_ref, exp_sem, w_sem = refs[-8:]
    own, count = exp_ref.shape[1], exp_ref.shape[0]
    exp_loads = copies(exp_hbm, exp_ref, exp_sem, first, 0, count)
    w_loads = copies(w_hbm, w_ref, w_sem, first, 0, count)
    start(w_loads, exp_loads)
    token_ref[...] = jnp.zeros(token_ref.shape, F32)
    relative_logs(logs, lse, 1, log_protos)

    @pl.loop(0, count)
    def _(k):
        copy_of(w_hbm, w_ref, w_sem, k, first).wait()

        def use(n, tiles):
            for t, tile in enumerate(tiles):
                prob[:, n + t * LANES : n + (t + 1) * LANES] = tile.astype(BF16)

        probabilities(unit, w_ref, k, lse, SCALE_STUDENT, use)
        copy_of(exp_hbm, exp_ref, exp_sem, k, first).wait()
        values = jnp.dot(scaled_ref[...], exp_ref[k], preferred_element_type=F32)
        values = values + jnp.dot(feat_ref[:, own:], prob[...], preferred_element_type=F32)
        grad[:, columns_of(k)] = values.astype(BF16)


def as_three(value):
    high = value.astype(BF16)
    rest = value - high.astype(F32)
    middle = rest.astype(BF16)
    return high, middle, (rest - middle.astype(F32)).astype(BF16)


def last_kernel(groups, factor_ref, own_hbm, student_hbm, exp_hbm, w_hbm, *refs):
    units, refs = refs[: groups - 1], refs[groups - 1 :]
    logs, cols, refs = refs[:groups], refs[groups : 2 * groups], refs[2 * groups :]
    (
        prob_hbm, scale_ref, out_ref, unit, lse, rows, own_rows, back, scaled, sums, prob_ref,
        exp_ref, w_ref, own_ref, student_ref, prob_sem, exp_sem, w_sem, sem,
    ) = refs[-19:]
    w_loads, exp_loads = copies(w_hbm, w_ref, w_sem), copies(exp_hbm, exp_ref, exp_sem)
    late_loads = whole_copies([(own_hbm, own_ref), (student_hbm, student_ref)], sem)
    start(w_loads, exp_loads)
    start(late_loads)
    slots, others, _ = prob_ref.shape
    own, chunks = exp_ref.shape[1], exp_ref.shape[0]
    tiles = (own + others) // LANES
    quarter = own // LANES
    scale_ref[...] = column_scales(cols, scale_ref.shape[0])
    rows[...] = jnp.zeros(rows.shape, F32)
    own_rows[...] = jnp.zeros(own_rows.shape, F32)
    back[...] = jnp.zeros(back.shape, F32)
    relative_logs(logs, lse, 0)
    for g in range(groups - 1):
        unit[g * own : (g + 1) * own, :] = units[g][...]
    partner = slice((groups // 2 - 1) * own, groups // 2 * own)

    def store(k):
        return pltpu.make_async_copy(prob_ref.at[lax.rem(k, slots)], prob_hbm.at[k], prob_sem.at[k])

    @pl.loop(0, chunks)
    def _(k):
        copy_of(w_hbm, w_ref, w_sem, k).wait()
        slot = lax.rem(k, slots)
        scale = chunk_scales(scale_ref, k)

        @pl.when(k >= slots)
        def _():
            store(k - slots).wait()

        def use(n, tiles):
            for t, tile in enumerate(tiles):
                prob_ref[slot, :, n + t * LANES : n + (t + 1) * LANES] = tile.astype(BF16)
            first = n // LANES
            tiles = [tile * scale[first + t : first + t + 1, :] for t, tile in enumerate(tiles)]
            rows[...] += add_up(tiles)
            for t, tile in enumerate(tiles):
                scaled[:, n + t * LANES : n + (t + 1) * LANES] = tile[partner, :].astype(BF16)

        probabilities(unit, w_ref, k, lse, SCALE_TEACHER, use)
        store(k).start()
        back[...] += nt_dot(scaled[...], w_ref[:, columns_of(k)])
        copy_of(exp_hbm, exp_ref, exp_sem, k).wait()
        add_row_sums(own_rows, exp_ref.at[k], scale)

    sums[...] = jnp.zeros(sums.shape, F32)
    pack_rows(sums.at[:quarter], jnp.sum(own_rows[...], axis=1, keepdims=True))
    sums[:quarter, :] = sums[:quarter, :] * factor_ref[:quarter, :]
    pack_rows(sums.at[quarter:tiles], jnp.sum(rows[...], axis=1, keepdims=True))
    wait(late_loads)
    half = unit_rows(own_ref[...])[0].astype(BF16).astype(F32)
    inner = jnp.sum(half * back[...], axis=1, keepdims=True)
    pack_rows(sums.at[tiles : tiles + quarter], inner)
    parts = out_ref.shape[0]
    share = own // parts
    protos = 1.0 * out_ref.shape[0] * w_ref.shape[1]
    student = []
    for a in range(quarter):
        factor = to_column(factor_ref[quarter + a : quarter + a + 1, :] * protos)
        student.append(student_ref[a * LANES : (a + 1) * LANES, :] * factor)
    student = jnp.concatenate(student, axis=0).astype(BF16)
    terms = list(as_three(sums[...]))
    terms.append(jnp.zeros((sums.shape[0], out_ref.shape[2] - 3 * LANES), BF16))
    terms = jnp.concatenate(terms, axis=1)
    for p in range(parts):
        here = slice(p * share, (p + 1) * share)
        out_ref[p] = jnp.concatenate(
            [student[here, :], back[here, :].astype(BF16), terms], axis=0
        )
    for k in range(max(0, chunks - slots), chunks):
        store(k).wait()


def total_sums(message_ref, first):
    parts = message_ref.shape[0]
    each = [
        add_up([t.astype(F32) for t in lane_tiles(message_ref[p, first:, : 3 * LANES])[::-1]])
        for p in range(parts)
    ]
    return add_up(each)


def rows_kernel(tiles, protos, place_ref, s_hbm, message_ref, logs_ref, *refs):
    out_ref, loss_ref, sums_ref, weight, s_ref, sem = refs[-6:]
    parts = message_ref.shape[0]
    share, own = out_ref.shape[1], weight.shape[0]
    mine = pl.ds(pl.multiple_of(place_ref[1] * share, share), share)
    load = pltpu.make_async_copy(s_hbm.at[mine], s_ref, sem)
    load.start()
    quarter = own // LANES
    first = tiles // 2
    totals = total_sums(message_ref, 2 * share)
    sums_ref[...] = totals
    scale = 1.0 / totals[first : first + quarter, :]
    spread_rows(weight, scale)
    total = add_up([message_ref[p, :share, :].astype(F32) for p in range(parts)])
    paired = add_up([message_ref[p, share : 2 * share, :].astype(F32) for p in range(parts)])
    total = total - paired * (weight[mine, :1] * protos)
    load.wait()
    unit, length = unit_rows(s_ref[...])
    total = (total - unit * jnp.sum(unit * total, axis=-1, keepdims=True)) / length
    out_ref[0] = total.astype(BF16)
    repeat(out_ref)
    height = logs_ref.shape[1] - 8
    logs = logs_ref[0, height + quarter : height + 2 * quarter, :]
    terms = logs / LOG2E - totals[tiles : tiles + quarter, :] * scale / TEMP_STUDENT
    loss_ref[...] = jnp.broadcast_to(jnp.sum(terms) / (tiles * LANES), loss_ref.shape)


def grad_kernel(counts, protos, exp_hbm, prob_hbm, feat_ref, scale_ref, sums_ref, factor_ref, *refs):
    parts = refs[: len(counts)]
    out_hbm, scaled, exp_ref, prob_ref, out, part_ref, exp_sem, prob_sem, sem, part_sem = refs[-10:]
    part_loads, where = {}, []
    for i, (count, part) in enumerate(zip(counts, parts)):
        for k in range(count):
            if i in FAR:
                slot = len(part_loads)
                part_loads[len(where)] = copy_of(part, part_ref, part_sem, slot, k - slot)
                where.append((part_ref, slot))
            else:
                where.append((part, k))
    exp_loads = copies(exp_hbm, exp_ref, exp_sem)
    prob_loads = copies(prob_hbm, prob_ref, prob_sem)
    start(exp_loads[:1], prob_loads[:1])
    start(list(part_loads.values()))
    start(exp_loads[1:], prob_loads[1:])
    own = exp_ref.shape[1]
    tiles = (own + prob_ref.shape[1]) // LANES
    rows = protos / sums_ref[:tiles, :]
    for a in range(tiles):
        other = (a + tiles // 2) % tiles
        feat = feat_ref[:, other * LANES : (other + 1) * LANES].astype(F32)
        row = rows[a : a + 1, :]
        if a < own // LANES:
            row = row * factor_ref[a : a + 1, :]
        scaled[:, a * LANES : (a + 1) * LANES] = (feat * row).astype(BF16)
    stores = copies(out, out_hbm, sem)
    for k, store in enumerate(stores):
        exp_loads[k].wait()
        prob_loads[k].wait()
        paired = jnp.dot(scaled[:, :own], exp_ref[k], preferred_element_type=F32)
        paired = paired + jnp.dot(
            scaled[:, own:], prob_ref[k], preferred_element_type=F32
        )
        part, there = where[k]
        if k in part_loads:
            part_loads[k].wait()
        for t, tile in enumerate(lane_tiles(paired)):
            lanes = slice(k * WIDE + t * LANES, k * WIDE + (t + 1) * LANES)
            scale = scale_ref[lanes.start // LANES : lanes.stop // LANES, :]
            own_part = part[:, there * WIDE + t * LANES : there * WIDE + (t + 1) * LANES]
            out[:, lanes] = (own_part.astype(F32) - tile * scale).astype(BF16)
        store.start()
    for store in stores:
        store.wait()


SMEM = pl.BlockSpec(memory_space=pltpu.SMEM)
VMEM = pl.BlockSpec(memory_space=pltpu.VMEM)
ANY = pl.BlockSpec(memory_space=pl.ANY)


def params(nbytes):
    return pltpu.CompilerParams(vmem_limit_bytes=int(nbytes) + 8 * 2**20)


def cost(flops, nbytes, exps=0):
    return pl.CostEstimate(flops=int(flops), bytes_accessed=int(nbytes), transcendentals=int(exps))


def exchange(value, axis):
    return lax.all_to_all(value, axis, 0, 0)


def following(value, axis):
    n = lax.axis_size(axis)
    return [lax.ppermute(value, axis, [(i, (i - s) % n) for i in range(n)]) for s in range(1, n)]


def tree_sum(value, axis):
    n = lax.axis_size(axis)
    values = [value] + [
        lax.ppermute(value, axis, [(i, i ^ s) for i in range(n)]) for s in range(1, n)
    ]
    while len(values) > 1:
        values = [a + b for a, b in zip(values[::2], values[1::2])]
    return values[0]


def local(teacher_feats, student_feats, proto_weight):
    parts, groups = lax.axis_size("proto"), lax.axis_size("batch")
    own, width = teacher_feats.shape
    local_protos = proto_weight.shape[1]
    rows = own * groups
    others = rows - own
    protos = local_protos * parts
    feats = width // groups
    share = own // parts
    tiles = rows // LANES
    height = local_protos // LANES
    chunks = local_protos // WIDE
    place = jnp.stack([lax.axis_index("batch"), lax.axis_index("proto")]).astype(jnp.int32)
    struct = jax.ShapeDtypeStruct
    weight_bytes = 2 * width * local_protos
    exp_bytes = 2 * own * local_protos
    others_bytes = 2 * others * local_protos
    spread = pltpu.VMEM((own, LANES), F32)
    w_buffer = pltpu.VMEM((width, local_protos), BF16)
    exp_buffer = pltpu.VMEM((chunks, own, WIDE), BF16)
    sems = pltpu.SemaphoreType.DMA((chunks,))
    log_protos = math.log2(protos)
    token = struct((8, LANES), F32)

    def far(value):
        return pltpu.with_memory_space_constraint(value, pltpu.HBM)

    weight = far(proto_weight)
    teacher_rows, student_rows = far(teacher_feats), far(student_feats)
    s_all = following(student_feats, "batch")

    exps = pltpu.HBM((chunks, own, WIDE), BF16)
    t_exp, s_exp, stats = pl.pallas_call(
        stats_kernel,
        in_specs=[ANY] * 3,
        out_specs=[ANY, ANY, VMEM],
        out_shape=[
            exps,
            exps,
            struct((parts, 4 * own // LANES, LANES), F32),
        ],
        scratch_shapes=[
            pltpu.VMEM((2, own, width), BF16),
            w_buffer,
            pltpu.VMEM((2 * own, width), BF16),
            pltpu.VMEM((2, chunks, own, WIDE), BF16),
            pltpu.VMEM((2 * own, local_protos), F32),
            pltpu.VMEM((2 * own, LANES), F32),
            pltpu.VMEM((2 * own, LANES), F32),
            pltpu.SemaphoreType.DMA((2,)),
            sems, sems, sems,
        ],
        compiler_params=params(weight_bytes + 6 * exp_bytes),
        cost_estimate=cost(4 * own * width * local_protos, weight_bytes),
        name="own_rows",
    )(teacher_rows, student_rows, weight)
    t_exp, s_exp = far(t_exp), far(s_exp)

    back_student = pl.pallas_call(
        own_back_kernel,
        in_specs=[ANY] * 3,
        out_specs=VMEM,
        out_shape=struct((own, width), F32),
        scratch_shapes=[exp_buffer, w_buffer, sems, sems],
        compiler_params=params(weight_bytes + exp_bytes),
        cost_estimate=cost(2 * own * width * local_protos, weight_bytes),
        name="own_back",
    )(stats, s_exp, weight)

    stats = exchange(stats, "proto")

    first_shape = (1, height + 8, LANES)
    factor, cols = pl.pallas_call(
        first_column_kernel,
        in_specs=[SMEM, VMEM, ANY, ANY] + [ANY] * (groups - 1),
        out_specs=[VMEM, VMEM],
        out_shape=[token, struct(first_shape, F32)],
        scratch_shapes=[spread, exp_buffer, sems],
        compiler_params=params(exp_bytes),
        cost_estimate=cost(2 * own * local_protos, exp_bytes),
        name="first_columns",
    )(place, stats, t_exp, back_student, *s_all)

    unit, feat, scaled, t_unit = pl.pallas_call(
        functools.partial(student_rows_kernel, float(protos)),
        in_specs=[SMEM, VMEM, VMEM, VMEM] + [VMEM] * (groups - 1) + [ANY],
        out_specs=[VMEM] * 4,
        out_shape=[
            struct((others, width), BF16), struct((feats, rows), BF16), struct((feats, own), BF16),
            struct((own, width), BF16),
        ],
        scratch_shapes=[pltpu.VMEM((width, rows), BF16)],
        compiler_params=params(2 * rows * width),
        cost_estimate=cost(8 * rows * width, 2 * rows * width),
        name="student_rows",
    )(place, factor, teacher_feats, student_feats, *s_all, cols)
    t_all = following(t_unit, "batch")
    cols = [cols] + following(cols, "batch")
    logs = cols

    counts = [c * chunks // 8 for c in (1, 1, 1, 5)]
    grad_parts = []

    def student_piece(before):
        turn = len(grad_parts)
        first, count = sum(counts[:turn]), counts[turn]
        grad_part, done = pl.pallas_call(
            functools.partial(student_kernel, log_protos, first, groups),
            in_specs=[VMEM] * 3 + [ANY] * 2 + [VMEM] * groups + [ANY],
            out_specs=[VMEM, VMEM],
            out_shape=[struct((feats, count * WIDE), BF16), token],
            scratch_shapes=[
                pltpu.VMEM((others, LANES), F32),
                pltpu.VMEM((others, WIDE), BF16),
                pltpu.VMEM((count, own, WIDE), BF16),
                pltpu.VMEM((width, count * WIDE), BF16),
            ]
            + [pltpu.SemaphoreType.DMA((count,))] * 2,
            compiler_params=params(16 * 2**20),
            cost_estimate=cost(2.5 * rows * width * WIDE * count, 2 * width * WIDE * count),
            name="student_side",
        )(unit, feat, scaled, s_exp, weight, *logs, before)
        grad_parts.append(grad_part)
        return done

    done = unit
    for turn in range(SWEEPS - 1):
        late = t_all if turn == 1 else []
        sums = pl.pallas_call(
            functools.partial(row_kernel, len(cols)),
            in_specs=[VMEM] * (len(cols) + 1) + [ANY] * (2 + len(late)),
            out_specs=VMEM,
            out_shape=struct((parts, 8, LANES), F32),
            scratch_shapes=[pltpu.VMEM((height, LANES), F32), spread, exp_buffer, sems],
            compiler_params=params(exp_bytes),
            cost_estimate=cost(2 * own * local_protos, exp_bytes),
            name="rows",
        )(*cols, factor, t_exp, done, *late)
        done = student_piece(sums)
        sums = exchange(sums, "proto")
        middle = turn < SWEEPS - 2
        cols = pl.pallas_call(
            column_kernel,
            in_specs=[VMEM, VMEM, ANY, ANY],
            out_specs=VMEM,
            out_shape=struct((groups if middle else 1, height, LANES), F32),
            scratch_shapes=[spread, exp_buffer, sems],
            compiler_params=params(exp_bytes),
            cost_estimate=cost(2 * own * local_protos, exp_bytes),
            name="columns",
        )(sums, factor, t_exp, done)
        if turn < SWEEPS - 2:
            done = student_piece(cols)
        if middle:
            cols = [exchange(cols, "batch")]
        else:
            cols = [cols] + following(cols, "batch")

    sum_rows = -(-(tiles + own // LANES) // 16) * 16
    message_shape = (parts, 2 * share + sum_rows, width)
    prob, col_scale, message = pl.pallas_call(
        functools.partial(last_kernel, groups),
        in_specs=[VMEM] + [ANY] * 4 + [VMEM] * (3 * groups - 1) + [ANY],
        out_specs=[ANY, VMEM, VMEM],
        out_shape=[
            pltpu.HBM((chunks, others, WIDE), BF16),
            struct((height, LANES), F32),
            struct(message_shape, BF16),
        ],
        scratch_shapes=[
            pltpu.VMEM((others, width), BF16),
            pltpu.VMEM((others, LANES), F32),
            pltpu.VMEM((others, LANES), F32),
            spread,
            pltpu.VMEM((own, width), F32),
            pltpu.VMEM((own, WIDE), BF16),
            pltpu.VMEM((sum_rows, LANES), F32),
            pltpu.VMEM((min(chunks, 3), others, WIDE), BF16),
            exp_buffer,
            w_buffer,
            pltpu.VMEM((own, width), BF16),
            pltpu.VMEM((own, width), F32),
            sems, sems, sems,
            pltpu.SemaphoreType.DMA((2,)),
        ],
        compiler_params=params(20 * 2**20 + weight_bytes + exp_bytes),
        cost_estimate=cost(2 * rows * width * local_protos, others_bytes),
        name="last_rows",
    )(
        factor, student_rows, far(back_student), t_exp, weight, *t_all, *logs, *cols, done,
    )
    done = student_piece(message)
    message = exchange(message, "proto")

    grad_rows, loss_part, sums = pl.pallas_call(
        functools.partial(rows_kernel, tiles, float(protos)),
        in_specs=[SMEM, ANY, VMEM, VMEM, ANY],
        out_specs=[VMEM] * 3,
        out_shape=[struct((parts, share, width), BF16), token, struct((sum_rows, LANES), F32)],
        scratch_shapes=[spread, pltpu.VMEM((share, width), BF16), pltpu.SemaphoreType.DMA],
        compiler_params=params(0),
        name="row_grads",
    )(place, student_rows, message, logs[0], done)
    grad_rows = exchange(grad_rows, "proto").reshape(own, width).astype(F32)
    loss = tree_sum(loss_part, "batch")[0, 0]

    grad_weight = pl.pallas_call(
        functools.partial(grad_kernel, counts, float(protos)),
        in_specs=[ANY] * 2
        + [VMEM] * 4
        + [ANY if i in FAR else VMEM for i in range(len(counts))],
        out_specs=ANY,
        out_shape=struct((feats, local_protos), BF16),
        scratch_shapes=[
            pltpu.VMEM((feats, rows), BF16),
            exp_buffer,
            pltpu.VMEM((chunks, others, WIDE), BF16),
            pltpu.VMEM((feats, local_protos), BF16),
            pltpu.VMEM((feats, sum(counts[i] for i in FAR) * WIDE), BF16),
            sems, sems, sems, sems,
        ],
        compiler_params=params(exp_bytes + others_bytes + 4 * feats * local_protos),
        cost_estimate=cost(2 * feats * rows * local_protos, others_bytes),
        name="weight_grads",
    )(t_exp, far(prob), feat, col_scale, sums, factor, *[far(x) if i in FAR else x for i, x in enumerate(grad_parts)])
    return grad_weight, grad_rows, loss


def solution(mesh):
    return jax.shard_map(
        local,
        mesh=mesh,
        in_specs=(P("batch", None), P("batch", None), P(None, "proto")),
        out_specs=(P("batch", "proto"), P("batch", None), P()),
        check_vma=False,
    )
```

```python
import functools
import math

import jax
import jax.numpy as jnp
from jax import lax
from jax.experimental import pallas as pl
from jax.experimental.pallas import tpu as pltpu
from jax.sharding import PartitionSpec as P

SWEEPS = 3
TEMP_TEACHER = 0.04
TEMP_STUDENT = 0.1
LOG2E = math.log2(math.e)
SCALE_TEACHER = LOG2E / TEMP_TEACHER
SCALE_STUDENT = LOG2E / TEMP_STUDENT
LANES = 128
WIDE = 1024
TILE = 512
FAR = (0, 1, 2)
F32 = jnp.float32
BF16 = jnp.bfloat16


def unit_rows(values):
    wide = values.astype(F32)
    length = jnp.sqrt(jnp.sum(wide * wide, axis=-1, keepdims=True) + 1e-06)
    return wide / length, length


def diagonal():
    shape = (LANES, LANES)
    return lax.broadcasted_iota(jnp.int32, shape, 0) == lax.broadcasted_iota(jnp.int32, shape, 1)


def to_column(row):
    spread = jnp.where(diagonal(), jnp.broadcast_to(row, (LANES, LANES)), 0.0)
    return jnp.sum(spread, axis=1, keepdims=True)


def to_row(column):
    spread = jnp.where(diagonal(), jnp.broadcast_to(column, (LANES, LANES)), 0.0)
    return jnp.sum(spread, axis=0, keepdims=True)


def spread_rows(ref, rows):
    for a in range(rows.shape[0]):
        ref[a * LANES : (a + 1) * LANES, :] = jnp.broadcast_to(
            to_column(rows[a : a + 1, :]), (LANES, LANES)
        )


def pack_rows(ref, columns):
    for a in range(columns.shape[0] // LANES):
        ref[a : a + 1, :] = to_row(columns[a * LANES : (a + 1) * LANES, :])


def lane_tiles(values):
    return [values[:, t * LANES : (t + 1) * LANES] for t in range(values.shape[1] // LANES)]


def fold(values):
    return functools.reduce(jnp.add, lane_tiles(values))


def column_sums(values):
    rows, cols = values.shape
    return jnp.sum(values.reshape(rows // 8, 8, cols), axis=0)


def nt_dot(a, b):
    return lax.dot_general(a, b, (((1,), (1,)), ((), ())), preferred_element_type=F32)


def add_up(values):
    return functools.reduce(jnp.add, values)


def repeat(out_ref):
    for p in range(1, out_ref.shape[0]):
        out_ref[p] = out_ref[0]


def chunk(k):
    return slice(k * WIDE, (k + 1) * WIDE)


def copies(source, target, sems, first=0, back=0, count=None):
    def chunks(ref):
        return ref.shape[0] if len(ref.shape) == 3 else ref.shape[1] // WIDE

    count = count or min(chunks(source), chunks(target))
    return [copy_of(source, target, sems, k, first, back) for k in range(count)]


def columns_of(k, first=0, count=WIDE):
    return pl.ds(pl.multiple_of(k * WIDE + first, LANES), count)


def copy_of(source, target, sems, k, first=0, back=0):
    def part(ref, k):
        return ref.at[k] if len(ref.shape) == 3 else ref.at[:, columns_of(k)]

    return pltpu.make_async_copy(part(source, first + k), part(target, back + k), sems.at[k])


def start(*lists):
    for each in zip(*lists):
        for copy in each:
            copy.start()


def whole_copies(pairs, sems):
    return [pltpu.make_async_copy(a, b, sems.at[i]) for i, (a, b) in enumerate(pairs)]


def wait(*lists):
    for each in lists:
        for copy in each:
            copy.wait()


def stats_kernel(
    t_hbm, s_hbm, w_hbm, t_out, s_out, out_ref,
    raw, w_ref, unit, exps, logits, top, total, raw_sem, w_sem, t_sem, s_sem,
):
    own = raw.shape[1]
    quarter = out_ref.shape[1] // 4
    chunks = exps.shape[1]
    halves = (slice(0, own), slice(own, 2 * own))
    loads = copies(w_hbm, w_ref, w_sem)
    raw_loads = [
        pltpu.make_async_copy(ref, raw.at[which], raw_sem.at[which])
        for which, ref in enumerate((t_hbm, s_hbm))
    ]
    start(raw_loads, loads[:2])
    start(loads[2:])
    top[...] = jnp.full(top.shape, -1e30, F32)
    total[...] = jnp.zeros(total.shape, F32)
    wait(raw_loads)
    for which in range(2):
        unit[halves[which], :] = unit_rows(raw[which])[0].astype(BF16)

    @pl.loop(0, chunks)
    def _(k):
        copy_of(w_hbm, w_ref, w_sem, k).wait()
        for n in range(0, WIDE, TILE):
            here = columns_of(k, n, TILE)
            values = jnp.dot(unit[...], w_ref[:, here], preferred_element_type=F32)
            for half, scale in zip(halves, (SCALE_TEACHER, SCALE_STUDENT)):
                part = values[half, :] * scale
                logits[half, here] = part
                top[half, :] = functools.reduce(jnp.maximum, lane_tiles(part), top[half, :])

    peak = jnp.max(top[...], axis=1, keepdims=True)
    top[...] = jnp.broadcast_to(peak, top.shape)

    @pl.loop(0, chunks)
    def _(k):
        for which, (half, out, sem) in enumerate(zip(halves, (t_out, s_out), (t_sem, s_sem))):
            shift = top[half, :]
            for n in range(0, WIDE, 2 * TILE):
                tiles = lane_tiles(logits[half, columns_of(k, n, 2 * TILE)])
                tiles = [jnp.exp2(tile - shift) for tile in tiles]
                for t, tile in enumerate(tiles):
                    lanes = slice(n + t * LANES, n + (t + 1) * LANES)
                    exps[which, k, :, lanes] = tile.astype(BF16)
                total[half, :] += add_up(tiles)
            copy_of(exps.at[which], out, sem, k).start()

    sums = jnp.sum(total[...], axis=1, keepdims=True)
    for which, half in enumerate(halves):
        for k, column in enumerate((peak, sums)):
            first = (2 * which + k) * quarter
            pack_rows(out_ref.at[0, first : first + quarter], column[half, :])
    repeat(out_ref)
    wait(copies(exps.at[0], t_out, t_sem), copies(exps.at[1], s_out, s_sem))


def merged(stats_ref, which):
    parts, height, _ = stats_ref.shape
    quarter = height // 4
    first = 2 * which * quarter
    tops = [stats_ref[p, first : first + quarter, :] for p in range(parts)]
    top = functools.reduce(jnp.maximum, tops)
    sums = [
        stats_ref[p, first + quarter : first + 2 * quarter, :] * jnp.exp2(tops[p] - top)
        for p in range(parts)
    ]
    return top + jnp.log2(add_up(sums))


def column_pass(exp_hbm, exp_ref, sem, weight, out_ref):
    height = WIDE // LANES

    @pl.loop(0, exp_ref.shape[0])
    def _(k):
        copy_of(exp_hbm, exp_ref, sem, k).wait()
        sums = jnp.zeros((8, WIDE), F32)
        for g in range(0, exp_ref.shape[1], 16):
            shift = weight[g : g + 16, :]
            tiles = lane_tiles(exp_ref[k, g : g + 16, :].astype(F32))
            sums = sums + column_sums(jnp.concatenate([tile * shift for tile in tiles], axis=1))
        sums = jnp.sum(sums, axis=0, keepdims=True)
        block = jnp.concatenate(lane_tiles(sums), axis=0)
        for g in range(out_ref.shape[0]):
            out_ref[g, pl.ds(pl.multiple_of(k * height, height), height), :] = block


def first_column_kernel(place_ref, stats_ref, exp_hbm, *refs):
    factor_ref, out_ref, weight, exp_ref, sem = refs[-5:]
    start(copies(exp_hbm, exp_ref, sem))
    quarter = stats_ref.shape[1] // 4
    height = out_ref.shape[1] - 8
    own = stats_ref[pl.ds(place_ref[1], 1)][0]
    factor_ref[...] = jnp.zeros(factor_ref.shape, F32)
    rows = []
    for which in range(2):
        log_sum = merged(stats_ref, which)
        here = slice(which * quarter, (which + 1) * quarter)
        factor_ref[here, :] = jnp.exp2(
            own[2 * which * quarter : (2 * which + 1) * quarter, :] - log_sum
        )
        rows.append(log_sum)
    rows.append(jnp.zeros((8 - 2 * quarter, LANES), F32))
    logs = jnp.concatenate(rows, axis=0)
    for g in range(out_ref.shape[0]):
        out_ref[g, height:, :] = logs
    spread_rows(weight, factor_ref[:quarter, :])
    column_pass(exp_hbm, exp_ref, sem, weight, out_ref)


def column_kernel(sums_ref, factor_ref, exp_hbm, *refs):
    out_ref, weight, exp_ref, sem = refs[-4:]
    start(copies(exp_hbm, exp_ref, sem))
    quarter = weight.shape[0] // LANES
    scale = 1.0 / add_up([sums_ref[p, :quarter, :] for p in range(sums_ref.shape[0])])
    spread_rows(weight, scale * factor_ref[:quarter, :])
    column_pass(exp_hbm, exp_ref, sem, weight, out_ref)


def column_scales(cols, height):
    return 1.0 / add_up([ref[g, :height, :] for ref in cols for g in range(ref.shape[0])])


def chunk_scales(scales, k):
    height = WIDE // LANES
    return scales[pl.ds(pl.multiple_of(k * height, height), height), :]


def add_row_sums(rows, values, scale):
    for g in range(0, values.shape[0], 32):
        total = rows[g : g + 32, :]
        for t, tile in enumerate(lane_tiles(values[g : g + 32, :].astype(F32))):
            total = total + tile * scale[t : t + 1, :]
        rows[g : g + 32, :] = total


def row_kernel(count, *refs):
    cols, (factor_ref, exp_hbm) = refs[:count], refs[count : count + 2]
    out_ref, scales, rows, exp_ref, sem = refs[-5:]
    start(copies(exp_hbm, exp_ref, sem))
    scales[...] = column_scales(cols, scales.shape[0])
    rows[...] = jnp.zeros(rows.shape, F32)
    quarter = rows.shape[0] // LANES
    out_ref[0] = jnp.zeros(out_ref.shape[1:], F32)

    @pl.loop(0, exp_ref.shape[0])
    def _(k):
        copy_of(exp_hbm, exp_ref, sem, k).wait()
        add_row_sums(rows, exp_ref.at[k], chunk_scales(scales, k))

    pack_rows(out_ref.at[0, :quarter], jnp.sum(rows[...], axis=1, keepdims=True))
    out_ref[0, :quarter, :] = out_ref[0, :quarter, :] * factor_ref[:quarter, :]
    repeat(out_ref)


def own_back_kernel(before_ref, exp_hbm, w_hbm, back_ref, exp_ref, w_ref, exp_sem, w_sem):
    start(copies(exp_hbm, exp_ref, exp_sem), copies(w_hbm, w_ref, w_sem))
    back_ref[...] = jnp.zeros(back_ref.shape, F32)

    @pl.loop(0, exp_ref.shape[0])
    def _(k):
        copy_of(exp_hbm, exp_ref, exp_sem, k).wait()
        copy_of(w_hbm, w_ref, w_sem, k).wait()
        back_ref[...] += nt_dot(exp_ref[k], w_ref[:, columns_of(k)])


def relative_logs(logs, lse, which, shift=0.0):
    own = lse.shape[0] // (len(logs) - 1)
    quarter = own // LANES
    for g, ref in enumerate(logs[1:]):
        first = ref.shape[1] - 8 + which * quarter
        spread_rows(lse.at[g * own : (g + 1) * own], ref[0, first : first + quarter, :] - shift)


def student_rows_kernel(protos, place_ref, factor_ref, t_ref, own_ref, *refs):
    unit_ref, feat_ref, scaled_ref, t_unit, turned = refs[-5:]
    t_unit[...] = unit_rows(t_ref[...])[0].astype(BF16)
    own = own_ref.shape[0]
    groups = turned.shape[1] // own
    raw = refs[: groups - 1]
    quarter, feats = own // LANES, feat_ref.shape[0]
    for g in range(groups):
        half = unit_rows((raw[g - 1] if g else own_ref)[...])[0].astype(BF16)
        if g:
            unit_ref[(g - 1) * own : g * own, :] = half
        half = half.astype(F32)
        for a in range(0, own, LANES):
            first = g * own + a
            turned[:, first : first + LANES] = jnp.transpose(half[a : a + LANES, :]).astype(BF16)
    feat = turned[pl.ds(pl.multiple_of(place_ref[0] * feats, feats), feats), :]
    feat_ref[...] = feat
    for a in range(quarter):
        lanes = slice(a * LANES, (a + 1) * LANES)
        factor = factor_ref[quarter + a : quarter + a + 1, :] * protos
        scaled_ref[:, lanes] = (feat[:, lanes].astype(F32) * factor).astype(BF16)


def probabilities(unit, w_ref, k, lse, scale, use):
    for n in range(0, WIDE, TILE):
        logits = jnp.dot(
            unit[...], w_ref[:, columns_of(k, n, TILE)], preferred_element_type=F32
        )
        shift = lse[...]
        use(n, [jnp.exp2(tile * scale - shift) for tile in lane_tiles(logits)])


def student_kernel(
    log_protos, first, groups, unit, feat_ref, scaled_ref, exp_hbm, w_hbm, *refs
):
    logs = refs[:groups]
    grad, token_ref, lse, prob, exp_ref, w_ref, exp_sem, w_sem = refs[-8:]
    own, count = exp_ref.shape[1], exp_ref.shape[0]
    exp_loads = copies(exp_hbm, exp_ref, exp_sem, first, 0, count)
    w_loads = copies(w_hbm, w_ref, w_sem, first, 0, count)
    start(w_loads, exp_loads)
    token_ref[...] = jnp.zeros(token_ref.shape, F32)
    relative_logs(logs, lse, 1, log_protos)

    @pl.loop(0, count)
    def _(k):
        copy_of(w_hbm, w_ref, w_sem, k, first).wait()

        def use(n, tiles):
            for t, tile in enumerate(tiles):
                prob[:, n + t * LANES : n + (t + 1) * LANES] = tile.astype(BF16)

        probabilities(unit, w_ref, k, lse, SCALE_STUDENT, use)
        copy_of(exp_hbm, exp_ref, exp_sem, k, first).wait()
        values = jnp.dot(scaled_ref[...], exp_ref[k], preferred_element_type=F32)
        values = values + jnp.dot(feat_ref[:, own:], prob[...], preferred_element_type=F32)
        grad[:, columns_of(k)] = values.astype(BF16)


def as_three(value):
    high = value.astype(BF16)
    rest = value - high.astype(F32)
    middle = rest.astype(BF16)
    return high, middle, (rest - middle.astype(F32)).astype(BF16)


def last_kernel(groups, factor_ref, own_hbm, student_hbm, exp_hbm, w_hbm, *refs):
    units, refs = refs[: groups - 1], refs[groups - 1 :]
    logs, cols, refs = refs[:groups], refs[groups : 2 * groups], refs[2 * groups :]
    (
        prob_hbm, scale_ref, out_ref, unit, lse, rows, own_rows, back, scaled, sums, prob_ref,
        exp_ref, w_ref, own_ref, student_ref, prob_sem, exp_sem, w_sem, sem,
    ) = refs[-19:]
    w_loads, exp_loads = copies(w_hbm, w_ref, w_sem), copies(exp_hbm, exp_ref, exp_sem)
    late_loads = whole_copies([(own_hbm, own_ref), (student_hbm, student_ref)], sem)
    start(w_loads, exp_loads)
    start(late_loads)
    slots, others, _ = prob_ref.shape
    own, chunks = exp_ref.shape[1], exp_ref.shape[0]
    tiles = (own + others) // LANES
    quarter = own // LANES
    scale_ref[...] = column_scales(cols, scale_ref.shape[0])
    rows[...] = jnp.zeros(rows.shape, F32)
    own_rows[...] = jnp.zeros(own_rows.shape, F32)
    back[...] = jnp.zeros(back.shape, F32)
    relative_logs(logs, lse, 0)
    for g in range(groups - 1):
        unit[g * own : (g + 1) * own, :] = units[g][...]
    partner = slice((groups // 2 - 1) * own, groups // 2 * own)

    def store(k):
        return pltpu.make_async_copy(prob_ref.at[lax.rem(k, slots)], prob_hbm.at[k], prob_sem.at[k])

    @pl.loop(0, chunks)
    def _(k):
        copy_of(w_hbm, w_ref, w_sem, k).wait()
        slot = lax.rem(k, slots)
        scale = chunk_scales(scale_ref, k)

        @pl.when(k >= slots)
        def _():
            store(k - slots).wait()

        def use(n, tiles):
            for t, tile in enumerate(tiles):
                prob_ref[slot, :, n + t * LANES : n + (t + 1) * LANES] = tile.astype(BF16)
            first = n // LANES
            tiles = [tile * scale[first + t : first + t + 1, :] for t, tile in enumerate(tiles)]
            rows[...] += add_up(tiles)
            for t, tile in enumerate(tiles):
                scaled[:, n + t * LANES : n + (t + 1) * LANES] = tile[partner, :].astype(BF16)

        probabilities(unit, w_ref, k, lse, SCALE_TEACHER, use)
        store(k).start()
        back[...] += nt_dot(scaled[...], w_ref[:, columns_of(k)])
        copy_of(exp_hbm, exp_ref, exp_sem, k).wait()
        add_row_sums(own_rows, exp_ref.at[k], scale)

    sums[...] = jnp.zeros(sums.shape, F32)
    pack_rows(sums.at[:quarter], jnp.sum(own_rows[...], axis=1, keepdims=True))
    sums[:quarter, :] = sums[:quarter, :] * factor_ref[:quarter, :]
    pack_rows(sums.at[quarter:tiles], jnp.sum(rows[...], axis=1, keepdims=True))
    wait(late_loads)
    half = unit_rows(own_ref[...])[0].astype(BF16).astype(F32)
    inner = jnp.sum(half * back[...], axis=1, keepdims=True)
    pack_rows(sums.at[tiles : tiles + quarter], inner)
    parts = out_ref.shape[0]
    share = own // parts
    protos = 1.0 * out_ref.shape[0] * w_ref.shape[1]
    student = []
    for a in range(quarter):
        factor = to_column(factor_ref[quarter + a : quarter + a + 1, :] * protos)
        student.append(student_ref[a * LANES : (a + 1) * LANES, :] * factor)
    student = jnp.concatenate(student, axis=0).astype(BF16)
    terms = list(as_three(sums[...]))
    terms.append(jnp.zeros((sums.shape[0], out_ref.shape[2] - 3 * LANES), BF16))
    terms = jnp.concatenate(terms, axis=1)
    for p in range(parts):
        here = slice(p * share, (p + 1) * share)
        out_ref[p] = jnp.concatenate(
            [student[here, :], back[here, :].astype(BF16), terms], axis=0
        )
    for k in range(max(0, chunks - slots), chunks):
        store(k).wait()


def total_sums(message_ref, first):
    parts = message_ref.shape[0]
    each = [
        add_up([t.astype(F32) for t in lane_tiles(message_ref[p, first:, : 3 * LANES])[::-1]])
        for p in range(parts)
    ]
    return add_up(each)


def rows_kernel(tiles, protos, place_ref, s_hbm, message_ref, logs_ref, *refs):
    out_ref, loss_ref, sums_ref, weight, s_ref, sem = refs[-6:]
    parts = message_ref.shape[0]
    share, own = out_ref.shape[1], weight.shape[0]
    mine = pl.ds(pl.multiple_of(place_ref[1] * share, share), share)
    load = pltpu.make_async_copy(s_hbm.at[mine], s_ref, sem)
    load.start()
    quarter = own // LANES
    first = tiles // 2
    totals = total_sums(message_ref, 2 * share)
    sums_ref[...] = totals
    scale = 1.0 / totals[first : first + quarter, :]
    spread_rows(weight, scale)
    total = add_up([message_ref[p, :share, :].astype(F32) for p in range(parts)])
    paired = add_up([message_ref[p, share : 2 * share, :].astype(F32) for p in range(parts)])
    total = total - paired * (weight[mine, :1] * protos)
    load.wait()
    unit, length = unit_rows(s_ref[...])
    total = (total - unit * jnp.sum(unit * total, axis=-1, keepdims=True)) / length
    out_ref[0] = total.astype(BF16)
    repeat(out_ref)
    height = logs_ref.shape[1] - 8
    logs = logs_ref[0, height + quarter : height + 2 * quarter, :]
    terms = logs / LOG2E - totals[tiles : tiles + quarter, :] * scale / TEMP_STUDENT
    loss_ref[...] = jnp.broadcast_to(jnp.sum(terms) / (tiles * LANES), loss_ref.shape)


def grad_kernel(counts, protos, exp_hbm, prob_hbm, feat_ref, scale_ref, sums_ref, factor_ref, *refs):
    parts = refs[: len(counts)]
    out_hbm, scaled, exp_ref, prob_ref, out, part_ref, exp_sem, prob_sem, sem, part_sem = refs[-10:]
    part_loads, where = {}, []
    for i, (count, part) in enumerate(zip(counts, parts)):
        for k in range(count):
            if i in FAR:
                slot = len(part_loads)
                part_loads[len(where)] = copy_of(part, part_ref, part_sem, slot, k - slot)
                where.append((part_ref, slot))
            else:
                where.append((part, k))
    exp_loads = copies(exp_hbm, exp_ref, exp_sem)
    prob_loads = copies(prob_hbm, prob_ref, prob_sem)
    start(exp_loads[:1], prob_loads[:1])
    start(list(part_loads.values()))
    start(exp_loads[1:], prob_loads[1:])
    own = exp_ref.shape[1]
    tiles = (own + prob_ref.shape[1]) // LANES
    rows = protos / sums_ref[:tiles, :]
    for a in range(tiles):
        other = (a + tiles // 2) % tiles
        feat = feat_ref[:, other * LANES : (other + 1) * LANES].astype(F32)
        row = rows[a : a + 1, :]
        if a < own // LANES:
            row = row * factor_ref[a : a + 1, :]
        scaled[:, a * LANES : (a + 1) * LANES] = (feat * row).astype(BF16)
    stores = copies(out, out_hbm, sem)
    for k, store in enumerate(stores):
        exp_loads[k].wait()
        prob_loads[k].wait()
        paired = jnp.dot(scaled[:, :own], exp_ref[k], preferred_element_type=F32)
        paired = paired + jnp.dot(
            scaled[:, own:], prob_ref[k], preferred_element_type=F32
        )
        part, there = where[k]
        if k in part_loads:
            part_loads[k].wait()
        for t, tile in enumerate(lane_tiles(paired)):
            lanes = slice(k * WIDE + t * LANES, k * WIDE + (t + 1) * LANES)
            scale = scale_ref[lanes.start // LANES : lanes.stop // LANES, :]
            own_part = part[:, there * WIDE + t * LANES : there * WIDE + (t + 1) * LANES]
            out[:, lanes] = (own_part.astype(F32) - tile * scale).astype(BF16)
        store.start()
    for store in stores:
        store.wait()


SMEM = pl.BlockSpec(memory_space=pltpu.SMEM)
VMEM = pl.BlockSpec(memory_space=pltpu.VMEM)
ANY = pl.BlockSpec(memory_space=pl.ANY)


def params(nbytes):
    return pltpu.CompilerParams(vmem_limit_bytes=int(nbytes) + 8 * 2**20)


def cost(flops, nbytes, exps=0):
    return pl.CostEstimate(flops=int(flops), bytes_accessed=int(nbytes), transcendentals=int(exps))


def exchange(value, axis):
    return lax.all_to_all(value, axis, 0, 0)


def following(value, axis):
    n = lax.axis_size(axis)
    return [lax.ppermute(value, axis, [(i, (i - s) % n) for i in range(n)]) for s in range(1, n)]


def tree_sum(value, axis):
    n = lax.axis_size(axis)
    values = [value] + [
        lax.ppermute(value, axis, [(i, i ^ s) for i in range(n)]) for s in range(1, n)
    ]
    while len(values) > 1:
        values = [a + b for a, b in zip(values[::2], values[1::2])]
    return values[0]


def local(teacher_feats, student_feats, proto_weight):
    parts, groups = lax.axis_size("proto"), lax.axis_size("batch")
    own, width = teacher_feats.shape
    local_protos = proto_weight.shape[1]
    rows = own * groups
    others = rows - own
    protos = local_protos * parts
    feats = width // groups
    share = own // parts
    tiles = rows // LANES
    height = local_protos // LANES
    chunks = local_protos // WIDE
    place = jnp.stack([lax.axis_index("batch"), lax.axis_index("proto")]).astype(jnp.int32)
    struct = jax.ShapeDtypeStruct
    weight_bytes = 2 * width * local_protos
    exp_bytes = 2 * own * local_protos
    others_bytes = 2 * others * local_protos
    spread = pltpu.VMEM((own, LANES), F32)
    w_buffer = pltpu.VMEM((width, local_protos), BF16)
    exp_buffer = pltpu.VMEM((chunks, own, WIDE), BF16)
    sems = pltpu.SemaphoreType.DMA((chunks,))
    log_protos = math.log2(protos)
    token = struct((8, LANES), F32)

    def far(value):
        return pltpu.with_memory_space_constraint(value, pltpu.HBM)

    weight = far(proto_weight)
    teacher_rows, student_rows = far(teacher_feats), far(student_feats)
    s_all = following(student_feats, "batch")

    exps = pltpu.HBM((chunks, own, WIDE), BF16)
    t_exp, s_exp, stats = pl.pallas_call(
        stats_kernel,
        in_specs=[ANY] * 3,
        out_specs=[ANY, ANY, VMEM],
        out_shape=[
            exps,
            exps,
            struct((parts, 4 * own // LANES, LANES), F32),
        ],
        scratch_shapes=[
            pltpu.VMEM((2, own, width), BF16),
            w_buffer,
            pltpu.VMEM((2 * own, width), BF16),
            pltpu.VMEM((2, chunks, own, WIDE), BF16),
            pltpu.VMEM((2 * own, local_protos), F32),
            pltpu.VMEM((2 * own, LANES), F32),
            pltpu.VMEM((2 * own, LANES), F32),
            pltpu.SemaphoreType.DMA((2,)),
            sems, sems, sems,
        ],
        compiler_params=params(weight_bytes + 6 * exp_bytes),
        cost_estimate=cost(4 * own * width * local_protos, weight_bytes),
        name="own_rows",
    )(teacher_rows, student_rows, weight)
    t_exp, s_exp = far(t_exp), far(s_exp)

    back_student = pl.pallas_call(
        own_back_kernel,
        in_specs=[ANY] * 3,
        out_specs=VMEM,
        out_shape=struct((own, width), F32),
        scratch_shapes=[exp_buffer, w_buffer, sems, sems],
        compiler_params=params(weight_bytes + exp_bytes),
        cost_estimate=cost(2 * own * width * local_protos, weight_bytes),
        name="own_back",
    )(stats, s_exp, weight)

    stats = exchange(stats, "proto")

    first_shape = (1, height + 8, LANES)
    factor, cols = pl.pallas_call(
        first_column_kernel,
        in_specs=[SMEM, VMEM, ANY, ANY] + [ANY] * (groups - 1),
        out_specs=[VMEM, VMEM],
        out_shape=[token, struct(first_shape, F32)],
        scratch_shapes=[spread, exp_buffer, sems],
        compiler_params=params(exp_bytes),
        cost_estimate=cost(2 * own * local_protos, exp_bytes),
        name="first_columns",
    )(place, stats, t_exp, back_student, *s_all)

    unit, feat, scaled, t_unit = pl.pallas_call(
        functools.partial(student_rows_kernel, float(protos)),
        in_specs=[SMEM, VMEM, VMEM, VMEM] + [VMEM] * (groups - 1) + [ANY],
        out_specs=[VMEM] * 4,
        out_shape=[
            struct((others, width), BF16), struct((feats, rows), BF16), struct((feats, own), BF16),
            struct((own, width), BF16),
        ],
        scratch_shapes=[pltpu.VMEM((width, rows), BF16)],
        compiler_params=params(2 * rows * width),
        cost_estimate=cost(8 * rows * width, 2 * rows * width),
        name="student_rows",
    )(place, factor, teacher_feats, student_feats, *s_all, cols)
    t_all = following(t_unit, "batch")
    cols = [cols] + following(cols, "batch")
    logs = cols

    counts = [c * chunks // 8 for c in (1, 1, 1, 5)]
    grad_parts = []

    def student_piece(before):
        turn = len(grad_parts)
        first, count = sum(counts[:turn]), counts[turn]
        grad_part, done = pl.pallas_call(
            functools.partial(student_kernel, log_protos, first, groups),
            in_specs=[VMEM] * 3 + [ANY] * 2 + [VMEM] * groups + [ANY],
            out_specs=[VMEM, VMEM],
            out_shape=[struct((feats, count * WIDE), BF16), token],
            scratch_shapes=[
                pltpu.VMEM((others, LANES), F32),
                pltpu.VMEM((others, WIDE), BF16),
                pltpu.VMEM((count, own, WIDE), BF16),
                pltpu.VMEM((width, count * WIDE), BF16),
            ]
            + [pltpu.SemaphoreType.DMA((count,))] * 2,
            compiler_params=params(16 * 2**20),
            cost_estimate=cost(2.5 * rows * width * WIDE * count, 2 * width * WIDE * count),
            name="student_side",
        )(unit, feat, scaled, s_exp, weight, *logs, before)
        grad_parts.append(grad_part)
        return done

    done = unit
    for turn in range(SWEEPS - 1):
        late = t_all if turn == 1 else []
        sums = pl.pallas_call(
            functools.partial(row_kernel, len(cols)),
            in_specs=[VMEM] * (len(cols) + 1) + [ANY] * (2 + len(late)),
            out_specs=VMEM,
            out_shape=struct((parts, 8, LANES), F32),
            scratch_shapes=[pltpu.VMEM((height, LANES), F32), spread, exp_buffer, sems],
            compiler_params=params(exp_bytes),
            cost_estimate=cost(2 * own * local_protos, exp_bytes),
            name="rows",
        )(*cols, factor, t_exp, done, *late)
        done = student_piece(sums)
        sums = exchange(sums, "proto")
        middle = turn < SWEEPS - 2
        cols = pl.pallas_call(
            column_kernel,
            in_specs=[VMEM, VMEM, ANY, ANY],
            out_specs=VMEM,
            out_shape=struct((groups if middle else 1, height, LANES), F32),
            scratch_shapes=[spread, exp_buffer, sems],
            compiler_params=params(exp_bytes),
            cost_estimate=cost(2 * own * local_protos, exp_bytes),
            name="columns",
        )(sums, factor, t_exp, done)
        if turn < SWEEPS - 2:
            done = student_piece(cols)
        if middle:
            cols = [exchange(cols, "batch")]
        else:
            cols = [cols] + following(cols, "batch")

    sum_rows = -(-(tiles + own // LANES) // 16) * 16
    message_shape = (parts, 2 * share + sum_rows, width)
    prob, col_scale, message = pl.pallas_call(
        functools.partial(last_kernel, groups),
        in_specs=[VMEM] + [ANY] * 4 + [VMEM] * (3 * groups - 1) + [ANY],
        out_specs=[ANY, VMEM, VMEM],
        out_shape=[
            pltpu.HBM((chunks, others, WIDE), BF16),
            struct((height, LANES), F32),
            struct(message_shape, BF16),
        ],
        scratch_shapes=[
            pltpu.VMEM((others, width), BF16),
            pltpu.VMEM((others, LANES), F32),
            pltpu.VMEM((others, LANES), F32),
            spread,
            pltpu.VMEM((own, width), F32),
            pltpu.VMEM((own, WIDE), BF16),
            pltpu.VMEM((sum_rows, LANES), F32),
            pltpu.VMEM((min(chunks, 3), others, WIDE), BF16),
            exp_buffer,
            w_buffer,
            pltpu.VMEM((own, width), BF16),
            pltpu.VMEM((own, width), F32),
            sems, sems, sems,
            pltpu.SemaphoreType.DMA((2,)),
        ],
        compiler_params=params(20 * 2**20 + weight_bytes + exp_bytes),
        cost_estimate=cost(2 * rows * width * local_protos, others_bytes),
        name="last_rows",
    )(
        factor, student_rows, far(back_student), t_exp, weight, *t_all, *logs, *cols, done,
    )
    done = student_piece(message)
    message = exchange(message, "proto")

    grad_rows, loss_part, sums = pl.pallas_call(
        functools.partial(rows_kernel, tiles, float(protos)),
        in_specs=[SMEM, ANY, VMEM, VMEM, ANY],
        out_specs=[VMEM] * 3,
        out_shape=[struct((parts, share, width), BF16), token, struct((sum_rows, LANES), F32)],
        scratch_shapes=[spread, pltpu.VMEM((share, width), BF16), pltpu.SemaphoreType.DMA],
        compiler_params=params(0),
        name="row_grads",
    )(place, student_rows, message, logs[0], done)
    grad_rows = exchange(grad_rows, "proto").reshape(own, width).astype(F32)
    loss = tree_sum(loss_part, "batch")[0, 0]

    grad_weight = pl.pallas_call(
        functools.partial(grad_kernel, counts, float(protos)),
        in_specs=[ANY] * 2
        + [VMEM] * 4
        + [ANY if i in FAR else VMEM for i in range(len(counts))],
        out_specs=ANY,
        out_shape=struct((feats, local_protos), BF16),
        scratch_shapes=[
            pltpu.VMEM((feats, rows), BF16),
            exp_buffer,
            pltpu.VMEM((chunks, others, WIDE), BF16),
            pltpu.VMEM((feats, local_protos), BF16),
            pltpu.VMEM((feats, sum(counts[i] for i in FAR) * WIDE), BF16),
            sems, sems, sems, sems,
        ],
        compiler_params=params(exp_bytes + others_bytes + 4 * feats * local_protos),
        cost_estimate=cost(2 * feats * rows * local_protos, others_bytes),
        name="weight_grads",
    )(t_exp, far(prob), feat, col_scale, sums, factor, *[far(x) if i in FAR else x for i, x in enumerate(grad_parts)])
    return grad_weight, grad_rows, loss


def solution(mesh):
    return jax.shard_map(
        local,
        mesh=mesh,
        in_specs=(P("batch", None), P("batch", None), P(None, "proto")),
        out_specs=(P("batch", "proto"), P("batch", None), P()),
        check_vma=False,
    )
```

```python
import functools
import math

import jax
import jax.numpy as jnp
from jax import lax
from jax.experimental import pallas as pl
from jax.experimental.pallas import tpu as pltpu
from jax.sharding import PartitionSpec as P

SWEEPS = 3
TEMP_TEACHER = 0.04
TEMP_STUDENT = 0.1
LOG2E = math.log2(math.e)
SCALE_TEACHER = LOG2E / TEMP_TEACHER
SCALE_STUDENT = LOG2E / TEMP_STUDENT
LANES = 128
WIDE = 1024
TILE = 1024
FAR = (0, 1, 2)
F32 = jnp.float32
BF16 = jnp.bfloat16


def unit_rows(values):
    wide = values.astype(F32)
    length = jnp.sqrt(jnp.sum(wide * wide, axis=-1, keepdims=True) + 1e-06)
    return wide / length, length


def diagonal():
    shape = (LANES, LANES)
    return lax.broadcasted_iota(jnp.int32, shape, 0) == lax.broadcasted_iota(jnp.int32, shape, 1)


def to_column(row):
    spread = jnp.where(diagonal(), jnp.broadcast_to(row, (LANES, LANES)), 0.0)
    return jnp.sum(spread, axis=1, keepdims=True)


def to_row(column):
    spread = jnp.where(diagonal(), jnp.broadcast_to(column, (LANES, LANES)), 0.0)
    return jnp.sum(spread, axis=0, keepdims=True)


def spread_rows(ref, rows):
    for a in range(rows.shape[0]):
        ref[a * LANES : (a + 1) * LANES, :] = jnp.broadcast_to(
            to_column(rows[a : a + 1, :]), (LANES, LANES)
        )


def pack_rows(ref, columns):
    for a in range(columns.shape[0] // LANES):
        ref[a : a + 1, :] = to_row(columns[a * LANES : (a + 1) * LANES, :])


def lane_tiles(values):
    return [values[:, t * LANES : (t + 1) * LANES] for t in range(values.shape[1] // LANES)]


def fold(values):
    return functools.reduce(jnp.add, lane_tiles(values))


def column_sums(values):
    rows, cols = values.shape
    return jnp.sum(values.reshape(rows // 8, 8, cols), axis=0)


def nt_dot(a, b):
    return lax.dot_general(a, b, (((1,), (1,)), ((), ())), preferred_element_type=F32)


def add_up(values):
    return functools.reduce(jnp.add, values)


def repeat(out_ref):
    for p in range(1, out_ref.shape[0]):
        out_ref[p] = out_ref[0]


def chunk(k):
    return slice(k * WIDE, (k + 1) * WIDE)


def copies(source, target, sems, first=0, back=0, count=None):
    def chunks(ref):
        return ref.shape[0] if len(ref.shape) == 3 else ref.shape[1] // WIDE

    count = count or min(chunks(source), chunks(target))
    return [copy_of(source, target, sems, k, first, back) for k in range(count)]


def columns_of(k, first=0, count=WIDE):
    return pl.ds(pl.multiple_of(k * WIDE + first, LANES), count)


def copy_of(source, target, sems, k, first=0, back=0):
    def part(ref, k):
        return ref.at[k] if len(ref.shape) == 3 else ref.at[:, columns_of(k)]

    return pltpu.make_async_copy(part(source, first + k), part(target, back + k), sems.at[k])


def start(*lists):
    for each in zip(*lists):
        for copy in each:
            copy.start()


def whole_copies(pairs, sems):
    return [pltpu.make_async_copy(a, b, sems.at[i]) for i, (a, b) in enumerate(pairs)]


def wait(*lists):
    for each in lists:
        for copy in each:
            copy.wait()


def stats_kernel(
    t_hbm, s_hbm, w_hbm, t_out, s_out, out_ref,
    raw, w_ref, unit, exps, logits, top, total, raw_sem, w_sem, t_sem, s_sem,
):
    own = raw.shape[1]
    quarter = out_ref.shape[1] // 4
    chunks = exps.shape[1]
    halves = (slice(0, own), slice(own, 2 * own))
    loads = copies(w_hbm, w_ref, w_sem)
    raw_loads = [
        pltpu.make_async_copy(ref, raw.at[which], raw_sem.at[which])
        for which, ref in enumerate((t_hbm, s_hbm))
    ]
    start(raw_loads, loads[:2])
    start(loads[2:])
    top[...] = jnp.full(top.shape, -1e30, F32)
    total[...] = jnp.zeros(total.shape, F32)
    wait(raw_loads)
    for which in range(2):
        unit[halves[which], :] = unit_rows(raw[which])[0].astype(BF16)

    @pl.loop(0, chunks)
    def _(k):
        copy_of(w_hbm, w_ref, w_sem, k).wait()
        for n in range(0, WIDE, TILE):
            here = columns_of(k, n, TILE)
            values = jnp.dot(unit[...], w_ref[:, here], preferred_element_type=F32)
            for half, scale in zip(halves, (SCALE_TEACHER, SCALE_STUDENT)):
                part = values[half, :] * scale
                logits[half, here] = part
                top[half, :] = functools.reduce(jnp.maximum, lane_tiles(part), top[half, :])

    peak = jnp.max(top[...], axis=1, keepdims=True)
    top[...] = jnp.broadcast_to(peak, top.shape)

    @pl.loop(0, chunks)
    def _(k):
        for which, (half, out, sem) in enumerate(zip(halves, (t_out, s_out), (t_sem, s_sem))):
            shift = top[half, :]
            for n in range(0, WIDE, TILE):
                tiles = lane_tiles(logits[half, columns_of(k, n, TILE)])
                tiles = [jnp.exp2(tile - shift) for tile in tiles]
                for t, tile in enumerate(tiles):
                    lanes = slice(n + t * LANES, n + (t + 1) * LANES)
                    exps[which, k, :, lanes] = tile.astype(BF16)
                total[half, :] += add_up(tiles)
            copy_of(exps.at[which], out, sem, k).start()

    sums = jnp.sum(total[...], axis=1, keepdims=True)
    for which, half in enumerate(halves):
        for k, column in enumerate((peak, sums)):
            first = (2 * which + k) * quarter
            pack_rows(out_ref.at[0, first : first + quarter], column[half, :])
    repeat(out_ref)
    wait(copies(exps.at[0], t_out, t_sem), copies(exps.at[1], s_out, s_sem))


def merged(stats_ref, which):
    parts, height, _ = stats_ref.shape
    quarter = height // 4
    first = 2 * which * quarter
    tops = [stats_ref[p, first : first + quarter, :] for p in range(parts)]
    top = functools.reduce(jnp.maximum, tops)
    sums = [
        stats_ref[p, first + quarter : first + 2 * quarter, :] * jnp.exp2(tops[p] - top)
        for p in range(parts)
    ]
    return top + jnp.log2(add_up(sums))


def column_pass(exp_hbm, exp_ref, sem, weight, out_ref):
    height = WIDE // LANES

    @pl.loop(0, exp_ref.shape[0])
    def _(k):
        copy_of(exp_hbm, exp_ref, sem, k).wait()
        sums = jnp.zeros((8, WIDE), F32)
        for g in range(0, exp_ref.shape[1], 16):
            shift = weight[g : g + 16, :]
            tiles = lane_tiles(exp_ref[k, g : g + 16, :].astype(F32))
            sums = sums + column_sums(jnp.concatenate([tile * shift for tile in tiles], axis=1))
        sums = jnp.sum(sums, axis=0, keepdims=True)
        block = jnp.concatenate(lane_tiles(sums), axis=0)
        for g in range(out_ref.shape[0]):
            out_ref[g, pl.ds(pl.multiple_of(k * height, height), height), :] = block


def first_column_kernel(place_ref, stats_ref, exp_hbm, *refs):
    factor_ref, out_ref, weight, exp_ref, sem = refs[-5:]
    start(copies(exp_hbm, exp_ref, sem))
    quarter = stats_ref.shape[1] // 4
    height = out_ref.shape[1] - 8
    own = stats_ref[pl.ds(place_ref[1], 1)][0]
    factor_ref[...] = jnp.zeros(factor_ref.shape, F32)
    rows = []
    for which in range(2):
        log_sum = merged(stats_ref, which)
        here = slice(which * quarter, (which + 1) * quarter)
        factor_ref[here, :] = jnp.exp2(
            own[2 * which * quarter : (2 * which + 1) * quarter, :] - log_sum
        )
        rows.append(log_sum)
    rows.append(jnp.zeros((8 - 2 * quarter, LANES), F32))
    logs = jnp.concatenate(rows, axis=0)
    for g in range(out_ref.shape[0]):
        out_ref[g, height:, :] = logs
    spread_rows(weight, factor_ref[:quarter, :])
    column_pass(exp_hbm, exp_ref, sem, weight, out_ref)


def column_kernel(sums_ref, factor_ref, exp_hbm, *refs):
    out_ref, weight, exp_ref, sem = refs[-4:]
    start(copies(exp_hbm, exp_ref, sem))
    quarter = weight.shape[0] // LANES
    scale = 1.0 / add_up([sums_ref[p, :quarter, :] for p in range(sums_ref.shape[0])])
    spread_rows(weight, scale * factor_ref[:quarter, :])
    column_pass(exp_hbm, exp_ref, sem, weight, out_ref)


def column_scales(cols, height):
    return 1.0 / add_up([ref[g, :height, :] for ref in cols for g in range(ref.shape[0])])


def chunk_scales(scales, k):
    height = WIDE // LANES
    return scales[pl.ds(pl.multiple_of(k * height, height), height), :]


def add_row_sums(rows, values, scale):
    for g in range(0, values.shape[0], 32):
        total = rows[g : g + 32, :]
        for t, tile in enumerate(lane_tiles(values[g : g + 32, :].astype(F32))):
            total = total + tile * scale[t : t + 1, :]
        rows[g : g + 32, :] = total


def row_kernel(count, *refs):
    cols, (factor_ref, exp_hbm) = refs[:count], refs[count : count + 2]
    out_ref, scales, rows, exp_ref, sem = refs[-5:]
    start(copies(exp_hbm, exp_ref, sem))
    scales[...] = column_scales(cols, scales.shape[0])
    rows[...] = jnp.zeros(rows.shape, F32)
    quarter = rows.shape[0] // LANES
    out_ref[0] = jnp.zeros(out_ref.shape[1:], F32)

    @pl.loop(0, exp_ref.shape[0])
    def _(k):
        copy_of(exp_hbm, exp_ref, sem, k).wait()
        add_row_sums(rows, exp_ref.at[k], chunk_scales(scales, k))

    pack_rows(out_ref.at[0, :quarter], jnp.sum(rows[...], axis=1, keepdims=True))
    out_ref[0, :quarter, :] = out_ref[0, :quarter, :] * factor_ref[:quarter, :]
    repeat(out_ref)


def own_back_kernel(before_ref, exp_hbm, w_hbm, back_ref, exp_ref, w_ref, exp_sem, w_sem):
    start(copies(exp_hbm, exp_ref, exp_sem), copies(w_hbm, w_ref, w_sem))
    back_ref[...] = jnp.zeros(back_ref.shape, F32)

    @pl.loop(0, exp_ref.shape[0])
    def _(k):
        copy_of(exp_hbm, exp_ref, exp_sem, k).wait()
        copy_of(w_hbm, w_ref, w_sem, k).wait()
        back_ref[...] += nt_dot(exp_ref[k], w_ref[:, columns_of(k)])


def relative_logs(logs, lse, which, shift=0.0):
    own = lse.shape[0] // (len(logs) - 1)
    quarter = own // LANES
    for g, ref in enumerate(logs[1:]):
        first = ref.shape[1] - 8 + which * quarter
        spread_rows(lse.at[g * own : (g + 1) * own], ref[0, first : first + quarter, :] - shift)


def student_rows_kernel(protos, place_ref, factor_ref, t_ref, own_ref, *refs):
    unit_ref, feat_ref, scaled_ref, t_unit, turned = refs[-5:]
    t_unit[...] = unit_rows(t_ref[...])[0].astype(BF16)
    own = own_ref.shape[0]
    groups = turned.shape[1] // own
    raw = refs[: groups - 1]
    quarter, feats = own // LANES, feat_ref.shape[0]
    for g in range(groups):
        half = unit_rows((raw[g - 1] if g else own_ref)[...])[0].astype(BF16)
        if g:
            unit_ref[(g - 1) * own : g * own, :] = half
        half = half.astype(F32)
        for a in range(0, own, LANES):
            first = g * own + a
            turned[:, first : first + LANES] = jnp.transpose(half[a : a + LANES, :]).astype(BF16)
    feat = turned[pl.ds(pl.multiple_of(place_ref[0] * feats, feats), feats), :]
    feat_ref[...] = feat
    for a in range(quarter):
        lanes = slice(a * LANES, (a + 1) * LANES)
        factor = factor_ref[quarter + a : quarter + a + 1, :] * protos
        scaled_ref[:, lanes] = (feat[:, lanes].astype(F32) * factor).astype(BF16)


def probabilities(unit, w_ref, k, lse, scale, use):
    for n in range(0, WIDE, TILE):
        logits = jnp.dot(
            unit[...], w_ref[:, columns_of(k, n, TILE)], preferred_element_type=F32
        )
        shift = lse[...]
        use(n, [jnp.exp2(tile * scale - shift) for tile in lane_tiles(logits)])


def student_kernel(
    log_protos, first, groups, unit, feat_ref, scaled_ref, exp_hbm, w_hbm, *refs
):
    logs = refs[:groups]
    grad, token_ref, lse, prob, exp_ref, w_ref, exp_sem, w_sem = refs[-8:]
    own, count = exp_ref.shape[1], exp_ref.shape[0]
    exp_loads = copies(exp_hbm, exp_ref, exp_sem, first, 0, count)
    w_loads = copies(w_hbm, w_ref, w_sem, first, 0, count)
    start(w_loads, exp_loads)
    token_ref[...] = jnp.zeros(token_ref.shape, F32)
    relative_logs(logs, lse, 1, log_protos)

    @pl.loop(0, count)
    def _(k):
        copy_of(w_hbm, w_ref, w_sem, k, first).wait()

        def use(n, tiles):
            for t, tile in enumerate(tiles):
                prob[:, n + t * LANES : n + (t + 1) * LANES] = tile.astype(BF16)

        probabilities(unit, w_ref, k, lse, SCALE_STUDENT, use)
        copy_of(exp_hbm, exp_ref, exp_sem, k, first).wait()
        values = jnp.dot(scaled_ref[...], exp_ref[k], preferred_element_type=F32)
        values = values + jnp.dot(feat_ref[:, own:], prob[...], preferred_element_type=F32)
        grad[:, columns_of(k)] = values.astype(BF16)


def as_three(value):
    high = value.astype(BF16)
    rest = value - high.astype(F32)
    middle = rest.astype(BF16)
    return high, middle, (rest - middle.astype(F32)).astype(BF16)


def last_kernel(groups, factor_ref, own_hbm, student_hbm, exp_hbm, w_hbm, *refs):
    units, refs = refs[: groups - 1], refs[groups - 1 :]
    logs, cols, refs = refs[:groups], refs[groups : 2 * groups], refs[2 * groups :]
    (
        prob_hbm, scale_ref, out_ref, unit, lse, rows, own_rows, back, scaled, sums, prob_ref,
        exp_ref, w_ref, own_ref, student_ref, prob_sem, exp_sem, w_sem, sem,
    ) = refs[-19:]
    w_loads, exp_loads = copies(w_hbm, w_ref, w_sem), copies(exp_hbm, exp_ref, exp_sem)
    late_loads = whole_copies([(own_hbm, own_ref), (student_hbm, student_ref)], sem)
    start(w_loads, exp_loads)
    start(late_loads)
    slots, others, _ = prob_ref.shape
    own, chunks = exp_ref.shape[1], exp_ref.shape[0]
    tiles = (own + others) // LANES
    quarter = own // LANES
    scale_ref[...] = column_scales(cols, scale_ref.shape[0])
    rows[...] = jnp.zeros(rows.shape, F32)
    own_rows[...] = jnp.zeros(own_rows.shape, F32)
    back[...] = jnp.zeros(back.shape, F32)
    relative_logs(logs, lse, 0)
    for g in range(groups - 1):
        unit[g * own : (g + 1) * own, :] = units[g][...]
    partner = slice((groups // 2 - 1) * own, groups // 2 * own)

    def store(k):
        return pltpu.make_async_copy(prob_ref.at[lax.rem(k, slots)], prob_hbm.at[k], prob_sem.at[k])

    @pl.loop(0, chunks)
    def _(k):
        copy_of(w_hbm, w_ref, w_sem, k).wait()
        slot = lax.rem(k, slots)
        scale = chunk_scales(scale_ref, k)

        @pl.when(k >= slots)
        def _():
            store(k - slots).wait()

        def use(n, tiles):
            for t, tile in enumerate(tiles):
                prob_ref[slot, :, n + t * LANES : n + (t + 1) * LANES] = tile.astype(BF16)
            first = n // LANES
            tiles = [tile * scale[first + t : first + t + 1, :] for t, tile in enumerate(tiles)]
            rows[...] += add_up(tiles)
            for t, tile in enumerate(tiles):
                scaled[:, n + t * LANES : n + (t + 1) * LANES] = tile[partner, :].astype(BF16)

        probabilities(unit, w_ref, k, lse, SCALE_TEACHER, use)
        store(k).start()
        back[...] += nt_dot(scaled[...], w_ref[:, columns_of(k)])
        copy_of(exp_hbm, exp_ref, exp_sem, k).wait()
        add_row_sums(own_rows, exp_ref.at[k], scale)

    sums[...] = jnp.zeros(sums.shape, F32)
    pack_rows(sums.at[:quarter], jnp.sum(own_rows[...], axis=1, keepdims=True))
    sums[:quarter, :] = sums[:quarter, :] * factor_ref[:quarter, :]
    pack_rows(sums.at[quarter:tiles], jnp.sum(rows[...], axis=1, keepdims=True))
    wait(late_loads)
    half = unit_rows(own_ref[...])[0].astype(BF16).astype(F32)
    inner = jnp.sum(half * back[...], axis=1, keepdims=True)
    pack_rows(sums.at[tiles : tiles + quarter], inner)
    parts = out_ref.shape[0]
    share = own // parts
    protos = 1.0 * out_ref.shape[0] * w_ref.shape[1]
    student = []
    for a in range(quarter):
        factor = to_column(factor_ref[quarter + a : quarter + a + 1, :] * protos)
        student.append(student_ref[a * LANES : (a + 1) * LANES, :] * factor)
    student = jnp.concatenate(student, axis=0).astype(BF16)
    terms = list(as_three(sums[...]))
    terms.append(jnp.zeros((sums.shape[0], out_ref.shape[2] - 3 * LANES), BF16))
    terms = jnp.concatenate(terms, axis=1)
    for p in range(parts):
        here = slice(p * share, (p + 1) * share)
        out_ref[p] = jnp.concatenate(
            [student[here, :], back[here, :].astype(BF16), terms], axis=0
        )
    for k in range(max(0, chunks - slots), chunks):
        store(k).wait()


def total_sums(message_ref, first):
    parts = message_ref.shape[0]
    each = [
        add_up([t.astype(F32) for t in lane_tiles(message_ref[p, first:, : 3 * LANES])[::-1]])
        for p in range(parts)
    ]
    return add_up(each)


def rows_kernel(tiles, protos, place_ref, s_hbm, message_ref, logs_ref, *refs):
    out_ref, loss_ref, sums_ref, weight, s_ref, sem = refs[-6:]
    parts = message_ref.shape[0]
    share, own = out_ref.shape[1], weight.shape[0]
    mine = pl.ds(pl.multiple_of(place_ref[1] * share, share), share)
    load = pltpu.make_async_copy(s_hbm.at[mine], s_ref, sem)
    load.start()
    quarter = own // LANES
    first = tiles // 2
    totals = total_sums(message_ref, 2 * share)
    sums_ref[...] = totals
    scale = 1.0 / totals[first : first + quarter, :]
    spread_rows(weight, scale)
    total = add_up([message_ref[p, :share, :].astype(F32) for p in range(parts)])
    paired = add_up([message_ref[p, share : 2 * share, :].astype(F32) for p in range(parts)])
    total = total - paired * (weight[mine, :1] * protos)
    load.wait()
    unit, length = unit_rows(s_ref[...])
    total = (total - unit * jnp.sum(unit * total, axis=-1, keepdims=True)) / length
    out_ref[0] = total.astype(BF16)
    repeat(out_ref)
    height = logs_ref.shape[1] - 8
    logs = logs_ref[0, height + quarter : height + 2 * quarter, :]
    terms = logs / LOG2E - totals[tiles : tiles + quarter, :] * scale / TEMP_STUDENT
    loss_ref[...] = jnp.broadcast_to(jnp.sum(terms) / (tiles * LANES), loss_ref.shape)


def grad_kernel(counts, protos, exp_hbm, prob_hbm, feat_ref, scale_ref, sums_ref, factor_ref, *refs):
    parts = refs[: len(counts)]
    out_hbm, scaled, exp_ref, prob_ref, out, part_ref, exp_sem, prob_sem, sem, part_sem = refs[-10:]
    part_loads, where = {}, []
    for i, (count, part) in enumerate(zip(counts, parts)):
        for k in range(count):
            if i in FAR:
                slot = len(part_loads)
                part_loads[len(where)] = copy_of(part, part_ref, part_sem, slot, k - slot)
                where.append((part_ref, slot))
            else:
                where.append((part, k))
    exp_loads = copies(exp_hbm, exp_ref, exp_sem)
    prob_loads = copies(prob_hbm, prob_ref, prob_sem)
    start(exp_loads[:1], prob_loads[:1])
    start(list(part_loads.values()))
    start(exp_loads[1:], prob_loads[1:])
    own = exp_ref.shape[1]
    tiles = (own + prob_ref.shape[1]) // LANES
    rows = protos / sums_ref[:tiles, :]
    for a in range(tiles):
        other = (a + tiles // 2) % tiles
        feat = feat_ref[:, other * LANES : (other + 1) * LANES].astype(F32)
        row = rows[a : a + 1, :]
        if a < own // LANES:
            row = row * factor_ref[a : a + 1, :]
        scaled[:, a * LANES : (a + 1) * LANES] = (feat * row).astype(BF16)
    stores = copies(out, out_hbm, sem)
    for k, store in enumerate(stores):
        exp_loads[k].wait()
        prob_loads[k].wait()
        paired = jnp.dot(scaled[:, :own], exp_ref[k], preferred_element_type=F32)
        paired = paired + jnp.dot(
            scaled[:, own:], prob_ref[k], preferred_element_type=F32
        )
        part, there = where[k]
        if k in part_loads:
            part_loads[k].wait()
        for t, tile in enumerate(lane_tiles(paired)):
            lanes = slice(k * WIDE + t * LANES, k * WIDE + (t + 1) * LANES)
            scale = scale_ref[lanes.start // LANES : lanes.stop // LANES, :]
            own_part = part[:, there * WIDE + t * LANES : there * WIDE + (t + 1) * LANES]
            out[:, lanes] = (own_part.astype(F32) - tile * scale).astype(BF16)
        store.start()
    for store in stores:
        store.wait()


SMEM = pl.BlockSpec(memory_space=pltpu.SMEM)
VMEM = pl.BlockSpec(memory_space=pltpu.VMEM)
ANY = pl.BlockSpec(memory_space=pl.ANY)


def params(nbytes):
    return pltpu.CompilerParams(vmem_limit_bytes=int(nbytes) + 8 * 2**20)


def cost(flops, nbytes, exps=0):
    return pl.CostEstimate(flops=int(flops), bytes_accessed=int(nbytes), transcendentals=int(exps))


def exchange(value, axis):
    return lax.all_to_all(value, axis, 0, 0)


def following(value, axis):
    n = lax.axis_size(axis)
    return [lax.ppermute(value, axis, [(i, (i - s) % n) for i in range(n)]) for s in range(1, n)]


def tree_sum(value, axis):
    n = lax.axis_size(axis)
    values = [value] + [
        lax.ppermute(value, axis, [(i, i ^ s) for i in range(n)]) for s in range(1, n)
    ]
    while len(values) > 1:
        values = [a + b for a, b in zip(values[::2], values[1::2])]
    return values[0]


def local(teacher_feats, student_feats, proto_weight):
    parts, groups = lax.axis_size("proto"), lax.axis_size("batch")
    own, width = teacher_feats.shape
    local_protos = proto_weight.shape[1]
    rows = own * groups
    others = rows - own
    protos = local_protos * parts
    feats = width // groups
    share = own // parts
    tiles = rows // LANES
    height = local_protos // LANES
    chunks = local_protos // WIDE
    place = jnp.stack([lax.axis_index("batch"), lax.axis_index("proto")]).astype(jnp.int32)
    struct = jax.ShapeDtypeStruct
    weight_bytes = 2 * width * local_protos
    exp_bytes = 2 * own * local_protos
    others_bytes = 2 * others * local_protos
    spread = pltpu.VMEM((own, LANES), F32)
    w_buffer = pltpu.VMEM((width, local_protos), BF16)
    exp_buffer = pltpu.VMEM((chunks, own, WIDE), BF16)
    sems = pltpu.SemaphoreType.DMA((chunks,))
    log_protos = math.log2(protos)
    token = struct((8, LANES), F32)

    def far(value):
        return pltpu.with_memory_space_constraint(value, pltpu.HBM)

    weight = far(proto_weight)
    teacher_rows, student_rows = far(teacher_feats), far(student_feats)
    s_all = following(student_feats, "batch")

    exps = pltpu.HBM((chunks, own, WIDE), BF16)
    t_exp, s_exp, stats = pl.pallas_call(
        stats_kernel,
        in_specs=[ANY] * 3,
        out_specs=[ANY, ANY, VMEM],
        out_shape=[
            exps,
            exps,
            struct((parts, 4 * own // LANES, LANES), F32),
        ],
        scratch_shapes=[
            pltpu.VMEM((2, own, width), BF16),
            w_buffer,
            pltpu.VMEM((2 * own, width), BF16),
            pltpu.VMEM((2, chunks, own, WIDE), BF16),
            pltpu.VMEM((2 * own, local_protos), F32),
            pltpu.VMEM((2 * own, LANES), F32),
            pltpu.VMEM((2 * own, LANES), F32),
            pltpu.SemaphoreType.DMA((2,)),
            sems, sems, sems,
        ],
        compiler_params=params(weight_bytes + 6 * exp_bytes),
        cost_estimate=cost(4 * own * width * local_protos, weight_bytes),
        name="own_rows",
    )(teacher_rows, student_rows, weight)
    t_exp, s_exp = far(t_exp), far(s_exp)

    back_student = pl.pallas_call(
        own_back_kernel,
        in_specs=[ANY] * 3,
        out_specs=VMEM,
        out_shape=struct((own, width), F32),
        scratch_shapes=[exp_buffer, w_buffer, sems, sems],
        compiler_params=params(weight_bytes + exp_bytes),
        cost_estimate=cost(2 * own * width * local_protos, weight_bytes),
        name="own_back",
    )(stats, s_exp, weight)

    stats = exchange(stats, "proto")

    first_shape = (1, height + 8, LANES)
    factor, cols = pl.pallas_call(
        first_column_kernel,
        in_specs=[SMEM, VMEM, ANY, ANY] + [ANY] * (groups - 1),
        out_specs=[VMEM, VMEM],
        out_shape=[token, struct(first_shape, F32)],
        scratch_shapes=[spread, exp_buffer, sems],
        compiler_params=params(exp_bytes),
        cost_estimate=cost(2 * own * local_protos, exp_bytes),
        name="first_columns",
    )(place, stats, t_exp, back_student, *s_all)

    unit, feat, scaled, t_unit = pl.pallas_call(
        functools.partial(student_rows_kernel, float(protos)),
        in_specs=[SMEM, VMEM, VMEM, VMEM] + [VMEM] * (groups - 1) + [ANY],
        out_specs=[VMEM] * 4,
        out_shape=[
            struct((others, width), BF16), struct((feats, rows), BF16), struct((feats, own), BF16),
            struct((own, width), BF16),
        ],
        scratch_shapes=[pltpu.VMEM((width, rows), BF16)],
        compiler_params=params(2 * rows * width),
        cost_estimate=cost(8 * rows * width, 2 * rows * width),
        name="student_rows",
    )(place, factor, teacher_feats, student_feats, *s_all, cols)
    t_all = following(t_unit, "batch")
    cols = [cols] + following(cols, "batch")
    logs = cols

    counts = [c * chunks // 8 for c in (1, 1, 1, 5)]
    grad_parts = []

    def student_piece(before):
        turn = len(grad_parts)
        first, count = sum(counts[:turn]), counts[turn]
        grad_part, done = pl.pallas_call(
            functools.partial(student_kernel, log_protos, first, groups),
            in_specs=[VMEM] * 3 + [ANY] * 2 + [VMEM] * groups + [ANY],
            out_specs=[VMEM, VMEM],
            out_shape=[struct((feats, count * WIDE), BF16), token],
            scratch_shapes=[
                pltpu.VMEM((others, LANES), F32),
                pltpu.VMEM((others, WIDE), BF16),
                pltpu.VMEM((count, own, WIDE), BF16),
                pltpu.VMEM((width, count * WIDE), BF16),
            ]
            + [pltpu.SemaphoreType.DMA((count,))] * 2,
            compiler_params=params(16 * 2**20),
            cost_estimate=cost(2.5 * rows * width * WIDE * count, 2 * width * WIDE * count),
            name="student_side",
        )(unit, feat, scaled, s_exp, weight, *logs, before)
        grad_parts.append(grad_part)
        return done

    done = unit
    for turn in range(SWEEPS - 1):
        late = t_all if turn == 1 else []
        sums = pl.pallas_call(
            functools.partial(row_kernel, len(cols)),
            in_specs=[VMEM] * (len(cols) + 1) + [ANY] * (2 + len(late)),
            out_specs=VMEM,
            out_shape=struct((parts, 8, LANES), F32),
            scratch_shapes=[pltpu.VMEM((height, LANES), F32), spread, exp_buffer, sems],
            compiler_params=params(exp_bytes),
            cost_estimate=cost(2 * own * local_protos, exp_bytes),
            name="rows",
        )(*cols, factor, t_exp, done, *late)
        done = student_piece(sums)
        sums = exchange(sums, "proto")
        middle = turn < SWEEPS - 2
        cols = pl.pallas_call(
            column_kernel,
            in_specs=[VMEM, VMEM, ANY, ANY],
            out_specs=VMEM,
            out_shape=struct((groups if middle else 1, height, LANES), F32),
            scratch_shapes=[spread, exp_buffer, sems],
            compiler_params=params(exp_bytes),
            cost_estimate=cost(2 * own * local_protos, exp_bytes),
            name="columns",
        )(sums, factor, t_exp, done)
        if turn < SWEEPS - 2:
            done = student_piece(cols)
        if middle:
            cols = [exchange(cols, "batch")]
        else:
            cols = [cols] + following(cols, "batch")

    sum_rows = -(-(tiles + own // LANES) // 16) * 16
    message_shape = (parts, 2 * share + sum_rows, width)
    prob, col_scale, message = pl.pallas_call(
        functools.partial(last_kernel, groups),
        in_specs=[VMEM] + [ANY] * 4 + [VMEM] * (3 * groups - 1) + [ANY],
        out_specs=[ANY, VMEM, VMEM],
        out_shape=[
            pltpu.HBM((chunks, others, WIDE), BF16),
            struct((height, LANES), F32),
            struct(message_shape, BF16),
        ],
        scratch_shapes=[
            pltpu.VMEM((others, width), BF16),
            pltpu.VMEM((others, LANES), F32),
            pltpu.VMEM((others, LANES), F32),
            spread,
            pltpu.VMEM((own, width), F32),
            pltpu.VMEM((own, WIDE), BF16),
            pltpu.VMEM((sum_rows, LANES), F32),
            pltpu.VMEM((min(chunks, 3), others, WIDE), BF16),
            exp_buffer,
            w_buffer,
            pltpu.VMEM((own, width), BF16),
            pltpu.VMEM((own, width), F32),
            sems, sems, sems,
            pltpu.SemaphoreType.DMA((2,)),
        ],
        compiler_params=params(20 * 2**20 + weight_bytes + exp_bytes),
        cost_estimate=cost(2 * rows * width * local_protos, others_bytes),
        name="last_rows",
    )(
        factor, student_rows, far(back_student), t_exp, weight, *t_all, *logs, *cols, done,
    )
    done = student_piece(message)
    message = exchange(message, "proto")

    grad_rows, loss_part, sums = pl.pallas_call(
        functools.partial(rows_kernel, tiles, float(protos)),
        in_specs=[SMEM, ANY, VMEM, VMEM, ANY],
        out_specs=[VMEM] * 3,
        out_shape=[struct((parts, share, width), BF16), token, struct((sum_rows, LANES), F32)],
        scratch_shapes=[spread, pltpu.VMEM((share, width), BF16), pltpu.SemaphoreType.DMA],
        compiler_params=params(0),
        name="row_grads",
    )(place, student_rows, message, logs[0], done)
    grad_rows = exchange(grad_rows, "proto").reshape(own, width).astype(F32)
    loss = tree_sum(loss_part, "batch")[0, 0]

    grad_weight = pl.pallas_call(
        functools.partial(grad_kernel, counts, float(protos)),
        in_specs=[ANY] * 2
        + [VMEM] * 4
        + [ANY if i in FAR else VMEM for i in range(len(counts))],
        out_specs=ANY,
        out_shape=struct((feats, local_protos), BF16),
        scratch_shapes=[
            pltpu.VMEM((feats, rows), BF16),
            exp_buffer,
            pltpu.VMEM((chunks, others, WIDE), BF16),
            pltpu.VMEM((feats, local_protos), BF16),
            pltpu.VMEM((feats, sum(counts[i] for i in FAR) * WIDE), BF16),
            sems, sems, sems, sems,
        ],
        compiler_params=params(exp_bytes + others_bytes + 4 * feats * local_protos),
        cost_estimate=cost(2 * feats * rows * local_protos, others_bytes),
        name="weight_grads",
    )(t_exp, far(prob), feat, col_scale, sums, factor, *[far(x) if i in FAR else x for i, x in enumerate(grad_parts)])
    return grad_weight, grad_rows, loss


def solution(mesh):
    return jax.shard_map(
        local,
        mesh=mesh,
        in_specs=(P("batch", None), P("batch", None), P(None, "proto")),
        out_specs=(P("batch", "proto"), P("batch", None), P()),
        check_vma=False,
    )
```
